32 devices in a mesh: weight: 4 (over z), context: 2 (over x), tensor: 4 (over y, core).
Axes of the slice: x: 2, y: 2, z: 4, core: 2. Of those that a mesh axis runs over, the one named last changes fastest.
Arguments:
- tokens: bfloat16 [4, 32, 32, 2240], P('weight', 'context'), may hold values from -6 to 6
- caption: bfloat16 [4, 300, 2240], P('weight', 'context'), may hold values from -6 to 6
- caption_lengths: int32 [4], P('weight'), may hold values from 37 to 300, as said below
- adapter_index: int32 [4], P('weight'), may hold values from 0 to 7
- modulation: float32 [4, 6, 2240], P('weight'), may hold values from -1 to 1
- cotangent: bfloat16 [4, 32, 32, 2240], P('weight', 'context'), may hold values from -6 to 6
- qkv_weight: bfloat16 [2240, 3, 2240], P('weight'), may hold values from -1 to 1
- proj_weight: bfloat16 [2240, 2240], P(None, 'weight'), may hold values from -1 to 1
- cross_q_weight: bfloat16 [2240, 2240], P('weight'), may hold values from -0.125 to 0.125
- cross_kv_weight: bfloat16 [2240, 2, 2240], P('weight'), may hold values from -0.125 to 0.125
- cross_out_weight: bfloat16 [2240, 2240], P(None, 'weight'), may hold values from -0.5 to 0.5
- inverted_weight: bfloat16 [2240, 2, 5600], P('weight', None, 'tensor'), may hold values from -0.125 to 0.125
- depth_weight: bfloat16 [3, 3, 2, 5600], P(None, None, None, 'tensor'), may hold values from -2 to 2
- point_weight: bfloat16 [5600, 2240], P('tensor', 'weight'), may hold values from -0.078125 to 0.078125
- qkv_down: bfloat16 [8, 2240, 16], replicated, may hold values from -0.125 to 0.125
- qkv_up: bfloat16 [8, 16, 3, 2240], replicated, may hold values from -0.75 to 0.75
- proj_down: bfloat16 [8, 2240, 16], replicated, may hold values from -1 to 1
- proj_up: bfloat16 [8, 16, 2240], replicated, may hold values from -0.75 to 0.75
- query_down: bfloat16 [8, 2240, 16], replicated, may hold values from -0.125 to 0.125
- query_up: bfloat16 [8, 16, 2240], replicated, may hold values from -0.75 to 0.75
- kv_down: bfloat16 [8, 2240, 16], replicated, may hold values from -0.125 to 0.125
- kv_up: bfloat16 [8, 16, 2, 2240], replicated, may hold values from -0.75 to 0.75
- cross_down: bfloat16 [8, 2240, 16], replicated, may hold values from -0.5 to 0.5
- cross_up: bfloat16 [8, 16, 2240], replicated, may hold values from -0.75 to 0.75
- inverted_down: bfloat16 [8, 2240, 16], replicated, may hold values from -0.125 to 0.125
- inverted_up: bfloat16 [8, 16, 2, 5600], replicated, may hold values from -0.75 to 0.75
- point_down: bfloat16 [8, 5600, 16], replicated, may hold values from -0.078125 to 0.078125
- point_up: bfloat16 [8, 16, 2240], replicated, may hold values from -0.75 to 0.75
Outputs:
- output: float32 [4, 32, 32, 2240], P('weight', 'context')
- input_grad: float32 [4, 32, 32, 2240], P('weight', 'context')
- qkv_down_sum: float32 [8, 2240, 16], P(None, ('weight', 'context'), 'tensor')
- qkv_up_sum: float32 [8, 16, 3, 2240], P(None, 'tensor', None, ('weight', 'context'))
- proj_down_sum: float32 [8, 2240, 16], P(None, ('weight', 'context'), 'tensor')
- proj_up_sum: float32 [8, 16, 2240], P(None, 'tensor', ('weight', 'context'))
- query_down_sum: float32 [8, 2240, 16], P(None, ('weight', 'context'), 'tensor')
- query_up_sum: float32 [8, 16, 2240], P(None, 'tensor', ('weight', 'context'))
- kv_down_sum: float32 [8, 2240, 16], P(None, ('weight', 'context'), 'tensor')
- kv_up_sum: float32 [8, 16, 2, 2240], P(None, 'tensor', None, ('weight', 'context'))
- cross_down_sum: float32 [8, 2240, 16], P(None, ('weight', 'context'), 'tensor')
- cross_up_sum: float32 [8, 16, 2240], P(None, 'tensor', ('weight', 'context'))
- inverted_down_sum: float32 [8, 2240, 16], P(None, ('weight', 'context'), 'tensor')
- inverted_up_sum: float32 [8, 16, 2, 5600], P(None, 'tensor', None, ('weight', 'context'))
- point_down_sum: float32 [8, 5600, 16], P(None, ('weight', 'context'), 'tensor')
- point_up_sum: float32 [8, 16, 2240], P(None, 'tensor', ('weight', 'context'))
The draws below stay inside these ranges and needn't reach their ends.
Inputs may be any that keep to these rules, and one draw needn't show every extreme that they name: Sequence b attends to its first caption_lengths[b] caption tokens; in every draw some sequence has all 300 and another has 37.
All inputs are finite; a program needn't handle non-finite values.
Results may differ from the reference program's by a relative error of at most 0.035.
The reference program's roundings to bfloat16 on the way count: a program that leaves them out, or rounds other values in their place, can miss the bound.
Values may be sent and summed in bfloat16 or wider, within the bound.
No kernel may reach another device: no remote copies, remote signals or barrier semaphores. Data moves between devices by JAX's collectives and lax.ppermute only.
A program may use at most 448 MiB of HBM per device.

```python
import jax
import jax.numpy as jnp
from jax import lax

D = 2240
HEADS = 70
HD = 32
FF = 5600
TEXT = 300
GRID = 32
R = 16
ADAPTERS = 8
SEQS = 4


def draw_caption_lengths(key, part):
    key_lens, key_high, key_low = jax.random.split(key, 3)
    lengths = jax.random.randint(key_lens, (SEQS,), TEXT // 8, TEXT + 1)
    highest_at = jax.random.randint(key_high, (), 0, SEQS)
    lowest_at = (highest_at + 1 + jax.random.randint(key_low, (), 0, SEQS - 1)) % SEQS
    lengths = lengths.at[highest_at].set(TEXT)
    lengths = lengths.at[lowest_at].set(TEXT // 8)
    return lengths.astype(jnp.int32)


def draw_qkv_weight(key, part):
    key_rows, key_common = jax.random.split(jax.random.fold_in(key, 7))
    scale_rows = D ** (-0.5)
    entries = jnp.clip(jax.random.normal(key_rows, (D, 3, D), jnp.float32), -4.0, 4.0)
    common = jnp.clip(jax.random.normal(key_common, (1, 3, D), jnp.float32), -4.0, 4.0)
    values = (0.8 * entries + 0.6 * common) * scale_rows
    return values.astype(jnp.bfloat16)


def place_ends(values, rng, smallest, high):
    spot = [jax.random.randint(jax.random.fold_in(rng, axis), (), 0, length) for axis, length in enumerate(values.shape)]
    longest = values.shape.index(max(values.shape))
    neighbour = spot[:longest] + [(spot[longest] + 1) % values.shape[longest]] + spot[longest + 1:]
    return values.at[tuple(spot)].set(smallest).at[tuple(neighbour)].set(high)


def level_of(key, dims, cuts, smallest, high):
    gain, own = 1.0, jax.random.fold_in(key, 6)
    for dim, shards_of in cuts:
        draws = jnp.exp(jax.random.uniform(jax.random.fold_in(own, dim), (shards_of,), jnp.float32, smallest / len(cuts), high / len(cuts)))
        gain = gain * jnp.repeat(draws, dims[dim] // shards_of).reshape([-1 if axis == dim else 1 for axis in range(len(dims))])
    return gain


def scatter_about(key, shape, deviation, most, cuts=(), dtype=jnp.bfloat16):
    level = level_of(key, shape, cuts, -0.22, 0.18) if cuts else 1.0
    array = jax.random.normal(key, shape, jnp.float32) * deviation * level
    return jnp.minimum(jnp.maximum(array, -most), most).astype(dtype)


def setup_inputs(seed: int = 0) -> dict:
    arg_keys = jax.random.split(jax.random.key(seed), 29)
    tokens = scatter_about(arg_keys[0], (SEQS, GRID, GRID, D), 1.0, 6.0, ((0, 4), (1, 2)))
    caption = scatter_about(arg_keys[1], (SEQS, TEXT, D), 1.0, 6.0, ((0, 4), (1, 2)))
    caption_lengths = draw_caption_lengths(jax.random.fold_in(arg_keys[28], 71), 0)
    adapter_index = place_ends(jax.random.randint(arg_keys[3], (SEQS,), 0, ADAPTERS), jax.random.fold_in(arg_keys[3], 1), 0, ADAPTERS - 1).astype(jnp.int32)
    modulation = jnp.clip(jax.random.uniform(arg_keys[4], (SEQS, 6, D), jnp.float32, -1.0, 1.0) * level_of(arg_keys[4], (SEQS, 6, D), ((0, 4),), -0.4, 0.0), -1.0, 1.0)
    cotangent = scatter_about(arg_keys[5], (SEQS, GRID, GRID, D), 1.0, 6.0, ((0, 4), (1, 2)))
    qkv_weight = draw_qkv_weight(jax.random.fold_in(arg_keys[28], 71), 0)
    proj_weight = scatter_about(arg_keys[7], (D, D), (max(D // (GRID * GRID // 16), 1)) ** -0.5, 1.0, ((1, 4),))
    cross_q_weight = scatter_about(arg_keys[8], (D, D), D ** -0.5, 0.125, ((0, 4),))
    cross_kv_weight = scatter_about(arg_keys[9], (D, 2, D), D ** -0.5, 0.125, ((0, 4),))
    cross_out_weight = scatter_about(arg_keys[10], (D, D), (max(D // 16, 1)) ** -0.5, 0.5, ((1, 4),))
    inverted_weight = scatter_about(arg_keys[11], (D, 2, FF), D ** -0.5, 0.125, ((0, 4), (2, 4)))
    depth_weight = scatter_about(arg_keys[12], (3, 3, 2, FF), 9 ** -0.5, 2.0, ((3, 4),))
    point_weight = scatter_about(arg_keys[13], (FF, D), FF ** -0.5, 0.078125, ((0, 4), (1, 4)))
    qkv_down = scatter_about(arg_keys[14], (ADAPTERS, D, R), D ** -0.5, 0.125)
    qkv_up = scatter_about(arg_keys[15], (ADAPTERS, R, 3, D), (4 * R) ** -0.5, 0.75)
    proj_down = scatter_about(arg_keys[16], (ADAPTERS, D, R), (max(D // (GRID * GRID // 16), 1)) ** -0.5, 1.0)
    proj_up = scatter_about(arg_keys[17], (ADAPTERS, R, D), (4 * R) ** -0.5, 0.75)
    query_down = scatter_about(arg_keys[18], (ADAPTERS, D, R), D ** -0.5, 0.125)
    query_up = scatter_about(arg_keys[19], (ADAPTERS, R, D), (4 * R) ** -0.5, 0.75)
    kv_down = scatter_about(arg_keys[20], (ADAPTERS, D, R), D ** -0.5, 0.125)
    kv_up = scatter_about(arg_keys[21], (ADAPTERS, R, 2, D), (4 * R) ** -0.5, 0.75)
    cross_down = scatter_about(arg_keys[22], (ADAPTERS, D, R), (max(D // 16, 1)) ** -0.5, 0.5)
    cross_up = scatter_about(arg_keys[23], (ADAPTERS, R, D), (4 * R) ** -0.5, 0.75)
    inverted_down = scatter_about(arg_keys[24], (ADAPTERS, D, R), D ** -0.5, 0.125)
    inverted_up = scatter_about(arg_keys[25], (ADAPTERS, R, 2, FF), (4 * R) ** -0.5, 0.75)
    point_down = scatter_about(arg_keys[26], (ADAPTERS, FF, R), FF ** -0.5, 0.078125)
    point_up = scatter_about(arg_keys[27], (ADAPTERS, R, D), (4 * R) ** -0.5, 0.75)
    return {"tokens": tokens, "caption": caption, "caption_lengths": caption_lengths, "adapter_index": adapter_index, "modulation": modulation, "cotangent": cotangent, "qkv_weight": qkv_weight, "proj_weight": proj_weight, "cross_q_weight": cross_q_weight, "cross_kv_weight": cross_kv_weight, "cross_out_weight": cross_out_weight, "inverted_weight": inverted_weight, "depth_weight": depth_weight, "point_weight": point_weight, "qkv_down": qkv_down, "qkv_up": qkv_up, "proj_down": proj_down, "proj_up": proj_up, "query_down": query_down, "query_up": query_up, "kv_down": kv_down, "kv_up": kv_up, "cross_down": cross_down, "cross_up": cross_up, "inverted_down": inverted_down, "inverted_up": inverted_up, "point_down": point_down, "point_up": point_up}


top_precision = lax.Precision.HIGHEST
norm_eps = 1e-06
attention_epsilon = 1e-06
masked_score = -1000000000.0

@jax.custom_vjp
def low(v):
    return lax.optimization_barrier(v.astype(jnp.bfloat16)).astype(jnp.float32)

@jax.custom_vjp
def low_back(v):
    return v

def low_keep(v):
    return (low(v), None)

def low_pass(kept, grad):
    return (grad,)

def back_keep(v):
    return (v, None)

def back_low(kept, grad):
    return (low(grad),)
low.defvjp(low_keep, low_pass)
low_back.defvjp(back_keep, back_low)

def layer_norm(values):
    center = values - lax.optimization_barrier(jnp.mean(values, axis=-1, keepdims=True))
    return center * lax.rsqrt(lax.optimization_barrier(jnp.mean(center * center, axis=-1, keepdims=True)) + norm_eps)

def project(inputs, weight, down_table, up_table):
    base_part = jnp.dot(inputs, weight.reshape(weight.shape[0], -1), precision=top_precision)
    latent = jnp.dot(inputs, down_table, precision=top_precision)
    adapter_part = jnp.dot(latent, up_table.reshape(up_table.shape[0], -1), precision=top_precision)
    return (base_part + adapter_part).reshape(inputs.shape[:1] + weight.shape[1:])

def depthwise(hidden, kernel):
    padded = jnp.pad(hidden, ((1, 1), (1, 1), (0, 0), (0, 0)))
    summed = jnp.zeros(hidden.shape, jnp.float32)
    for row_shift in range(3):
        for col_shift in range(3):
            summed = summed + padded[row_shift:row_shift + GRID, col_shift:col_shift + GRID] * kernel[row_shift, col_shift]
    return summed

def forward(latents, caption_rows, mod_rows, length, weights, down_tables, up_tables):
    qkv_weight, proj_weight, cross_q_weight, cross_kv_weight, cross_out_weight, inverted_weight, depth_weight, point_weight = weights
    positions = GRID * GRID
    attn_input = low(layer_norm(latents) * (1.0 + mod_rows[1]) + mod_rows[0])
    qkv_rows = low_back(project(attn_input, qkv_weight, down_tables[0], up_tables[0]))
    query_matrix = jax.nn.relu(qkv_rows[:, 0].reshape(positions, HEADS, HD))
    key_matrix_rows = jax.nn.relu(qkv_rows[:, 1].reshape(positions, HEADS, HD))
    value_matrix_rows = qkv_rows[:, 2].reshape(positions, HEADS, HD)
    key_value_state = jnp.einsum('phi,phj->hij', key_matrix_rows, value_matrix_rows, precision=top_precision)
    summed_keys = lax.optimization_barrier(jnp.sum(key_matrix_rows, axis=0))
    linear_numerator = jnp.einsum('phi,hij->phj', query_matrix, key_value_state, precision=top_precision)
    linear_denominator = jnp.einsum('phi,hi->ph', query_matrix, summed_keys, precision=top_precision) + attention_epsilon
    mixed_heads = low((linear_numerator / linear_denominator[:, :, None]).reshape(positions, D))
    attn_out = low_back(project(mixed_heads, proj_weight, down_tables[1], up_tables[1]))
    after_attn = latents + mod_rows[2] * attn_out
    cross_in = low(after_attn)
    cross_query = low(low_back(project(cross_in, cross_q_weight, down_tables[2], up_tables[2]))).reshape(positions, HEADS, HD)
    cross_kv = low(low_back(project(caption_rows, cross_kv_weight, down_tables[3], up_tables[3])))
    cross_key = cross_kv[:, 0].reshape(TEXT, HEADS, HD)
    cross_value = cross_kv[:, 1].reshape(TEXT, HEADS, HD)
    scores = low_back(jnp.einsum('phd,thd->hpt', cross_query, cross_key, precision=top_precision) * HD ** (-0.5))
    live_keys = jnp.arange(TEXT) < length
    scores = jnp.where(live_keys[None, None, :], scores, masked_score)
    row_max = lax.optimization_barrier(jnp.max(scores, axis=-1, keepdims=True))
    exp_scores = jnp.exp(scores - row_max)
    probs = low(exp_scores / lax.optimization_barrier(jnp.sum(exp_scores, axis=-1, keepdims=True)))
    cross_mix = low(low_back(jnp.einsum('hpt,thd->phd', probs, cross_value, precision=top_precision))).reshape(positions, D)
    cross_out = low_back(project(cross_mix, cross_out_weight, down_tables[4], up_tables[4]))
    after_cross = after_attn + cross_out
    ffn_input = low(layer_norm(after_cross) * (1.0 + mod_rows[4]) + mod_rows[3])
    hidden_pre = low_back(project(ffn_input, inverted_weight, down_tables[5], up_tables[5]))
    hidden = low(jax.nn.silu(hidden_pre)).reshape(GRID, GRID, 2, FF)
    conv_out = low_back(depthwise(hidden, depth_weight)).reshape(positions, 2, FF)
    gated_rows = low(conv_out[:, 0] * jax.nn.silu(conv_out[:, 1]))
    ffn_out = low_back(project(gated_rows, point_weight, down_tables[6], up_tables[6]))
    return after_cross + mod_rows[5] * ffn_out

def reference(tokens, caption, caption_lengths, adapter_index, modulation, cotangent, qkv_weight, proj_weight, cross_q_weight, cross_kv_weight, cross_out_weight, inverted_weight, depth_weight, point_weight, qkv_down, qkv_up, proj_down, proj_up, query_down, query_up, kv_down, kv_up, cross_down, cross_up, inverted_down, inverted_up, point_down, point_up):
    weights = tuple((matrix.astype(jnp.float32) for matrix in (qkv_weight, proj_weight, cross_q_weight, cross_kv_weight, cross_out_weight, inverted_weight, depth_weight, point_weight)))
    down_all = tuple((table.astype(jnp.float32) for table in (qkv_down, proj_down, query_down, kv_down, cross_down, inverted_down, point_down)))
    up_all = tuple((table.astype(jnp.float32) for table in (qkv_up, proj_up, query_up, kv_up, cross_up, inverted_up, point_up)))
    positions = GRID * GRID

    def one_sequence(carry, block_items):
        grad_downs, grad_ups = carry
        tokens_one, caption_one, mods_one, length_one, index_one, cotangent_one = block_items
        caption_rows = caption_one.astype(jnp.float32)
        index_int = index_one.astype(jnp.int32)

        def local_forward(latents, down_tables, up_tables):
            down_sel = tuple((lax.dynamic_index_in_dim(table, index_int, 0, keepdims=False) for table in down_tables))
            up_sel = tuple((lax.dynamic_index_in_dim(table, index_int, 0, keepdims=False) for table in up_tables))
            return forward(latents, caption_rows, mods_one, length_one, weights, down_sel, up_sel)
        result, pullback = jax.vjp(local_forward, tokens_one.reshape(positions, D).astype(jnp.float32), down_all, up_all)
        grad_in, grad_down_tables, grad_up_tables = pullback(cotangent_one.reshape(positions, D).astype(jnp.float32))
        grad_downs = tuple((total + grad_one for total, grad_one in zip(grad_downs, grad_down_tables)))
        grad_ups = tuple((total + grad_one for total, grad_one in zip(grad_ups, grad_up_tables)))
        return ((grad_downs, grad_ups), (result.reshape(GRID, GRID, D), grad_in.reshape(GRID, GRID, D)))
    initial = (tuple((jnp.zeros_like(table) for table in down_all)), tuple((jnp.zeros_like(table) for table in up_all)))
    (grad_downs, grad_ups), (outputs, input_grads) = lax.scan(one_sequence, initial, (tokens, caption, modulation, caption_lengths, adapter_index, cotangent))
    return (outputs, input_grads, grad_downs[0], grad_ups[0], grad_downs[1], grad_ups[1], grad_downs[2], grad_ups[2], grad_downs[3], grad_ups[3], grad_downs[4], grad_ups[4], grad_downs[5], grad_ups[5], grad_downs[6], grad_ups[6])
```

```python
import jax
import jax.numpy as jnp
from jax import lax
from jax.sharding import PartitionSpec as P

W, C, T = "weight", "context", "tensor"
HD = 32
bf16, f32 = jnp.bfloat16, jnp.float32
full_precision = lax.Precision.HIGHEST
norm_eps = 1e-06
attention_epsilon = 1e-06
masked_score = -1000000000.0


def ring_order(n):
    return list(range(0, n, 2)) + list(range(n - 1 - n % 2, 0, -2))


def ring_pairs(n):
    order = ring_order(n)
    return [(order[i], order[(i + 1) % n]) for i in range(n)]


def ring_source(n, step):
    z = lax.axis_index(W)
    place = jnp.where(z % 2 == 0, z // 2, n - 1 - z // 2)
    from_place = (place - step + n) % n
    return jnp.where(2 * from_place < n, 2 * from_place, 2 * (n - 1 - from_place) + 1)


def swap_pairs(n, distance):
    return [(i, i ^ distance) for i in range(n)]


def gather_pair(first, second, tie):
    n = lax.axis_size(W)
    c = lax.axis_index(C)
    rows, cols = first.shape
    buf = jnp.zeros((2, n * rows, cols), bf16)
    buf = lax.dynamic_update_slice(buf, jnp.stack([first, second]), (0, lax.axis_index(W) * rows, 0))
    moving = jnp.where(c == 0, first, second)
    if tie is not None:
        moving, tie = lax.optimization_barrier((moving, tie))
    for step in range(1, n):
        moving = lax.ppermute(moving, W, ring_pairs(n))
        other = lax.ppermute(moving, C, swap_pairs(2, 1))
        at = ring_source(n, step) * rows
        buf = lax.dynamic_update_slice(buf, moving[None], (c, at, 0))
        buf = lax.dynamic_update_slice(buf, other[None], (1 - c, at, 0))
    return buf, moving[:16, :128]


def sum_halves(partial):
    groups = lax.axis_size(T)
    b = lax.axis_index(T) % 2
    half = partial.shape[0] // 2
    away = lax.dynamic_slice_in_dim(partial, (1 - b) * half, half, 0).astype(bf16)
    mine = lax.dynamic_slice_in_dim(partial, b * half, half, 0)
    total = mine + lax.ppermute(away, T, swap_pairs(groups, 1)).astype(f32)
    distance = 2
    while distance < groups:
        low = total.astype(bf16)
        total = low.astype(f32) + lax.ppermute(low, T, swap_pairs(groups, distance)).astype(f32)
        distance *= 2
    return total


def share_halves(mine):
    b = lax.axis_index(T) % 2
    other = lax.ppermute(mine, T, swap_pairs(lax.axis_size(T), 1))
    return jnp.where(b == 0, jnp.concatenate([mine, other]), jnp.concatenate([other, mine]))


def add_context(values):
    return values + lax.ppermute(values, C, swap_pairs(2, 1))


def layer_stats(values):
    center = values - jnp.mean(values, axis=-1, keepdims=True)
    inverse = lax.rsqrt(jnp.mean(center * center, axis=-1, keepdims=True) + norm_eps)
    return center * inverse, inverse


def norm_back(normed, inverse, grad):
    return inverse * (
        grad
        - jnp.mean(grad, axis=-1, keepdims=True)
        - normed * jnp.mean(grad * normed, axis=-1, keepdims=True)
    )


def dot(a, b, ca=1, cb=0):
    return lax.dot_general(a, b, (((ca,), (cb,)), ((), ())), preferred_element_type=f32)


def two_parts(values, axis):
    high = lax.reduce_precision(values, 8, 7)
    return jnp.concatenate([high.astype(bf16), (values - high).astype(bf16)], axis=axis)


def twice(table, axis=0):
    return jnp.concatenate([table, table], axis=axis)


def thin_dot(latent, table):
    return dot(two_parts(latent, 1), twice(table))


def outer_sum(latent, values):
    both = dot(two_parts(latent, 1), values, 0, 0)
    half = both.shape[0] // 2
    return both[:half] + both[half:]


def shifted(rows_of, kernel, flip):
    height = rows_of.shape[0] - 2
    width = rows_of.shape[1]
    padded = jnp.pad(rows_of, ((0, 0), (1, 1), (0, 0)))
    total = jnp.zeros((height, width, rows_of.shape[2]), f32)
    for i in range(3):
        for j in range(3):
            tap = kernel[2 - i, 2 - j] if flip else kernel[i, j]
            total = total + padded[i : i + height, j : j + width] * tap
    return total


def with_halo(blocks):
    c = lax.axis_index(C)
    edge = jnp.stack([jnp.where(c == 0, v[-1], v[0]) for v in blocks])
    got = lax.ppermute(edge, C, swap_pairs(2, 1))
    zero = jnp.zeros_like(got)
    above = jnp.where(c == 0, zero, got)
    below = jnp.where(c == 0, got, zero)
    return [
        jnp.concatenate([above[i][None], v, below[i][None]]) for i, v in enumerate(blocks)
    ]


def silu_slope(values):
    sig = jax.nn.sigmoid(values)
    return sig * (1.0 + values * (1.0 - sig))


def slot_layout(groups, rank, heads):
    per, left = heads // groups, heads % groups
    slots = per + (1 if left else 0)
    own_first = rank * per + jnp.minimum(rank, left)
    own_count = per + jnp.where(rank < left, 1, 0)
    first = jnp.minimum(own_first, heads - slots)
    slot = first + jnp.arange(slots, dtype=jnp.int32)
    owned = ((slot >= own_first) & (slot < own_first + own_count)).astype(f32)
    return slots, first, owned


def slot_ranges(groups, heads):
    per, left = heads // groups, heads % groups
    slots = per + (1 if left else 0)
    out = []
    for rank in range(groups):
        own_first = rank * per + min(rank, left)
        count = per + (1 if rank < left else 0)
        skip = own_first - min(own_first, heads - slots)
        out.append((skip, count))
    return out


def shards(
    tokens, caption, caption_lengths, adapter_index, modulation, cotangent,
    qkv_weight, proj_weight, cross_q_weight, cross_kv_weight, cross_out_weight,
    inverted_weight, depth_weight, point_weight,
    qkv_down, qkv_up, proj_down, proj_up, query_down, query_up, kv_down, kv_up,
    cross_down, cross_up, inverted_down, inverted_up, point_down, point_up,
):
    grid_rows, grid_cols, D = tokens.shape[1:]
    n = grid_rows * grid_cols
    heads = D // HD
    groups = lax.axis_size(T)
    rank = lax.axis_index(T)
    c = lax.axis_index(C)
    b = rank % 2
    half = n // 2
    adapters, R = qkv_up.shape[:2]
    slots, slot_first, owned = slot_layout(groups, rank, heads)
    width = slots * HD
    col = slot_first * HD
    owned_cols = jnp.repeat(owned, HD)
    hid = inverted_weight.shape[2]
    hh = hid // 2
    hid_first = rank * hid
    index = adapter_index[0]

    def cut(table, start, size, axis):
        return lax.dynamic_slice_in_dim(table, start, size, axis)

    def pick(table):
        return lax.dynamic_index_in_dim(table, index, 0, keepdims=False)

    qkv_cut = cut(qkv_weight, col, width, 2)
    kv_cut = cut(cross_kv_weight, col, width, 2)
    proj_t = cut(proj_weight, col, width, 0).T
    out_t = cut(cross_out_weight, col, width, 0).T
    query_cut = cut(cross_q_weight, col, width, 1)
    point_t = point_weight.T
    w_a, t_a = gather_pair(qkv_cut[:, 0], qkv_cut[:, 1], None)
    w_b, t_b = gather_pair(qkv_cut[:, 2], proj_t, None)
    w_c, t_c = gather_pair(query_cut, kv_cut[:, 0], t_a)
    w_d, t_d = gather_pair(kv_cut[:, 1], out_t, t_b)
    w_v, t_v = gather_pair(inverted_weight[:, 0, :hh], inverted_weight[:, 0, hh:], t_c)
    w_g, t_g = gather_pair(inverted_weight[:, 1, :hh], inverted_weight[:, 1, hh:], t_d)
    w_p, t_p = gather_pair(point_t[:, :hh], point_t[:, hh:], t_v)

    qkv_d, qkv_u = pick(qkv_down), cut(pick(qkv_up), col, width, 2)
    proj_d, proj_u = cut(pick(proj_down), col, width, 0), pick(proj_up)
    query_d, query_u = pick(query_down), cut(pick(query_up), col, width, 1)
    kv_d, kv_u = pick(kv_down), cut(pick(kv_up), col, width, 2)
    cross_d, cross_u = cut(pick(cross_down), col, width, 0), pick(cross_up)
    inv_d, inv_u = pick(inverted_down), cut(pick(inverted_up), hid_first, hid, 2)
    point_d, point_u = cut(pick(point_down), hid_first, hid, 0), pick(point_up)

    mods = modulation[0]
    shift_a, scale_a, gate_a, shift_f, scale_f, gate_f = (mods[i : i + 1] for i in range(6))
    low_tokens = tokens.reshape(n, D)
    x_all = low_tokens.astype(f32)
    x_half = cut(low_tokens, b * half, half, 0).astype(f32)
    cot_all = cotangent.reshape(n, D)
    cot_half = cut(cot_all, b * half, half, 0).astype(f32)

    def per_head(values):
        return values.reshape(values.shape[0], slots, HD)

    normed, unused = layer_stats(x_all)
    attn_in = (normed * (1.0 + scale_a) + shift_a).astype(bf16)
    qkv_lat = dot(attn_in, qkv_d)
    q_raw, k_raw, v_raw = (
        dot(attn_in, w) + thin_dot(qkv_lat, qkv_u[:, i])
        for i, w in enumerate((w_a[0], w_a[1], w_b[0]))
    )
    q_h, k_h, v_h = per_head(jax.nn.relu(q_raw)), per_head(jax.nn.relu(k_raw)), per_head(v_raw)
    state = jnp.einsum("pha,phb->hab", k_h, v_h, precision=full_precision)
    keys = jnp.sum(k_h, axis=0)
    state_keys = add_context(jnp.concatenate([state, keys[:, None]], axis=1))
    state, keys = state_keys[:, :HD], state_keys[:, HD]
    numer = jnp.einsum("pha,hab->phb", q_h, state, precision=full_precision)
    denom = jnp.sum(q_h * keys, axis=-1, keepdims=True) + attention_epsilon
    ratio = numer / denom
    mixed = (ratio * owned[:, None]).reshape(n, width).astype(bf16)
    proj_lat = dot(mixed, proj_d)
    attn_part = dot(mixed, w_b[1], 1, 1) + thin_dot(proj_lat, proj_u)
    after_attn = x_half + gate_a * sum_halves(attn_part)
    cross_in = share_halves(after_attn.astype(bf16))

    text_here = caption.shape[1]
    kv_lat = dot(caption[0], kv_d)
    key_rows = dot(caption[0], w_c[1]) + thin_dot(kv_lat, kv_u[:, 0])
    value_rows = dot(caption[0], w_d[0]) + thin_dot(kv_lat, kv_u[:, 1])
    kv_own = jnp.concatenate([key_rows, value_rows], axis=1).astype(bf16)
    kv_other = lax.ppermute(kv_own, C, swap_pairs(2, 1))
    kv_all = jnp.concatenate([kv_own, kv_other])
    key_all, value_all = per_head(kv_all[:, :width]), per_head(kv_all[:, width:])
    places = jnp.arange(text_here)
    places = jnp.concatenate([c * text_here + places, (1 - c) * text_here + places])
    live = places < caption_lengths[0]
    query_lat = dot(cross_in, query_d)
    query = (dot(cross_in, w_c[0]) + thin_dot(query_lat, query_u)).astype(bf16)
    query_h = per_head(query)

    def raw_scores():
        s = jnp.einsum("phd,thd->hpt", query_h, key_all, preferred_element_type=f32)
        return jnp.where(live, s * HD ** (-0.5), masked_score)

    scores = raw_scores()
    row_max = jnp.max(scores, axis=-1, keepdims=True)
    exps = jnp.exp(scores - row_max)
    row_sum = jnp.sum(exps, axis=-1, keepdims=True)
    log_total = row_max + jnp.log(row_sum)
    probs = (exps / row_sum).astype(bf16)
    mix = jnp.einsum("hpt,thd->phd", probs, value_all, preferred_element_type=f32)
    mix = (mix * owned[:, None]).reshape(n, width).astype(bf16)
    cross_lat = dot(mix, cross_d)
    cross_part = dot(mix, w_d[1], 1, 1) + thin_dot(cross_lat, cross_u)
    after_cross = after_attn + sum_halves(cross_part)

    normed_f, inverse_f = layer_stats(after_cross)
    ffn_in = share_halves((normed_f * (1.0 + scale_f) + shift_f).astype(bf16))
    inv_lat = dot(ffn_in, inv_d)
    pre = []
    for part, w in enumerate((w_v, w_g)):
        for h in range(2):
            pre.append(dot(ffn_in, w[h]) + thin_dot(inv_lat, inv_u[:, part, h * hh : (h + 1) * hh]))
    grid = (grid_rows, grid_cols, hh)
    hidden = [jax.nn.silu(v).astype(bf16).reshape(grid) for v in pre]
    taps = depth_weight.astype(f32)
    taps = [taps[:, :, p, h * hh : (h + 1) * hh] for p in range(2) for h in range(2)]
    conv = [shifted(v, t, False).reshape(n, hh) for v, t in zip(with_halo(hidden), taps)]
    conv_v, conv_g = conv[:2], conv[2:]
    acts = [jax.nn.silu(g) for g in conv_g]
    gated = [(v * a).astype(bf16) for v, a in zip(conv_v, acts)]
    point_lat = dot(gated[0], point_d[:hh]) + dot(gated[1], point_d[hh:])
    ffn_part = (
        dot(gated[0], w_p[0], 1, 1) + dot(gated[1], w_p[1], 1, 1) + thin_dot(point_lat, point_u)
    )
    output = after_cross + gate_f * sum_halves(ffn_part)
    output = share_halves(output)

    grad_ffn = (gate_f * cot_all.astype(f32)).astype(bf16)
    point_gl = dot(grad_ffn, point_u, 1, 1)
    grad_conv = []
    for h in range(2):
        grad_gated = dot(grad_ffn, w_p[h]) + dot(
            two_parts(point_gl, 1), twice(point_d[h * hh : (h + 1) * hh], 1), 1, 1
        )
        grad_conv.append((grad_gated * acts[h], grad_gated * conv_v[h] * silu_slope(conv_g[h])))
    grad_conv = [grad_conv[h][p].astype(bf16).reshape(grid) for p in range(2) for h in range(2)]
    grad_pre = []
    for v, t, s in zip(with_halo(grad_conv), taps, pre):
        grad_pre.append((shifted(v, t, True).reshape(n, hh) * silu_slope(s)).astype(bf16))
    inv_ups = [inv_u[:, p, h * hh : (h + 1) * hh] for p in range(2) for h in range(2)]
    inv_ws = [w_v[0], w_v[1], w_g[0], w_g[1]]
    inv_gl = sum(dot(g, u, 1, 1) for g, u in zip(grad_pre, inv_ups))
    ffn_in_part = sum(dot(g, w, 1, 1) for g, w in zip(grad_pre, inv_ws)) + dot(
        two_parts(inv_gl, 1), twice(inv_d, 1), 1, 1
    )
    grad_cross = cot_half + norm_back(
        normed_f, inverse_f, sum_halves(ffn_in_part) * (1.0 + scale_f)
    )
    grad_cross_low = share_halves(grad_cross.astype(bf16))

    cross_gl = dot(grad_cross_low, cross_u, 1, 1)
    grad_mix = dot(grad_cross_low, w_d[1]) + dot(
        two_parts(cross_gl, 1), twice(cross_d, 1), 1, 1
    )
    grad_mix = per_head((grad_mix * owned_cols).astype(bf16))
    probs_wide = jnp.exp(raw_scores() - log_total)
    grad_probs = jnp.einsum("phd,thd->hpt", grad_mix, value_all, preferred_element_type=f32)
    grad_value = jnp.einsum(
        "hpt,phd->thd", probs_wide.astype(bf16), grad_mix, preferred_element_type=f32
    )
    inner = jnp.sum(probs_wide * grad_probs, axis=-1, keepdims=True)
    grad_scores = (probs_wide * (grad_probs - inner)).astype(bf16)
    grad_query = jnp.einsum("hpt,thd->phd", grad_scores, key_all, preferred_element_type=f32)
    grad_key = jnp.einsum("hpt,phd->thd", grad_scores, query_h, preferred_element_type=f32)
    grad_query = (grad_query * HD ** (-0.5)).reshape(n, width).astype(bf16)
    kv_terms = jnp.concatenate(
        [
            (grad_key * HD ** (-0.5)).reshape(2 * text_here, width),
            grad_value.reshape(2 * text_here, width),
        ],
        axis=1,
    )
    kv_got = lax.ppermute(kv_terms[text_here:], C, swap_pairs(2, 1))
    grad_kv = (kv_terms[:text_here] + kv_got).astype(bf16)
    query_gl = dot(grad_query, query_u, 1, 1)
    cross_in_part = dot(grad_query, w_c[0], 1, 1) + dot(
        two_parts(query_gl, 1), twice(query_d, 1), 1, 1
    )
    kv_gl = dot(grad_kv[:, :width], kv_u[:, 0], 1, 1) + dot(grad_kv[:, width:], kv_u[:, 1], 1, 1)
    grad_after = grad_cross + sum_halves(cross_in_part)

    grad_attn = share_halves((gate_a * grad_after).astype(bf16))
    proj_gl = dot(grad_attn, proj_u, 1, 1)
    grad_heads = dot(grad_attn, w_b[1]) + dot(two_parts(proj_gl, 1), twice(proj_d, 1), 1, 1)
    grad_heads = per_head(grad_heads * owned_cols)
    grad_numer = grad_heads / denom
    grad_den = -jnp.sum(grad_heads * ratio, axis=-1, keepdims=True) / denom
    grad_q = (
        jnp.einsum("phb,hab->pha", grad_numer, state, precision=full_precision) + grad_den * keys
    )
    state_grad = jnp.einsum("pha,phb->hab", q_h, grad_numer, precision=full_precision)
    keys_grad = jnp.sum(grad_den * q_h, axis=0)
    both_grad = add_context(jnp.concatenate([state_grad, keys_grad[:, None]], axis=1))
    state_grad, keys_grad = both_grad[:, :HD], both_grad[:, HD]
    grad_k = (
        jnp.einsum("phb,hab->pha", v_h, state_grad, precision=full_precision) + keys_grad
    )
    grad_v = jnp.einsum("pha,hab->phb", k_h, state_grad, precision=full_precision)
    grad_q = (grad_q.reshape(n, width) * (q_raw > 0)).astype(bf16)
    grad_k = (grad_k.reshape(n, width) * (k_raw > 0)).astype(bf16)
    grad_v = grad_v.reshape(n, width).astype(bf16)
    qkv_gl = sum(dot(g, qkv_u[:, i], 1, 1) for i, g in enumerate((grad_q, grad_k, grad_v)))
    attn_in_part = (
        dot(grad_q, w_a[0], 1, 1)
        + dot(grad_k, w_a[1], 1, 1)
        + dot(grad_v, w_b[0], 1, 1)
        + dot(two_parts(qkv_gl, 1), twice(qkv_d, 1), 1, 1)
    )
    normed_half, inverse_half = layer_stats(x_half)
    input_grad = grad_after + norm_back(
        normed_half, inverse_half, sum_halves(attn_in_part) * (1.0 + scale_a)
    )
    input_grad = share_halves(input_grad)

    part_r = R // groups
    blocks = lax.axis_size(W) * lax.axis_size(C)
    ranges = slot_ranges(groups, heads)

    def by_rank(*values):
        joined = jnp.concatenate(values, axis=1)
        sent = joined.reshape(groups, part_r, joined.shape[1])
        return lax.all_to_all(sent, T, 0, 0, tiled=True)

    def slots_to_heads(got):
        return jnp.concatenate(
            [got[t][:, s * HD : (s + m) * HD] for t, (s, m) in enumerate(ranges)], axis=1
        )

    def hidden_to_full(got):
        return jnp.concatenate([got[t] for t in range(groups)], axis=1)

    def finish(values):
        sizes = [v.shape[1] // blocks for v in values]
        payload = jnp.concatenate([v.reshape(part_r, blocks, -1) for v in values], axis=2)
        payload = payload.transpose(1, 0, 2)
        mark = jnp.full((blocks, part_r, 1), 0.0, f32) + index.astype(f32)
        got = lax.all_to_all(jnp.concatenate([payload, mark], axis=2), (W, C), 0, 0, tiled=True)
        owner = got[:, 0, -1]
        chosen = (owner[None, :] == jnp.arange(adapters, dtype=f32)[:, None]).astype(f32)
        table = jnp.einsum("as,srk->ark", chosen, got[:, :, :-1], precision=full_precision)
        out, at = [], 0
        for size in sizes:
            out.append(table[:, :, at : at + size])
            at += size
        return out

    lat_cols = [proj_lat.T, cross_lat.T, point_lat.T, inv_gl.T, query_gl.T, kv_gl.T]
    got = jnp.sum(by_rank(*lat_cols), axis=0)
    proj_s, cross_s, point_s, inv_s, query_s, kv_s = (
        got[:, i * n : (i + 1) * n] if i < 5 else got[:, 5 * n :] for i in range(6)
    )
    qkv_s = jnp.sum(by_rank(qkv_gl.T), axis=0)

    def thin_sum(latent, values):
        return outer_sum(latent.T, values)

    low_caption = caption[0]
    early = [
        outer_sum(cross_gl, mix),
        outer_sum(query_lat, grad_query),
        outer_sum(kv_lat, grad_kv[:, :width]),
        outer_sum(kv_lat, grad_kv[:, width:]),
        outer_sum(point_gl, gated[0]),
        outer_sum(point_gl, gated[1]),
    ] + [outer_sum(inv_lat, g) for g in grad_pre]
    got = by_rank(*early)
    pieces, at = [], 0
    for v in early:
        pieces.append(got[:, :, at : at + v.shape[1]])
        at += v.shape[1]
    cross_down_g, query_up_g, key_up_g, value_up_g = (slots_to_heads(p) for p in pieces[:4])
    point_down_g = hidden_to_full(jnp.concatenate(pieces[4:6], axis=2))
    inv_up_g = [hidden_to_full(jnp.concatenate(pieces[i : i + 2], axis=2)) for i in (6, 8)]
    first = finish(
        [
            thin_sum(cross_s, grad_cross_low),
            thin_sum(point_s, grad_ffn),
            thin_sum(inv_s, ffn_in),
            thin_sum(query_s, cross_in),
            thin_sum(kv_s, low_caption),
            cross_down_g,
            query_up_g,
            key_up_g,
            value_up_g,
            point_down_g,
        ]
        + inv_up_g
    )
    late = [outer_sum(proj_gl, mixed)] + [
        outer_sum(qkv_lat, g) for g in (grad_q, grad_k, grad_v)
    ]
    got = by_rank(*late)
    late = [slots_to_heads(got[:, :, i * width : (i + 1) * width]) for i in range(4)]
    second = finish([thin_sum(proj_s, grad_attn), thin_sum(qkv_s, attn_in)] + late)

    def down_of(t):
        return t.transpose(0, 2, 1)

    return (
        output.reshape(tokens.shape),
        input_grad.reshape(tokens.shape),
        down_of(second[1]),
        jnp.stack(second[3:6], axis=2),
        down_of(second[2]),
        second[0],
        down_of(first[3]),
        first[6],
        down_of(first[4]),
        jnp.stack(first[7:9], axis=2),
        down_of(first[5]),
        first[0],
        down_of(first[2]),
        jnp.stack(first[10:12], axis=2),
        down_of(first[9]),
        first[1],
    )


def solution(mesh):
    down = P(None, (W, C), T)
    up3 = P(None, T, (W, C))
    up4 = P(None, T, None, (W, C))
    rows = P(W, C)
    return jax.shard_map(
        shards,
        mesh=mesh,
        in_specs=(
            rows, rows, P(W), P(W), P(W), rows,
            P(W), P(None, W), P(W), P(W), P(None, W),
            P(W, None, T), P(None, None, None, T), P(T, W),
        )
        + (P(),) * 14,
        out_specs=(
            rows, rows, down, up4, down, up3, down, up3, down, up4, down, up3, down, up4, down, up3,
        ),
        check_vma=False,
    )
```

```python
import functools
import jax
import jax.numpy as jnp
from jax import lax
from jax.experimental import pallas as pl
from jax.experimental.pallas import tpu as pltpu
from jax.sharding import PartitionSpec as P

W, C, T = "weight", "context", "tensor"
HD = 32
LANES = 128
bf16, f32 = jnp.bfloat16, jnp.float32
full_precision = lax.Precision.HIGHEST
norm_eps = 1e-06
attention_epsilon = 1e-06
masked_score = -1000000000.0
big = pltpu.CompilerParams(vmem_limit_bytes=58 * 1024 * 1024)


def shape(dims, dtype):
    return jax.ShapeDtypeStruct(dims, dtype)


def mm(a, b, ca=1, cb=0):
    return lax.dot_general(a, b, (((ca,), (cb,)), ((), ())), preferred_element_type=f32)


def two(pair):
    high = pair.astype(bf16)
    rest = (pair - high.astype(f32)).astype(bf16)
    lane = lax.broadcasted_iota(jnp.int32, pair.shape, 1)
    return jnp.where(lane < pair.shape[1] // 2, high.astype(f32), rest.astype(f32)).astype(bf16)


def split(values):
    high = values.astype(bf16)
    return high, (values - high.astype(f32)).astype(bf16)


def mm3(a, b, ca=1, cb=0):
    ah, al = split(a)
    bh, bl = split(b)
    return mm(ah, bh, ca, cb) + mm(ah, bl, ca, cb) + mm(al, bh, ca, cb)


def head_mask(width):
    row = lax.broadcasted_iota(jnp.int32, (width, width), 0) // HD
    col = lax.broadcasted_iota(jnp.int32, (width, width), 1) // HD
    return (row == col).astype(f32)


def head_total(values, mask):
    high, low = split(values)
    low_mask = mask.astype(bf16)
    return mm(high, low_mask) + mm(low, low_mask)


def squeeze_heads(square, mask):
    kept = square * mask
    total = kept[:HD]
    for h in range(1, kept.shape[0] // HD):
        total = total + kept[h * HD : (h + 1) * HD]
    return total


def spread_heads(state, width, mask):
    return jnp.concatenate([state] * (width // HD), axis=0) * mask


def sigmoid(values):
    return 1.0 / (1.0 + jnp.exp(-values))


def row_stats(values):
    center = values - jnp.mean(values, axis=-1, keepdims=True)
    inverse = lax.rsqrt(jnp.mean(center * center, axis=-1, keepdims=True) + norm_eps)
    return center * inverse, inverse


def put(out, rows, values):
    width = values.shape[1]
    out[rows, :width] = values.astype(out.dtype)
    if width < out.shape[1]:
        out[rows, width:] = jnp.zeros((values.shape[0], out.shape[1] - width), out.dtype)


everything = slice(None)


def attn_front(w, x, mods, d2, u2, a_out, q_out, k_out, v_out, lat_out, st_out):
    n = x.shape[0]
    step = 64

    def norm(i, carry):
        at = pl.ds(pl.multiple_of(i * step, step), step)
        normed, unused = row_stats(x[at, :].astype(f32))
        a_out[at, :] = (normed * (1.0 + mods[1:2, :]) + mods[0:1, :]).astype(bf16)
        return carry

    lax.fori_loop(0, n // step, norm, 0)
    a = a_out[...]
    lat = mm(a, d2[...])
    lat_out[...] = lat
    pair = two(lat)
    for i, (out, weight, j) in enumerate(((q_out, w[0], 0), (k_out, w[0], 1), (v_out, w[1], 0))):
        out[...] = mm(a, weight.take(j)) + mm(pair, u2[i])
    keys = jnp.maximum(k_out[...], 0.0)
    width = keys.shape[1]
    st_out[:HD, :] = squeeze_heads(mm3(v_out[...], keys, 0, 0), head_mask(width))
    st_out[HD:, :] = jnp.broadcast_to(jnp.sum(keys, axis=0, keepdims=True), (8, width))


def put_partial(low, lat_pair, w, u2, mine, away):
    half = mine.shape[0]
    put(mine, everything, mm(low[:half], w, 1, 1) + mm(lat_pair[:half], u2))
    put(away, everything, mm(low[half:], w, 1, 1) + mm(lat_pair[half:], u2))


def attn_back(w, q, st1, st2, owned, d2, u2, ratio_out, den_out, mixed_out, lat_out, mine, away):
    st = st1[...] + st2[...]
    width = q.shape[1]
    mask = head_mask(width)
    queries = jnp.maximum(q[...], 0.0)
    numer = mm3(queries, spread_heads(st[:HD], width, mask), 1, 1)
    den = head_total(queries * st[HD : HD + 1], mask) + attention_epsilon
    ratio = numer / den
    ratio_out[...] = ratio
    den_out[...] = den
    mixed = (ratio * owned[...]).astype(bf16)
    mixed_out[...] = mixed
    lat = mm(mixed, d2[...])
    lat_out[...] = lat
    put_partial(mixed, two(lat), w[0].take(0), u2[...], mine, away)


def caption_rows(w, cap, d2, u2, kv_out, lat_out):
    lat = mm(cap[...], d2[...])
    lat_out[...] = lat
    pair = two(lat)
    kv_out[0] = (mm(cap[...], w[0].take(0)) + mm(pair, u2[0])).astype(bf16)
    kv_out[1] = (mm(cap[...], w[1].take(0)) + mm(pair, u2[1])).astype(bf16)


def lane_groups(width):
    return [(at, min(LANES, width - at)) for at in range(0, width, LANES)]


def only_head(values, j):
    lane = lax.broadcasted_iota(jnp.int32, values.shape, 1) // HD
    return jnp.where(lane == j, values.astype(f32), 0.0).astype(values.dtype)


def cross_fwd(
    w, xo, xt, kv1, kv2, live, owned, qd2, qu2, cd2, cu2,
    q_out, mix_out, qlat_out, clat_out, lse_out, mine, away, keys, vals,
):
    half = xo.shape[0]
    width = q_out.shape[1]
    here = kv1.shape[1]
    for buf, i in ((keys, 0), (vals, 1)):
        buf[:here, :] = kv1[i]
        buf[here:, :] = kv2[i]
    depth = qd2.shape[0]
    weight = w[0].take(0)
    for i, rows in enumerate((xo, xt)):
        at = pl.ds(i * half, half)
        lat = mm(rows[:, :depth], qd2[...])
        qlat_out[at, :] = lat
        q_out[at, :] = (mm(rows[:, :depth], weight) + mm(two(lat), qu2[...])).astype(bf16)

    def block(i, carry):
        at = pl.ds(pl.multiple_of(i * half, half), half)
        for first, size in lane_groups(width):
            cols = slice(first, first + size)
            query = q_out[at, cols]
            total = jnp.zeros((half, size), f32)
            for j in range(size // HD):
                scores = mm(query, only_head(keys[:, cols], j), 1, 1) * HD ** (-0.5)
                scores = jnp.where(live[...] > 0.0, scores, masked_score)
                top = jnp.max(scores, axis=-1, keepdims=True)
                exps = jnp.exp(scores - top)
                tot = jnp.sum(exps, axis=-1, keepdims=True)
                h = first // HD + j
                lse_out[at, h : h + 1] = top + jnp.log(tot)
                probs = (exps * (1.0 / tot)).astype(bf16)
                total = total + mm(probs, only_head(vals[:, cols], j))
            mix_out[at, cols] = (total * owned[:, cols]).astype(bf16)
        return carry

    lax.fori_loop(0, 2, block, 0)
    mix = mix_out[...]
    lat = mm(mix, cd2[...])
    clat_out[...] = lat
    put_partial(mix, two(lat), w[1].take(0), cu2[...], mine, away)


def ffn_front(w, xo, xt, d2, uv, ug, pv, pg, hv, hg, lat_out, u):
    half = xo.shape[0]
    depth = d2.shape[0]
    h = pl.program_id(0)

    @pl.when(h == 0)
    def first():
        u[:half, :] = xo[:, :depth]
        u[half:, :] = xt[:, :depth]
        lat_out[...] = mm(u[...], d2[...])

    pair = two(lat_out[...])
    for weight, up, pre, hid in ((w[0], uv, pv, hv), (w[1], ug, pg, hg)):
        s = mm(u[...], weight.take(h)) + mm(pair, up[0])
        pre[0] = s
        hid[0] = (s * sigmoid(s)).astype(bf16)


def fill_grid(buf, rows, halo, b, c):
    half = rows.shape[0] // 2
    edge = halo.shape[0]
    buf[pl.ds(pl.multiple_of(edge + b * half, edge), half), :] = rows[:half, :].astype(f32)
    buf[pl.ds(pl.multiple_of(edge + (1 - b) * half, edge), half), :] = rows[half:, :].astype(f32)
    zero = jnp.zeros(halo.shape, f32)
    got = halo.astype(f32)
    buf[:edge, :] = jnp.where(c == 0, zero, got)
    buf[buf.shape[0] - edge :, :] = jnp.where(c == 0, got, zero)


def conv_row(buf, taps, r, edge, flip):
    sums = []
    rows = [buf[pl.ds(pl.multiple_of((r + i) * edge, edge), edge), :] for i in range(3)]
    for j in range(3):
        total = None
        for i in range(3):
            k = (2 - i) * 3 + 2 - j if flip else i * 3 + j
            term = rows[i] * taps[k : k + 1, :]
            total = term if total is None else total + term
        sums.append(total)
    cell = lax.broadcasted_iota(jnp.int32, sums[0].shape, 0)
    left = jnp.where(cell == 0, 0.0, pltpu.roll(sums[0], 1, 0))
    right = jnp.where(cell == edge - 1, 0.0, pltpu.roll(sums[2], edge - 1, 0))
    return left + sums[1] + right


def own_first(r, edge, half, b):
    per = half // edge
    return pl.multiple_of(jnp.where(r // per == b, 0, half) + (r % per) * edge, edge)


def ffn_mid(
    w, where, hv, hg, halo, taps, cot, gate, d2, u2,
    gated_out, gcv_out, gcg_out, gffn_out, gl_out, lat_out, mine, away, bv, bg, gg, acc,
):
    h = pl.program_id(0)
    b, c = where[0], where[1]
    n = hv.shape[1]
    half = n // 2
    edge = halo.shape[2]

    @pl.when(h == 0)
    def first():
        gffn_out[...] = (gate[...] * cot[...].astype(f32)).astype(bf16)
        gl_out[...] = mm(gffn_out[...], u2[...], 1, 1)

    fill_grid(bv, hv[0], halo[0, 0], b, c)
    fill_grid(bg, hg[0], halo[0, 1], b, c)
    weight = w[0].take(h)
    gg[...] = mm(gffn_out[...], weight) + mm(two(gl_out[...]), d2[0], 1, 1)

    def row(r, carry):
        v = conv_row(bv, taps[0, 0], r, edge, False)
        g = conv_row(bg, taps[0, 1], r, edge, False)
        sig = sigmoid(g)
        act = g * sig
        at = pl.ds(own_first(r, edge, half, b), edge)
        gated_out[0, at, :] = (v * act).astype(bf16)
        grad = gg[at, :]
        gcv_out[0, at, :] = (grad * act).astype(bf16)
        gcg_out[0, at, :] = (grad * v * (sig * (1.0 + g * (1.0 - sig)))).astype(bf16)
        return carry

    lax.fori_loop(0, n // edge, row, 0)
    gated = gated_out[0]
    part = mm(gated, weight, 1, 1)
    lat = mm(gated, d2[0])

    @pl.when(h == 0)
    def start():
        acc[...] = part
        lat_out[...] = lat

    @pl.when(h == 1)
    def end():
        total = lat_out[...] + lat
        lat_out[...] = total
        full = acc[...] + part + mm(two(total), u2[...])
        put(mine, everything, full[:half])
        put(away, everything, full[half:])


def ffn_back(
    w, where, gcv, gcg, halo, taps, pv, pg, lat, d2, uv, ug,
    gpv_out, gpg_out, up_out, gl_out, mine, away, bv, bg, acc,
):
    h = pl.program_id(0)
    b, c = where[0], where[1]
    n = gcv.shape[1]
    half = n // 2
    edge = halo.shape[2]
    fill_grid(bv, gcv[0], halo[0, 0], b, c)
    fill_grid(bg, gcg[0], halo[0, 1], b, c)

    def row(r, carry):
        at = pl.ds(own_first(r, edge, half, b), edge)
        for i, (buf, pre, out) in enumerate(((bv, pv, gpv_out), (bg, pg, gpg_out))):
            grad = conv_row(buf, taps[0, i], r, edge, True)
            s = pre[0, at, :]
            sig = sigmoid(s)
            out[0, at, :] = (grad * (sig * (1.0 + s * (1.0 - sig)))).astype(bf16)
        return carry

    lax.fori_loop(0, n // edge, row, 0)
    gpv, gpg = gpv_out[0], gpg_out[0]
    part = mm(gpv, w[0].take(h), 1, 1) + mm(gpg, w[1].take(h), 1, 1)
    gl = mm(gpv, uv[0], 1, 1) + mm(gpg, ug[0], 1, 1)
    pair = two(lat[...])
    up_out[0, 0] = mm(pair, gpv, 0, 0)
    up_out[0, 1] = mm(pair, gpg, 0, 0)

    @pl.when(h == 0)
    def start():
        acc[...] = part
        gl_out[...] = gl

    @pl.when(h == 1)
    def end():
        total = gl_out[...] + gl
        gl_out[...] = total
        full = acc[...] + part + mm(two(total), d2[...], 1, 1)
        put(mine, everything, full[:half])
        put(away, everything, full[half:])


def cross_bwd(
    w, go, gt, kv1, kv2, live, owned, qd2, qu2, cd2, cu2, query, lse,
    gq_out, gkv_out, qgl_out, cgl_out, mine, away, keys, vals, gm, gqs,
):
    half = go.shape[0]
    width = query.shape[1]
    here = kv1.shape[1]
    for buf, i in ((keys, 0), (vals, 1)):
        buf[:here, :] = kv1[i]
        buf[here:, :] = kv2[i]
    depth = cu2.shape[1]
    weight = w[1].take(0)
    for i, rows in enumerate((go, gt)):
        at = pl.ds(i * half, half)
        gl = mm(rows[:, :depth], cu2[...], 1, 1)
        cgl_out[at, :] = gl
        grad = mm(rows[:, :depth], weight) + mm(two(gl), cd2[...], 1, 1)
        gm[at, :] = (grad * owned[...]).astype(bf16)
    scale = HD ** (-0.5)

    def block(i, carry):
        at = pl.ds(pl.multiple_of(i * half, half), half)
        for first, size in lane_groups(width):
            cols = slice(first, first + size)
            q_all, g_all = query[at, cols], gm[at, cols]
            grad_q = jnp.zeros((half, size), f32)
            grad_k = jnp.zeros((2 * here, size), f32)
            grad_v = jnp.zeros((2 * here, size), f32)
            for j in range(size // HD):
                key, val = only_head(keys[:, cols], j), only_head(vals[:, cols], j)
                h = first // HD + j
                scores = mm(q_all, key, 1, 1) * scale
                scores = jnp.where(live[...] > 0.0, scores, masked_score)
                probs = jnp.exp(scores - lse[at, h : h + 1])
                grad_p = mm(g_all, val, 1, 1)
                grad_v = grad_v + mm(probs.astype(bf16), only_head(g_all, j), 0, 0)
                inner = jnp.sum(probs * grad_p, axis=-1, keepdims=True)
                grad_s = (probs * (grad_p - inner)).astype(bf16)
                grad_q = grad_q + mm(grad_s, key)
                grad_k = grad_k + mm(grad_s, only_head(q_all, j), 0, 0)
            gqs[at, cols] = grad_q
            for side, new in ((0, grad_k * scale), (1, grad_v)):
                old = jnp.where(i == 0, 0.0, gkv_out[side, :, cols])
                gkv_out[side, :, cols] = old + new
        return carry

    lax.fori_loop(0, 2, block, 0)
    gq = (gqs[...] * scale).astype(bf16)
    gq_out[...] = gq
    gl = mm(gq, qu2[...], 1, 1)
    qgl_out[...] = gl
    pair = two(gl)
    weight = w[0].take(0)
    put(mine, everything, mm(gq[:half], weight, 1, 1) + mm(pair[:half], qd2[...], 1, 1))
    put(away, everything, mm(gq[half:], weight, 1, 1) + mm(pair[half:], qd2[...], 1, 1))


def linear_bwd(
    w, go, gt, q, st1, st2, ratio, den, owned, d2, u2, gq_out, gl_out, st_out, gh,
):
    half = go.shape[0]
    width = q.shape[1]
    depth = u2.shape[1]
    weight = w[0].take(0)
    for i, rows in enumerate((go, gt)):
        at = pl.ds(i * half, half)
        gl = mm(rows[:, :depth], u2[...], 1, 1)
        gl_out[at, :] = gl
        gh[at, :] = (mm(rows[:, :depth], weight) + mm(two(gl), d2[...], 1, 1)) * owned[...]
    st = st1[...] + st2[...]
    mask = head_mask(width)
    grad = gh[...]
    inverse = 1.0 / den[...]
    numer = grad * inverse
    grad_den = -head_total(grad * ratio[...], mask) * inverse
    raw = q[...]
    queries = jnp.maximum(raw, 0.0)
    grad_q = mm3(numer, spread_heads(st[:HD], width, mask)) + grad_den * st[HD : HD + 1]
    gq_out[...] = jnp.where(raw > 0.0, grad_q, 0.0).astype(bf16)
    st_out[:HD, :] = squeeze_heads(mm3(numer, queries, 0, 0), mask)
    total = jnp.sum(grad_den * queries, axis=0, keepdims=True)
    st_out[HD:, :] = jnp.broadcast_to(total, (8, width))


def linear_end(
    w, gq, k, v, st1, st2, d2, u2, gk_out, gv_out, gl_out, mine, away,
):
    width = k.shape[1]
    half = mine.shape[0]
    st = st1[...] + st2[...]
    mask = head_mask(width)
    wide = spread_heads(st[:HD], width, mask)
    raw = k[...]
    grad_k = mm3(v[...], wide) + st[HD : HD + 1]
    gk_out[...] = jnp.where(raw > 0.0, grad_k, 0.0).astype(bf16)
    gv_out[...] = mm3(jnp.maximum(raw, 0.0), wide, 1, 1).astype(bf16)
    grads = (gq, gk_out, gv_out)
    gl = sum(mm(g[...], u2[i], 1, 1) for i, g in enumerate(grads))
    gl_out[...] = gl
    pair = two(gl)
    weights = (w[0].take(0), w[0].take(1), w[1].take(0))

    def part(rows):
        total = mm(pair[rows], d2[...], 1, 1)
        for g, weight in zip(grads, weights):
            total = total + mm(g[rows, :], weight, 1, 1)
        return total

    put(mine, everything, part(slice(0, half)))
    put(away, everything, part(slice(half, 2 * half)))


def in_steps(rows, body, step=32):
    def one(i, carry):
        body(pl.ds(pl.multiple_of(i * step, step), step))
        return carry

    lax.fori_loop(0, rows // step, one, 0)


def slope_of_norm(values, grad):
    normed, inverse = row_stats(values)
    return inverse * (
        grad
        - jnp.mean(grad, axis=-1, keepdims=True)
        - normed * jnp.mean(grad * normed, axis=-1, keepdims=True)
    )


def total_of(low, got, at, width):
    return low[at, :width].astype(f32) + got[at, :width].astype(f32)


def end_attn(low, got, x, mods, after_out, own_out):
    def body(at):
        after = x[at, :].astype(f32) + mods[2:3, :] * total_of(low, got, at, x.shape[1])
        after_out[at, :] = after
        put(own_out, at, after)

    in_steps(x.shape[0], body)


def end_cross(low, got, before, mods, after_out, own_out):
    def body(at):
        after = before[at, :] + total_of(low, got, at, before.shape[1])
        after_out[at, :] = after
        normed, unused = row_stats(after)
        put(own_out, at, normed * (1.0 + mods[4:5, :]) + mods[3:4, :])

    in_steps(before.shape[0], body)


def end_output(low, got, before, mods, out):
    def body(at):
        put(out, at, before[at, :] + mods[5:6, :] * total_of(low, got, at, before.shape[1]))

    in_steps(before.shape[0], body)


def end_ffn_back(low, got, after, cot, mods, grad_out, own_out):
    def body(at):
        grad = total_of(low, got, at, after.shape[1]) * (1.0 + mods[4:5, :])
        grad = cot[at, :].astype(f32) + slope_of_norm(after[at, :], grad)
        grad_out[at, :] = grad
        put(own_out, at, grad)

    in_steps(after.shape[0], body)


def end_cross_back(low, got, before, mods, grad_out, own_out):
    def body(at):
        grad = before[at, :] + total_of(low, got, at, before.shape[1])
        grad_out[at, :] = grad
        put(own_out, at, mods[2:3, :] * grad)

    in_steps(before.shape[0], body)


def end_attn_back(low, got, before, x, mods, out):
    def body(at):
        grad = total_of(low, got, at, before.shape[1]) * (1.0 + mods[1:2, :])
        put(out, at, before[at, :] + slope_of_norm(x[at, :].astype(f32), grad))

    in_steps(before.shape[0], body)


def place_rows(where, own, other, out):
    half = own.shape[0]
    width = out.shape[1]
    out[pl.ds(pl.multiple_of(where[0] * half, half), half), :] = own[:, :width]
    out[pl.ds(pl.multiple_of((1 - where[0]) * half, half), half), :] = other[:, :width]


def ring_order(n):
    return list(range(0, n, 2)) + list(range(n - 1 - n % 2, 0, -2))


def ring_pairs(n):
    order = ring_order(n)
    return [(order[i], order[(i + 1) % n]) for i in range(n)]


def ring_source(n, step):
    z = lax.axis_index(W)
    place = jnp.where(z % 2 == 0, z // 2, n - 1 - z // 2)
    from_place = (place - step + n) % n
    return jnp.where(2 * from_place < n, 2 * from_place, 2 * (n - 1 - from_place) + 1)


def swap_pairs(n, distance):
    return [(i, i ^ distance) for i in range(n)]


def across(values, axis, distance=1):
    return lax.ppermute(values, axis, swap_pairs(lax.axis_size(axis), distance))


class Stream:
    def __init__(self, makers, order):
        self.n = lax.axis_size(W)
        self.makers, self.order = makers, list(order)
        self.own, self.got, self.crossed = {}, {}, {}
        self.flying, self.crossing = [], []

    def launch(self, name, step):
        if step == 1:
            self.own[name] = self.makers[name]()
            moving = self.own[name][0]
        else:
            moving = self.got[name, step - 1]
        self.flying.append((name, step, lax.ppermute(moving, W, ring_pairs(self.n))))

    def settle(self, done, crossed, values):
        leaves, tree = jax.tree.flatten((values, [d[2] for d in done], [d[2] for d in crossed]))
        values, arrived, over = jax.tree.unflatten(tree, lax.optimization_barrier(leaves))
        for (name, step, unused), v in zip(crossed, over):
            self.crossed[name, step] = v
        for (name, step, unused), v in zip(done, arrived):
            self.got[name, step] = v
            self.crossing.append((name, step, across(v, C)))
        return values

    def tick(self, values):
        done = [self.flying.pop(0)] if self.flying else []
        crossed = [self.crossing.pop(0)] if self.crossing and (len(self.crossing) > 1 or not done) else []
        values = self.settle(done, crossed, values)
        while len(self.flying) < 2 and self.order:
            name, step = self.order[0]
            if step > 1 and (name, step - 1) not in self.got:
                break
            self.order.pop(0)
            self.launch(name, step)
        return values

    def ready(self, names, values):
        last = [(name, self.n - 1) for name in names]
        while not all(key in self.got for key in last):
            values = self.tick(values)
        if self.flying:
            values = self.tick(values)
        left = [d for d in self.crossing if d[0] in names]
        self.crossing = [d for d in self.crossing if d[0] not in names]
        return self.settle([], left, values)

    def pieces(self, name):
        steps = range(1, self.n)
        mine = [self.own[name][0]] + [self.got[name, s] for s in steps]
        other = [self.own[name][1]] + [self.crossed[name, s] for s in steps]
        rows = mine[0].shape[0]
        if rows % 16 == 0:
            return mine + other
        c = lax.axis_index(C)
        buf = jnp.zeros((2, self.n * rows, mine[0].shape[1]), bf16)
        for s in range(self.n):
            at = ring_source(self.n, s) * rows
            buf = lax.dynamic_update_slice(buf, mine[s][None], (c, at, 0))
            buf = lax.dynamic_update_slice(buf, other[s][None], (1 - c, at, 0))
        return [buf]


class Weight:
    def __init__(self, meta, pieces, buf, sems, halves):
        self.meta, self.pieces, self.buf, self.sems, self.halves = meta, pieces, buf, sems, halves

    def copies(self, j, pieces):
        rows = pieces[0].shape[0]
        return [
            pltpu.make_async_copy(
                piece,
                self.buf.at[j, pl.ds(pl.multiple_of(self.meta[1 + k] * rows, rows), rows), :],
                self.sems.at[j, k],
            )
            for k, piece in enumerate(pieces)
        ]

    def start(self):
        count = len(self.pieces) // 2
        for j, half in enumerate(self.halves):
            if not count:
                pltpu.make_async_copy(self.pieces[0].at[half], self.buf.at[j], self.sems.at[j, 0]).start()
                continue

            @pl.when(self.meta[0] == half)
            def mine():
                for copy in self.copies(j, self.pieces[:count]):
                    copy.start()

            @pl.when(self.meta[0] != half)
            def other():
                for copy in self.copies(j, self.pieces[count:]):
                    copy.start()

    def take(self, j):
        count = len(self.pieces) // 2
        if not count:
            pltpu.make_async_copy(self.pieces[0].at[0], self.buf.at[j], self.sems.at[j, 0]).wait()
        else:
            for copy in self.copies(j, self.pieces[:count]):
                copy.wait()
        return self.buf[j]


def per_step(a):
    zeros = (0,) * (a.ndim - 1)
    return pl.BlockSpec((1,) + tuple(a.shape[1:]), lambda h: (h,) + zeros)


def all_of(a):
    zeros = (0,) * len(a.shape)
    return pl.BlockSpec(tuple(a.shape), lambda *g: zeros)


def scalars(a):
    return pl.BlockSpec(memory_space=pltpu.SMEM)


def anywhere(a):
    return pl.BlockSpec(memory_space=pl.ANY)


def run(kernel, ins, outs, scratch=(), steps=1, weights=(), meta=None):
    args, specs = [], []
    if weights:
        args.append(meta)
        specs.append(scalars(meta))
    counts, extra = [], []
    for pieces, halves in weights:
        counts.append((len(pieces), halves))
        args += pieces
        specs += [anywhere(p) for p in pieces]
        rows = pieces[0].shape[0] * len(pieces) // 2 if len(pieces) > 1 else pieces[0].shape[1]
        extra.append(pltpu.VMEM((len(halves), rows, pieces[0].shape[-1]), bf16))
        extra.append(pltpu.SemaphoreType.DMA((len(halves), max(len(pieces) // 2, 1))))
    first = len(args)
    for item in ins:
        a, spec = item if isinstance(item, tuple) else (item, all_of)
        args.append(a)
        specs.append(spec(a))
    shapes, out_specs = [], []
    for item in outs:
        dims, dtype, spec = item if len(item) == 3 else item + (all_of,)
        shapes.append(shape(dims, dtype))
        out_specs.append(spec(shapes[-1]))

    def body(*refs):
        if not weights:
            return kernel(*refs)
        at, loaders = 1, []
        tail = refs[len(refs) - len(extra) :]
        for i, (count, halves) in enumerate(counts):
            loaders.append(Weight(refs[0], refs[at : at + count], tail[2 * i], tail[2 * i + 1], halves))
            at += count

        @pl.when(pl.program_id(0) == 0)
        def begin():
            for loader in loaders:
                loader.start()

        kernel(loaders, *refs[first : len(refs) - len(extra)])

    return pl.pallas_call(
        body,
        grid=(steps,),
        in_specs=specs,
        out_specs=out_specs,
        out_shape=shapes,
        scratch_shapes=list(scratch) + extra,
        compiler_params=big,
    )(*args)


def twice(table, axis):
    return jnp.concatenate([table, table], axis=axis)


def two_parts(values, axis):
    high = lax.reduce_precision(values, 8, 7)
    return jnp.concatenate([high.astype(bf16), (values - high).astype(bf16)], axis=axis)


def fold(both):
    half = both.shape[0] // 2
    return both[:half] + both[half:]


def outer_sum(latent, values, axis=0):
    return fold(mm(two_parts(latent, 1 - axis), values, axis, 0))


def slot_layout(groups, rank, heads):
    per, left = heads // groups, heads % groups
    slots = per + (1 if left else 0)
    own_start = rank * per + jnp.minimum(rank, left)
    own_count = per + jnp.where(rank < left, 1, 0)
    first = jnp.minimum(own_start, heads - slots)
    slot = first + jnp.arange(slots, dtype=jnp.int32)
    owned = ((slot >= own_start) & (slot < own_start + own_count)).astype(f32)
    return slots, first, owned


def slot_ranges(groups, heads):
    per, left = heads // groups, heads % groups
    slots = per + (1 if left else 0)
    out = []
    for rank in range(groups):
        own_start = rank * per + min(rank, left)
        count = per + (1 if rank < left else 0)
        out.append((own_start - min(own_start, heads - slots), count))
    return out


def shards(
    tokens, caption, caption_lengths, adapter_index, modulation, cotangent,
    qkv_weight, proj_weight, cross_q_weight, cross_kv_weight, cross_out_weight,
    inverted_weight, depth_weight, point_weight,
    qkv_down, qkv_up, proj_down, proj_up, query_down, query_up, kv_down, kv_up,
    cross_down, cross_up, inverted_down, inverted_up, point_down, point_up,
):
    grid_rows, grid_cols, D = tokens.shape[1:]
    n = grid_rows * grid_cols
    half = n // 2
    heads = D // HD
    groups = lax.axis_size(T)
    rank = lax.axis_index(T)
    c = lax.axis_index(C)
    b = rank % 2
    adapters, R = qkv_up.shape[:2]
    slots, slot_first, owned = slot_layout(groups, rank, heads)
    width = slots * HD
    col = slot_first * HD
    owned = jnp.repeat(owned, HD)[None]
    hid = inverted_weight.shape[2]
    hh = hid // 2
    hid_first = rank * hid
    index = adapter_index[0]
    where = jnp.stack([b, c]).astype(jnp.int32)

    def cut(table, start, size, axis):
        return lax.dynamic_slice_in_dim(table, start, size, axis)

    def pick(table):
        return lax.dynamic_index_in_dim(table, index, 0, keepdims=False)

    def own_rows(rows):
        own = cut(rows, b * half, half, 0)
        return own, jnp.concatenate([own, cut(rows, (1 - b) * half, half, 0)])

    late = {}
    def pair_of(first, second):
        return [jnp.where(c == 0, first, second), jnp.where(c == 0, second, first)]

    def taken(table, middle, start, size):
        return lax.dynamic_slice(table, (0, middle, start), (table.shape[0], 1, size))[:, 0]

    def sides(make):
        return [make(c), make(1 - c)]

    makers = dict(
        a=lambda: sides(lambda i: taken(qkv_weight, i, col, width)),
        b=lambda: pair_of(taken(qkv_weight, 2, col, width), cut(proj_weight, col, width, 0).T),
        c=lambda: pair_of(cut(late["q"], col, width, 1), taken(late["kv"], 0, col, width)),
        d=lambda: pair_of(taken(late["kv"], 1, col, width), cut(late["o"], col, width, 0).T),
        v=lambda: sides(lambda i: taken(late["i"], 0, i * hh, hh)),
        g=lambda: sides(lambda i: taken(late["i"], 1, i * hh, hh)),
        p=lambda: sides(lambda i: cut(late["p"], i * hh, hh, 0).T),
    )
    size = lax.axis_size(W)
    order = []
    for pair in (("a", "b"), ("c", "d"), ("v", "g"), ("p",)):
        order += [(name, step) for step in range(1, size) for name in pair]
    if size == 4:
        order[-4:] = [("p", 1), ("g", 3), ("p", 2), ("p", 3)]
    stream = Stream(makers, order)
    tick = stream.tick

    def spread(first, last):
        return range(len(order) * first // 21, len(order) * last // 21)

    tick(())
    mods = modulation[0]
    low_tokens = tokens.reshape(n, D)
    x_low, x_rows = own_rows(low_tokens)
    qd2, qu2 = twice(pick(qkv_down), 1), twice(cut(pick(qkv_up), col, width, 2), 0).transpose(1, 0, 2)
    pd2, pu2 = twice(cut(pick(proj_down), col, width, 0), 1), twice(pick(proj_up), 0)
    raw = dict(q=cross_q_weight, kv=cross_kv_weight, o=cross_out_weight, i=inverted_weight, p=point_weight)
    tables = [query_down, query_up, kv_down, kv_up, cross_down, cross_up]
    tables_f = [inverted_down, inverted_up, point_down, point_up, depth_weight]
    for i in spread(0, 3):
        raw, tables, tables_f, caption, cotangent = tick((raw, tables, tables_f, caption, cotangent))
    late["q"], late["kv"], late["o"] = raw["q"], raw["kv"], raw["o"]
    query_down, query_up, kv_down, kv_up, cross_down, cross_up = tables
    cd2 = twice(cut(pick(cross_down), col, width, 0), 1)
    cu2 = twice(pick(cross_up), 0)
    xd2, xu2 = twice(pick(query_down), 1), twice(cut(pick(query_up), col, width, 1), 0)
    kd2, ku2 = twice(pick(kv_down), 1), twice(cut(pick(kv_up), col, width, 2), 0).transpose(1, 0, 2)
    text_here = caption.shape[1]
    text_rows = -(-text_here // 16) * 16
    cap = jnp.pad(caption[0], ((0, text_rows - text_here), (0, 0)))
    for i in spread(3, 6):
        raw, tables_f, cotangent = tick((raw, tables_f, cotangent))
    late["i"], late["p"] = raw["i"], raw["p"]
    inverted_down, inverted_up, point_down, point_up, depth_weight = tables_f
    x_rows = stream.ready("ab", x_rows)

    w_a, w_b = stream.pieces("a"), stream.pieces("b")
    meta = jnp.stack([c] + [ring_source(size, s) for s in range(size)]).astype(jnp.int32)
    padded = -(-D // LANES) * LANES
    rows_bf = ((n, D), bf16)
    thin = ((n, 2 * R), f32)
    wide = ((n, width), f32)
    wide_bf = ((n, width), bf16)
    pair = [((half, padded), f32), ((half, padded), bf16)]
    ended = [((half, D), f32), ((half, padded), bf16)]
    state_of = ((HD + 8, width), f32)
    attn_in, q_raw, k_raw, v_raw, qkv_lat, st_own = run(
        attn_front, [x_rows, mods, qd2, qu2], [rows_bf, wide, wide, wide, thin, state_of],
        weights=[(w_a, (0, 1)), (w_b, (0,))], meta=meta,
    )
    st_other = across(st_own, C)
    for i in spread(7, 8):
        st_own, st_other = tick((st_own, st_other))
    ratio, denom, mixed, proj_lat, mine, away = run(
        attn_back, [q_raw, st_own, st_other, owned, pd2, pu2], [wide, wide, wide_bf, thin] + pair,
        weights=[(w_b, (1,))], meta=meta,
    )

    def core_sum(mine, away):
        return (mine + across(away, T).astype(f32)).astype(bf16)

    def summed(mine, away, span):
        low, distance = core_sum(mine, away), 2
        while True:
            got = across(low, T, distance)
            for i in span:
                low = tick(low)
            distance, span = distance * 2, ()
            if distance >= groups:
                return low, got
            low = (low.astype(f32) + got.astype(f32)).astype(bf16)

    low, got = summed(mine, away, spread(8, 10))
    after_attn, cross_own = run(end_attn, [low, got, x_low, mods], ended)
    cross_other = across(cross_own, T)

    cross_own, cross_other, after_attn = stream.ready("cd", (cross_own, cross_other, after_attn))
    w_c, w_d = stream.pieces("c"), stream.pieces("d")
    kv_own, kv_lat = run(
        caption_rows, [cap, kd2, ku2], [((2, text_rows, width), bf16), ((text_rows, 2 * R), f32)],
        weights=[(w_c, (1,)), (w_d, (0,))], meta=meta,
    )
    kv_other = across(kv_own, C)
    places = jnp.arange(text_rows)
    live = jnp.concatenate([c * text_here + places, (1 - c) * text_here + places])
    live = (live < caption_lengths[0]) & (jnp.concatenate([places, places]) < text_here)
    live = live.astype(f32)[None]
    for i in spread(13, 14):
        kv_own, kv_other = tick((kv_own, kv_other))
    key_buf = pltpu.VMEM((2 * text_rows, width), bf16)
    query, mix, query_lat, cross_lat, lse, mine, away = run(
        cross_fwd,
        [cross_own, cross_other, kv_own, kv_other, live, owned, xd2, xu2, cd2, cu2],
        [wide_bf, wide_bf, thin, thin, ((n, LANES), f32)] + pair,
        [key_buf, key_buf],
        weights=[(w_c, (0,)), (w_d, (1,))], meta=meta,
    )
    low, got = summed(mine, away, spread(14, 16))
    after_cross, ffn_own = run(end_cross, [low, got, after_attn, mods], ended)
    ffn_other = across(ffn_own, T)

    fd2, fu2 = twice(pick(inverted_down), 1), twice(cut(pick(inverted_up), hid_first, hid, 2), 0)
    fu2 = fu2.reshape(2 * R, 2, 2, hh).transpose(1, 2, 0, 3)
    od2 = twice(cut(pick(point_down), hid_first, hid, 0), 1).reshape(2, hh, 2 * R)
    ou2 = twice(pick(point_up), 0)
    taps = depth_weight.astype(f32).reshape(9, 2, 2, hh).transpose(2, 1, 0, 3)
    cot = cotangent.reshape(n, D)
    cot_low, cot = own_rows(cot)
    ffn_own, ffn_other, after_cross = stream.ready("vg", (ffn_own, ffn_other, after_cross))
    w_v, w_g = stream.pieces("v"), stream.pieces("g")
    hid_f, hid_bf = ((2, n, hh), f32, per_step), ((2, n, hh), bf16, per_step)
    pre_v, pre_g, hid_v, hid_g, inv_lat = run(
        ffn_front,
        [ffn_own, ffn_other, fd2, (fu2[0], per_step), (fu2[1], per_step)],
        [hid_f, hid_f, hid_bf, hid_bf, thin],
        [pltpu.VMEM((n, D), bf16)],
        2,
        weights=[(w_v, (0, 1)), (w_g, (0, 1))], meta=meta,
    )

    def edge_rows(v, g):
        row = jnp.where(c == 0, grid_rows - 1, 0)
        at = jnp.where(c == 0, jnp.where(b == 1, half, 2 * half) - grid_cols, jnp.where(b == 0, 0, half))
        edge = jnp.stack([cut(v, at, grid_cols, 1), cut(g, at, grid_cols, 1)], axis=1)
        return across(edge, C)

    halo = edge_rows(hid_v, hid_g)
    hid_v, halo = stream.ready("p", (hid_v, halo))
    w_p = stream.pieces("p")
    grid_buf = pltpu.VMEM((n + 2 * grid_cols, hh), f32)
    row_acc = pltpu.VMEM((n, D), f32)
    gated, gcv, gcg, grad_ffn, point_gl, point_lat, mine, away = run(
        ffn_mid,
        [
            (where, scalars), (hid_v, per_step), (hid_g, per_step), (halo, per_step), (taps, per_step),
            cot, mods[5:6], (od2, per_step), ou2,
        ],
        [hid_bf, hid_bf, hid_bf, rows_bf, thin, thin] + pair,
        [grid_buf, grid_buf, pltpu.VMEM((n, hh), f32), row_acc],
        2,
        weights=[(w_p, (0, 1))], meta=meta,
    )
    halo = edge_rows(gcv, gcg)
    low, got = summed(mine, away, ())
    (output,) = run(end_output, [low, got, after_cross, mods], [((half, padded), f32)])
    output_other = across(output, T)

    gpv, gpg, inv_up_g, inv_gl, mine, away = run(
        ffn_back,
        [
            (where, scalars), (gcv, per_step), (gcg, per_step), (halo, per_step), (taps, per_step),
            (pre_v, per_step), (pre_g, per_step), inv_lat, fd2,
            (fu2[0], per_step), (fu2[1], per_step),
        ],
        [hid_bf, hid_bf, ((2, 2, 2 * R, hh), f32, per_step), thin] + pair,
        [grid_buf, grid_buf, row_acc],
        2,
        weights=[(w_v, (0, 1)), (w_g, (0, 1))], meta=meta,
    )
    low, got = summed(mine, away, ())
    grad_cross, gc_own = run(end_ffn_back, [low, got, after_cross, cot_low, mods], ended)
    gc_other = across(gc_own, T)

    grad_query, gkv, query_gl, cross_gl, mine, away = run(
        cross_bwd,
        [
            gc_own, gc_other, kv_own, kv_other, live, owned,
            xd2, xu2, cd2, cu2, query, lse,
        ],
        [wide_bf, ((2, 2 * text_rows, width), f32), thin, thin] + pair,
        [key_buf, key_buf, pltpu.VMEM((n, width), bf16), pltpu.VMEM((n, width), f32)],
        weights=[(w_c, (0,)), (w_d, (1,))], meta=meta,
    )
    gkv_got = across(gkv[:, text_rows:], C)
    low, got = summed(mine, away, ())
    grad_after, ga_own = run(end_cross_back, [low, got, grad_cross, mods], ended)
    ga_other = across(ga_own, T)
    grad_kv = (gkv[:, :text_rows] + gkv_got).astype(bf16)
    kv_gl = mm(grad_kv[0], ku2[0], 1, 1) + mm(grad_kv[1], ku2[1], 1, 1)

    grad_q, proj_gl, sg_own = run(
        linear_bwd,
        [ga_own, ga_other, q_raw, st_own, st_other, ratio, denom, owned, pd2, pu2],
        [wide_bf, thin, state_of],
        [pltpu.VMEM((n, width), f32)],
        weights=[(w_b, (1,))], meta=meta,
    )
    sg_other = across(sg_own, C)
    grad_k, grad_v, qkv_gl, mine, away = run(
        linear_end,
        [grad_q, k_raw, v_raw, sg_own, sg_other, qd2, qu2],
        [wide_bf, wide_bf, thin] + pair,
        weights=[(w_a, (0, 1)), (w_b, (0,))], meta=meta,
    )
    low, got = summed(mine, away, ())
    (input_grad,) = run(end_attn_back, [low, got, grad_after, x_low, mods], [((half, padded), f32)])
    input_other = across(input_grad, T)

    def in_order(own, other):
        return run(place_rows, [(where, scalars), own, other], [((n, D), f32)])[0]

    part_r = R // groups
    blocks = lax.axis_size(W) * lax.axis_size(C)
    ranges = slot_ranges(groups, heads)

    def by_rank(*values):
        joined = jnp.concatenate(values, axis=1)
        sent = joined.reshape(groups, part_r, joined.shape[1])
        return lax.all_to_all(sent, T, 0, 0, tiled=True)

    def slots_to_heads(got):
        return jnp.concatenate(
            [got[t][:, s * HD : (s + m) * HD] for t, (s, m) in enumerate(ranges)], axis=1
        )

    def hidden_to_full(got):
        return jnp.concatenate([got[t] for t in range(groups)], axis=1)

    def finish(values):
        sizes = [v.shape[1] // blocks for v in values]
        payload = jnp.concatenate([v.reshape(part_r, blocks, -1) for v in values], axis=2)
        payload = payload.transpose(1, 0, 2)
        mark = jnp.full((blocks, part_r, 1), 0.0, f32) + index.astype(f32)
        got = lax.all_to_all(jnp.concatenate([payload, mark], axis=2), (W, C), 0, 0, tiled=True)
        owner = got[:, 0, -1]
        chosen = (owner[None, :] == jnp.arange(adapters, dtype=f32)[:, None]).astype(f32)
        table = jnp.einsum("as,srk->ark", chosen, got[:, :, :-1], precision=full_precision)
        out, at = [], 0
        for size in sizes:
            out.append(table[:, :, at : at + size])
            at += size
        return out

    def lat(v):
        return v[:, :R]

    def turned(v):
        return jnp.where(b == 0, v, jnp.concatenate([v[:, half:], v[:, :half]], axis=1))

    lat_cols = [turned(lat(v).T) for v in (proj_lat, cross_lat, point_lat, inv_gl, query_gl)]
    got = jnp.sum(by_rank(*lat_cols, lat(kv_gl).T), axis=0)
    proj_s, cross_s, point_s, inv_s, query_s = (
        turned(got[:, i * n : (i + 1) * n]) for i in range(5)
    )
    kv_s = got[:, 5 * n :]

    def thin_sum(latent, values):
        return outer_sum(latent, values, 1)

    early = [
        outer_sum(lat(cross_gl), mix),
        outer_sum(lat(query_lat), grad_query),
        outer_sum(lat(kv_lat), grad_kv[0]),
        outer_sum(lat(kv_lat), grad_kv[1]),
        outer_sum(lat(point_gl), gated[0]),
        outer_sum(lat(point_gl), gated[1]),
    ] + [fold(inv_up_g[h, p]) for p in range(2) for h in range(2)]
    got = by_rank(*early)
    pieces, at = [], 0
    for v in early:
        pieces.append(got[:, :, at : at + v.shape[1]])
        at += v.shape[1]
    cross_down_g, query_up_g, key_up_g, value_up_g = (slots_to_heads(p) for p in pieces[:4])
    point_down_g = hidden_to_full(jnp.concatenate(pieces[4:6], axis=2))
    inv_up_full = [hidden_to_full(jnp.concatenate(pieces[i : i + 2], axis=2)) for i in (6, 8)]

    def joint(latent, own, other):
        both = thin_sum(latent[:, :half], own) + thin_sum(latent[:, half:], other)
        return both[:, :D]

    first = finish(
        [
            joint(cross_s, gc_own, gc_other),
            thin_sum(point_s, grad_ffn),
            joint(inv_s, ffn_own, ffn_other),
            joint(query_s, cross_own, cross_other),
            thin_sum(kv_s, cap),
            cross_down_g,
            query_up_g,
            key_up_g,
            value_up_g,
            point_down_g,
        ]
        + inv_up_full
    )
    qkv_s = turned(jnp.sum(by_rank(turned(lat(qkv_gl).T)), axis=0))
    last = [outer_sum(lat(proj_gl), mixed)] + [
        outer_sum(lat(qkv_lat), g) for g in (grad_q, grad_k, grad_v)
    ]
    got = by_rank(*last)
    last = [slots_to_heads(got[:, :, i * width : (i + 1) * width]) for i in range(4)]
    second = finish([joint(proj_s, ga_own, ga_other), thin_sum(qkv_s, attn_in)] + last)

    def down_of(t):
        return t.transpose(0, 2, 1)

    return (
        in_order(output, output_other).reshape(tokens.shape),
        in_order(input_grad, input_other).reshape(tokens.shape),
        down_of(second[1]),
        jnp.stack(second[3:6], axis=2),
        down_of(second[2]),
        second[0],
        down_of(first[3]),
        first[6],
        down_of(first[4]),
        jnp.stack(first[7:9], axis=2),
        down_of(first[5]),
        first[0],
        down_of(first[2]),
        jnp.stack(first[10:12], axis=2),
        down_of(first[9]),
        first[1],
    )


def solution(mesh):
    down = P(None, (W, C), T)
    up3 = P(None, T, (W, C))
    up4 = P(None, T, None, (W, C))
    rows = P(W, C)
    return jax.shard_map(
        shards,
        mesh=mesh,
        in_specs=(
            rows, rows, P(W), P(W), P(W), rows,
            P(W), P(None, W), P(W), P(W), P(None, W),
            P(W, None, T), P(None, None, None, T), P(T, W),
        )
        + (P(),) * 14,
        out_specs=(
            rows, rows, down, up4, down, up3, down, up3, down, up4, down, up3, down, up4, down, up3,
        ),
        check_vma=False,
    )
```

```python
import functools
import jax
import jax.numpy as jnp
from jax import lax
from jax.experimental import pallas as pl
from jax.experimental.pallas import tpu as pltpu
from jax.sharding import PartitionSpec as P

W, C, T = "weight", "context", "tensor"
HD = 32
LANES = 128
bf16, f32 = jnp.bfloat16, jnp.float32
full_precision = lax.Precision.HIGHEST
norm_eps = 1e-06
attention_epsilon = 1e-06
masked_score = -1000000000.0
big = pltpu.CompilerParams(vmem_limit_bytes=58 * 1024 * 1024)


def shape(dims, dtype):
    return jax.ShapeDtypeStruct(dims, dtype)


def mm(a, b, ca=1, cb=0):
    return lax.dot_general(a, b, (((ca,), (cb,)), ((), ())), preferred_element_type=f32)


def two(pair):
    high = pair.astype(bf16)
    rest = (pair - high.astype(f32)).astype(bf16)
    lane = lax.broadcasted_iota(jnp.int32, pair.shape, 1)
    return jnp.where(lane < pair.shape[1] // 2, high.astype(f32), rest.astype(f32)).astype(bf16)


def split(values):
    high = values.astype(bf16)
    return high, (values - high.astype(f32)).astype(bf16)


def mm3(a, b, ca=1, cb=0):
    ah, al = split(a)
    bh, bl = split(b)
    return mm(ah, bh, ca, cb) + mm(ah, bl, ca, cb) + mm(al, bh, ca, cb)


def head_mask(width):
    row = lax.broadcasted_iota(jnp.int32, (width, width), 0) // HD
    col = lax.broadcasted_iota(jnp.int32, (width, width), 1) // HD
    return (row == col).astype(f32)


def head_total(values, mask):
    high, low = split(values)
    low_mask = mask.astype(bf16)
    return mm(high, low_mask) + mm(low, low_mask)


def squeeze_heads(square, mask):
    kept = square * mask
    total = kept[:HD]
    for h in range(1, kept.shape[0] // HD):
        total = total + kept[h * HD : (h + 1) * HD]
    return total


def spread_heads(state, width, mask):
    return jnp.concatenate([state] * (width // HD), axis=0) * mask


def sigmoid(values):
    return 1.0 / (1.0 + jnp.exp(-values))


def row_stats(values):
    center = values - jnp.mean(values, axis=-1, keepdims=True)
    inverse = lax.rsqrt(jnp.mean(center * center, axis=-1, keepdims=True) + norm_eps)
    return center * inverse, inverse


def put(out, rows, values):
    width = values.shape[1]
    out[rows, :width] = values.astype(out.dtype)
    if width < out.shape[1]:
        out[rows, width:] = jnp.zeros((values.shape[0], out.shape[1] - width), out.dtype)


everything = slice(None)


def attn_front(w, x, mods, d2, u2, a_out, q_out, k_out, lat_out):
    n = x.shape[0]
    step = 64

    def norm(i, carry):
        at = pl.ds(pl.multiple_of(i * step, step), step)
        normed, unused = row_stats(x[at, :].astype(f32))
        a_out[at, :] = (normed * (1.0 + mods[1:2, :]) + mods[0:1, :]).astype(bf16)
        return carry

    lax.fori_loop(0, n // step, norm, 0)
    a = a_out[...]
    lat = mm(a, d2[...])
    lat_out[...] = lat
    pair = two(lat)
    width = q_out.shape[1]
    both = mm(a, w[0].take(0))
    q_out[...] = both[:, :width] + mm(pair, u2[0])
    k_out[...] = both[:, width:] + mm(pair, u2[1])


def attn_state(w, a, k, lat, u2, v_out, st_out):
    w[0].take(0)
    v_out[...] = mm(a[...], w[0].columns(0, 0, v_out.shape[1])) + mm(two(lat[...]), u2[2])
    keys = jnp.maximum(k[...], 0.0)
    width = keys.shape[1]
    st_out[:HD, :] = squeeze_heads(mm3(v_out[...], keys, 0, 0), head_mask(width))
    st_out[HD:, :] = jnp.broadcast_to(jnp.sum(keys, axis=0, keepdims=True), (8, width))


def put_partial(low, lat_pair, w, u2, mine, away):
    half = mine.shape[0]
    put(mine, everything, mm(low[:half], w, 1, 1) + mm(lat_pair[:half], u2))
    put(away, everything, mm(low[half:], w, 1, 1) + mm(lat_pair[half:], u2))


def attn_back(w, q, st1, st2, owned, d2, u2, ratio_out, den_out, mixed_out, lat_out, mine, away):
    st = st1[...] + st2[...]
    width = q.shape[1]
    mask = head_mask(width)
    queries = jnp.maximum(q[...], 0.0)
    numer = mm3(queries, spread_heads(st[:HD], width, mask), 1, 1)
    den = head_total(queries * st[HD : HD + 1], mask) + attention_epsilon
    ratio = numer / den
    ratio_out[...] = ratio
    den_out[...] = den
    mixed = (ratio * owned[...]).astype(bf16)
    mixed_out[...] = mixed
    lat = mm(mixed, d2[...])
    lat_out[...] = lat
    w[0].take(0)
    put_partial(mixed, two(lat), w[0].columns(0, width, width), u2[...], mine, away)


def caption_rows(w, own, other, d2, u2, kv_out, lat_out):
    here = own.shape[0]
    depth = d2.shape[0]
    width = u2.shape[2]
    weight = w[0].take(0)
    for i, rows in enumerate((own, other)):
        lat = mm(rows[:, :depth], d2[...])
        if i == 0:
            lat_out[...] = lat
        both = mm(rows[:, :depth], weight)
        for j in range(2):
            out = both[:, j * width : (j + 1) * width] + mm(two(lat), u2[j])
            kv_out[j, i * here : (i + 1) * here, :] = out.astype(bf16)


def lane_groups(width):
    return [(at, min(LANES, width - at)) for at in range(0, width, LANES)]


def only_head(values, j):
    lane = lax.broadcasted_iota(jnp.int32, values.shape, 1) // HD
    return jnp.where(lane == j, values.astype(f32), 0.0).astype(values.dtype)


def cross_fwd(
    w, rows, kv, live, owned, qd2, qu2, cd2, cu2, q_out, mix_out, qlat_out, clat_out, lse_out, part,
):
    width = q_out.shape[1]
    depth = qd2.shape[0]
    w[0].take(0)
    lat = mm(rows[:, :depth], qd2[...])
    qlat_out[...] = lat
    q_out[...] = (mm(rows[:, :depth], w[0].columns(0, 0, width)) + mm(two(lat), qu2[...])).astype(bf16)
    for first, size in lane_groups(width):
        cols = slice(first, first + size)
        query = q_out[:, cols]
        total = None
        for j in range(size // HD):
            scores = mm(query, only_head(kv[0, :, cols], j), 1, 1) * HD ** (-0.5)
            scores = jnp.where(live[...] > 0.0, scores, masked_score)
            top = jnp.max(scores, axis=-1, keepdims=True)
            exps = jnp.exp(scores - top)
            tot = jnp.sum(exps, axis=-1, keepdims=True)
            h = first // HD + j
            lse_out[:, h : h + 1] = top + jnp.log(tot)
            probs = (exps * (1.0 / tot)).astype(bf16)
            term = mm(probs, only_head(kv[1, :, cols], j))
            total = term if total is None else total + term
        mix_out[:, cols] = (total * owned[:, cols]).astype(bf16)
    mix = mix_out[...]
    lat = mm(mix, cd2[...])
    clat_out[...] = lat
    put(part, everything, mm(mix, w[0].columns(0, width, width), 1, 1) + mm(two(lat), cu2[...]))


def edge_rows(where, rows, edge):
    r = jnp.where(where[1] == 0, rows // edge - 1, 0)
    return pl.ds(own_first(r, edge, rows // 2, where[0]), edge)


def ffn_front(w, where, xo, xt, d2, uv, ug, pv, pg, hv, hg, lat_out, ev, eg, u):
    half = xo.shape[0]
    depth = d2.shape[0]
    h = pl.program_id(0)

    @pl.when(h == 0)
    def first():
        u[:half, :] = xo[:, :depth]
        u[half:, :] = xt[:, :depth]
        lat_out[...] = mm(u[...], d2[...])

    both = mm(u[...], w[0].take(h))
    pair = two(lat_out[...])
    hh = uv.shape[2]
    at = edge_rows(where, u.shape[0], ev.shape[1])
    for i, (up, pre, hid, edge) in enumerate(((uv, pv, hv, ev), (ug, pg, hg, eg))):
        s = both[:, i * hh : (i + 1) * hh] + mm(pair, up[0])
        pre[0] = s
        hid[0] = (s * sigmoid(s)).astype(bf16)
        edge[0] = hid[0, at, :]


def fill_grid(buf, rows, halo, b, c):
    half = rows.shape[0] // 2
    edge = halo.shape[0]
    buf[pl.ds(pl.multiple_of(edge + b * half, edge), half), :] = rows[:half, :].astype(f32)
    buf[pl.ds(pl.multiple_of(edge + (1 - b) * half, edge), half), :] = rows[half:, :].astype(f32)
    zero = jnp.zeros(halo.shape, f32)
    got = halo.astype(f32)
    buf[:edge, :] = jnp.where(c == 0, zero, got)
    buf[buf.shape[0] - edge :, :] = jnp.where(c == 0, got, zero)


def conv_row(buf, taps, r, edge, flip):
    sums = []
    rows = [buf[pl.ds(pl.multiple_of((r + i) * edge, edge), edge), :] for i in range(3)]
    for j in range(3):
        total = None
        for i in range(3):
            k = (2 - i) * 3 + 2 - j if flip else i * 3 + j
            term = rows[i] * taps[k : k + 1, :]
            total = term if total is None else total + term
        sums.append(total)
    cell = lax.broadcasted_iota(jnp.int32, sums[0].shape, 0)
    left = jnp.where(cell == 0, 0.0, pltpu.roll(sums[0], 1, 0))
    right = jnp.where(cell == edge - 1, 0.0, pltpu.roll(sums[2], edge - 1, 0))
    return left + sums[1] + right


def own_first(r, edge, half, b):
    per = half // edge
    return pl.multiple_of(jnp.where(r // per == b, 0, half) + (r % per) * edge, edge)


def ffn_mid(
    w, where, hv, hg, halo_v, halo_g, taps, cot, gate, d2, u2,
    gated_out, gcv_out, gcg_out, gffn_out, gl_out, lat_out, down_out, edge_out, mine, away, bv, bg, gg, acc,
):
    h = pl.program_id(0)
    b, c = where[0], where[1]
    n = hv.shape[1]
    half = n // 2
    edge = halo_v.shape[1]

    @pl.when(h == 0)
    def first():
        gffn_out[...] = (gate[...] * cot[...].astype(f32)).astype(bf16)
        gl_out[...] = mm(gffn_out[...], u2[...], 1, 1)

    fill_grid(bv, hv[0], halo_v[0], b, c)
    fill_grid(bg, hg[0], halo_g[0], b, c)
    weight = w[0].take(h)
    gg[...] = mm(gffn_out[...], weight) + mm(two(gl_out[...]), d2[0], 1, 1)

    def row(r, carry):
        v = conv_row(bv, taps[0, 0], r, edge, False)
        g = conv_row(bg, taps[0, 1], r, edge, False)
        sig = sigmoid(g)
        act = g * sig
        at = pl.ds(own_first(r, edge, half, b), edge)
        gated_out[0, at, :] = (v * act).astype(bf16)
        grad = gg[at, :]
        gcv_out[0, at, :] = (grad * act).astype(bf16)
        gcg_out[0, at, :] = (grad * v * (sig * (1.0 + g * (1.0 - sig)))).astype(bf16)
        return carry

    lax.fori_loop(0, n // edge, row, 0)
    at = edge_rows(where, n, edge)
    edge_out[0, 0] = gcv_out[0, at, :]
    edge_out[0, 1] = gcg_out[0, at, :]
    gated = gated_out[0]
    down_out[0] = mm(two(gl_out[...]), gated, 0, 0)
    part = mm(gated, weight, 1, 1)
    lat = mm(gated, d2[0])

    @pl.when(h == 0)
    def start():
        acc[...] = part
        lat_out[...] = lat

    @pl.when(h == 1)
    def end():
        total = lat_out[...] + lat
        lat_out[...] = total
        full = acc[...] + part + mm(two(total), u2[...])
        put(mine, everything, full[:half])
        put(away, everything, full[half:])


def ffn_back(
    w, where, gcv, gcg, halo, taps, pv, pg, lat, d2, uv, ug,
    gpv_out, gpg_out, up_out, gl_out, mine, away, bv, bg, acc,
):
    h = pl.program_id(0)
    b, c = where[0], where[1]
    n = gcv.shape[1]
    half = n // 2
    edge = halo.shape[2]
    fill_grid(bv, gcv[0], halo[0, 0], b, c)
    fill_grid(bg, gcg[0], halo[0, 1], b, c)

    def row(r, carry):
        at = pl.ds(own_first(r, edge, half, b), edge)
        for i, (buf, pre, out) in enumerate(((bv, pv, gpv_out), (bg, pg, gpg_out))):
            grad = conv_row(buf, taps[0, i], r, edge, True)
            s = pre[0, at, :]
            sig = sigmoid(s)
            out[0, at, :] = (grad * (sig * (1.0 + s * (1.0 - sig)))).astype(bf16)
        return carry

    lax.fori_loop(0, n // edge, row, 0)
    gpv, gpg = gpv_out[0], gpg_out[0]
    part = mm(jnp.concatenate([gpv, gpg], axis=1), w[0].take(h), 1, 1)
    gl = mm(gpv, uv[0], 1, 1) + mm(gpg, ug[0], 1, 1)
    pair = two(lat[...])
    up_out[0, 0] = mm(pair, gpv, 0, 0)
    up_out[0, 1] = mm(pair, gpg, 0, 0)

    @pl.when(h == 0)
    def start():
        acc[...] = part
        gl_out[...] = gl

    @pl.when(h == 1)
    def end():
        total = gl_out[...] + gl
        gl_out[...] = total
        full = acc[...] + part + mm(two(total), d2[...], 1, 1)
        put(mine, everything, full[:half])
        put(away, everything, full[half:])


def cross_bwd(
    w, go, gt, kv, live, owned, qd2, qu2, cd2, cu2, qo, qt, lo, lt,
    gq_out, gkv_out, qgl_out, cgl_out, mine, away, gm, gqs,
):
    half = go.shape[0]
    width = qo.shape[1]
    w[0].take(0)
    depth = cu2.shape[1]
    weight = w[0].columns(0, width, width)
    scale = HD ** (-0.5)
    for i, (rows, query, lse) in enumerate(((go, qo, lo), (gt, qt, lt))):
        at = slice(i * half, (i + 1) * half)
        gl = mm(rows[:, :depth], cu2[...], 1, 1)
        cgl_out[at, :] = gl
        grad = mm(rows[:, :depth], weight) + mm(two(gl), cd2[...], 1, 1)
        gm[...] = (grad * owned[...]).astype(bf16)
        for first, size in lane_groups(width):
            cols = slice(first, first + size)
            q_all, g_all = query[:, cols], gm[:, cols]
            grad_q, grad_k, grad_v = 0.0, 0.0, 0.0
            for j in range(size // HD):
                key, val = only_head(kv[0, :, cols], j), only_head(kv[1, :, cols], j)
                h = first // HD + j
                scores = mm(q_all, key, 1, 1) * scale
                scores = jnp.where(live[...] > 0.0, scores, masked_score)
                probs = jnp.exp(scores - lse[:, h : h + 1])
                grad_p = mm(g_all, val, 1, 1)
                grad_v = grad_v + mm(probs.astype(bf16), only_head(g_all, j), 0, 0)
                inner = jnp.sum(probs * grad_p, axis=-1, keepdims=True)
                grad_s = (probs * (grad_p - inner)).astype(bf16)
                grad_q = grad_q + mm(grad_s, key)
                grad_k = grad_k + mm(grad_s, only_head(q_all, j), 0, 0)
            gqs[at, cols] = grad_q
            for side, new in ((0, grad_k * scale), (1, grad_v)):
                gkv_out[side, :, cols] = new if i == 0 else gkv_out[side, :, cols] + new
    gq = (gqs[...] * scale).astype(bf16)
    gq_out[...] = gq
    gl = mm(gq, qu2[...], 1, 1)
    qgl_out[...] = gl
    pair = two(gl)
    weight = w[0].columns(0, 0, width)
    put(mine, everything, mm(gq[:half], weight, 1, 1) + mm(pair[:half], qd2[...], 1, 1))
    put(away, everything, mm(gq[half:], weight, 1, 1) + mm(pair[half:], qd2[...], 1, 1))


def linear_bwd(
    w, go, gt, q, st1, st2, ratio, den, owned, d2, u2, gq_out, gl_out, st_out, gh,
):
    half = go.shape[0]
    width = q.shape[1]
    depth = u2.shape[1]
    w[0].take(0)
    weight = w[0].columns(0, width, width)
    for i, rows in enumerate((go, gt)):
        at = pl.ds(i * half, half)
        gl = mm(rows[:, :depth], u2[...], 1, 1)
        gl_out[at, :] = gl
        gh[at, :] = (mm(rows[:, :depth], weight) + mm(two(gl), d2[...], 1, 1)) * owned[...]
    st = st1[...] + st2[...]
    mask = head_mask(width)
    grad = gh[...]
    inverse = 1.0 / den[...]
    numer = grad * inverse
    grad_den = -head_total(grad * ratio[...], mask) * inverse
    raw = q[...]
    queries = jnp.maximum(raw, 0.0)
    grad_q = mm3(numer, spread_heads(st[:HD], width, mask)) + grad_den * st[HD : HD + 1]
    gq_out[...] = jnp.where(raw > 0.0, grad_q, 0.0).astype(bf16)
    st_out[:HD, :] = squeeze_heads(mm3(numer, queries, 0, 0), mask)
    total = jnp.sum(grad_den * queries, axis=0, keepdims=True)
    st_out[HD:, :] = jnp.broadcast_to(total, (8, width))


def linear_end(
    w, gq, k, v, st1, st2, d2, u2, gk_out, gv_out, gl_out, mine, away,
):
    width = k.shape[1]
    half = mine.shape[0]
    st = st1[...] + st2[...]
    mask = head_mask(width)
    wide = spread_heads(st[:HD], width, mask)
    raw = k[...]
    grad_k = mm3(v[...], wide) + st[HD : HD + 1]
    gk_out[...] = jnp.where(raw > 0.0, grad_k, 0.0).astype(bf16)
    gv_out[...] = mm3(jnp.maximum(raw, 0.0), wide, 1, 1).astype(bf16)
    grads = (gq, gk_out, gv_out)
    gl = sum(mm(g[...], u2[i], 1, 1) for i, g in enumerate(grads))
    gl_out[...] = gl
    pair = two(gl)
    w[0].take(0)
    w[0].take(1)
    weights = [w[0].columns(j, first, width) for j, first in ((0, 0), (0, width), (1, 0))]

    def part(rows):
        total = mm(pair[rows], d2[...], 1, 1)
        for g, weight in zip(grads, weights):
            total = total + mm(g[rows, :], weight, 1, 1)
        return total

    put(mine, everything, part(slice(0, half)))
    put(away, everything, part(slice(half, 2 * half)))


def in_steps(rows, body, step=32):
    def one(i, carry):
        body(pl.ds(pl.multiple_of(i * step, step), step))
        return carry

    lax.fori_loop(0, rows // step, one, 0)


def slope_of_norm(values, grad):
    normed, inverse = row_stats(values)
    return inverse * (
        grad
        - jnp.mean(grad, axis=-1, keepdims=True)
        - normed * jnp.mean(grad * normed, axis=-1, keepdims=True)
    )


def total_of(low, got, at, width):
    return low[at, :width].astype(f32) + got[at, :width].astype(f32)


def end_attn(low, got, x, mods, after_out, own_out):
    def body(at):
        after = x[at, :].astype(f32) + mods[2:3, :] * total_of(low, got, at, x.shape[1])
        after_out[at, :] = after
        put(own_out, at, after)

    in_steps(x.shape[0], body)


def end_cross(low, got, before, mods, after_out, own_out):
    def body(at):
        after = before[at, :] + total_of(low, got, at, before.shape[1])
        after_out[at, :] = after
        normed, unused = row_stats(after)
        put(own_out, at, normed * (1.0 + mods[4:5, :]) + mods[3:4, :])

    in_steps(before.shape[0], body)


def end_output(low, got, before, mods, out):
    def body(at):
        put(out, at, before[at, :] + mods[5:6, :] * total_of(low, got, at, before.shape[1]))

    in_steps(before.shape[0], body)


def end_ffn_back(low, got, after, cot, mods, grad_out, own_out):
    def body(at):
        grad = total_of(low, got, at, after.shape[1]) * (1.0 + mods[4:5, :])
        grad = cot[at, :].astype(f32) + slope_of_norm(after[at, :], grad)
        grad_out[at, :] = grad
        put(own_out, at, grad)

    in_steps(after.shape[0], body)


def end_cross_back(low, got, before, mods, grad_out, own_out):
    def body(at):
        grad = before[at, :] + total_of(low, got, at, before.shape[1])
        grad_out[at, :] = grad
        put(own_out, at, mods[2:3, :] * grad)

    in_steps(before.shape[0], body)


def end_attn_back(low, got, before, x, mods, out):
    def body(at):
        grad = total_of(low, got, at, before.shape[1]) * (1.0 + mods[1:2, :])
        put(out, at, before[at, :] + slope_of_norm(x[at, :].astype(f32), grad))

    in_steps(before.shape[0], body)


def place_rows(where, own, other, out):
    width = out.shape[2]
    out[where[0]] = own[:, :width]
    out[1 - where[0]] = other[:, :width]


def fold(both):
    half = both.shape[0] // 2
    return both[:half] + both[half:]


def turned(v, b):
    half = v.shape[1] // 2
    return jnp.where(b == 0, v, jnp.concatenate([v[:, half:], v[:, :half]], axis=1))


def thin_sum(latent, *rows):
    high = latent.astype(bf16).astype(f32)
    both = jnp.concatenate([high, latent - high], axis=0).astype(bf16)
    total, at = None, 0
    for values in rows:
        size = values.shape[0]
        term = mm(both[:, at : at + size], values[...])
        total = term if total is None else total + term
        at += size
    return fold(total)


def outer_sum(latent, *rows):
    total, at = None, 0
    pair = two(latent)
    for values in rows:
        size = values.shape[0]
        term = mm(pair[at : at + size], values[...], 0, 0)
        total = term if total is None else total + term
        at += size
    return fold(total)


def set_segments(out, segments, width):
    for i, v in enumerate(segments):
        put(out.at[:, i * width : (i + 1) * width], everything, v)


def pack_first(where, point, up, l0, l1, l2, l3, sums):
    pieces = [point[0], point[1]] + [up[h, p] for p in range(2) for h in range(2)]
    n = l0.shape[0]
    first = sums.shape[1] - 4 * n
    set_segments(sums, [fold(v) for v in pieces], first // 6)
    for i, v in enumerate((l0, l1, l2, l3)):
        sums[:, first + i * n : first + (i + 1) * n] = turned(v[...].T[: sums.shape[0]], where[0])


def to_blocks(home, first, table):
    blocks = home.shape[0]
    size = table.shape[1] // blocks
    rows = table.shape[0]
    for i in range(blocks):
        home[i, first : first + rows, :size] = table[:, i * size : (i + 1) * size]


def set_mark(where, home, first):
    home[:, first:, :] = jnp.zeros((home.shape[0], home.shape[1] - first, home.shape[2]), f32) + where[2].astype(f32)


def second_sums(
    where, sums, gco, gct, fo, ft, gffn, mixo, mixt, cgl, qlat, gq, qgl, gkv, ggot, klat, ku2,
    home_out, projs, out, home,
):
    n, depth = gffn.shape
    b = where[0]
    first = sums.shape[2] - 4 * n
    parts = []
    for i in range(4):
        at = slice(first + i * n, first + (i + 1) * n)
        parts.append(turned(sums[0, :, at] + sums[1, :, at] + sums[2, :, at] + sums[3, :, at], b))
    projs[...] = parts[0]
    rows = parts[0].shape[0]
    home[...] = jnp.zeros(home.shape, f32)
    to_blocks(home, 0, thin_sum(parts[1], gco, gct)[:, :depth])
    to_blocks(home, rows, thin_sum(parts[2], gffn))
    to_blocks(home, 2 * rows, thin_sum(parts[3], fo, ft)[:, :depth])
    pad, hh = first // 6, home.shape[2] * home.shape[0] // 8
    size = home.shape[2]
    for j in range(3):
        for i in range(home.shape[0]):
            t, h, at = i * size // (2 * hh), i * size % (2 * hh) // hh, i * size % hh
            at += (2 * j + h) * pad
            home[i, (3 + j) * rows : (4 + j) * rows, :] = sums[t, :, at : at + size]
    set_mark(where, home, 6 * rows)
    home_out[...] = home[...].astype(home_out.dtype)
    here = ggot.shape[1]
    gk = (gkv[0, :here, :] + ggot[0]).astype(bf16)
    gv = (gkv[1, :here, :] + ggot[1]).astype(bf16)
    segments = [outer_sum(cgl[...], mixo, mixt), outer_sum(qlat[...], gq)]
    segments += [outer_sum(klat[...], gk), outer_sum(klat[...], gv)]
    pad = -(-gq.shape[1] // LANES) * LANES
    set_segments(out, segments, pad)
    rank = out.shape[0]
    out[:, 4 * pad : 4 * pad + n] = turned(qgl[...].T[:rank], b)
    kvgl = mm(gk, ku2[0], 1, 1) + mm(gv, ku2[1], 1, 1)
    put(out.at[:, 4 * pad + n :], everything, kvgl.T[:rank])


def third_sums(where, before, pgl, mixed, qlat, gq, gk, gv, qgl, out):
    first = before.shape[1]
    out[:, :first] = before[...]
    segments = [outer_sum(pgl[...], mixed)] + [outer_sum(qlat[...], g) for g in (gq, gk, gv)]
    pad = -(-gq.shape[1] // LANES) * LANES
    set_segments(out.at[:, first : first + 4 * pad], segments, pad)
    out[:, first + 4 * pad :] = turned(qgl[...].T[: out.shape[0]], where[0])


def last_sums(ranges, where, sums, projs, gao, gat, xo, xt, cap, a, home_out, home):
    n, depth = a.shape
    b = where[0]
    text = -(-cap.shape[0] // LANES) * LANES
    pad = (sums.shape[2] - 2 * n - text) // 8
    second = 4 * pad + n + text
    rows = projs.shape[0]

    def summed(first, size):
        return sum(sums[t, :, first : first + size] for t in range(sums.shape[0]))

    def heads(first):
        parts = [sums[t, :, first + s * HD : first + (s + m) * HD] for t, (s, m) in enumerate(ranges)]
        return jnp.concatenate(parts, axis=1)

    tables = [
        thin_sum(turned(summed(4 * pad, n), b), xo, xt)[:, :depth],
        thin_sum(summed(4 * pad + n, cap.shape[0]), cap)[:, :depth],
        thin_sum(projs[...], gao, gat)[:, :depth],
    ]
    tables += [heads(j * pad) for j in range(4)] + [heads(second + j * pad) for j in range(4)]
    tables.append(thin_sum(turned(summed(second + 4 * pad, n), b), a))
    for j, table in enumerate(tables):
        to_blocks(home, j * rows, table)
    set_mark(where, home, len(tables) * rows)
    home_out[...] = home[...].astype(home_out.dtype)


def adapter_tables(got, out):
    last = got.shape[1] - 1
    for i in range(out.shape[0]):
        total = None
        for s in range(got.shape[0]):
            values = got[s].astype(f32)
            term = jnp.where(values[last:, :1] == float(i), values, 0.0)
            total = term if total is None else total + term
        out[i] = total


def ring_order(n):
    return list(range(0, n, 2)) + list(range(n - 1 - n % 2, 0, -2))


def ring_pairs(n):
    order = ring_order(n)
    return [(order[i], order[(i + 1) % n]) for i in range(n)]


def ring_source(n, step):
    z = lax.axis_index(W)
    place = jnp.where(z % 2 == 0, z // 2, n - 1 - z // 2)
    from_place = (place - step + n) % n
    return jnp.where(2 * from_place < n, 2 * from_place, 2 * (n - 1 - from_place) + 1)


def swap_pairs(n, distance):
    return [(i, i ^ distance) for i in range(n)]


def across(values, axis, distance=1):
    return lax.ppermute(values, axis, swap_pairs(lax.axis_size(axis), distance))


class Stream:
    def __init__(self, makers, order):
        self.n = lax.axis_size(W)
        self.makers, self.order = makers, list(order)
        self.own, self.got, self.crossed = {}, {}, {}
        self.flying, self.crossing = [], []

    def launch(self):
        while not self.flying and self.order:
            name, step = self.order[0]
            if step == 1:
                self.own[name] = self.makers[name]()
                moving = self.own[name][0]
            elif (name, step - 1) in self.got:
                moving = self.got[name, step - 1]
            else:
                break
            self.order.pop(0)
            self.flying.append((name, step, lax.ppermute(moving, W, ring_pairs(self.n))))

    def fence(self, values):
        done = [self.flying.pop(0)] if self.flying else []
        crossed, self.crossing = self.crossing, []
        leaves, tree = jax.tree.flatten((values, [d[2] for d in done], [d[2] for d in crossed]))
        values, arrived, over = jax.tree.unflatten(tree, lax.optimization_barrier(leaves))
        for d, v in zip(crossed, over):
            self.crossed[d[0], d[1]] = v
        for d, v in zip(done, arrived):
            self.got[d[0], d[1]] = v
            self.crossing.append((d[0], d[1], across(v, C)))
        self.launch()
        return values

    def fences(self, count, values):
        for i in range(count * (self.n - 1) // 3):
            values = self.fence(values)
        return values

    def ready(self, names, values):
        while not all((name, self.n - 1) in self.crossed for name in names):
            values = self.fence(values)
        return values

    def pieces(self, name):
        steps = range(1, self.n)
        mine = [self.own[name][0]] + [self.got[name, s] for s in steps]
        other = [self.own[name][1]] + [self.crossed[name, s] for s in steps]
        rows = mine[0].shape[0]
        if rows % 16 == 0:
            return mine + other
        c = lax.axis_index(C)
        buf = jnp.zeros((2, self.n * rows, mine[0].shape[1]), bf16)
        for s in range(self.n):
            at = ring_source(self.n, s) * rows
            buf = lax.dynamic_update_slice(buf, mine[s][None], (c, at, 0))
            buf = lax.dynamic_update_slice(buf, other[s][None], (1 - c, at, 0))
        return [buf]


class Weight:
    def __init__(self, meta, pieces, buf, sems, halves):
        self.meta, self.pieces, self.buf, self.sems, self.halves = meta, pieces, buf, sems, halves

    def copies(self, j, pieces):
        rows = pieces[0].shape[0]
        return [
            pltpu.make_async_copy(
                piece,
                self.buf.at[j, pl.ds(pl.multiple_of(self.meta[1 + k] * rows, rows), rows), :],
                self.sems.at[j, k],
            )
            for k, piece in enumerate(pieces)
        ]

    def start(self):
        count = len(self.pieces) // 2
        for j, half in enumerate(self.halves):
            if not count:
                pltpu.make_async_copy(self.pieces[0].at[half], self.buf.at[j], self.sems.at[j, 0]).start()
                continue

            @pl.when(self.meta[0] == half)
            def mine():
                for copy in self.copies(j, self.pieces[:count]):
                    copy.start()

            @pl.when(self.meta[0] != half)
            def other():
                for copy in self.copies(j, self.pieces[count:]):
                    copy.start()

    def take(self, j):
        count = len(self.pieces) // 2
        if not count:
            pltpu.make_async_copy(self.pieces[0].at[0], self.buf.at[j], self.sems.at[j, 0]).wait()
        else:
            for copy in self.copies(j, self.pieces[:count]):
                copy.wait()
        return self.buf[j]

    def columns(self, j, first, size):
        return self.buf[j, :, first : first + size]


def per_step(a):
    zeros = (0,) * (a.ndim - 1)
    return pl.BlockSpec((1,) + tuple(a.shape[1:]), lambda h: (h,) + zeros)


def row_block(a):
    return pl.BlockSpec((a.shape[0] // 4, a.shape[1]), lambda i: (i, 0))


def both_blocks(a):
    return pl.BlockSpec((2, a.shape[1] // 4, a.shape[2]), lambda i: (0, i, 0))


def all_of(a):
    zeros = (0,) * len(a.shape)
    return pl.BlockSpec(tuple(a.shape), lambda *g: zeros)


def scalars(a):
    return pl.BlockSpec(memory_space=pltpu.SMEM)


def anywhere(a):
    return pl.BlockSpec(memory_space=pl.ANY)


def run(kernel, ins, outs, scratch=(), steps=1, weights=(), meta=None):
    args, specs = [], []
    if weights:
        args.append(meta)
        specs.append(scalars(meta))
    counts, extra = [], []
    for pieces, halves in weights:
        counts.append((len(pieces), halves))
        args += pieces
        specs += [anywhere(p) for p in pieces]
        rows = pieces[0].shape[0] * len(pieces) // 2 if len(pieces) > 1 else pieces[0].shape[1]
        extra.append(pltpu.VMEM((len(halves), rows, pieces[0].shape[-1]), bf16))
        extra.append(pltpu.SemaphoreType.DMA((len(halves), max(len(pieces) // 2, 1))))
    first = len(args)
    for item in ins:
        a, spec = item if isinstance(item, tuple) else (item, all_of)
        args.append(a)
        specs.append(spec(a))
    shapes, out_specs = [], []
    for item in outs:
        dims, dtype, spec = item if len(item) == 3 else item + (all_of,)
        shapes.append(shape(dims, dtype))
        out_specs.append(spec(shapes[-1]))

    def body(*refs):
        if not weights:
            return kernel(*refs)
        at, loaders = 1, []
        tail = refs[len(refs) - len(extra) :]
        for i, (count, halves) in enumerate(counts):
            loaders.append(Weight(refs[0], refs[at : at + count], tail[2 * i], tail[2 * i + 1], halves))
            at += count

        @pl.when(pl.program_id(0) == 0)
        def begin():
            for loader in loaders:
                loader.start()

        kernel(loaders, *refs[first : len(refs) - len(extra)])

    return pl.pallas_call(
        body,
        grid=(steps,),
        in_specs=specs,
        out_specs=out_specs,
        out_shape=shapes,
        scratch_shapes=list(scratch) + extra,
        compiler_params=big,
    )(*args)


def twice(table, axis):
    return jnp.concatenate([table, table], axis=axis)


def slot_layout(groups, rank, heads):
    per, left = heads // groups, heads % groups
    slots = per + (1 if left else 0)
    own_start = rank * per + jnp.minimum(rank, left)
    own_count = per + jnp.where(rank < left, 1, 0)
    first = jnp.minimum(own_start, heads - slots)
    slot = first + jnp.arange(slots, dtype=jnp.int32)
    owned = ((slot >= own_start) & (slot < own_start + own_count)).astype(f32)
    return slots, first, owned


def slot_ranges(groups, heads):
    per, left = heads // groups, heads % groups
    slots = per + (1 if left else 0)
    out = []
    for rank in range(groups):
        own_start = rank * per + min(rank, left)
        count = per + (1 if rank < left else 0)
        out.append((own_start - min(own_start, heads - slots), count))
    return out


def shards(
    tokens, caption, caption_lengths, adapter_index, modulation, cotangent,
    qkv_weight, proj_weight, cross_q_weight, cross_kv_weight, cross_out_weight,
    inverted_weight, depth_weight, point_weight,
    qkv_down, qkv_up, proj_down, proj_up, query_down, query_up, kv_down, kv_up,
    cross_down, cross_up, inverted_down, inverted_up, point_down, point_up,
):
    grid_rows, grid_cols, D = tokens.shape[1:]
    n = grid_rows * grid_cols
    half = n // 2
    heads = D // HD
    groups = lax.axis_size(T)
    rank = lax.axis_index(T)
    c = lax.axis_index(C)
    b = rank % 2
    adapters, R = qkv_up.shape[:2]
    slots, slot_first, owned = slot_layout(groups, rank, heads)
    width = slots * HD
    col = slot_first * HD
    owned = jnp.repeat(owned, HD)[None]
    hid = inverted_weight.shape[2]
    hh = hid // 2
    hid_first = rank * hid
    index = adapter_index[0]
    where = jnp.stack([b, c, index]).astype(jnp.int32)

    def cut(table, start, size, axis):
        return lax.dynamic_slice_in_dim(table, start, size, axis)

    def pick(table):
        return lax.dynamic_index_in_dim(table, index, 0, keepdims=False)

    def own_rows(rows):
        own = cut(rows, b * half, half, 0)
        return own, jnp.concatenate([own, cut(rows, (1 - b) * half, half, 0)])

    late = {}
    def pair_of(first, second):
        return [jnp.where(c == 0, first, second), jnp.where(c == 0, second, first)]

    def taken(table, middle, start, size):
        return lax.dynamic_slice(table, (0, middle, start), (table.shape[0], 1, size))[:, 0]

    def beside(*values):
        return jnp.concatenate(values, axis=1)

    def hidden_columns(i):
        return beside(taken(inverted_weight, 0, i * hh, hh), taken(inverted_weight, 1, i * hh, hh))

    def both(table, start):
        return beside(taken(table, 0, start, width), taken(table, 1, start, width))

    makers = dict(
        ab=lambda: pair_of(
            both(qkv_weight, col), beside(taken(qkv_weight, 2, col, width), cut(proj_weight, col, width, 0).T)
        ),
        cd=lambda: pair_of(
            both(cross_kv_weight, late["col"]),
            beside(cut(cross_q_weight, late["col"], width, 1), cut(cross_out_weight, late["col"], width, 0).T),
        ),
        vg=lambda: [hidden_columns(late["c"]), hidden_columns(1 - late["c"])],
        p=lambda: [cut(point_weight, late["c"] * hh, hh, 0).T, cut(point_weight, (1 - late["c"]) * hh, hh, 0).T],
    )
    size = lax.axis_size(W)
    order = [(name, step) for name in ("ab", "cd", "vg", "p") for step in range(1, size)]
    stream = Stream(makers, order)
    fences = stream.fences

    stream.launch()
    mods = modulation[0]
    low_tokens = tokens.reshape(n, D)
    x_low, x_rows = own_rows(low_tokens)
    qd2, qu2 = twice(pick(qkv_down), 1), twice(cut(pick(qkv_up), col, width, 2), 0).transpose(1, 0, 2)
    pd2, pu2 = twice(cut(pick(proj_down), col, width, 0), 1), twice(pick(proj_up), 0)
    text_here = caption.shape[1]
    text_rows = -(-text_here // 16) * 16
    padded = -(-D // LANES) * LANES
    cap = jnp.pad(caption[0], ((0, text_rows - text_here), (0, padded - D)))
    cap_other = across(cap, C)
    late.update(col=col, c=c)

    def later(values):
        late["col"], late["c"], values = fences(1, (late["col"], late["c"], values))
        return values

    tables = [query_down, query_up, kv_down, kv_up, cross_down, cross_up]
    tables_f = [inverted_down, inverted_up, point_down, point_up, depth_weight]
    tables, tables_f, cap, cap_other, cotangent = later((tables, tables_f, cap, cap_other, cotangent))
    query_down, query_up, kv_down, kv_up, cross_down, cross_up = tables
    cd2 = twice(cut(pick(cross_down), col, width, 0), 1)
    cu2 = twice(pick(cross_up), 0)
    xd2, xu2 = twice(pick(query_down), 1), twice(cut(pick(query_up), col, width, 1), 0)
    kd2, ku2 = twice(pick(kv_down), 1), twice(cut(pick(kv_up), col, width, 2), 0).transpose(1, 0, 2)
    tables_f, cotangent = later((tables_f, cotangent))
    inverted_down, inverted_up, point_down, point_up, depth_weight = tables_f
    fd2, fu2 = twice(pick(inverted_down), 1), twice(cut(pick(inverted_up), hid_first, hid, 2), 0)
    fu2 = fu2.reshape(2 * R, 2, 2, hh).transpose(1, 2, 0, 3)
    od2 = twice(cut(pick(point_down), hid_first, hid, 0), 1).reshape(2, hh, 2 * R)
    ou2 = twice(pick(point_up), 0)
    taps = depth_weight.astype(f32).reshape(9, 2, 2, hh).transpose(2, 1, 0, 3)
    cot_low, cot = own_rows(cotangent.reshape(n, D))
    places = jnp.arange(text_rows)
    live = jnp.concatenate([c * text_here + places, (1 - c) * text_here + places])
    live = (live < caption_lengths[0]) & (jnp.concatenate([places, places]) < text_here)
    live = live.astype(f32)[None]
    tables = [cd2, cu2, xd2, xu2, kd2, ku2, fd2, fu2, od2, ou2, taps, cot_low, cot, live]
    x_rows, tables = later((x_rows, tables))
    cd2, cu2, xd2, xu2, kd2, ku2, fd2, fu2, od2, ou2, taps, cot_low, cot, live = tables
    x_rows = stream.ready(["ab"], x_rows)

    w_ab = stream.pieces("ab")
    meta = jnp.stack([c] + [ring_source(size, s) for s in range(size)]).astype(jnp.int32)
    rows_bf = ((n, D), bf16)
    thin = ((n, 2 * R), f32)
    wide = ((n, width), f32)
    wide_bf = ((n, width), bf16)
    pair = [((half, padded), f32), ((half, padded), bf16)]
    ended = [((half, D), f32, row_block), ((half, padded), bf16, row_block)]

    def finish_rows(kernel, arrays, outs):
        return run(kernel, [(v, row_block) for v in arrays] + [mods], outs, steps=4)

    state_of = ((HD + 8, width), f32)
    attn_in, q_raw, k_raw, qkv_lat = run(
        attn_front, [x_rows, mods, qd2, qu2], [rows_bf, wide, wide, thin], weights=[(w_ab, (0,))], meta=meta,
    )
    v_raw, st_own = run(
        attn_state, [attn_in, k_raw, qkv_lat, qu2], [wide, state_of], weights=[(w_ab, (1,))], meta=meta,
    )
    st_own, st_other = fences(1, (st_own, across(st_own, C)))
    ratio, denom, mixed, proj_lat, mine, away = run(
        attn_back, [q_raw, st_own, st_other, owned, pd2, pu2], [wide, wide, wide_bf, thin] + pair,
        weights=[(w_ab, (1,))], meta=meta,
    )

    def exchanged(mine, away, pace=lambda low: low):
        low, distance = (mine + across(away, T).astype(f32)).astype(bf16), 2
        while True:
            low = pace(low)
            got = across(low, T, distance)
            distance *= 2
            if distance >= groups:
                return low, got
            low = (low.astype(f32) + got.astype(f32)).astype(bf16)

    def while_streaming(mine, away):
        return fences(1, exchanged(mine, away))

    mine, away = fences(1, (mine, away))
    low, got = while_streaming(mine, away)
    after_attn, cross_own = finish_rows(end_attn, [low, got, x_low], ended)
    cross_other = across(cross_own, T)

    cap, cross_own, cross_other, after_attn = stream.ready(["cd"], (cap, cross_own, cross_other, after_attn))
    w_cd = stream.pieces("cd")
    kv_all, kv_lat = run(
        caption_rows, [cap, cap_other, kd2, ku2], [((2, 2 * text_rows, width), bf16), ((text_rows, 2 * R), f32)],
        weights=[(w_cd, (0,))], meta=meta,
    )
    kv_all, cross_own, cross_other = fences(1, (kv_all, cross_own, cross_other))
    half_bf, half_thin = ((half, width), bf16), ((half, 2 * R), f32)

    def cross_part(rows, kv, dtype):
        return run(
            cross_fwd,
            [rows, kv, live, owned, xd2, xu2, cd2, cu2],
            [half_bf, half_bf, half_thin, half_thin, ((half, LANES), f32), ((half, padded), dtype)],
            weights=[(w_cd, (1,))], meta=meta,
        )

    *cross_t, away = cross_part(cross_other, kv_all, bf16)
    away, cross_tied, kv_tied = lax.optimization_barrier((away, cross_own, kv_all))
    *cross_o, mine = cross_part(cross_tied, kv_tied, f32)
    mine, away = fences(1, (mine, away))
    query, mix, query_lat, cross_lat, lse = zip(cross_o, cross_t)
    low, got = while_streaming(mine, away)
    after_cross, ffn_own = finish_rows(end_cross, [low, got, after_attn], ended)
    ffn_other = across(ffn_own, T)

    query_lat, cross_lat = jnp.concatenate(query_lat), jnp.concatenate(cross_lat)

    ffn_own, ffn_other, after_cross = stream.ready(["vg"], fences(1, (ffn_own, ffn_other, after_cross)))
    w_vg = stream.pieces("vg")
    hid_f, hid_bf = ((2, n, hh), f32, per_step), ((2, n, hh), bf16, per_step)
    edge_of = ((2, grid_cols, hh), bf16, per_step)
    pre_v, pre_g, hid_v, hid_g, inv_lat, edge_v, edge_g = run(
        ffn_front, [(where, scalars), ffn_own, ffn_other, fd2, (fu2[0], per_step), (fu2[1], per_step)],
        [hid_f, hid_f, hid_bf, hid_bf, thin, edge_of, edge_of], [pltpu.VMEM((n, D), bf16)], 2,
        weights=[(w_vg, (0, 1))], meta=meta,
    )
    hid_v, edge_v, edge_g = fences(1, (hid_v, edge_v, edge_g))
    halo_v, halo_g = across(edge_v, C), across(edge_g, C)
    hid_v, halo_v, halo_g = stream.ready(["p"], (hid_v, halo_v, halo_g))
    w_p = stream.pieces("p")
    grid_buf = pltpu.VMEM((n + 2 * grid_cols, hh), f32)
    row_acc = pltpu.VMEM((n, D), f32)
    gated, gcv, gcg, grad_ffn, point_gl, point_lat, point_down_g, edge, mine, away = run(
        ffn_mid,
        [
            (where, scalars), (hid_v, per_step), (hid_g, per_step), (halo_v, per_step), (halo_g, per_step), (taps, per_step),
            cot, mods[5:6], (od2, per_step), ou2,
        ],
        [hid_bf, hid_bf, hid_bf, rows_bf, thin, thin, ((2, 2 * R, hh), f32, per_step)]
        + [((2, 2, grid_cols, hh), bf16, per_step)] + pair,
        [grid_buf, grid_buf, pltpu.VMEM((n, hh), f32), row_acc],
        2,
        weights=[(w_p, (0, 1))], meta=meta,
    )
    halo = across(edge, C)
    tied = []

    def after_halo(low):
        low, *tied[:] = lax.optimization_barrier((low, halo, gcv, gcg))
        return low

    out_low, out_got = exchanged(mine, away, after_halo)
    halo, gcv, gcg = tied

    gpv, gpg, inv_up_g, inv_gl, mine, away = run(
        ffn_back,
        [
            (where, scalars), (gcv, per_step), (gcg, per_step), (halo, per_step), (taps, per_step),
            (pre_v, per_step), (pre_g, per_step), inv_lat, fd2,
            (fu2[0], per_step), (fu2[1], per_step),
        ],
        [hid_bf, hid_bf, ((2, 2, 2 * R, hh), f32, per_step), thin] + pair,
        [grid_buf, grid_buf, row_acc],
        2,
        weights=[(w_vg, (0, 1))], meta=meta,
    )
    part_r = R // groups
    blocks = size * lax.axis_size(C)
    ranges = slot_ranges(groups, heads)

    def swapped(sent):
        return lax.all_to_all(sent.reshape(groups, part_r, sent.shape[1]), T, 0, 0, tiled=True)

    def sent_home(values):
        got = lax.all_to_all(values, (W, C), 0, 0, tiled=True)
        return run(adapter_tables, [got], [((adapters,) + got.shape[1:], f32)])[0]

    def up_to_tiles(size):
        return -(-size // LANES) * LANES

    def table_rows(table, i, size):
        return table[:, i * part_r : (i + 1) * part_r, : size // blocks]

    def down_rows(table, i, size):
        return table_rows(table, i, size).transpose(0, 2, 1)

    def together(*values):
        return lax.optimization_barrier(values)

    def during(mine, away, inputs, work):
        held = []

        def pace(low):
            low, tied = together(low, inputs)
            held[:] = [tied]
            return low

        low, got = exchanged(mine, away, pace)
        return together(low, got, work(*held[0]))

    def first_work(out_low, out_got, after_cross, inv_up_g, point_down_g, lats):
        (output,) = finish_rows(end_output, [out_low, out_got, after_cross], [((half, padded), f32, row_block)])
        (sums,) = run(
            pack_first, [(where, scalars), point_down_g, inv_up_g, *lats], [((R, 6 * up_to_tiles(hh) + 4 * n), f32)],
        )
        return output, sums

    mine, away, out_low, out_got = together(mine, away, out_low, out_got)
    low, got, (output, sums_f) = during(
        mine, away,
        (out_low, out_got, after_cross, inv_up_g, point_down_g, (proj_lat, cross_lat, point_lat, inv_gl)),
        first_work,
    )
    grad_cross, gc_own = finish_rows(end_ffn_back, [low, got, after_cross, cot_low], ended)
    gc_other = across(gc_own, T)

    gc_own, gc_other, output, sums_f = together(gc_own, gc_other, output, sums_f)
    output_other = across(output, T)
    sums_f = swapped(sums_f)
    grad_query, gkv, query_gl, cross_gl, mine, away = run(
        cross_bwd,
        [
            gc_own, gc_other, kv_all, live, owned,
            xd2, xu2, cd2, cu2, *query, *lse,
        ],
        [wide_bf, ((2, 2 * text_rows, width), f32), thin, thin] + pair,
        [pltpu.VMEM((half, width), bf16), pltpu.VMEM((n, width), f32)],
        weights=[(w_cd, (1,))], meta=meta,
    )
    mine, away, output_other, sums_f, gkv = together(mine, away, output_other, sums_f, gkv)
    gkv_got = across(gkv[:, text_rows:], C)

    def in_order(own, other):
        (rows,) = run(
            place_rows, [(where, scalars), (own, row_block), (other, row_block)],
            [((2, half, D), f32, both_blocks)], steps=4,
        )
        return rows.reshape(tokens.shape)

    seg = up_to_tiles(width)

    seg = up_to_tiles(width)
    home_dims = (blocks, 8 * part_r, 4 * 2 * hh // blocks)
    last_dims = (blocks, 16 * part_r, D // blocks)

    def second_work(output, output_other, sums, cross_gl, grad_query, query_gl):
        return [in_order(output, output_other)] + list(run(
            second_sums,
            [
                (where, scalars), sums, gc_own, gc_other, ffn_own, ffn_other, grad_ffn, *mix, cross_gl,
                query_lat, grad_query, query_gl, gkv, gkv_got, kv_lat, ku2,
            ],
            [(home_dims, bf16), ((part_r, n), f32), ((R, 4 * seg + n + up_to_tiles(text_rows)), f32)],
            [pltpu.VMEM(home_dims, f32)],
        ))

    low, got, (output, home, proj_s, sums_c) = during(
        mine, away, (output, output_other, sums_f, cross_gl, grad_query, query_gl), second_work
    )
    grad_after, ga_own = finish_rows(end_cross_back, [low, got, grad_cross], ended)
    ga_other = across(ga_own, T)

    grad_q, proj_gl, sg_own = run(
        linear_bwd,
        [ga_own, ga_other, q_raw, st_own, st_other, ratio, denom, owned, pd2, pu2],
        [wide_bf, thin, state_of],
        [pltpu.VMEM((n, width), f32)],
        weights=[(w_ab, (1,))], meta=meta,
    )
    sg_other = across(sg_own, C)
    grad_k, grad_v, qkv_gl, mine, away = run(
        linear_end,
        [grad_q, k_raw, v_raw, sg_own, sg_other, qd2, qu2],
        [wide_bf, wide_bf, thin] + pair,
        weights=[(w_ab, (0, 1))], meta=meta,
    )

    def third_work(home, sums_c, proj_gl, qkv_gl, grad_q, grad_k, grad_v):
        home = lax.all_to_all(home, (W, C), 0, 0, tiled=True)
        return run(
            third_sums, [(where, scalars), sums_c, proj_gl, mixed, qkv_lat, grad_q, grad_k, grad_v, qkv_gl],
            [((R, sums_c.shape[1] + 4 * seg + n), f32)],
        )[0], run(adapter_tables, [home], [((adapters,) + home.shape[1:], f32)])[0]

    low, got, (sums, tables) = during(
        mine, away, (home, sums_c, proj_gl, qkv_gl, grad_q, grad_k, grad_v), third_work
    )
    sums = swapped(sums)
    (input_grad,) = finish_rows(end_attn_back, [low, got, grad_after, x_low], [((half, padded), f32, row_block)])
    input_grad, sums = together(input_grad, sums)
    input_other = across(input_grad, T)
    (last,) = run(
        functools.partial(last_sums, ranges),
        [(where, scalars), sums, proj_s, ga_own, ga_other, cross_own, cross_other, cap, attn_in],
        [(last_dims, bf16)],
        [pltpu.VMEM(last_dims, f32)],
    )
    last = sent_home(last)

    def rows_of(i):
        return table_rows(last, i, D)

    return (
        output,
        in_order(input_grad, input_other),
        down_rows(last, 11, D),
        jnp.stack([rows_of(8), rows_of(9), rows_of(10)], axis=2),
        down_rows(last, 7, D),
        rows_of(2),
        down_rows(last, 0, D),
        rows_of(4),
        down_rows(last, 1, D),
        jnp.stack([rows_of(5), rows_of(6)], axis=2),
        down_rows(last, 3, D),
        table_rows(tables, 0, D),
        down_rows(tables, 2, D),
        jnp.stack([table_rows(tables, i, 8 * hh) for i in (4, 5)], axis=2),
        down_rows(tables, 3, 8 * hh),
        table_rows(tables, 1, D),
    )


def solution(mesh):
    down = P(None, (W, C), T)
    up3 = P(None, T, (W, C))
    up4 = P(None, T, None, (W, C))
    rows = P(W, C)
    return jax.shard_map(
        shards,
        mesh=mesh,
        in_specs=(
            rows, rows, P(W), P(W), P(W), rows,
            P(W), P(None, W), P(W), P(W), P(None, W),
            P(W, None, T), P(None, None, None, T), P(T, W),
        )
        + (P(),) * 14,
        out_specs=(
            rows, rows, down, up4, down, up3, down, up3, down, up4, down, up3, down, up4, down, up3,
        ),
        check_vma=False,
    )
```

```python
import functools
import jax
import jax.numpy as jnp
from jax import lax
from jax.experimental import pallas as pl
from jax.experimental.pallas import tpu as pltpu
from jax.sharding import PartitionSpec as P

W, C, T = "weight", "context", "tensor"
HD = 32
LANES = 128
bf16, f32 = jnp.bfloat16, jnp.float32
full_precision = lax.Precision.HIGHEST
norm_eps = 1e-06
attention_epsilon = 1e-06
masked_score = -1000000000.0
big = pltpu.CompilerParams(vmem_limit_bytes=58 * 1024 * 1024)


def shape(dims, dtype):
    return jax.ShapeDtypeStruct(dims, dtype)


def mm(a, b, ca=1, cb=0):
    return lax.dot_general(a, b, (((ca,), (cb,)), ((), ())), preferred_element_type=f32)


def two(pair):
    high = pair.astype(bf16)
    rest = (pair - high.astype(f32)).astype(bf16)
    lane = lax.broadcasted_iota(jnp.int32, pair.shape, 1)
    return jnp.where(lane < pair.shape[1] // 2, high.astype(f32), rest.astype(f32)).astype(bf16)


def split(values):
    high = values.astype(bf16)
    return high, (values - high.astype(f32)).astype(bf16)


def mm3(a, b, ca=1, cb=0):
    ah, al = split(a)
    bh, bl = split(b)
    return mm(ah, bh, ca, cb) + mm(ah, bl, ca, cb) + mm(al, bh, ca, cb)


def head_blocks(width):
    return [slice(at, min(at + 2 * LANES, width)) for at in range(0, width, 2 * LANES)]


def head_mask(width):
    row = lax.broadcasted_iota(jnp.int32, (width, width), 0) // HD
    col = lax.broadcasted_iota(jnp.int32, (width, width), 1) // HD
    return (row == col).astype(f32)


def by_blocks(one, *arrays):
    parts = [one(*[v[:, cols] for v in arrays]) for cols in head_blocks(arrays[0].shape[1])]
    return jnp.concatenate(parts, axis=1)


def head_total(values):
    def one(v):
        high, low = split(v)
        mask = head_mask(v.shape[1]).astype(bf16)
        return mm(high, mask) + mm(low, mask)

    return by_blocks(one, values)


def head_outer(a, b):
    def one(x, y):
        kept = mm3(x, y, 0, 0) * head_mask(x.shape[1])
        return sum(kept[h * HD : (h + 1) * HD] for h in range(kept.shape[0] // HD))

    return by_blocks(one, a, b)


def head_product(values, state, over):
    def one(v, s):
        size = v.shape[1]
        wide = jnp.concatenate([s] * (size // HD), axis=0) * head_mask(size)
        return mm3(v, wide, 1, over)

    return by_blocks(one, values, state)


def sigmoid(values):
    return 1.0 / (1.0 + jnp.exp(-values))


def row_stats(values):
    center = values - jnp.mean(values, axis=-1, keepdims=True)
    inverse = lax.rsqrt(jnp.mean(center * center, axis=-1, keepdims=True) + norm_eps)
    return center * inverse, inverse


def put(out, rows, values):
    width = values.shape[1]
    out[rows, :width] = values.astype(out.dtype)
    if width < out.shape[1]:
        out[rows, width:] = jnp.zeros((values.shape[0], out.shape[1] - width), out.dtype)


everything = slice(None)


def attn_front(w, x, mods, d2, u2, a_out, q_out, k_out, lat_out):
    n = x.shape[0]
    step = 64

    def norm(i, carry):
        at = pl.ds(pl.multiple_of(i * step, step), step)
        normed, unused = row_stats(x[at, :].astype(f32))
        a_out[at, :] = (normed * (1.0 + mods[1:2, :]) + mods[0:1, :]).astype(bf16)
        return carry

    lax.fori_loop(0, n // step, norm, 0)
    a = a_out[...]
    lat = mm(a, d2[...])
    lat_out[...] = lat
    pair = two(lat)
    width = q_out.shape[1]
    both = mm(a, w[0].take(0))
    q_out[...] = both[:, :width] + mm(pair, u2[0])
    k_out[...] = both[:, width:] + mm(pair, u2[1])


def attn_state(w, a, k, lat, u2, v_out, st_out):
    w[0].take(0)
    v_out[...] = mm(a[...], w[0].columns(0, 0, v_out.shape[1])) + mm(two(lat[...]), u2[2])
    keys = jnp.maximum(k[...], 0.0)
    width = keys.shape[1]
    st_out[:HD, :] = head_outer(v_out[...], keys)
    st_out[HD:, :] = jnp.broadcast_to(jnp.sum(keys, axis=0, keepdims=True), (8, width))


def put_partial(low, lat_pair, w, u2, mine, away):
    half = mine.shape[0]
    put(mine, everything, mm(low[:half], w, 1, 1) + mm(lat_pair[:half], u2))
    put(away, everything, mm(low[half:], w, 1, 1) + mm(lat_pair[half:], u2))


def attn_back(w, q, st1, st2, owned, d2, u2, ratio_out, den_out, mixed_out, lat_out, mine, away):
    st = st1[...] + st2[...]
    width = q.shape[1]
    queries = jnp.maximum(q[...], 0.0)
    numer = head_product(queries, st[:HD], 1)
    den = head_total(queries * st[HD : HD + 1]) + attention_epsilon
    ratio = numer / den
    ratio_out[...] = ratio
    den_out[...] = den
    mixed = (ratio * owned[...]).astype(bf16)
    mixed_out[...] = mixed
    lat = mm(mixed, d2[...])
    lat_out[...] = lat
    w[0].take(0)
    put_partial(mixed, two(lat), w[0].columns(0, width, width), u2[...], mine, away)


def caption_rows(w, own, other, d2, u2, kv_out, lat_out):
    here = own.shape[0]
    depth = d2.shape[0]
    width = u2.shape[2]
    weight = w[0].take(0)
    for i, rows in enumerate((own, other)):
        lat = mm(rows[:, :depth], d2[...])
        if i == 0:
            lat_out[...] = lat
        both = mm(rows[:, :depth], weight)
        for j in range(2):
            out = both[:, j * width : (j + 1) * width] + mm(two(lat), u2[j])
            kv_out[j, i * here : (i + 1) * here, :] = out.astype(bf16)


def lane_groups(width):
    return [(at, min(LANES, width - at)) for at in range(0, width, LANES)]


def only_head(values, j):
    lane = lax.broadcasted_iota(jnp.int32, values.shape, 1) // HD
    return jnp.where(lane == j, values.astype(f32), 0.0).astype(values.dtype)


def cross_fwd(
    w, rows, kv, live, owned, qd2, qu2, cd2, cu2, q_out, mix_out, qlat_out, clat_out, lse_out, part, logs,
):
    width = q_out.shape[1]
    depth = qd2.shape[0]
    w[0].take(0)
    lat = mm(rows[:, :depth], qd2[...])
    qlat_out[...] = lat
    q_out[...] = (mm(rows[:, :depth], w[0].columns(0, 0, width)) + mm(two(lat), qu2[...])).astype(bf16)
    for first, size in lane_groups(width):
        cols = slice(first, first + size)
        query = q_out[:, cols]
        total = None
        for j in range(size // HD):
            scores = mm(query, only_head(kv[0, :, cols], j), 1, 1) * HD ** (-0.5)
            scores = jnp.where(live[...] > 0.0, scores, masked_score)
            top = jnp.max(scores, axis=-1, keepdims=True)
            exps = jnp.exp(scores - top)
            tot = jnp.sum(exps, axis=-1, keepdims=True)
            h = first // HD + j
            logs[:, h : h + 1] = top + jnp.log(tot)
            probs = (exps * (1.0 / tot)).astype(bf16)
            term = mm(probs, only_head(kv[1, :, cols], j))
            total = term if total is None else total + term
        mix_out[:, cols] = (total * owned[:, cols]).astype(bf16)
    lse_out[...] = logs[...].T
    mix = mix_out[...]
    lat = mm(mix, cd2[...])
    clat_out[...] = lat
    put(part, everything, mm(mix, w[0].columns(0, width, width), 1, 1) + mm(two(lat), cu2[...]))


def edge_rows(where, rows, edge):
    r = jnp.where(where[1] == 0, rows // edge - 1, 0)
    return pl.ds(own_first(r, edge, rows // 2, where[0]), edge)


def ffn_front(h, w, where, xo, xt, d2, uv, ug, *refs):
    half = xo.shape[0]
    depth = d2.shape[0]
    pv, pg, hv, hg, ev, eg = refs[:6] if h == 0 else refs[-7:-1]
    u = refs[-1]
    u[:half, :] = xo[:, :depth]
    u[half:, :] = xt[:, :depth]
    if h == 0:
        refs[6][...] = mm(u[...], d2[...])
    pair = two(refs[6][...] if h == 0 else refs[0][...])
    both = mm(u[...], w[0].take(0))
    hh = uv.shape[2]
    at = edge_rows(where, u.shape[0], ev.shape[1])
    for i, (up, pre, hid, edge) in enumerate(((uv, pv, hv, ev), (ug, pg, hg, eg))):
        s = both[:, i * hh : (i + 1) * hh] + mm(pair, up[0])
        pre[0] = s
        hid[0] = (s * sigmoid(s)).astype(bf16)
        edge[0] = hid[0, at, :]


def fill_grid(buf, rows, halo, b, c):
    half = rows.shape[0] // 2
    edge = halo.shape[0]
    buf[pl.ds(pl.multiple_of(edge + b * half, edge), half), :] = rows[:half, :].astype(f32)
    buf[pl.ds(pl.multiple_of(edge + (1 - b) * half, edge), half), :] = rows[half:, :].astype(f32)
    zero = jnp.zeros(halo.shape, f32)
    got = halo.astype(f32)
    buf[:edge, :] = jnp.where(c == 0, zero, got)
    buf[buf.shape[0] - edge :, :] = jnp.where(c == 0, got, zero)


def conv_row(buf, taps, r, edge, flip):
    sums = []
    rows = [buf[pl.ds(pl.multiple_of((r + i) * edge, edge), edge), :] for i in range(3)]
    for j in range(3):
        total = None
        for i in range(3):
            k = (2 - i) * 3 + 2 - j if flip else i * 3 + j
            term = rows[i] * taps[k : k + 1, :]
            total = term if total is None else total + term
        sums.append(total)
    cell = lax.broadcasted_iota(jnp.int32, sums[0].shape, 0)
    left = jnp.where(cell == 0, 0.0, pltpu.roll(sums[0], 1, 0))
    right = jnp.where(cell == edge - 1, 0.0, pltpu.roll(sums[2], edge - 1, 0))
    return left + sums[1] + right


def own_first(r, edge, half, b):
    per = half // edge
    return pl.multiple_of(jnp.where(r // per == b, 0, half) + (r % per) * edge, edge)


def ffn_mid(
    w, where, hv, hg, halo_v, halo_g, taps, cot, gate, d2, u2,
    gated_out, gcv_out, gcg_out, gffn_out, gl_out, lat_out, down_out, edge_out, mine, away, bv, bg, gg, acc,
):
    h = pl.program_id(0)
    b, c = where[0], where[1]
    n = hv.shape[1]
    half = n // 2
    edge = halo_v.shape[1]

    @pl.when(h == 0)
    def first():
        gffn_out[...] = (gate[...] * cot[...].astype(f32)).astype(bf16)
        gl_out[...] = mm(gffn_out[...], u2[...], 1, 1)

    fill_grid(bv, hv[0], halo_v[0], b, c)
    fill_grid(bg, hg[0], halo_g[0], b, c)
    weight = w[0].take(h)
    gg[...] = mm(gffn_out[...], weight) + mm(two(gl_out[...]), d2[0], 1, 1)

    def row(r, carry):
        v = conv_row(bv, taps[0, 0], r, edge, False)
        g = conv_row(bg, taps[0, 1], r, edge, False)
        sig = sigmoid(g)
        act = g * sig
        at = pl.ds(own_first(r, edge, half, b), edge)
        gated_out[0, at, :] = (v * act).astype(bf16)
        grad = gg[at, :]
        gcv_out[0, at, :] = (grad * act).astype(bf16)
        gcg_out[0, at, :] = (grad * v * (sig * (1.0 + g * (1.0 - sig)))).astype(bf16)
        return carry

    lax.fori_loop(0, n // edge, row, 0)
    at = edge_rows(where, n, edge)
    edge_out[0, 0] = gcv_out[0, at, :]
    edge_out[0, 1] = gcg_out[0, at, :]
    gated = gated_out[0]
    down_out[0] = mm(two(gl_out[...]), gated, 0, 0)
    part = mm(gated, weight, 1, 1)
    lat = mm(gated, d2[0])

    @pl.when(h == 0)
    def start():
        acc[...] = part
        lat_out[...] = lat

    @pl.when(h == 1)
    def end():
        total = lat_out[...] + lat
        lat_out[...] = total
        full = acc[...] + part + mm(two(total), u2[...])
        put(mine, everything, full[:half])
        put(away, everything, full[half:])


def ffn_back(
    w, where, gcv, gcg, halo, taps, pv, pg, lat, d2, uv, ug,
    gpv_out, gpg_out, up_out, gl_out, mine, away, bv, bg, acc,
):
    h = pl.program_id(0)
    b, c = where[0], where[1]
    n = gcv.shape[1]
    half = n // 2
    edge = halo.shape[2]
    fill_grid(bv, gcv[0], halo[0, 0], b, c)
    fill_grid(bg, gcg[0], halo[0, 1], b, c)

    def row(r, carry):
        at = pl.ds(own_first(r, edge, half, b), edge)
        for i, (buf, pre, out) in enumerate(((bv, pv, gpv_out), (bg, pg, gpg_out))):
            grad = conv_row(buf, taps[0, i], r, edge, True)
            s = pre[0, at, :]
            sig = sigmoid(s)
            out[0, at, :] = (grad * (sig * (1.0 + s * (1.0 - sig)))).astype(bf16)
        return carry

    lax.fori_loop(0, n // edge, row, 0)
    gpv, gpg = gpv_out[0], gpg_out[0]
    part = mm(jnp.concatenate([gpv, gpg], axis=1), w[0].take(h), 1, 1)
    gl = mm(gpv, uv[0], 1, 1) + mm(gpg, ug[0], 1, 1)
    pair = two(lat[...])
    up_out[0, 0] = mm(pair, gpv, 0, 0)
    up_out[0, 1] = mm(pair, gpg, 0, 0)

    @pl.when(h == 0)
    def start():
        acc[...] = part
        gl_out[...] = gl

    @pl.when(h == 1)
    def end():
        total = gl_out[...] + gl
        gl_out[...] = total
        full = acc[...] + part + mm(two(total), d2[...], 1, 1)
        put(mine, everything, full[:half])
        put(away, everything, full[half:])


def cross_bwd(
    w, go, gt, kv, live, owned, qd2, qu2, cd2, cu2, qo, qt, lo, lt,
    gq_out, gkv_out, qgl_out, cgl_out, mine, away, gm, gqs,
):
    half = go.shape[0]
    width = qo.shape[1]
    w[0].take(0)
    depth = cu2.shape[1]
    weight = w[0].columns(0, width, width)
    scale = HD ** (-0.5)
    for i, (rows, query, lse) in enumerate(((go, qo, lo), (gt, qt, lt))):
        at = slice(i * half, (i + 1) * half)
        gl = mm(rows[:, :depth], cu2[...], 1, 1)
        cgl_out[at, :] = gl
        grad = mm(rows[:, :depth], weight) + mm(two(gl), cd2[...], 1, 1)
        gm[...] = (grad * owned[...]).astype(bf16)
        for first, size in lane_groups(width):
            cols = slice(first, first + size)
            q_all, g_all = query[:, cols], gm[:, cols]
            grad_q, grad_k, grad_v = 0.0, 0.0, 0.0
            for j in range(size // HD):
                key, val = only_head(kv[0, :, cols], j), only_head(kv[1, :, cols], j)
                h = first // HD + j
                scores = mm(key, q_all, 1, 1) * scale
                scores = jnp.where(live[...] > 0.0, scores, masked_score)
                probs = jnp.exp(scores - lse[h : h + 1, :])
                grad_p = mm(val, g_all, 1, 1)
                grad_v = grad_v + mm(probs.astype(bf16), only_head(g_all, j))
                inner = jnp.sum(probs * grad_p, axis=0, keepdims=True)
                grad_s = (probs * (grad_p - inner)).astype(bf16)
                grad_q = grad_q + mm(grad_s, key, 0, 0)
                grad_k = grad_k + mm(grad_s, only_head(q_all, j))
            gqs[at, cols] = grad_q
            for side, new in ((0, grad_k * scale), (1, grad_v)):
                gkv_out[side, :, cols] = new if i == 0 else gkv_out[side, :, cols] + new
    gq = (gqs[...] * scale).astype(bf16)
    gq_out[...] = gq
    gl = mm(gq, qu2[...], 1, 1)
    qgl_out[...] = gl
    pair = two(gl)
    total = mm(gq, w[0].columns(0, 0, width), 1, 1) + mm(pair, qd2[...], 1, 1)
    put(mine, everything, total[:half])
    put(away, everything, total[half:])


def linear_bwd(
    w, go, gt, q, st1, st2, ratio, den, owned, d2, u2, gq_out, gl_out, st_out, gh,
):
    half = go.shape[0]
    width = q.shape[1]
    depth = u2.shape[1]
    w[0].take(0)
    weight = w[0].columns(0, width, width)
    for i, rows in enumerate((go, gt)):
        at = pl.ds(i * half, half)
        gl = mm(rows[:, :depth], u2[...], 1, 1)
        gl_out[at, :] = gl
        gh[at, :] = (mm(rows[:, :depth], weight) + mm(two(gl), d2[...], 1, 1)) * owned[...]
    st = st1[...] + st2[...]
    grad = gh[...]
    inverse = 1.0 / den[...]
    numer = grad * inverse
    grad_den = -head_total(grad * ratio[...]) * inverse
    raw = q[...]
    queries = jnp.maximum(raw, 0.0)
    grad_q = head_product(numer, st[:HD], 0) + grad_den * st[HD : HD + 1]
    gq_out[...] = jnp.where(raw > 0.0, grad_q, 0.0).astype(bf16)
    st_out[:HD, :] = head_outer(numer, queries)
    total = jnp.sum(grad_den * queries, axis=0, keepdims=True)
    st_out[HD:, :] = jnp.broadcast_to(total, (8, width))


def linear_end(
    w, gq, k, v, st1, st2, d2, u2, gk_out, gv_out, gl_out, mine, away,
):
    width = k.shape[1]
    half = mine.shape[0]
    st = st1[...] + st2[...]
    raw = k[...]
    grad_k = head_product(v[...], st[:HD], 0) + st[HD : HD + 1]
    gk_out[...] = jnp.where(raw > 0.0, grad_k, 0.0).astype(bf16)
    gv_out[...] = head_product(jnp.maximum(raw, 0.0), st[:HD], 1).astype(bf16)
    grads = (gq, gk_out, gv_out)
    gl = sum(mm(g[...], u2[i], 1, 1) for i, g in enumerate(grads))
    gl_out[...] = gl
    pair = two(gl)
    w[0].take(0)
    w[0].take(1)
    both = jnp.concatenate([gq[...], gk_out[...]], axis=1)
    total = mm(both, w[0].columns(0, 0, 2 * width), 1, 1) + mm(gv_out[...], w[0].columns(1, 0, width), 1, 1)
    total = total + mm(pair, d2[...], 1, 1)
    put(mine, everything, total[:half])
    put(away, everything, total[half:])


def in_steps(rows, body, step=64):
    def one(i, carry):
        body(pl.ds(pl.multiple_of(i * step, step), step))
        return carry

    lax.fori_loop(0, rows // step, one, 0)


def slope_of_norm(values, grad):
    normed, inverse = row_stats(values)
    return inverse * (
        grad
        - jnp.mean(grad, axis=-1, keepdims=True)
        - normed * jnp.mean(grad * normed, axis=-1, keepdims=True)
    )


def total_of(low, got, at, width):
    return low[at, :width].astype(f32) + got[at, :width].astype(f32)


def end_attn(low, got, x, mods, after_out, own_out):
    def body(at):
        after = x[at, :].astype(f32) + mods[2:3, :] * total_of(low, got, at, x.shape[1])
        after_out[at, :] = after
        put(own_out, at, after)

    in_steps(x.shape[0], body)


def end_cross(low, got, before, mods, after_out, own_out):
    def body(at):
        after = before[at, :] + total_of(low, got, at, before.shape[1])
        after_out[at, :] = after
        normed, unused = row_stats(after)
        put(own_out, at, normed * (1.0 + mods[4:5, :]) + mods[3:4, :])

    in_steps(before.shape[0], body)


def end_output(low, got, before, mods, out):
    def body(at):
        put(out, at, before[at, :] + mods[5:6, :] * total_of(low, got, at, before.shape[1]))

    in_steps(before.shape[0], body)


def end_ffn_back(low, got, after, cot, mods, grad_out, own_out):
    def body(at):
        grad = total_of(low, got, at, after.shape[1]) * (1.0 + mods[4:5, :])
        grad = cot[at, :].astype(f32) + slope_of_norm(after[at, :], grad)
        grad_out[at, :] = grad
        put(own_out, at, grad)

    in_steps(after.shape[0], body)


def end_cross_back(low, got, before, mods, grad_out, own_out):
    def body(at):
        grad = before[at, :] + total_of(low, got, at, before.shape[1])
        grad_out[at, :] = grad
        put(own_out, at, mods[2:3, :] * grad)

    in_steps(before.shape[0], body)


def end_attn_back(low, got, before, x, mods, out):
    def body(at):
        grad = total_of(low, got, at, before.shape[1]) * (1.0 + mods[1:2, :])
        put(out, at, before[at, :] + slope_of_norm(x[at, :].astype(f32), grad))

    in_steps(before.shape[0], body)


def place_rows(where, own, other, out):
    width = out.shape[2]
    out[where[0]] = own[:, :width]
    out[1 - where[0]] = other[:, :width]


def fold(both):
    half = both.shape[0] // 2
    return both[:half] + both[half:]


def turned(v, b):
    half = v.shape[1] // 2
    return jnp.where(b == 0, v, jnp.concatenate([v[:, half:], v[:, :half]], axis=1))


def thin_sum(latent, *rows):
    high = latent.astype(bf16).astype(f32)
    both = jnp.concatenate([high, latent - high], axis=0).astype(bf16)
    total, at = None, 0
    for values in rows:
        size = values.shape[0]
        term = mm(both[:, at : at + size], values[...])
        total = term if total is None else total + term
        at += size
    return fold(total)


def outer_sum(latent, *rows):
    total, at = None, 0
    pair = two(latent)
    for values in rows:
        size = values.shape[0]
        term = mm(pair[at : at + size], values[...], 0, 0)
        total = term if total is None else total + term
        at += size
    return fold(total)


def set_segments(out, segments, width):
    for i, v in enumerate(segments):
        put(out.at[:, i * width : (i + 1) * width], everything, v)


def pack_first(where, point, up, l0, l1, l2, l3, sums):
    pieces = [point[0], point[1]] + [up[h, p] for p in range(2) for h in range(2)]
    n = l0.shape[0]
    first = sums.shape[1] - 4 * n
    set_segments(sums, [fold(v) for v in pieces], first // 6)
    for i, v in enumerate((l0, l1, l2, l3)):
        sums[:, first + i * n : first + (i + 1) * n] = turned(v[...].T[: sums.shape[0]], where[0])


def to_blocks(home, first, table):
    blocks = home.shape[0]
    size = table.shape[1] // blocks
    rows = table.shape[0]
    for i in range(blocks):
        home[i, first : first + rows, :size] = table[:, i * size : (i + 1) * size]


def set_mark(where, home, first):
    home[:, first:, :] = jnp.zeros((home.shape[0], home.shape[1] - first, home.shape[2]), f32) + where[2].astype(f32)


def second_sums(
    where, sums, gco, gct, fo, ft, gffn, mixo, mixt, cgl, qlat, gq, qgl, gkv, ggot, klat, ku2,
    home_out, projs, out, home,
):
    n, depth = gffn.shape
    b = where[0]
    first = sums.shape[2] - 4 * n
    parts = []
    for i in range(4):
        at = slice(first + i * n, first + (i + 1) * n)
        parts.append(turned(sums[0, :, at] + sums[1, :, at] + sums[2, :, at] + sums[3, :, at], b))
    projs[...] = parts[0]
    rows = parts[0].shape[0]
    home[...] = jnp.zeros(home.shape, f32)
    to_blocks(home, 0, thin_sum(parts[1], gco, gct)[:, :depth])
    to_blocks(home, rows, thin_sum(parts[2], gffn))
    to_blocks(home, 2 * rows, thin_sum(parts[3], fo, ft)[:, :depth])
    pad, hh = first // 6, home.shape[2] * home.shape[0] // 8
    size = home.shape[2]
    for j in range(3):
        for i in range(home.shape[0]):
            t, h, at = i * size // (2 * hh), i * size % (2 * hh) // hh, i * size % hh
            at += (2 * j + h) * pad
            home[i, (3 + j) * rows : (4 + j) * rows, :] = sums[t, :, at : at + size]
    set_mark(where, home, 6 * rows)
    home_out[...] = home[...].astype(home_out.dtype)
    here = ggot.shape[1]
    gk = (gkv[0, :here, :] + ggot[0]).astype(bf16)
    gv = (gkv[1, :here, :] + ggot[1]).astype(bf16)
    segments = [outer_sum(cgl[...], mixo, mixt), outer_sum(qlat[...], gq)]
    segments += [outer_sum(klat[...], gk), outer_sum(klat[...], gv)]
    pad = -(-gq.shape[1] // LANES) * LANES
    set_segments(out, segments, pad)
    rank = out.shape[0]
    out[:, 4 * pad : 4 * pad + n] = turned(qgl[...].T[:rank], b)
    kvgl = mm(gk, ku2[0], 1, 1) + mm(gv, ku2[1], 1, 1)
    put(out.at[:, 4 * pad + n :], everything, kvgl.T[:rank])


def third_sums(where, before, pgl, mixed, qlat, gq, gk, gv, qgl, out):
    first = before.shape[1]
    out[:, :first] = before[...]
    segments = [outer_sum(pgl[...], mixed)] + [outer_sum(qlat[...], g) for g in (gq, gk, gv)]
    pad = -(-gq.shape[1] // LANES) * LANES
    set_segments(out.at[:, first : first + 4 * pad], segments, pad)
    out[:, first + 4 * pad :] = turned(qgl[...].T[: out.shape[0]], where[0])


def last_sums(ranges, where, sums, projs, gao, gat, xo, xt, cap, a, home_out, home):
    n, depth = a.shape
    b = where[0]
    text = -(-cap.shape[0] // LANES) * LANES
    pad = (sums.shape[2] - 2 * n - text) // 8
    second = 4 * pad + n + text
    rows = projs.shape[0]

    def summed(first, size):
        return sum(sums[t, :, first : first + size] for t in range(sums.shape[0]))

    def heads(first):
        parts = [sums[t, :, first + s * HD : first + (s + m) * HD] for t, (s, m) in enumerate(ranges)]
        return jnp.concatenate(parts, axis=1)

    tables = [
        thin_sum(turned(summed(4 * pad, n), b), xo, xt)[:, :depth],
        thin_sum(summed(4 * pad + n, cap.shape[0]), cap)[:, :depth],
        thin_sum(projs[...], gao, gat)[:, :depth],
    ]
    tables += [heads(j * pad) for j in range(4)] + [heads(second + j * pad) for j in range(4)]
    tables.append(thin_sum(turned(summed(second + 4 * pad, n), b), a))
    for j, table in enumerate(tables):
        to_blocks(home, j * rows, table)
    set_mark(where, home, len(tables) * rows)
    home_out[...] = home[...].astype(home_out.dtype)


def adapter_tables(got, out):
    last = got.shape[1] - 1
    for i in range(out.shape[0]):
        total = None
        for s in range(got.shape[0]):
            values = got[s].astype(f32)
            term = jnp.where(values[last:, :1] == float(i), values, 0.0)
            total = term if total is None else total + term
        out[i] = total


def ring_order(n):
    return list(range(0, n, 2)) + list(range(n - 1 - n % 2, 0, -2))


def ring_pairs(n):
    order = ring_order(n)
    return [(order[i], order[(i + 1) % n]) for i in range(n)]


def ring_source(n, step):
    z = lax.axis_index(W)
    place = jnp.where(z % 2 == 0, z // 2, n - 1 - z // 2)
    from_place = (place - step + n) % n
    return jnp.where(2 * from_place < n, 2 * from_place, 2 * (n - 1 - from_place) + 1)


def swap_pairs(n, distance):
    return [(i, i ^ distance) for i in range(n)]


def across(values, axis, distance=1):
    return lax.ppermute(values, axis, swap_pairs(lax.axis_size(axis), distance))


class Stream:
    def __init__(self, order):
        self.n = lax.axis_size(W)
        self.order = list(order)
        self.own, self.got, self.crossed = {}, {}, {}
        self.flying, self.crossing = [], []

    def launch(self):
        while not self.flying and self.order:
            name, step = self.order[0]
            if step == 1:
                moving = self.own[name][0]
            elif (name, step - 1) in self.got:
                moving = self.got[name, step - 1]
            else:
                break
            self.order.pop(0)
            self.flying.append((name, step, lax.ppermute(moving, W, ring_pairs(self.n))))

    def fence(self, values):
        done = [self.flying.pop(0)] if self.flying else []
        crossed, self.crossing = self.crossing, []
        leaves, tree = jax.tree.flatten((values, [d[2] for d in done], [d[2] for d in crossed]))
        values, arrived, over = jax.tree.unflatten(tree, lax.optimization_barrier(leaves))
        for d, v in zip(crossed, over):
            self.crossed[d[0], d[1]] = v
        for d, v in zip(done, arrived):
            self.got[d[0], d[1]] = v
            self.crossing.append((d[0], d[1], across(v, C)))
        self.launch()
        return values

    def fences(self, count, values):
        for i in range(count * (self.n - 1) // 3):
            values = self.fence(values)
        return values

    def ready(self, names, values):
        while not all((name, self.n - 1) in self.crossed for name in names):
            values = self.fence(values)
        return values

    def pieces(self, name):
        steps = range(1, self.n)
        mine = [self.own[name][0]] + [self.got[name, s] for s in steps]
        other = [self.own[name][1]] + [self.crossed[name, s] for s in steps]
        rows = mine[0].shape[0]
        if rows % 16 == 0:
            return mine + other
        c = lax.axis_index(C)
        buf = jnp.zeros((2, self.n * rows, mine[0].shape[1]), bf16)
        for s in range(self.n):
            at = ring_source(self.n, s) * rows
            buf = lax.dynamic_update_slice(buf, mine[s][None], (c, at, 0))
            buf = lax.dynamic_update_slice(buf, other[s][None], (1 - c, at, 0))
        return [buf]


class Weight:
    def __init__(self, meta, pieces, buf, sems, halves):
        self.meta, self.pieces, self.buf, self.sems, self.halves = meta, pieces, buf, sems, halves

    def copies(self, j, pieces):
        rows = pieces[0].shape[0]
        return [
            pltpu.make_async_copy(
                piece,
                self.buf.at[j, pl.ds(pl.multiple_of(self.meta[1 + k] * rows, rows), rows), :],
                self.sems.at[j, k],
            )
            for k, piece in enumerate(pieces)
        ]

    def start(self):
        count = len(self.pieces) // 2
        for j, half in enumerate(self.halves):
            if not count:
                pltpu.make_async_copy(self.pieces[0].at[half], self.buf.at[j], self.sems.at[j, 0]).start()
                continue

            @pl.when(self.meta[0] == half)
            def mine():
                for copy in self.copies(j, self.pieces[:count]):
                    copy.start()

            @pl.when(self.meta[0] != half)
            def other():
                for copy in self.copies(j, self.pieces[count:]):
                    copy.start()

    def take(self, j):
        count = len(self.pieces) // 2
        if not count:
            pltpu.make_async_copy(self.pieces[0].at[0], self.buf.at[j], self.sems.at[j, 0]).wait()
        else:
            for copy in self.copies(j, self.pieces[:count]):
                copy.wait()
        return self.buf[j]

    def columns(self, j, first, size):
        return self.buf[j, :, first : first + size]


def per_step(a):
    zeros = (0,) * (a.ndim - 1)
    return pl.BlockSpec((1,) + tuple(a.shape[1:]), lambda h: (h,) + zeros)


def half_block(i):
    def spec(a):
        zeros = (0,) * (len(a.shape) - 1)
        return pl.BlockSpec((1,) + tuple(a.shape[1:]), lambda *g: (i,) + zeros)

    return spec


def row_block(a):
    return pl.BlockSpec((a.shape[0] // 4, a.shape[1]), lambda i: (i, 0))


def both_blocks(a):
    return pl.BlockSpec((2, a.shape[1] // 4, a.shape[2]), lambda i: (0, i, 0))


def all_of(a):
    zeros = (0,) * len(a.shape)
    return pl.BlockSpec(tuple(a.shape), lambda *g: zeros)


def scalars(a):
    return pl.BlockSpec(memory_space=pltpu.SMEM)


def anywhere(a):
    return pl.BlockSpec(memory_space=pl.ANY)


def run(kernel, ins, outs, scratch=(), steps=1, weights=(), meta=None, same=()):
    args, specs = [], []
    if weights:
        args.append(meta)
        specs.append(scalars(meta))
    counts, extra = [], []
    for pieces, halves in weights:
        counts.append((len(pieces), halves))
        args += pieces
        specs += [anywhere(p) for p in pieces]
        rows = pieces[0].shape[0] * len(pieces) // 2 if len(pieces) > 1 else pieces[0].shape[1]
        extra.append(pltpu.VMEM((len(halves), rows, pieces[0].shape[-1]), bf16))
        extra.append(pltpu.SemaphoreType.DMA((len(halves), max(len(pieces) // 2, 1))))
    first = len(args)
    for item in ins:
        a, spec = item if isinstance(item, tuple) else (item, all_of)
        args.append(a)
        specs.append(spec(a))
    shapes, out_specs = [], []
    for item in outs:
        dims, dtype, spec = item if len(item) == 3 else item + (all_of,)
        shapes.append(shape(dims, dtype))
        out_specs.append(spec(shapes[-1]))

    def body(*refs):
        if not weights:
            return kernel(*refs)
        at, loaders = 1, []
        tail = refs[len(refs) - len(extra) :]
        for i, (count, halves) in enumerate(counts):
            loaders.append(Weight(refs[0], refs[at : at + count], tail[2 * i], tail[2 * i + 1], halves))
            at += count

        @pl.when(pl.program_id(0) == 0)
        def begin():
            for loader in loaders:
                loader.start()

        kernel(loaders, *refs[first : len(refs) - len(extra)])

    return pl.pallas_call(
        body,
        grid=(steps,),
        in_specs=specs,
        out_specs=out_specs,
        out_shape=shapes,
        input_output_aliases={first + i: j for i, j in same},
        scratch_shapes=list(scratch) + extra,
        compiler_params=big,
    )(*args)


def twice(table, axis):
    return jnp.concatenate([table, table], axis=axis)


def slot_layout(groups, rank, heads):
    per, left = heads // groups, heads % groups
    slots = per + (1 if left else 0)
    own_start = rank * per + jnp.minimum(rank, left)
    own_count = per + jnp.where(rank < left, 1, 0)
    first = jnp.minimum(own_start, heads - slots)
    slot = first + jnp.arange(slots, dtype=jnp.int32)
    owned = ((slot >= own_start) & (slot < own_start + own_count)).astype(f32)
    return slots, first, owned


def slot_ranges(groups, heads):
    per, left = heads // groups, heads % groups
    slots = per + (1 if left else 0)
    out = []
    for rank in range(groups):
        own_start = rank * per + min(rank, left)
        count = per + (1 if rank < left else 0)
        out.append((own_start - min(own_start, heads - slots), count))
    return out


def shards(
    tokens, caption, caption_lengths, adapter_index, modulation, cotangent,
    qkv_weight, proj_weight, cross_q_weight, cross_kv_weight, cross_out_weight,
    inverted_weight, depth_weight, point_weight,
    qkv_down, qkv_up, proj_down, proj_up, query_down, query_up, kv_down, kv_up,
    cross_down, cross_up, inverted_down, inverted_up, point_down, point_up,
):
    grid_rows, grid_cols, D = tokens.shape[1:]
    n = grid_rows * grid_cols
    half = n // 2
    heads = D // HD
    groups = lax.axis_size(T)
    rank = lax.axis_index(T)
    c = lax.axis_index(C)
    b = rank % 2
    adapters, R = qkv_up.shape[:2]
    slots, slot_first, owned = slot_layout(groups, rank, heads)
    width = slots * HD
    col = slot_first * HD
    owned = jnp.repeat(owned, HD)[None]
    hid = inverted_weight.shape[2]
    hh = hid // 2
    hid_first = rank * hid
    index = adapter_index[0]
    where = jnp.stack([b, c, index]).astype(jnp.int32)

    def cut(table, start, size, axis):
        return lax.dynamic_slice_in_dim(table, start, size, axis)

    def pick(table):
        return lax.dynamic_index_in_dim(table, index, 0, keepdims=False)

    def own_rows(rows):
        own = cut(rows, b * half, half, 0)
        return own, jnp.concatenate([own, cut(rows, (1 - b) * half, half, 0)])

    def pair_of(first, second):
        return [jnp.where(c == 0, first, second), jnp.where(c == 0, second, first)]

    def taken(table, middle, start, size):
        return lax.dynamic_slice(table, (0, middle, start), (table.shape[0], 1, size))[:, 0]

    def beside(*values):
        return jnp.concatenate(values, axis=1)

    def both(table, start, size=width):
        return beside(taken(table, 0, start, size), taken(table, 1, start, size))

    size = lax.axis_size(W)
    order = [(name, step) for name in ("ab", "cd", "vg", "p") for step in range(1, size)]
    stream = Stream(order)
    fences = stream.fences

    side_qk = both(qkv_weight, col)
    side_vo = beside(taken(qkv_weight, 2, col, width), cut(proj_weight, col, width, 0).T)
    stream.own["ab"] = [jnp.where(c == 0, side_qk, side_vo), None]
    c_late, caption, stream.own["ab"][0] = lax.optimization_barrier((c, caption, stream.own["ab"][0]))
    stream.own["ab"][1] = jnp.where(c_late == 0, side_vo, side_qk)
    stream.launch()
    mods = modulation[0]
    low_tokens = tokens.reshape(n, D)
    x_low, x_rows = own_rows(low_tokens)
    qd2, qu2 = twice(pick(qkv_down), 1), twice(cut(pick(qkv_up), col, width, 2), 0).transpose(1, 0, 2)
    pd2, pu2 = twice(cut(pick(proj_down), col, width, 0), 1), twice(pick(proj_up), 0)
    text_here = caption.shape[1]
    text_rows = -(-text_here // 16) * 16
    padded = -(-D // LANES) * LANES
    cap = jnp.pad(caption[0], ((0, text_rows - text_here), (0, padded - D)))
    cap_other = across(cap, C)
    tables = [query_down, query_up, kv_down, kv_up, cross_down, cross_up]
    tables_f = [inverted_down, inverted_up, point_down, point_up, depth_weight]
    raw = [cross_kv_weight, cross_q_weight, cross_out_weight]
    raw_f = [inverted_weight, point_weight]
    raw, raw_f, tables, tables_f, cap, cap_other, cotangent = fences(
        1, (raw, raw_f, tables, tables_f, cap, cap_other, cotangent)
    )
    pair_cd = pair_of(both(raw[0], col), beside(cut(raw[1], col, width, 1), cut(raw[2], col, width, 0).T))
    query_down, query_up, kv_down, kv_up, cross_down, cross_up = tables
    cd2 = twice(cut(pick(cross_down), col, width, 0), 1)
    cu2 = twice(pick(cross_up), 0)
    xd2, xu2 = twice(pick(query_down), 1), twice(cut(pick(query_up), col, width, 1), 0)
    kd2, ku2 = twice(pick(kv_down), 1), twice(cut(pick(kv_up), col, width, 2), 0).transpose(1, 0, 2)
    front = [x_low, x_rows, qd2, qu2, pd2, pu2]
    pair_cd, raw_f, tables_f, cotangent, front = fences(1, (pair_cd, raw_f, tables_f, cotangent, front))
    stream.own["cd"] = pair_cd
    x_low, x_rows, qd2, qu2, pd2, pu2 = front
    pair_vg = [both(raw_f[0], i * hh, hh) for i in (c, 1 - c)]
    pair_p = [cut(raw_f[1], i * hh, hh, 0).T for i in (c, 1 - c)]
    pair_vg, pair_p, tables_f, cotangent = fences(1, (pair_vg, pair_p, tables_f, cotangent))
    stream.own.update(vg=pair_vg, p=pair_p)
    inverted_down, inverted_up, point_down, point_up, depth_weight = tables_f
    fd2, fu2 = twice(pick(inverted_down), 1), twice(cut(pick(inverted_up), hid_first, hid, 2), 0)
    fu2 = fu2.reshape(2 * R, 2, 2, hh).transpose(1, 2, 0, 3)
    od2 = twice(cut(pick(point_down), hid_first, hid, 0), 1).reshape(2, hh, 2 * R)
    ou2 = twice(pick(point_up), 0)
    taps = depth_weight.astype(f32).reshape(9, 2, 2, hh).transpose(2, 1, 0, 3)
    cot_low, cot = own_rows(cotangent.reshape(n, D))
    places = jnp.arange(text_rows)
    live = jnp.concatenate([c * text_here + places, (1 - c) * text_here + places])
    live = (live < caption_lengths[0]) & (jnp.concatenate([places, places]) < text_here)
    live = live.astype(f32)[None]
    tables = [cd2, cu2, xd2, xu2, kd2, ku2, fd2, fu2[0], fu2[1], od2, ou2, taps, cot_low, cot, live]
    x_rows, tables = stream.ready(["ab"], (x_rows, tables))
    cd2, cu2, xd2, xu2, kd2, ku2, fd2, fuv, fug, od2, ou2, taps, cot_low, cot, live = tables

    w_ab = stream.pieces("ab")
    meta = jnp.stack([c] + [ring_source(size, s) for s in range(size)]).astype(jnp.int32)
    rows_bf = ((n, D), bf16)
    thin = ((n, 2 * R), f32)
    wide = ((n, width), f32)
    wide_bf = ((n, width), bf16)
    pair = [((half, padded), bf16)] * 2
    ended = [((half, D), f32, row_block), ((half, padded), bf16, row_block)]

    def finish_rows(kernel, arrays, outs):
        return run(kernel, [(v, row_block) for v in arrays] + [mods], outs, steps=4)

    state_of = ((HD + 8, width), f32)
    attn_in, q_raw, k_raw, qkv_lat = run(
        attn_front, [x_rows, mods, qd2, qu2], [rows_bf, wide, wide, thin], weights=[(w_ab, (0,))], meta=meta,
    )
    v_raw, st_own = run(
        attn_state, [attn_in, k_raw, qkv_lat, qu2], [wide, state_of], weights=[(w_ab, (1,))], meta=meta,
    )
    st_own, st_other = fences(1, (st_own, across(st_own, C)))
    ratio, denom, mixed, proj_lat, mine, away = run(
        attn_back, [q_raw, st_own, st_other, owned, pd2, pu2], [wide, wide, wide_bf, thin] + pair,
        weights=[(w_ab, (1,))], meta=meta,
    )

    def exchanged(mine, away, pace=lambda low: low):
        low, distance = (mine.astype(f32) + across(away, T).astype(f32)).astype(bf16), 2
        while True:
            low = pace(low)
            got = across(low, T, distance)
            distance *= 2
            if distance >= groups:
                return low, got
            low = (low.astype(f32) + got.astype(f32)).astype(bf16)

    def while_streaming(mine, away):
        return fences(1, exchanged(mine, away))

    mine, away = fences(1, (mine, away))
    low, got = while_streaming(mine, away)
    after_attn, cross_own = finish_rows(end_attn, [low, got, x_low], ended)
    cross_other = across(cross_own, T)

    cap, cross_own, cross_other, after_attn = stream.ready(["cd"], (cap, cross_own, cross_other, after_attn))
    w_cd = stream.pieces("cd")
    kv_all, kv_lat = run(
        caption_rows, [cap, cap_other, kd2, ku2], [((2, 2 * text_rows, width), bf16), ((text_rows, 2 * R), f32)],
        weights=[(w_cd, (0,))], meta=meta,
    )
    kv_all, cross_own, cross_other = fences(1, (kv_all, cross_own, cross_other))
    half_bf, half_thin = ((half, width), bf16), ((half, 2 * R), f32)

    def cross_part(rows, kv):
        return run(
            cross_fwd,
            [rows, kv, live, owned, xd2, xu2, cd2, cu2],
            [half_bf, half_bf, half_thin, half_thin, ((LANES, half), f32), ((half, padded), bf16)],
            [pltpu.VMEM((half, LANES), f32)],
            weights=[(w_cd, (1,))], meta=meta,
        )

    *cross_t, away = cross_part(cross_other, kv_all)
    away, cross_tied, kv_tied = lax.optimization_barrier((away, cross_own, kv_all))
    *cross_o, mine = cross_part(cross_tied, kv_tied)
    mine, away = fences(1, (mine, away))
    query, mix, query_lat, cross_lat, lse = zip(cross_o, cross_t)
    low, got = while_streaming(mine, away)
    after_cross, ffn_own = finish_rows(end_cross, [low, got, after_attn], ended)
    ffn_own, after_cross = fences(1, (ffn_own, after_cross))
    ffn_other = across(ffn_own, T)

    query_lat, cross_lat = jnp.concatenate(query_lat), jnp.concatenate(cross_lat)

    ffn_own, ffn_other, after_cross = stream.ready(["vg"], (ffn_own, ffn_other, after_cross))
    w_vg = stream.pieces("vg")
    hid_bf = ((2, n, hh), bf16, per_step)

    def ffn_part(h, more, same):
        outs = [((2, n, hh), f32)] * 2 + [((2, n, hh), bf16)] * 2 + [((2, grid_cols, hh), bf16)] * 2
        return run(
            functools.partial(ffn_front, h),
            [(where, scalars), ffn_own, ffn_other, fd2, (fuv, half_block(h)), (fug, half_block(h))] + more,
            [out + (half_block(h),) for out in outs] + [thin][h:],
            [pltpu.VMEM((n, D), bf16)],
            weights=[(w_vg, (h,))], meta=meta, same=same,
        )

    *started, inv_lat = ffn_part(0, [], ())
    ffn_own, started, inv_lat = fences(1, (ffn_own, started, inv_lat))
    pre_v, pre_g, hid_v, hid_g, edge_v, edge_g = ffn_part(
        1, [inv_lat] + [(v, anywhere) for v in started], [(7 + i, i) for i in range(6)]
    )
    halo_v, halo_g = across(edge_v, C), across(edge_g, C)
    hid_v, halo_v, halo_g = stream.ready(["p"], (hid_v, halo_v, halo_g))
    w_p = stream.pieces("p")
    grid_buf = pltpu.VMEM((n + 2 * grid_cols, hh), f32)
    row_acc = pltpu.VMEM((n, D), f32)
    gated, gcv, gcg, grad_ffn, point_gl, point_lat, point_down_g, edge, mine, away = run(
        ffn_mid,
        [
            (where, scalars), (hid_v, per_step), (hid_g, per_step), (halo_v, per_step), (halo_g, per_step), (taps, per_step),
            cot, mods[5:6], (od2, per_step), ou2,
        ],
        [hid_bf, hid_bf, hid_bf, rows_bf, thin, thin, ((2, 2 * R, hh), f32, per_step)]
        + [((2, 2, grid_cols, hh), bf16, per_step)] + pair,
        [grid_buf, grid_buf, pltpu.VMEM((n, hh), f32), row_acc],
        2,
        weights=[(w_p, (0, 1))], meta=meta,
    )
    halo = across(edge, C)
    tied = []

    def after_halo(low):
        low, *tied[:] = lax.optimization_barrier((low, halo, gcv, gcg))
        return low

    out_low, out_got = exchanged(mine, away, after_halo)
    halo, gcv, gcg = tied

    gpv, gpg, inv_up_g, inv_gl, mine, away = run(
        ffn_back,
        [
            (where, scalars), (gcv, per_step), (gcg, per_step), (halo, per_step), (taps, per_step),
            (pre_v, per_step), (pre_g, per_step), inv_lat, fd2,
            (fuv, per_step), (fug, per_step),
        ],
        [hid_bf, hid_bf, ((2, 2, 2 * R, hh), f32, per_step), thin] + pair,
        [grid_buf, grid_buf, row_acc],
        2,
        weights=[(w_vg, (0, 1))], meta=meta,
    )
    part_r = R // groups
    blocks = size * lax.axis_size(C)
    ranges = slot_ranges(groups, heads)

    def swapped(sent):
        return lax.all_to_all(sent.reshape(groups, part_r, sent.shape[1]), T, 0, 0, tiled=True)

    def up_to_tiles(size):
        return -(-size // LANES) * LANES

    def table_rows(table, i, size):
        return table[:, i * part_r : (i + 1) * part_r, : size // blocks]

    def down_rows(table, i, size):
        return table_rows(table, i, size).transpose(0, 2, 1)

    def together(*values):
        return lax.optimization_barrier(values)

    def during(mine, away, inputs, work):
        held = []

        def pace(low):
            low, tied = together(low, inputs)
            held[:] = [tied]
            return low

        low, got = exchanged(mine, away, pace)
        return together(low, got, work(*held[0]))

    def first_work(out_low, out_got, after_cross, inv_up_g, point_down_g, lats):
        (output,) = finish_rows(end_output, [out_low, out_got, after_cross], [((half, padded), f32, row_block)])
        (sums,) = run(
            pack_first, [(where, scalars), point_down_g, inv_up_g, *lats], [((R, 6 * up_to_tiles(hh) + 4 * n), f32)],
        )
        return output, sums

    mine, away, out_low, out_got = together(mine, away, out_low, out_got)
    low, got, (output, sums_f) = during(
        mine, away,
        (out_low, out_got, after_cross, inv_up_g, point_down_g, (proj_lat, cross_lat, point_lat, inv_gl)),
        first_work,
    )
    grad_cross, gc_own = finish_rows(end_ffn_back, [low, got, after_cross, cot_low], ended)
    gc_other = across(gc_own, T)

    gc_own, gc_other, output, sums_f = together(gc_own, gc_other, output, sums_f)
    output_other = across(output, T)
    sums_f = swapped(sums_f)
    grad_query, gkv, query_gl, cross_gl, mine, away = run(
        cross_bwd,
        [
            gc_own, gc_other, kv_all, live.T, owned,
            xd2, xu2, cd2, cu2, *query, *lse,
        ],
        [wide_bf, ((2, 2 * text_rows, width), f32), thin, thin] + pair,
        [pltpu.VMEM((half, width), bf16), pltpu.VMEM((n, width), f32)],
        weights=[(w_cd, (1,))], meta=meta,
    )
    mine, away, output_other, sums_f, gkv = together(mine, away, output_other, sums_f, gkv)
    gkv_got = across(gkv[:, text_rows:], C)

    def in_order(own, other):
        (rows,) = run(
            place_rows, [(where, scalars), (own, row_block), (other, row_block)],
            [((2, half, D), f32, both_blocks)], steps=4,
        )
        return rows.reshape(tokens.shape)

    seg = up_to_tiles(width)

    seg = up_to_tiles(width)
    home_dims = (blocks, 8 * part_r, 4 * 2 * hh // blocks)
    last_dims = (blocks, 16 * part_r, D // blocks)

    def second_work(output, output_other, sums, cross_gl, grad_query, query_gl):
        return [in_order(output, output_other)] + list(run(
            second_sums,
            [
                (where, scalars), sums, gc_own, gc_other, ffn_own, ffn_other, grad_ffn, *mix, cross_gl,
                query_lat, grad_query, query_gl, gkv, gkv_got, kv_lat, ku2,
            ],
            [(home_dims, bf16), ((part_r, n), f32), ((R, 4 * seg + n + up_to_tiles(text_rows)), f32)],
            [pltpu.VMEM(home_dims, f32)],
        ))

    low, got, (output, home, proj_s, sums_c) = during(
        mine, away, (output, output_other, sums_f, cross_gl, grad_query, query_gl), second_work
    )
    grad_after, ga_own = finish_rows(end_cross_back, [low, got, grad_cross], ended)
    ga_other = across(ga_own, T)

    grad_q, proj_gl, sg_own = run(
        linear_bwd,
        [ga_own, ga_other, q_raw, st_own, st_other, ratio, denom, owned, pd2, pu2],
        [wide_bf, thin, state_of],
        [pltpu.VMEM((n, width), f32)],
        weights=[(w_ab, (1,))], meta=meta,
    )
    sg_other = across(sg_own, C)
    grad_k, grad_v, qkv_gl, mine, away = run(
        linear_end,
        [grad_q, k_raw, v_raw, sg_own, sg_other, qd2, qu2],
        [wide_bf, wide_bf, thin] + pair,
        weights=[(w_ab, (0, 1))], meta=meta,
    )

    def third_work(home, sums_c, proj_gl, qkv_gl, grad_q, grad_k, grad_v):
        home = lax.all_to_all(home, (W, C), 0, 0, tiled=True)
        (sums,) = run(
            third_sums, [(where, scalars), sums_c, proj_gl, mixed, qkv_lat, grad_q, grad_k, grad_v, qkv_gl],
            [((R, sums_c.shape[1] + 4 * seg + n), f32)],
        )
        return swapped(sums), run(adapter_tables, [home], [((adapters,) + home.shape[1:], f32)])[0]

    low, got, (sums, tables) = during(
        mine, away, (home, sums_c, proj_gl, qkv_gl, grad_q, grad_k, grad_v), third_work
    )
    (input_grad,) = finish_rows(end_attn_back, [low, got, grad_after, x_low], [((half, padded), f32, row_block)])
    input_other = across(input_grad, T)
    (last,) = run(
        functools.partial(last_sums, ranges),
        [(where, scalars), sums, proj_s, ga_own, ga_other, cross_own, cross_other, cap, attn_in],
        [(last_dims, bf16)],
        [pltpu.VMEM(last_dims, f32)],
    )
    last = lax.all_to_all(last, (W, C), 0, 0, tiled=True)
    input_grad = in_order(input_grad, input_other)
    last, input_grad = together(last, input_grad)
    (last,) = run(adapter_tables, [last], [((adapters,) + last.shape[1:], f32)])

    def rows_of(i):
        return table_rows(last, i, D)

    return (
        output,
        input_grad,
        down_rows(last, 11, D),
        jnp.stack([rows_of(8), rows_of(9), rows_of(10)], axis=2),
        down_rows(last, 7, D),
        rows_of(2),
        down_rows(last, 0, D),
        rows_of(4),
        down_rows(last, 1, D),
        jnp.stack([rows_of(5), rows_of(6)], axis=2),
        down_rows(last, 3, D),
        table_rows(tables, 0, D),
        down_rows(tables, 2, D),
        jnp.stack([table_rows(tables, i, 8 * hh) for i in (4, 5)], axis=2),
        down_rows(tables, 3, 8 * hh),
        table_rows(tables, 1, D),
    )


def solution(mesh):
    down = P(None, (W, C), T)
    up3 = P(None, T, (W, C))
    up4 = P(None, T, None, (W, C))
    rows = P(W, C)
    return jax.shard_map(
        shards,
        mesh=mesh,
        in_specs=(
            rows, rows, P(W), P(W), P(W), rows,
            P(W), P(None, W), P(W), P(W), P(None, W),
            P(W, None, T), P(None, None, None, T), P(T, W),
        )
        + (P(),) * 14,
        out_specs=(
            rows, rows, down, up4, down, up3, down, up3, down, up4, down, up3, down, up4, down, up3,
        ),
        check_vma=False,
    )
```

```python
import functools
import jax
import jax.numpy as jnp
from jax import lax
from jax.experimental import pallas as pl
from jax.experimental.pallas import tpu as pltpu
from jax.sharding import PartitionSpec as P

W, C, T = "weight", "context", "tensor"
HD = 32
LANES = 128
bf16, f32 = jnp.bfloat16, jnp.float32
full_precision = lax.Precision.HIGHEST
norm_eps = 1e-06
attention_epsilon = 1e-06
masked_score = -1000000000.0
big = pltpu.CompilerParams(vmem_limit_bytes=58 * 1024 * 1024)


def shape(dims, dtype):
    return jax.ShapeDtypeStruct(dims, dtype)


def mm(a, b, ca=1, cb=0):
    return lax.dot_general(a, b, (((ca,), (cb,)), ((), ())), preferred_element_type=f32)


def two(pair):
    high = pair.astype(bf16)
    rest = (pair - high.astype(f32)).astype(bf16)
    lane = lax.broadcasted_iota(jnp.int32, pair.shape, 1)
    return jnp.where(lane < pair.shape[1] // 2, high.astype(f32), rest.astype(f32)).astype(bf16)


def split(values):
    high = values.astype(bf16)
    return high, (values - high.astype(f32)).astype(bf16)


def mm3(a, b, ca=1, cb=0):
    ah, al = split(a)
    bh, bl = split(b)
    return mm(ah, bh, ca, cb) + mm(ah, bl, ca, cb) + mm(al, bh, ca, cb)


def head_blocks(width):
    return [slice(at, min(at + 2 * LANES, width)) for at in range(0, width, 2 * LANES)]


def head_mask(width):
    row = lax.broadcasted_iota(jnp.int32, (width, width), 0) // HD
    col = lax.broadcasted_iota(jnp.int32, (width, width), 1) // HD
    return (row == col).astype(f32)


def by_blocks(one, *arrays):
    parts = [one(*[v[:, cols] for v in arrays]) for cols in head_blocks(arrays[0].shape[1])]
    return jnp.concatenate(parts, axis=1)


def head_total(values):
    def one(v):
        high, low = split(v)
        mask = head_mask(v.shape[1]).astype(bf16)
        return mm(high, mask) + mm(low, mask)

    return by_blocks(one, values)


def head_outer(a, b):
    def one(x, y):
        kept = mm3(x, y, 0, 0) * head_mask(x.shape[1])
        return sum(kept[h * HD : (h + 1) * HD] for h in range(kept.shape[0] // HD))

    return by_blocks(one, a, b)


def head_product(values, state, over):
    def one(v, s):
        size = v.shape[1]
        wide = jnp.concatenate([s] * (size // HD), axis=0) * head_mask(size)
        return mm3(v, wide, 1, over)

    return by_blocks(one, values, state)


def sigmoid(values):
    return 1.0 / (1.0 + jnp.exp(-values))


def row_stats(values):
    center = values - jnp.mean(values, axis=-1, keepdims=True)
    inverse = lax.rsqrt(jnp.mean(center * center, axis=-1, keepdims=True) + norm_eps)
    return center * inverse, inverse


def put(out, rows, values):
    width = values.shape[1]
    out[rows, :width] = values.astype(out.dtype)
    if width < out.shape[1]:
        out[rows, width:] = jnp.zeros((values.shape[0], out.shape[1] - width), out.dtype)


everything = slice(None)


def attn_front(w, x, mods, d2, u2, a_out, q_out, k_out, lat_out):
    n = x.shape[0]
    step = 64

    def norm(i, carry):
        at = pl.ds(pl.multiple_of(i * step, step), step)
        normed, unused = row_stats(x[at, :].astype(f32))
        a_out[at, :] = (normed * (1.0 + mods[1:2, :]) + mods[0:1, :]).astype(bf16)
        return carry

    lax.fori_loop(0, n // step, norm, 0)
    a = a_out[...]
    lat = mm(a, d2[...])
    lat_out[...] = lat
    pair = two(lat)
    width = q_out.shape[1]
    both = mm(a, w[0].take(0))
    q_out[...] = both[:, :width] + mm(pair, u2[0])
    k_out[...] = both[:, width:] + mm(pair, u2[1])


def attn_state(w, a, k, lat, u2, v_out, st_out):
    w[0].take(0)
    v_out[...] = mm(a[...], w[0].columns(0, 0, v_out.shape[1])) + mm(two(lat[...]), u2[2])
    keys = jnp.maximum(k[...], 0.0)
    width = keys.shape[1]
    st_out[:HD, :] = head_outer(v_out[...], keys)
    st_out[HD:, :] = jnp.broadcast_to(jnp.sum(keys, axis=0, keepdims=True), (8, width))


def put_partial(low, lat_pair, w, u2, mine, away):
    half = mine.shape[0]
    put(mine, everything, mm(low[:half], w, 1, 1) + mm(lat_pair[:half], u2))
    put(away, everything, mm(low[half:], w, 1, 1) + mm(lat_pair[half:], u2))


def attn_back(w, q, st1, st2, owned, d2, u2, ratio_out, den_out, mixed_out, lat_out, mine, away):
    st = st1[...] + st2[...]
    width = q.shape[1]
    queries = jnp.maximum(q[...], 0.0)
    numer = head_product(queries, st[:HD], 1)
    den = head_total(queries * st[HD : HD + 1]) + attention_epsilon
    ratio = numer / den
    ratio_out[...] = ratio
    den_out[...] = den
    mixed = (ratio * owned[...]).astype(bf16)
    mixed_out[...] = mixed
    lat = mm(mixed, d2[...])
    lat_out[...] = lat
    w[0].take(0)
    put_partial(mixed, two(lat), w[0].columns(0, width, width), u2[...], mine, away)


def caption_rows(w, own, other, d2, u2, kv_out, lat_out):
    here = own.shape[0]
    depth = d2.shape[0]
    width = u2.shape[2]
    weight = w[0].take(0)
    for i, rows in enumerate((own, other)):
        lat = mm(rows[:, :depth], d2[...])
        if i == 0:
            lat_out[...] = lat
        both = mm(rows[:, :depth], weight)
        for j in range(2):
            out = both[:, j * width : (j + 1) * width] + mm(two(lat), u2[j])
            kv_out[j, i * here : (i + 1) * here, :] = out.astype(bf16)


def lane_groups(width):
    return [(at, min(LANES, width - at)) for at in range(0, width, LANES)]


def only_head(values, j):
    lane = lax.broadcasted_iota(jnp.int32, values.shape, 1) // HD
    return jnp.where(lane == j, values.astype(f32), 0.0).astype(values.dtype)


def cross_fwd(
    w, rows, kv, live, owned, qd2, qu2, cd2, cu2, q_out, mix_out, qlat_out, clat_out, lse_out, part, logs,
):
    width = q_out.shape[1]
    depth = qd2.shape[0]
    w[0].take(0)
    lat = mm(rows[:, :depth], qd2[...])
    qlat_out[...] = lat
    q_out[...] = (mm(rows[:, :depth], w[0].columns(0, 0, width)) + mm(two(lat), qu2[...])).astype(bf16)
    for first, size in lane_groups(width):
        cols = slice(first, first + size)
        query = q_out[:, cols]
        total = None
        for j in range(size // HD):
            scores = mm(query, only_head(kv[0, :, cols], j), 1, 1) * HD ** (-0.5)
            scores = jnp.where(live[...] > 0.0, scores, masked_score)
            top = jnp.max(scores, axis=-1, keepdims=True)
            exps = jnp.exp(scores - top)
            tot = jnp.sum(exps, axis=-1, keepdims=True)
            h = first // HD + j
            logs[:, h : h + 1] = top + jnp.log(tot)
            probs = (exps * (1.0 / tot)).astype(bf16)
            term = mm(probs, only_head(kv[1, :, cols], j))
            total = term if total is None else total + term
        mix_out[:, cols] = (total * owned[:, cols]).astype(bf16)
    lse_out[...] = logs[...].T
    mix = mix_out[...]
    lat = mm(mix, cd2[...])
    clat_out[...] = lat
    put(part, everything, mm(mix, w[0].columns(0, width, width), 1, 1) + mm(two(lat), cu2[...]))


def edge_rows(where, rows, edge):
    r = jnp.where(where[1] == 0, rows // edge - 1, 0)
    return pl.ds(own_first(r, edge, rows // 2, where[0]), edge)


def ffn_front(h, w, where, xo, xt, d2, uv, ug, *refs):
    half = xo.shape[0]
    depth = d2.shape[0]
    pv, pg, hv, hg, ev, eg = refs[:6] if h == 0 else refs[-7:-1]
    u = refs[-1]
    u[:half, :] = xo[:, :depth]
    u[half:, :] = xt[:, :depth]
    if h == 0:
        refs[6][...] = mm(u[...], d2[...])
    pair = two(refs[6][...] if h == 0 else refs[0][...])
    both = mm(u[...], w[0].take(0))
    hh = uv.shape[2]
    at = edge_rows(where, u.shape[0], ev.shape[1])
    for i, (up, pre, hid, edge) in enumerate(((uv, pv, hv, ev), (ug, pg, hg, eg))):
        s = both[:, i * hh : (i + 1) * hh] + mm(pair, up[0])
        pre[0] = s
        hid[0] = (s * sigmoid(s)).astype(bf16)
        edge[0] = hid[0, at, :]


def fill_grid(buf, rows, halo, b, c):
    half = rows.shape[0] // 2
    edge = halo.shape[0]
    buf[pl.ds(pl.multiple_of(edge + b * half, edge), half), :] = rows[:half, :].astype(f32)
    buf[pl.ds(pl.multiple_of(edge + (1 - b) * half, edge), half), :] = rows[half:, :].astype(f32)
    zero = jnp.zeros(halo.shape, f32)
    got = halo.astype(f32)
    buf[:edge, :] = jnp.where(c == 0, zero, got)
    buf[buf.shape[0] - edge :, :] = jnp.where(c == 0, got, zero)


def conv_row(buf, taps, r, edge, flip):
    sums = []
    rows = [buf[pl.ds(pl.multiple_of((r + i) * edge, edge), edge), :] for i in range(3)]
    for j in range(3):
        total = None
        for i in range(3):
            k = (2 - i) * 3 + 2 - j if flip else i * 3 + j
            term = rows[i] * taps[k : k + 1, :]
            total = term if total is None else total + term
        sums.append(total)
    cell = lax.broadcasted_iota(jnp.int32, sums[0].shape, 0)
    left = jnp.where(cell == 0, 0.0, pltpu.roll(sums[0], 1, 0))
    right = jnp.where(cell == edge - 1, 0.0, pltpu.roll(sums[2], edge - 1, 0))
    return left + sums[1] + right


def own_first(r, edge, half, b):
    per = half // edge
    return pl.multiple_of(jnp.where(r // per == b, 0, half) + (r % per) * edge, edge)


def ffn_mid(
    w, where, hv, hg, halo_v, halo_g, taps, cot, gate, d2, u2,
    gated_out, gcv_out, gcg_out, gffn_out, gl_out, lat_out, down_out, edge_out, mine, away, bv, bg, gg, acc,
):
    h = pl.program_id(0)
    b, c = where[0], where[1]
    n = hv.shape[1]
    half = n // 2
    edge = halo_v.shape[1]

    @pl.when(h == 0)
    def first():
        gffn_out[...] = (gate[...] * cot[...].astype(f32)).astype(bf16)
        gl_out[...] = mm(gffn_out[...], u2[...], 1, 1)

    fill_grid(bv, hv[0], halo_v[0], b, c)
    fill_grid(bg, hg[0], halo_g[0], b, c)
    weight = w[0].take(h)
    gg[...] = mm(gffn_out[...], weight) + mm(two(gl_out[...]), d2[0], 1, 1)

    def row(r, carry):
        v = conv_row(bv, taps[0, 0], r, edge, False)
        g = conv_row(bg, taps[0, 1], r, edge, False)
        sig = sigmoid(g)
        act = g * sig
        at = pl.ds(own_first(r, edge, half, b), edge)
        gated_out[0, at, :] = (v * act).astype(bf16)
        grad = gg[at, :]
        gcv_out[0, at, :] = (grad * act).astype(bf16)
        gcg_out[0, at, :] = (grad * v * (sig * (1.0 + g * (1.0 - sig)))).astype(bf16)
        return carry

    lax.fori_loop(0, n // edge, row, 0)
    at = edge_rows(where, n, edge)
    edge_out[0, 0] = gcv_out[0, at, :]
    edge_out[0, 1] = gcg_out[0, at, :]
    gated = gated_out[0]
    down_out[0] = mm(two(gl_out[...]), gated, 0, 0)
    part = mm(gated, weight, 1, 1)
    lat = mm(gated, d2[0])

    @pl.when(h == 0)
    def start():
        acc[...] = part
        lat_out[...] = lat

    @pl.when(h == 1)
    def end():
        total = lat_out[...] + lat
        lat_out[...] = total
        full = acc[...] + part + mm(two(total), u2[...])
        put(mine, everything, full[:half])
        put(away, everything, full[half:])


def ffn_back(
    w, where, gcv, gcg, halo, taps, pv, pg, lat, d2, uv, ug,
    gpv_out, gpg_out, up_out, gl_out, mine, away, bv, bg, acc,
):
    h = pl.program_id(0)
    b, c = where[0], where[1]
    n = gcv.shape[1]
    half = n // 2
    edge = halo.shape[2]
    fill_grid(bv, gcv[0], halo[0, 0], b, c)
    fill_grid(bg, gcg[0], halo[0, 1], b, c)

    def row(r, carry):
        at = pl.ds(own_first(r, edge, half, b), edge)
        for i, (buf, pre, out) in enumerate(((bv, pv, gpv_out), (bg, pg, gpg_out))):
            grad = conv_row(buf, taps[0, i], r, edge, True)
            s = pre[0, at, :]
            sig = sigmoid(s)
            out[0, at, :] = (grad * (sig * (1.0 + s * (1.0 - sig)))).astype(bf16)
        return carry

    lax.fori_loop(0, n // edge, row, 0)
    gpv, gpg = gpv_out[0], gpg_out[0]
    part = mm(jnp.concatenate([gpv, gpg], axis=1), w[0].take(h), 1, 1)
    gl = mm(gpv, uv[0], 1, 1) + mm(gpg, ug[0], 1, 1)
    pair = two(lat[...])
    up_out[0, 0] = mm(pair, gpv, 0, 0)
    up_out[0, 1] = mm(pair, gpg, 0, 0)

    @pl.when(h == 0)
    def start():
        acc[...] = part
        gl_out[...] = gl

    @pl.when(h == 1)
    def end():
        total = gl_out[...] + gl
        gl_out[...] = total
        full = acc[...] + part + mm(two(total), d2[...], 1, 1)
        put(mine, everything, full[:half])
        put(away, everything, full[half:])


def cross_bwd(
    w, go, gt, kv, live, owned, qd2, qu2, cd2, cu2, qo, qt, lo, lt,
    gq_out, gkv_out, qgl_out, cgl_out, mine, away, gm, gqs,
):
    half = go.shape[0]
    width = qo.shape[1]
    w[0].take(0)
    depth = cu2.shape[1]
    weight = w[0].columns(0, width, width)
    scale = HD ** (-0.5)
    for i, (rows, query, lse) in enumerate(((go, qo, lo), (gt, qt, lt))):
        at = slice(i * half, (i + 1) * half)
        gl = mm(rows[:, :depth], cu2[...], 1, 1)
        cgl_out[at, :] = gl
        grad = mm(rows[:, :depth], weight) + mm(two(gl), cd2[...], 1, 1)
        gm[...] = (grad * owned[...]).astype(bf16)
        for first, size in lane_groups(width):
            cols = slice(first, first + size)
            q_all, g_all = query[:, cols], gm[:, cols]
            grad_q, grad_k, grad_v = 0.0, 0.0, 0.0
            for j in range(size // HD):
                key, val = only_head(kv[0, :, cols], j), only_head(kv[1, :, cols], j)
                h = first // HD + j
                scores = mm(key, q_all, 1, 1) * scale
                scores = jnp.where(live[...] > 0.0, scores, masked_score)
                probs = jnp.exp(scores - lse[h : h + 1, :])
                grad_p = mm(val, g_all, 1, 1)
                grad_v = grad_v + mm(probs.astype(bf16), only_head(g_all, j))
                inner = jnp.sum(probs * grad_p, axis=0, keepdims=True)
                grad_s = (probs * (grad_p - inner)).astype(bf16)
                grad_q = grad_q + mm(grad_s, key, 0, 0)
                grad_k = grad_k + mm(grad_s, only_head(q_all, j))
            gqs[at, cols] = grad_q
            for side, new in ((0, grad_k * scale), (1, grad_v)):
                gkv_out[side, :, cols] = new if i == 0 else gkv_out[side, :, cols] + new
    gq = (gqs[...] * scale).astype(bf16)
    gq_out[...] = gq
    gl = mm(gq, qu2[...], 1, 1)
    qgl_out[...] = gl
    pair = two(gl)
    total = mm(gq, w[0].columns(0, 0, width), 1, 1) + mm(pair, qd2[...], 1, 1)
    put(mine, everything, total[:half])
    put(away, everything, total[half:])


def linear_bwd(
    w, go, gt, q, st1, st2, ratio, den, owned, d2, u2, gq_out, gl_out, st_out, gh,
):
    half = go.shape[0]
    width = q.shape[1]
    depth = u2.shape[1]
    w[0].take(0)
    weight = w[0].columns(0, width, width)
    for i, rows in enumerate((go, gt)):
        at = pl.ds(i * half, half)
        gl = mm(rows[:, :depth], u2[...], 1, 1)
        gl_out[at, :] = gl
        gh[at, :] = (mm(rows[:, :depth], weight) + mm(two(gl), d2[...], 1, 1)) * owned[...]
    st = st1[...] + st2[...]
    grad = gh[...]
    inverse = 1.0 / den[...]
    numer = grad * inverse
    grad_den = -head_total(grad * ratio[...]) * inverse
    raw = q[...]
    queries = jnp.maximum(raw, 0.0)
    grad_q = head_product(numer, st[:HD], 0) + grad_den * st[HD : HD + 1]
    gq_out[...] = jnp.where(raw > 0.0, grad_q, 0.0).astype(bf16)
    st_out[:HD, :] = head_outer(numer, queries)
    total = jnp.sum(grad_den * queries, axis=0, keepdims=True)
    st_out[HD:, :] = jnp.broadcast_to(total, (8, width))


def linear_end(
    w, gq, k, v, st1, st2, d2, u2, gk_out, gv_out, gl_out, mine, away,
):
    width = k.shape[1]
    half = mine.shape[0]
    st = st1[...] + st2[...]
    raw = k[...]
    grad_k = head_product(v[...], st[:HD], 0) + st[HD : HD + 1]
    gk_out[...] = jnp.where(raw > 0.0, grad_k, 0.0).astype(bf16)
    gv_out[...] = head_product(jnp.maximum(raw, 0.0), st[:HD], 1).astype(bf16)
    grads = (gq, gk_out, gv_out)
    gl = sum(mm(g[...], u2[i], 1, 1) for i, g in enumerate(grads))
    gl_out[...] = gl
    pair = two(gl)
    w[0].take(0)
    w[0].take(1)
    both = jnp.concatenate([gq[...], gk_out[...]], axis=1)
    total = mm(both, w[0].columns(0, 0, 2 * width), 1, 1) + mm(gv_out[...], w[0].columns(1, 0, width), 1, 1)
    total = total + mm(pair, d2[...], 1, 1)
    put(mine, everything, total[:half])
    put(away, everything, total[half:])


def in_steps(rows, body, step=64):
    def one(i, carry):
        body(pl.ds(pl.multiple_of(i * step, step), step))
        return carry

    lax.fori_loop(0, rows // step, one, 0)


def slope_of_norm(values, grad):
    normed, inverse = row_stats(values)
    return inverse * (
        grad
        - jnp.mean(grad, axis=-1, keepdims=True)
        - normed * jnp.mean(grad * normed, axis=-1, keepdims=True)
    )


def total_of(low, got, at, width):
    return low[at, :width].astype(f32) + got[at, :width].astype(f32)


def end_attn(low, got, x, mods, after_out, own_out):
    def body(at):
        after = x[at, :].astype(f32) + mods[2:3, :] * total_of(low, got, at, x.shape[1])
        after_out[at, :] = after
        put(own_out, at, after)

    in_steps(x.shape[0], body)


def end_cross(low, got, before, mods, after_out, own_out):
    def body(at):
        after = before[at, :] + total_of(low, got, at, before.shape[1])
        after_out[at, :] = after
        normed, unused = row_stats(after)
        put(own_out, at, normed * (1.0 + mods[4:5, :]) + mods[3:4, :])

    in_steps(before.shape[0], body)


def end_output(low, got, before, mods, out):
    def body(at):
        put(out, at, before[at, :] + mods[5:6, :] * total_of(low, got, at, before.shape[1]))

    in_steps(before.shape[0], body)


def end_ffn_back(low, got, after, cot, mods, grad_out, own_out):
    def body(at):
        grad = total_of(low, got, at, after.shape[1]) * (1.0 + mods[4:5, :])
        grad = cot[at, :].astype(f32) + slope_of_norm(after[at, :], grad)
        grad_out[at, :] = grad
        put(own_out, at, grad)

    in_steps(after.shape[0], body)


def end_cross_back(low, got, before, mods, grad_out, own_out):
    def body(at):
        grad = before[at, :] + total_of(low, got, at, before.shape[1])
        grad_out[at, :] = grad
        put(own_out, at, mods[2:3, :] * grad)

    in_steps(before.shape[0], body)


def end_attn_back(low, got, before, x, mods, out):
    def body(at):
        grad = total_of(low, got, at, before.shape[1]) * (1.0 + mods[1:2, :])
        put(out, at, before[at, :] + slope_of_norm(x[at, :].astype(f32), grad))

    in_steps(before.shape[0], body)


def place_rows(where, own, other, out):
    width = out.shape[2]
    out[where[0]] = own[:, :width]
    out[1 - where[0]] = other[:, :width]


def fold(both):
    half = both.shape[0] // 2
    return both[:half] + both[half:]


def turned(v, b):
    half = v.shape[1] // 2
    return jnp.where(b == 0, v, jnp.concatenate([v[:, half:], v[:, :half]], axis=1))


def thin_sum(latent, *rows):
    high = latent.astype(bf16).astype(f32)
    both = jnp.concatenate([high, latent - high], axis=0).astype(bf16)
    total, at = None, 0
    for values in rows:
        size = values.shape[0]
        term = mm(both[:, at : at + size], values[...])
        total = term if total is None else total + term
        at += size
    return fold(total)


def outer_sum(latent, *rows):
    total, at = None, 0
    pair = two(latent)
    for values in rows:
        size = values.shape[0]
        term = mm(pair[at : at + size], values[...], 0, 0)
        total = term if total is None else total + term
        at += size
    return fold(total)


def set_segments(out, segments, width):
    for i, v in enumerate(segments):
        put(out.at[:, i * width : (i + 1) * width], everything, v)


def set_ranks(out, first, pad, values):
    rows = out.shape[1]
    for t in range(out.shape[0]):
        put(out.at[t, :, first : first + pad], everything, values[t * rows : (t + 1) * rows])


def pack_first(where, point, up, l0, l1, l2, l3, sums):
    pieces = [point[0], point[1]] + [up[h, p] for p in range(2) for h in range(2)]
    n = l0.shape[0]
    rank = sums.shape[0] * sums.shape[1]
    first = sums.shape[2] - 4 * n
    pad = first // 6
    for i, v in enumerate(pieces):
        set_ranks(sums, i * pad, pad, fold(v))
    for i, v in enumerate((l0, l1, l2, l3)):
        set_ranks(sums, first + i * n, n, turned(v[...].T[:rank], where[0]))


def to_blocks(home, first, table):
    blocks = home.shape[0]
    size = table.shape[1] // blocks
    rows = table.shape[0]
    for i in range(blocks):
        home[i, first : first + rows, :size] = table[:, i * size : (i + 1) * size]


def set_mark(where, home, first):
    home[:, first:, :] = jnp.zeros((home.shape[0], home.shape[1] - first, home.shape[2]), f32) + where[2].astype(f32)


def second_sums(
    where, sums, gco, gct, fo, ft, gffn, mixo, mixt, cgl, qlat, gq, qgl, gkv, ggot, klat, ku2,
    home_out, projs, out, home,
):
    n, depth = gffn.shape
    b = where[0]
    first = sums.shape[2] - 4 * n
    parts = []
    for i in range(4):
        at = slice(first + i * n, first + (i + 1) * n)
        parts.append(turned(sums[0, :, at] + sums[1, :, at] + sums[2, :, at] + sums[3, :, at], b))
    projs[...] = parts[0]
    rows = parts[0].shape[0]
    home[...] = jnp.zeros(home.shape, f32)
    to_blocks(home, 0, thin_sum(parts[1], gco, gct)[:, :depth])
    to_blocks(home, rows, thin_sum(parts[2], gffn))
    to_blocks(home, 2 * rows, thin_sum(parts[3], fo, ft)[:, :depth])
    pad, hh = first // 6, home.shape[2] * home.shape[0] // 8
    size = home.shape[2]
    for j in range(3):
        for i in range(home.shape[0]):
            t, h, at = i * size // (2 * hh), i * size % (2 * hh) // hh, i * size % hh
            at += (2 * j + h) * pad
            home[i, (3 + j) * rows : (4 + j) * rows, :] = sums[t, :, at : at + size]
    set_mark(where, home, 6 * rows)
    home_out[...] = home[...].astype(home_out.dtype)
    here = ggot.shape[1]
    gk = (gkv[0, :here, :] + ggot[0]).astype(bf16)
    gv = (gkv[1, :here, :] + ggot[1]).astype(bf16)
    segments = [outer_sum(cgl[...], mixo, mixt), outer_sum(qlat[...], gq)]
    segments += [outer_sum(klat[...], gk), outer_sum(klat[...], gv)]
    pad = -(-gq.shape[1] // LANES) * LANES
    set_segments(out, segments, pad)
    rank = out.shape[0]
    out[:, 4 * pad : 4 * pad + n] = turned(qgl[...].T[:rank], b)
    kvgl = mm(gk, ku2[0], 1, 1) + mm(gv, ku2[1], 1, 1)
    put(out.at[:, 4 * pad + n :], everything, kvgl.T[:rank])


def third_sums(where, before, pgl, mixed, qlat, gq, gk, gv, qgl, out):
    rank, first = before.shape
    set_ranks(out, 0, first, before[...])
    segments = [outer_sum(pgl[...], mixed)] + [outer_sum(qlat[...], g) for g in (gq, gk, gv)]
    pad = -(-gq.shape[1] // LANES) * LANES
    for i, v in enumerate(segments):
        set_ranks(out, first + i * pad, pad, v)
    set_ranks(out, first + 4 * pad, qgl.shape[0], turned(qgl[...].T[:rank], where[0]))


def last_sums(ranges, where, sums, projs, gao, gat, xo, xt, cap, a, home_out, home):
    n, depth = a.shape
    b = where[0]
    text = -(-cap.shape[0] // LANES) * LANES
    pad = (sums.shape[2] - 2 * n - text) // 8
    second = 4 * pad + n + text
    rows = projs.shape[0]

    def summed(first, size):
        return sum(sums[t, :, first : first + size] for t in range(sums.shape[0]))

    def heads(first):
        parts = [sums[t, :, first + s * HD : first + (s + m) * HD] for t, (s, m) in enumerate(ranges)]
        return jnp.concatenate(parts, axis=1)

    tables = [
        thin_sum(turned(summed(4 * pad, n), b), xo, xt)[:, :depth],
        thin_sum(summed(4 * pad + n, cap.shape[0]), cap)[:, :depth],
        thin_sum(projs[...], gao, gat)[:, :depth],
    ]
    tables += [heads(j * pad) for j in range(4)] + [heads(second + j * pad) for j in range(4)]
    tables.append(thin_sum(turned(summed(second + 4 * pad, n), b), a))
    for j, table in enumerate(tables):
        to_blocks(home, j * rows, table)
    set_mark(where, home, len(tables) * rows)
    home_out[...] = home[...].astype(home_out.dtype)


def adapter_tables(got, out):
    last = got.shape[1] - 1
    for i in range(out.shape[0]):
        total = None
        for s in range(got.shape[0]):
            values = got[s].astype(f32)
            term = jnp.where(values[last:, :1] == float(i), values, 0.0)
            total = term if total is None else total + term
        out[i] = total


def ring_order(n):
    return list(range(0, n, 2)) + list(range(n - 1 - n % 2, 0, -2))


def ring_pairs(n):
    order = ring_order(n)
    return [(order[i], order[(i + 1) % n]) for i in range(n)]


def ring_source(n, step):
    z = lax.axis_index(W)
    place = jnp.where(z % 2 == 0, z // 2, n - 1 - z // 2)
    from_place = (place - step + n) % n
    return jnp.where(2 * from_place < n, 2 * from_place, 2 * (n - 1 - from_place) + 1)


def swap_pairs(n, distance):
    return [(i, i ^ distance) for i in range(n)]


def across(values, axis, distance=1):
    return lax.ppermute(values, axis, swap_pairs(lax.axis_size(axis), distance))


class Stream:
    def __init__(self, order):
        self.n = lax.axis_size(W)
        self.order = list(order)
        self.own, self.got, self.crossed = {}, {}, {}
        self.flying, self.crossing = [], []

    def launch(self):
        while self.order and (not self.flying or len(self.flying) < 2 and self.order[0][1] == 1):
            name, step = self.order[0]
            if step == 1 and name in self.own:
                moving = self.own[name][0]
            elif (name, step - 1) in self.got:
                moving = self.got[name, step - 1]
            else:
                break
            self.order.pop(0)
            self.flying.append((name, step, lax.ppermute(moving, W, ring_pairs(self.n))))

    def fence(self, values, take=1, cross=None):
        done, self.flying = self.flying[:take], self.flying[take:]
        count = len(self.crossing) if cross is None else cross
        crossed, self.crossing = self.crossing[:count], self.crossing[count:]
        leaves, tree = jax.tree.flatten((values, [d[2] for d in done], [d[2] for d in crossed]))
        values, arrived, over = jax.tree.unflatten(tree, lax.optimization_barrier(leaves))
        for d, v in zip(crossed, over):
            self.crossed[d[0], d[1]] = v
        for d, v in zip(done, arrived):
            self.got[d[0], d[1]] = v
            self.crossing.append((d[0], d[1], across(v, C)))
        self.launch()
        return values

    def fences(self, count, values):
        for i in range(count * (self.n - 1) // 3):
            values = self.fence(values)
        return values

    def ready(self, names, values):
        while not all((name, self.n - 1) in self.crossed for name in names):
            values = self.fence(values)
        return values

    def pieces(self, name):
        steps = range(1, self.n)
        mine = [self.own[name][0]] + [self.got[name, s] for s in steps]
        other = [self.own[name][1]] + [self.crossed[name, s] for s in steps]
        rows = mine[0].shape[0]
        if rows % 16 == 0:
            return mine + other
        c = lax.axis_index(C)
        buf = jnp.zeros((2, self.n * rows, mine[0].shape[1]), bf16)
        for s in range(self.n):
            at = ring_source(self.n, s) * rows
            buf = lax.dynamic_update_slice(buf, mine[s][None], (c, at, 0))
            buf = lax.dynamic_update_slice(buf, other[s][None], (1 - c, at, 0))
        return [buf]


class Weight:
    def __init__(self, meta, pieces, buf, sems, halves):
        self.meta, self.pieces, self.buf, self.sems, self.halves = meta, pieces, buf, sems, halves

    def copies(self, j, pieces):
        rows = pieces[0].shape[0]
        return [
            pltpu.make_async_copy(
                piece,
                self.buf.at[j, pl.ds(pl.multiple_of(self.meta[1 + k] * rows, rows), rows), :],
                self.sems.at[j, k],
            )
            for k, piece in enumerate(pieces)
        ]

    def start(self):
        count = len(self.pieces) // 2
        for j, half in enumerate(self.halves):
            if not count:
                pltpu.make_async_copy(self.pieces[0].at[half], self.buf.at[j], self.sems.at[j, 0]).start()
                continue

            @pl.when(self.meta[0] == half)
            def mine():
                for copy in self.copies(j, self.pieces[:count]):
                    copy.start()

            @pl.when(self.meta[0] != half)
            def other():
                for copy in self.copies(j, self.pieces[count:]):
                    copy.start()

    def take(self, j):
        count = len(self.pieces) // 2
        if not count:
            pltpu.make_async_copy(self.pieces[0].at[0], self.buf.at[j], self.sems.at[j, 0]).wait()
        else:
            for copy in self.copies(j, self.pieces[:count]):
                copy.wait()
        return self.buf[j]

    def columns(self, j, first, size):
        return self.buf[j, :, first : first + size]


def per_step(a):
    zeros = (0,) * (a.ndim - 1)
    return pl.BlockSpec((1,) + tuple(a.shape[1:]), lambda h: (h,) + zeros)


def half_block(i):
    def spec(a):
        zeros = (0,) * (len(a.shape) - 1)
        return pl.BlockSpec((1,) + tuple(a.shape[1:]), lambda *g: (i,) + zeros)

    return spec


def row_block(a):
    return pl.BlockSpec((a.shape[0] // 4, a.shape[1]), lambda i: (i, 0))


def both_blocks(a):
    return pl.BlockSpec((2, a.shape[1] // 4, a.shape[2]), lambda i: (0, i, 0))


def all_of(a):
    zeros = (0,) * len(a.shape)
    return pl.BlockSpec(tuple(a.shape), lambda *g: zeros)


def scalars(a):
    return pl.BlockSpec(memory_space=pltpu.SMEM)


def anywhere(a):
    return pl.BlockSpec(memory_space=pl.ANY)


def run(kernel, ins, outs, scratch=(), steps=1, weights=(), meta=None, same=()):
    args, specs = [], []
    if weights:
        args.append(meta)
        specs.append(scalars(meta))
    counts, extra = [], []
    for pieces, halves in weights:
        counts.append((len(pieces), halves))
        args += pieces
        specs += [anywhere(p) for p in pieces]
        rows = pieces[0].shape[0] * len(pieces) // 2 if len(pieces) > 1 else pieces[0].shape[1]
        extra.append(pltpu.VMEM((len(halves), rows, pieces[0].shape[-1]), bf16))
        extra.append(pltpu.SemaphoreType.DMA((len(halves), max(len(pieces) // 2, 1))))
    first = len(args)
    for item in ins:
        a, spec = item if isinstance(item, tuple) else (item, all_of)
        args.append(a)
        specs.append(spec(a))
    shapes, out_specs = [], []
    for item in outs:
        dims, dtype, spec = item if len(item) == 3 else item + (all_of,)
        shapes.append(shape(dims, dtype))
        out_specs.append(spec(shapes[-1]))

    def body(*refs):
        if not weights:
            return kernel(*refs)
        at, loaders = 1, []
        tail = refs[len(refs) - len(extra) :]
        for i, (count, halves) in enumerate(counts):
            loaders.append(Weight(refs[0], refs[at : at + count], tail[2 * i], tail[2 * i + 1], halves))
            at += count

        @pl.when(pl.program_id(0) == 0)
        def begin():
            for loader in loaders:
                loader.start()

        kernel(loaders, *refs[first : len(refs) - len(extra)])

    return pl.pallas_call(
        body,
        grid=(steps,),
        in_specs=specs,
        out_specs=out_specs,
        out_shape=shapes,
        input_output_aliases={first + i: j for i, j in same},
        scratch_shapes=list(scratch) + extra,
        compiler_params=big,
    )(*args)


def twice(table, axis):
    return jnp.concatenate([table, table], axis=axis)


def slot_layout(groups, rank, heads):
    per, left = heads // groups, heads % groups
    slots = per + (1 if left else 0)
    own_start = rank * per + jnp.minimum(rank, left)
    own_count = per + jnp.where(rank < left, 1, 0)
    first = jnp.minimum(own_start, heads - slots)
    slot = first + jnp.arange(slots, dtype=jnp.int32)
    owned = ((slot >= own_start) & (slot < own_start + own_count)).astype(f32)
    return slots, first, owned


def slot_ranges(groups, heads):
    per, left = heads // groups, heads % groups
    slots = per + (1 if left else 0)
    out = []
    for rank in range(groups):
        own_start = rank * per + min(rank, left)
        count = per + (1 if rank < left else 0)
        out.append((own_start - min(own_start, heads - slots), count))
    return out


def shards(
    tokens, caption, caption_lengths, adapter_index, modulation, cotangent,
    qkv_weight, proj_weight, cross_q_weight, cross_kv_weight, cross_out_weight,
    inverted_weight, depth_weight, point_weight,
    qkv_down, qkv_up, proj_down, proj_up, query_down, query_up, kv_down, kv_up,
    cross_down, cross_up, inverted_down, inverted_up, point_down, point_up,
):
    grid_rows, grid_cols, D = tokens.shape[1:]
    n = grid_rows * grid_cols
    half = n // 2
    heads = D // HD
    groups = lax.axis_size(T)
    rank = lax.axis_index(T)
    c = lax.axis_index(C)
    b = rank % 2
    adapters, R = qkv_up.shape[:2]
    slots, slot_first, owned = slot_layout(groups, rank, heads)
    width = slots * HD
    col = slot_first * HD
    owned = jnp.repeat(owned, HD)[None]
    hid = inverted_weight.shape[2]
    hh = hid // 2
    hid_first = rank * hid
    index = adapter_index[0]
    where = jnp.stack([b, c, index]).astype(jnp.int32)

    def cut(table, start, size, axis):
        return lax.dynamic_slice_in_dim(table, start, size, axis)

    def pick(table):
        return lax.dynamic_index_in_dim(table, index, 0, keepdims=False)

    def own_rows(rows):
        own = cut(rows, b * half, half, 0)
        return own, jnp.concatenate([own, cut(rows, (1 - b) * half, half, 0)])

    def pair_of(first, second):
        return [jnp.where(c == 0, first, second), jnp.where(c == 0, second, first)]

    def taken(table, middle, start, size):
        return lax.dynamic_slice(table, (0, middle, start), (table.shape[0], 1, size))[:, 0]

    def beside(*values):
        return jnp.concatenate(values, axis=1)

    def both(table, start, size=width):
        return beside(taken(table, 0, start, size), taken(table, 1, start, size))

    size = lax.axis_size(W)
    order = [(name, step) for name in ("ab", "cd", "vg", "p") for step in range(1, size)]
    stream = Stream(order)
    fences = stream.fences

    side_qk = both(qkv_weight, col)
    side_vo = beside(taken(qkv_weight, 2, col, width), cut(proj_weight, col, width, 0).T)
    stream.own["ab"] = [jnp.where(c == 0, side_qk, side_vo), None]
    c_late, caption, stream.own["ab"][0] = lax.optimization_barrier((c, caption, stream.own["ab"][0]))
    stream.own["ab"][1] = jnp.where(c_late == 0, side_vo, side_qk)
    stream.launch()
    mods = modulation[0]
    low_tokens = tokens.reshape(n, D)
    x_low, x_rows = own_rows(low_tokens)
    qd2, qu2 = twice(pick(qkv_down), 1), twice(cut(pick(qkv_up), col, width, 2), 0).transpose(1, 0, 2)
    pd2, pu2 = twice(cut(pick(proj_down), col, width, 0), 1), twice(pick(proj_up), 0)
    text_here = caption.shape[1]
    text_rows = -(-text_here // 16) * 16
    padded = -(-D // LANES) * LANES
    cap = jnp.pad(caption[0], ((0, text_rows - text_here), (0, padded - D)))
    cap_other = across(cap, C)
    tables = [query_down, query_up, kv_down, kv_up, cross_down, cross_up]
    tables_f = [inverted_down, inverted_up, point_down, point_up, depth_weight]
    raw = [cross_kv_weight, cross_q_weight, cross_out_weight]
    raw_f = [inverted_weight, point_weight]
    raw, raw_f, tables, tables_f, cap, cap_other, cotangent = fences(
        1, (raw, raw_f, tables, tables_f, cap, cap_other, cotangent)
    )
    pair_cd = pair_of(both(raw[0], col), beside(cut(raw[1], col, width, 1), cut(raw[2], col, width, 0).T))
    query_down, query_up, kv_down, kv_up, cross_down, cross_up = tables
    cd2 = twice(cut(pick(cross_down), col, width, 0), 1)
    cu2 = twice(pick(cross_up), 0)
    xd2, xu2 = twice(pick(query_down), 1), twice(cut(pick(query_up), col, width, 1), 0)
    kd2, ku2 = twice(pick(kv_down), 1), twice(cut(pick(kv_up), col, width, 2), 0).transpose(1, 0, 2)
    front = [x_low, x_rows, qd2, qu2, pd2, pu2, stream.own["ab"][1]]
    pair_cd, raw_f, tables_f, cotangent, front = fences(1, (pair_cd, raw_f, tables_f, cotangent, front))
    stream.own["cd"] = pair_cd
    x_low, x_rows, qd2, qu2, pd2, pu2, stream.own["ab"][1] = front
    pair_vg = [both(raw_f[0], i * hh, hh) for i in (c, 1 - c)]
    pair_p = [cut(raw_f[1], i * hh, hh, 0).T for i in (c, 1 - c)]
    pair_vg, pair_p, tables_f, cotangent = fences(1, (pair_vg, pair_p, tables_f, cotangent))
    stream.own.update(vg=pair_vg, p=pair_p)
    inverted_down, inverted_up, point_down, point_up, depth_weight = tables_f
    fd2, fu2 = twice(pick(inverted_down), 1), twice(cut(pick(inverted_up), hid_first, hid, 2), 0)
    fu2 = fu2.reshape(2 * R, 2, 2, hh).transpose(1, 2, 0, 3)
    od2 = twice(cut(pick(point_down), hid_first, hid, 0), 1).reshape(2, hh, 2 * R)
    ou2 = twice(pick(point_up), 0)
    taps = depth_weight.astype(f32).reshape(9, 2, 2, hh).transpose(2, 1, 0, 3)
    cot_low, cot = own_rows(cotangent.reshape(n, D))
    places = jnp.arange(text_rows)
    live = jnp.concatenate([c * text_here + places, (1 - c) * text_here + places])
    live = (live < caption_lengths[0]) & (jnp.concatenate([places, places]) < text_here)
    live = live.astype(f32)[None]
    tables = [cd2, cu2, xd2, xu2, kd2, ku2, fd2, fu2[0], fu2[1], od2, ou2, taps, cot_low, cot, live]
    x_rows, tables = stream.ready(["ab"], (x_rows, tables))
    cd2, cu2, xd2, xu2, kd2, ku2, fd2, fuv, fug, od2, ou2, taps, cot_low, cot, live = tables

    w_ab = stream.pieces("ab")
    meta = jnp.stack([c] + [ring_source(size, s) for s in range(size)]).astype(jnp.int32)
    rows_bf = ((n, D), bf16)
    thin = ((n, 2 * R), f32)
    wide = ((n, width), f32)
    wide_bf = ((n, width), bf16)
    pair = [((half, padded), bf16)] * 2
    ended = [((half, D), f32, row_block), ((half, padded), bf16, row_block)]

    def finish_rows(kernel, arrays, outs):
        return run(kernel, [(v, row_block) for v in arrays] + [mods], outs, steps=4)

    state_of = ((HD + 8, width), f32)
    attn_in, q_raw, k_raw, qkv_lat = run(
        attn_front, [x_rows, mods, qd2, qu2], [rows_bf, wide, wide, thin], weights=[(w_ab, (0,))], meta=meta,
    )
    v_raw, st_own = run(
        attn_state, [attn_in, k_raw, qkv_lat, qu2], [wide, state_of], weights=[(w_ab, (1,))], meta=meta,
    )
    st_own, st_other = fences(1, (st_own, across(st_own, C)))
    ratio, denom, mixed, proj_lat, mine, away = run(
        attn_back, [q_raw, st_own, st_other, owned, pd2, pu2], [wide, wide, wide_bf, thin] + pair,
        weights=[(w_ab, (1,))], meta=meta,
    )

    def exchanged(mine, away, pace=lambda low: low):
        low, distance = (mine.astype(f32) + across(away, T).astype(f32)).astype(bf16), 2
        while True:
            low = pace(low)
            got = across(low, T, distance)
            distance *= 2
            if distance >= groups:
                return low, got
            low = (low.astype(f32) + got.astype(f32)).astype(bf16)

    def while_streaming(mine, away):
        return exchanged(mine, away)

    mine, away = fences(1, (mine, away))
    low, got = fences(1, while_streaming(mine, away))
    after_attn, cross_own = finish_rows(end_attn, [low, got, x_low], ended)
    cross_other = across(cross_own, T)

    cap, cross_own, cross_other, after_attn = stream.ready(["cd"], (cap, cross_own, cross_other, after_attn))
    w_cd = stream.pieces("cd")
    kv_all, kv_lat = run(
        caption_rows, [cap, cap_other, kd2, ku2], [((2, 2 * text_rows, width), bf16), ((text_rows, 2 * R), f32)],
        weights=[(w_cd, (0,))], meta=meta,
    )
    kv_all, cross_own, cross_other = fences(1, (kv_all, cross_own, cross_other))
    half_bf, half_thin = ((half, width), bf16), ((half, 2 * R), f32)

    def cross_part(rows, kv):
        return run(
            cross_fwd,
            [rows, kv, live, owned, xd2, xu2, cd2, cu2],
            [half_bf, half_bf, half_thin, half_thin, ((LANES, half), f32), ((half, padded), bf16)],
            [pltpu.VMEM((half, LANES), f32)],
            weights=[(w_cd, (1,))], meta=meta,
        )

    *cross_t, away = cross_part(cross_other, kv_all)
    away, cross_tied, kv_tied = lax.optimization_barrier((away, cross_own, kv_all))
    *cross_o, mine = cross_part(cross_tied, kv_tied)
    mine, away = fences(1, (mine, away))
    query, mix, query_lat, cross_lat, lse = zip(cross_o, cross_t)
    low, got = while_streaming(mine, away)
    low, got = stream.fence((stream.fence(low, 1, 0), got), 0, 1)
    after_cross, ffn_own = finish_rows(end_cross, [low, got, after_attn], ended)
    ffn_own, after_cross = stream.fence((ffn_own, after_cross), 1, 1)
    ffn_other = across(ffn_own, T)

    query_lat, cross_lat = jnp.concatenate(query_lat), jnp.concatenate(cross_lat)

    ffn_own, ffn_other, after_cross = stream.ready(["vg"], (ffn_own, ffn_other, after_cross))
    w_vg = stream.pieces("vg")
    hid_bf = ((2, n, hh), bf16, per_step)

    def ffn_part(h, more, same):
        outs = [((2, n, hh), f32)] * 2 + [((2, n, hh), bf16)] * 2 + [((2, grid_cols, hh), bf16)] * 2
        return run(
            functools.partial(ffn_front, h),
            [(where, scalars), ffn_own, ffn_other, fd2, (fuv, half_block(h)), (fug, half_block(h))] + more,
            [out + (half_block(h),) for out in outs] + [thin][h:],
            [pltpu.VMEM((n, D), bf16)],
            weights=[(w_vg, (h,))], meta=meta, same=same,
        )

    *started, inv_lat = ffn_part(0, [], ())
    ffn_own, started, inv_lat = stream.fence((ffn_own, started, inv_lat), 1, 1)
    pre_v, pre_g, hid_v, hid_g, edge_v, edge_g = ffn_part(
        1, [inv_lat] + [(v, anywhere) for v in started], [(7 + i, i) for i in range(6)]
    )
    halo_v, halo_g = across(edge_v, C), across(edge_g, C)
    hid_v, halo_v, halo_g = stream.ready(["p"], (hid_v, halo_v, halo_g))
    w_p = stream.pieces("p")
    grid_buf = pltpu.VMEM((n + 2 * grid_cols, hh), f32)
    row_acc = pltpu.VMEM((n, D), f32)
    gated, gcv, gcg, grad_ffn, point_gl, point_lat, point_down_g, edge, mine, away = run(
        ffn_mid,
        [
            (where, scalars), (hid_v, per_step), (hid_g, per_step), (halo_v, per_step), (halo_g, per_step), (taps, per_step),
            cot, mods[5:6], (od2, per_step), ou2,
        ],
        [hid_bf, hid_bf, hid_bf, rows_bf, thin, thin, ((2, 2 * R, hh), f32, per_step)]
        + [((2, 2, grid_cols, hh), bf16, per_step)] + pair,
        [grid_buf, grid_buf, pltpu.VMEM((n, hh), f32), row_acc],
        2,
        weights=[(w_p, (0, 1))], meta=meta,
    )
    halo = across(edge, C)
    tied = []

    def after_halo(low):
        low, *tied[:] = lax.optimization_barrier((low, halo, gcv, gcg))
        return low

    out_low, out_got = exchanged(mine, away, after_halo)
    halo, gcv, gcg = tied

    gpv, gpg, inv_up_g, inv_gl, mine, away = run(
        ffn_back,
        [
            (where, scalars), (gcv, per_step), (gcg, per_step), (halo, per_step), (taps, per_step),
            (pre_v, per_step), (pre_g, per_step), inv_lat, fd2,
            (fuv, per_step), (fug, per_step),
        ],
        [hid_bf, hid_bf, ((2, 2, 2 * R, hh), f32, per_step), thin] + pair,
        [grid_buf, grid_buf, row_acc],
        2,
        weights=[(w_vg, (0, 1))], meta=meta,
    )
    part_r = R // groups
    blocks = size * lax.axis_size(C)
    ranges = slot_ranges(groups, heads)

    def swapped(sent):
        return lax.all_to_all(sent, T, 0, 0, tiled=True)

    def up_to_tiles(size):
        return -(-size // LANES) * LANES

    def table_rows(table, i, size):
        return table[:, i * part_r : (i + 1) * part_r, : size // blocks]

    def down_rows(table, i, size):
        return table_rows(table, i, size).transpose(0, 2, 1)

    def together(*values):
        return lax.optimization_barrier(values)

    def during(mine, away, inputs, work):
        held = []

        def pace(low):
            low, tied = together(low, inputs)
            held[:] = [tied]
            return low

        low, got = exchanged(mine, away, pace)
        return together(low, got, work(*held[0]))

    def first_work(out_low, out_got, after_cross, inv_up_g, point_down_g, lats):
        (output,) = finish_rows(end_output, [out_low, out_got, after_cross], [((half, padded), f32, row_block)])
        (sums,) = run(
            pack_first, [(where, scalars), point_down_g, inv_up_g, *lats], [((groups, part_r, 6 * up_to_tiles(hh) + 4 * n), f32)],
        )
        return output, sums

    mine, away, out_low, out_got = together(mine, away, out_low, out_got)
    low, got, (output, sums_f) = during(
        mine, away,
        (out_low, out_got, after_cross, inv_up_g, point_down_g, (proj_lat, cross_lat, point_lat, inv_gl)),
        first_work,
    )
    grad_cross, gc_own = finish_rows(end_ffn_back, [low, got, after_cross, cot_low], ended)
    gc_other = across(gc_own, T)

    gc_own, gc_other, output, sums_f = together(gc_own, gc_other, output, sums_f)
    output_other = across(output, T)
    sums_f = swapped(sums_f)
    grad_query, gkv, query_gl, cross_gl, mine, away = run(
        cross_bwd,
        [
            gc_own, gc_other, kv_all, live.T, owned,
            xd2, xu2, cd2, cu2, *query, *lse,
        ],
        [wide_bf, ((2, 2 * text_rows, width), f32), thin, thin] + pair,
        [pltpu.VMEM((half, width), bf16), pltpu.VMEM((n, width), f32)],
        weights=[(w_cd, (1,))], meta=meta,
    )
    mine, away, output_other, sums_f, gkv = together(mine, away, output_other, sums_f, gkv)
    gkv_got = across(gkv[:, text_rows:], C)

    def in_order(own, other):
        (rows,) = run(
            place_rows, [(where, scalars), (own, row_block), (other, row_block)],
            [((2, half, D), f32, both_blocks)], steps=4,
        )
        return rows.reshape(tokens.shape)

    seg = up_to_tiles(width)

    seg = up_to_tiles(width)
    home_dims = (blocks, 8 * part_r, 4 * 2 * hh // blocks)
    last_dims = (blocks, 16 * part_r, D // blocks)

    def second_work(output, output_other, sums, cross_gl, grad_query, query_gl):
        return [in_order(output, output_other)] + list(run(
            second_sums,
            [
                (where, scalars), sums, gc_own, gc_other, ffn_own, ffn_other, grad_ffn, *mix, cross_gl,
                query_lat, grad_query, query_gl, gkv, gkv_got, kv_lat, ku2,
            ],
            [(home_dims, bf16), ((part_r, n), f32), ((R, 4 * seg + n + up_to_tiles(text_rows)), f32)],
            [pltpu.VMEM(home_dims, f32)],
        ))

    low, got, (output, home, proj_s, sums_c) = during(
        mine, away, (output, output_other, sums_f, cross_gl, grad_query, query_gl), second_work
    )
    grad_after, ga_own = finish_rows(end_cross_back, [low, got, grad_cross], ended)
    ga_other = across(ga_own, T)

    grad_q, proj_gl, sg_own = run(
        linear_bwd,
        [ga_own, ga_other, q_raw, st_own, st_other, ratio, denom, owned, pd2, pu2],
        [wide_bf, thin, state_of],
        [pltpu.VMEM((n, width), f32)],
        weights=[(w_ab, (1,))], meta=meta,
    )
    sg_other = across(sg_own, C)
    grad_k, grad_v, qkv_gl, mine, away = run(
        linear_end,
        [grad_q, k_raw, v_raw, sg_own, sg_other, qd2, qu2],
        [wide_bf, wide_bf, thin] + pair,
        weights=[(w_ab, (0, 1))], meta=meta,
    )

    def third_work(home, sums_c, proj_gl, qkv_gl, grad_q, grad_k, grad_v):
        home = lax.all_to_all(home, (W, C), 0, 0, tiled=True)
        (sums,) = run(
            third_sums, [(where, scalars), sums_c, proj_gl, mixed, qkv_lat, grad_q, grad_k, grad_v, qkv_gl],
            [((groups, part_r, sums_c.shape[1] + 4 * seg + n), f32)],
        )
        return swapped(sums), run(adapter_tables, [home], [((adapters,) + home.shape[1:], f32)])[0]

    low, got, (sums, tables) = during(
        mine, away, (home, sums_c, proj_gl, qkv_gl, grad_q, grad_k, grad_v), third_work
    )
    (input_grad,) = finish_rows(end_attn_back, [low, got, grad_after, x_low], [((half, padded), f32, row_block)])
    input_other = across(input_grad, T)
    (last,) = run(
        functools.partial(last_sums, ranges),
        [(where, scalars), sums, proj_s, ga_own, ga_other, cross_own, cross_other, cap, attn_in],
        [(last_dims, bf16)],
        [pltpu.VMEM(last_dims, f32)],
    )
    last = lax.all_to_all(last, (W, C), 0, 0, tiled=True)
    input_grad = in_order(input_grad, input_other)
    last, input_grad = together(last, input_grad)
    (last,) = run(adapter_tables, [last], [((adapters,) + last.shape[1:], f32)])

    def rows_of(i):
        return table_rows(last, i, D)

    return (
        output,
        input_grad,
        down_rows(last, 11, D),
        jnp.stack([rows_of(8), rows_of(9), rows_of(10)], axis=2),
        down_rows(last, 7, D),
        rows_of(2),
        down_rows(last, 0, D),
        rows_of(4),
        down_rows(last, 1, D),
        jnp.stack([rows_of(5), rows_of(6)], axis=2),
        down_rows(last, 3, D),
        table_rows(tables, 0, D),
        down_rows(tables, 2, D),
        jnp.stack([table_rows(tables, i, 8 * hh) for i in (4, 5)], axis=2),
        down_rows(tables, 3, 8 * hh),
        table_rows(tables, 1, D),
    )


def solution(mesh):
    down = P(None, (W, C), T)
    up3 = P(None, T, (W, C))
    up4 = P(None, T, None, (W, C))
    rows = P(W, C)
    return jax.shard_map(
        shards,
        mesh=mesh,
        in_specs=(
            rows, rows, P(W), P(W), P(W), rows,
            P(W), P(None, W), P(W), P(W), P(None, W),
            P(W, None, T), P(None, None, None, T), P(T, W),
        )
        + (P(),) * 14,
        out_specs=(
            rows, rows, down, up4, down, up3, down, up3, down, up4, down, up3, down, up4, down, up3,
        ),
        check_vma=False,
    )
```

```python
import functools
import jax
import jax.numpy as jnp
from jax import lax
from jax.experimental import pallas as pl
from jax.experimental.pallas import tpu as pltpu
from jax.sharding import PartitionSpec as P

W, C, T = "weight", "context", "tensor"
HD = 32
LANES = 128
bf16, f32 = jnp.bfloat16, jnp.float32
full_precision = lax.Precision.HIGHEST
norm_eps = 1e-06
attention_epsilon = 1e-06
masked_score = -1000000000.0
LOG2E = 1.4426950408889634
big = pltpu.CompilerParams(vmem_limit_bytes=58 * 1024 * 1024)


def shape(dims, dtype):
    return jax.ShapeDtypeStruct(dims, dtype)


def mm(a, b, ca=1, cb=0):
    return lax.dot_general(a, b, (((ca,), (cb,)), ((), ())), preferred_element_type=f32)


def two(pair):
    high = pair.astype(bf16)
    rest = (pair - high.astype(f32)).astype(bf16)
    lane = lax.broadcasted_iota(jnp.int32, pair.shape, 1)
    return jnp.where(lane < pair.shape[1] // 2, high.astype(f32), rest.astype(f32)).astype(bf16)


def split(values):
    high = values.astype(bf16)
    return high, (values - high.astype(f32)).astype(bf16)


def mm3(a, b, ca=1, cb=0):
    ah, al = split(a)
    bh, bl = split(b)
    return mm(ah, bh, ca, cb) + mm(ah, bl, ca, cb) + mm(al, bh, ca, cb)


def head_blocks(width):
    return [slice(at, min(at + 2 * LANES, width)) for at in range(0, width, 2 * LANES)]


def head_mask(width):
    row = lax.broadcasted_iota(jnp.int32, (width, width), 0) // HD
    col = lax.broadcasted_iota(jnp.int32, (width, width), 1) // HD
    return (row == col).astype(f32)


def by_blocks(one, *arrays):
    parts = [one(*[v[:, cols] for v in arrays]) for cols in head_blocks(arrays[0].shape[1])]
    return jnp.concatenate(parts, axis=1)


def head_total(values):
    def one(v):
        high, low = split(v)
        mask = head_mask(v.shape[1]).astype(bf16)
        return mm(high, mask) + mm(low, mask)

    return by_blocks(one, values)


def head_outer(a, b):
    def one(x, y):
        kept = mm3(x, y, 0, 0) * head_mask(x.shape[1])
        return sum(kept[h * HD : (h + 1) * HD] for h in range(kept.shape[0] // HD))

    return by_blocks(one, a, b)


def head_product(values, state, over):
    def one(v, s):
        size = v.shape[1]
        wide = jnp.concatenate([s] * (size // HD), axis=0) * head_mask(size)
        return mm3(v, wide, 1, over)

    return by_blocks(one, values, state)


def sigmoid(values):
    return 1.0 / (1.0 + jnp.exp(-values))


def row_stats(values):
    center = values - jnp.mean(values, axis=-1, keepdims=True)
    inverse = lax.rsqrt(jnp.mean(center * center, axis=-1, keepdims=True) + norm_eps)
    return center * inverse, inverse


def put(out, rows, values):
    width = values.shape[1]
    out[rows, :width] = values.astype(out.dtype)
    if width < out.shape[1]:
        out[rows, width:] = jnp.zeros((values.shape[0], out.shape[1] - width), out.dtype)


everything = slice(None)


def attn_front(w, x, mods, d2, u2, a_out, q_out, k_out, lat_out):
    n = x.shape[0]
    step = 64

    def norm(i, carry):
        at = pl.ds(pl.multiple_of(i * step, step), step)
        normed, unused = row_stats(x[at, :].astype(f32))
        a_out[at, :] = (normed * (1.0 + mods[1:2, :]) + mods[0:1, :]).astype(bf16)
        return carry

    lax.fori_loop(0, n // step, norm, 0)
    a = a_out[...]
    lat = mm(a, d2[...])
    lat_out[...] = lat
    pair = two(lat)
    width = q_out.shape[1]
    both = mm(a, w[0].take(0))
    q_out[...] = both[:, :width] + mm(pair, u2[0])
    k_out[...] = both[:, width:] + mm(pair, u2[1])


def attn_state(w, a, k, lat, u2, v_out, st_out):
    w[0].take(0)
    v_out[...] = mm(a[...], w[0].columns(0, 0, v_out.shape[1])) + mm(two(lat[...]), u2[2])
    keys = jnp.maximum(k[...], 0.0)
    width = keys.shape[1]
    st_out[:HD, :] = head_outer(v_out[...], keys)
    st_out[HD:, :] = jnp.broadcast_to(jnp.sum(keys, axis=0, keepdims=True), (8, width))


def put_partial(low, lat_pair, w, u2, mine, away):
    half = mine.shape[0]
    put(mine, everything, mm(low[:half], w, 1, 1) + mm(lat_pair[:half], u2))
    put(away, everything, mm(low[half:], w, 1, 1) + mm(lat_pair[half:], u2))


def attn_back(w, q, st1, st2, owned, d2, u2, ratio_out, den_out, mixed_out, lat_out, mine, away):
    st = st1[...] + st2[...]
    width = q.shape[1]
    queries = jnp.maximum(q[...], 0.0)
    numer = head_product(queries, st[:HD], 1)
    den = head_total(queries * st[HD : HD + 1]) + attention_epsilon
    ratio = numer / den
    ratio_out[...] = ratio
    den_out[...] = den
    mixed = (ratio * owned[...]).astype(bf16)
    mixed_out[...] = mixed
    lat = mm(mixed, d2[...])
    lat_out[...] = lat
    w[0].take(0)
    put_partial(mixed, two(lat), w[0].columns(0, width, width), u2[...], mine, away)


def caption_rows(w, own, other, d2, u2, kv_out, lat_out):
    here = own.shape[0]
    depth = d2.shape[0]
    width = u2.shape[2]
    weight = w[0].take(0)
    for i, rows in enumerate((own, other)):
        lat = mm(rows[:, :depth], d2[...])
        if i == 0:
            lat_out[...] = lat
        both = mm(rows[:, :depth], weight)
        for j in range(2):
            out = both[:, j * width : (j + 1) * width] + mm(two(lat), u2[j])
            kv_out[j, i * here : (i + 1) * here, :] = out.astype(bf16)


def lane_groups(width):
    return [(at, min(LANES, width - at)) for at in range(0, width, LANES)]


def only_head(values, j):
    lane = lax.broadcasted_iota(jnp.int32, (1, values.shape[1]), 1) // HD
    return values * (lane == j).astype(f32).astype(values.dtype)


def cross_fwd(
    w, rows, kv, live, owned, qd2, qu2, cd2, cu2, q_out, mix_out, qlat_out, clat_out, lse_out, part, logs,
):
    width = q_out.shape[1]
    depth = qd2.shape[0]
    w[0].take(0)
    lat = mm(rows[:, :depth], qd2[...])
    qlat_out[...] = lat
    q_out[...] = (mm(rows[:, :depth], w[0].columns(0, 0, width)) + mm(two(lat), qu2[...])).astype(bf16)
    for first, size in lane_groups(width):
        cols = slice(first, first + size)
        query = q_out[:, cols]
        total = None
        for j in range(size // HD):
            scores = mm(query, only_head(kv[0, :, cols], j), 1, 1) * HD ** (-0.5)
            scores = jnp.where(live[...] > 0.0, scores, masked_score)
            top = jnp.max(scores, axis=-1, keepdims=True)
            exps = jnp.exp(scores - top)
            tot = jnp.sum(exps, axis=-1, keepdims=True)
            h = first // HD + j
            logs[:, h : h + 1] = top + jnp.log(tot)
            probs = (exps * (1.0 / tot)).astype(bf16)
            term = mm(probs, only_head(kv[1, :, cols], j))
            total = term if total is None else total + term
        mix_out[:, cols] = (total * owned[:, cols]).astype(bf16)
    lse_out[...] = logs[...].T
    mix = mix_out[...]
    lat = mm(mix, cd2[...])
    clat_out[...] = lat
    put(part, everything, mm(mix, w[0].columns(0, width, width), 1, 1) + mm(two(lat), cu2[...]))


def edge_rows(where, rows, edge):
    r = jnp.where(where[1] == 0, rows // edge - 1, 0)
    return pl.ds(own_first(r, edge, rows // 2, where[0]), edge)


def ffn_front(h, w, where, xo, xt, d2, uv, ug, *refs):
    half = xo.shape[0]
    depth = d2.shape[0]
    pv, pg, hv, hg, ev, eg = refs[:6] if h == 0 else refs[-7:-1]
    u = refs[-1]
    u[:half, :] = xo[:, :depth]
    u[half:, :] = xt[:, :depth]
    if h == 0:
        refs[6][...] = mm(u[...], d2[...])
    pair = two(refs[6][...] if h == 0 else refs[0][...])
    both = mm(u[...], w[0].take(0))
    hh = uv.shape[2]
    at = edge_rows(where, u.shape[0], ev.shape[1])
    for i, (up, pre, hid, edge) in enumerate(((uv, pv, hv, ev), (ug, pg, hg, eg))):
        s = both[:, i * hh : (i + 1) * hh] + mm(pair, up[0])
        pre[0] = s
        hid[0] = (s * sigmoid(s)).astype(bf16)
        edge[0] = hid[0, at, :]


def fill_grid(buf, rows, halo, b, c):
    half = rows.shape[0] // 2
    edge = halo.shape[0]
    buf[pl.ds(pl.multiple_of(edge + b * half, edge), half), :] = rows[:half, :].astype(f32)
    buf[pl.ds(pl.multiple_of(edge + (1 - b) * half, edge), half), :] = rows[half:, :].astype(f32)
    zero = jnp.zeros(halo.shape, f32)
    got = halo.astype(f32)
    buf[:edge, :] = jnp.where(c == 0, zero, got)
    buf[buf.shape[0] - edge :, :] = jnp.where(c == 0, got, zero)


def conv_row(buf, taps, r, edge, flip):
    sums = []
    rows = [buf[pl.ds(pl.multiple_of((r + i) * edge, edge), edge), :] for i in range(3)]
    for j in range(3):
        total = None
        for i in range(3):
            k = (2 - i) * 3 + 2 - j if flip else i * 3 + j
            term = rows[i] * taps[k : k + 1, :]
            total = term if total is None else total + term
        sums.append(total)
    cell = lax.broadcasted_iota(jnp.int32, sums[0].shape, 0)
    left = jnp.where(cell == 0, 0.0, pltpu.roll(sums[0], 1, 0))
    right = jnp.where(cell == edge - 1, 0.0, pltpu.roll(sums[2], edge - 1, 0))
    return left + sums[1] + right


def own_first(r, edge, half, b):
    per = half // edge
    return pl.multiple_of(jnp.where(r // per == b, 0, half) + (r % per) * edge, edge)


def ffn_mid(
    w, where, hv, hg, halo_v, halo_g, taps, cot, gate, d2, u2,
    gated_out, gcv_out, gcg_out, gffn_out, gl_out, lat_out, down_out, edge_out, mine, away, bv, bg, gg, acc,
):
    h = pl.program_id(0)
    b, c = where[0], where[1]
    n = hv.shape[1]
    half = n // 2
    edge = halo_v.shape[1]

    @pl.when(h == 0)
    def first():
        gffn_out[...] = (gate[...] * cot[...].astype(f32)).astype(bf16)
        gl_out[...] = mm(gffn_out[...], u2[...], 1, 1)

    fill_grid(bv, hv[0], halo_v[0], b, c)
    fill_grid(bg, hg[0], halo_g[0], b, c)
    weight = w[0].take(h)
    gg[...] = mm(gffn_out[...], weight) + mm(two(gl_out[...]), d2[0], 1, 1)

    def row(r, carry):
        v = conv_row(bv, taps[0, 0], r, edge, False)
        g = conv_row(bg, taps[0, 1], r, edge, False)
        sig = sigmoid(g)
        act = g * sig
        at = pl.ds(own_first(r, edge, half, b), edge)
        gated_out[0, at, :] = (v * act).astype(bf16)
        grad = gg[at, :]
        gcv_out[0, at, :] = (grad * act).astype(bf16)
        gcg_out[0, at, :] = (grad * v * (sig * (1.0 + g * (1.0 - sig)))).astype(bf16)
        return carry

    lax.fori_loop(0, n // edge, row, 0)
    at = edge_rows(where, n, edge)
    edge_out[0, 0] = gcv_out[0, at, :]
    edge_out[0, 1] = gcg_out[0, at, :]
    gated = gated_out[0]
    down_out[0] = mm(two(gl_out[...]), gated, 0, 0)
    part = mm(gated, weight, 1, 1)
    lat = mm(gated, d2[0])

    @pl.when(h == 0)
    def start():
        acc[...] = part
        lat_out[...] = lat

    @pl.when(h == 1)
    def end():
        total = lat_out[...] + lat
        lat_out[...] = total
        full = acc[...] + part + mm(two(total), u2[...])
        put(mine, everything, full[:half])
        put(away, everything, full[half:])


def ffn_back(
    w, where, gcv, gcg, halo, taps, pv, pg, lat, d2, uv, ug,
    gpv_out, gpg_out, up_out, gl_out, mine, away, bv, bg, acc,
):
    h = pl.program_id(0)
    b, c = where[0], where[1]
    n = gcv.shape[1]
    half = n // 2
    edge = halo.shape[2]
    fill_grid(bv, gcv[0], halo[0, 0], b, c)
    fill_grid(bg, gcg[0], halo[0, 1], b, c)

    def row(r, carry):
        at = pl.ds(own_first(r, edge, half, b), edge)
        for i, (buf, pre, out) in enumerate(((bv, pv, gpv_out), (bg, pg, gpg_out))):
            grad = conv_row(buf, taps[0, i], r, edge, True)
            s = pre[0, at, :]
            sig = sigmoid(s)
            out[0, at, :] = (grad * (sig * (1.0 + s * (1.0 - sig)))).astype(bf16)
        return carry

    lax.fori_loop(0, n // edge, row, 0)
    gpv, gpg = gpv_out[0], gpg_out[0]
    part = mm(jnp.concatenate([gpv, gpg], axis=1), w[0].take(h), 1, 1)
    gl = mm(gpv, uv[0], 1, 1) + mm(gpg, ug[0], 1, 1)
    pair = two(lat[...])
    up_out[0, 0] = mm(pair, gpv, 0, 0)
    up_out[0, 1] = mm(pair, gpg, 0, 0)

    @pl.when(h == 0)
    def start():
        acc[...] = part
        gl_out[...] = gl

    @pl.when(h == 1)
    def end():
        total = gl_out[...] + gl
        gl_out[...] = total
        full = acc[...] + part + mm(two(total), d2[...], 1, 1)
        put(mine, everything, full[:half])
        put(away, everything, full[half:])


def cross_bwd(
    w, go, gt, kv, live, owned, qd2, qu2, cd2, cu2, qo, qt, lo, lt,
    gq_out, gkv_out, qgl_out, cgl_out, mine, away, gm, gqs,
):
    half = go.shape[0]
    width = qo.shape[1]
    w[0].take(0)
    depth = cu2.shape[1]
    weight = w[0].columns(0, width, width)
    scale = HD ** (-0.5)
    hidden_text = jnp.where(live[...] > 0.0, 0.0, masked_score)
    for i, (rows, query, lse) in enumerate(((go, qo, lo), (gt, qt, lt))):
        at = slice(i * half, (i + 1) * half)
        gl = mm(rows[:, :depth], cu2[...], 1, 1)
        cgl_out[at, :] = gl
        grad = mm(rows[:, :depth], weight) + mm(two(gl), cd2[...], 1, 1)
        gm[...] = (grad * owned[...]).astype(bf16)
        for first, size in lane_groups(width):
            cols = slice(first, first + size)
            q_all, g_all = query[:, cols], gm[:, cols]
            grad_q, grad_k, grad_v = 0.0, 0.0, 0.0
            for j in range(size // HD):
                key, val = only_head(kv[0, :, cols], j), only_head(kv[1, :, cols], j)
                h = first // HD + j
                scores = mm(key, q_all, 1, 1) * (scale * LOG2E) + hidden_text
                probs = jnp.exp2(scores - lse[h : h + 1, :] * LOG2E)
                grad_p = mm(val, g_all, 1, 1)
                grad_v = grad_v + mm(probs.astype(bf16), only_head(g_all, j))
                inner = jnp.sum(probs * grad_p, axis=0, keepdims=True)
                grad_s = (probs * (grad_p - inner)).astype(bf16)
                grad_q = grad_q + mm(grad_s, key, 0, 0)
                grad_k = grad_k + mm(grad_s, only_head(q_all, j))
            gqs[at, cols] = grad_q
            for side, new in ((0, grad_k * scale), (1, grad_v)):
                gkv_out[side, :, cols] = new if i == 0 else gkv_out[side, :, cols] + new
    gq = (gqs[...] * scale).astype(bf16)
    gq_out[...] = gq
    gl = mm(gq, qu2[...], 1, 1)
    qgl_out[...] = gl
    pair = two(gl)
    total = mm(gq, w[0].columns(0, 0, width), 1, 1) + mm(pair, qd2[...], 1, 1)
    put(mine, everything, total[:half])
    put(away, everything, total[half:])


def linear_bwd(
    w, go, gt, q, st1, st2, ratio, den, owned, d2, u2, gq_out, gl_out, st_out, gh,
):
    half = go.shape[0]
    width = q.shape[1]
    depth = u2.shape[1]
    w[0].take(0)
    weight = w[0].columns(0, width, width)
    for i, rows in enumerate((go, gt)):
        at = pl.ds(i * half, half)
        gl = mm(rows[:, :depth], u2[...], 1, 1)
        gl_out[at, :] = gl
        gh[at, :] = (mm(rows[:, :depth], weight) + mm(two(gl), d2[...], 1, 1)) * owned[...]
    st = st1[...] + st2[...]
    grad = gh[...]
    inverse = 1.0 / den[...]
    numer = grad * inverse
    grad_den = -head_total(grad * ratio[...]) * inverse
    raw = q[...]
    queries = jnp.maximum(raw, 0.0)
    grad_q = head_product(numer, st[:HD], 0) + grad_den * st[HD : HD + 1]
    gq_out[...] = jnp.where(raw > 0.0, grad_q, 0.0).astype(bf16)
    st_out[:HD, :] = head_outer(numer, queries)
    total = jnp.sum(grad_den * queries, axis=0, keepdims=True)
    st_out[HD:, :] = jnp.broadcast_to(total, (8, width))


def linear_end(
    w, gq, k, v, st1, st2, d2, u2, gk_out, gv_out, gl_out, mine, away,
):
    width = k.shape[1]
    half = mine.shape[0]
    st = st1[...] + st2[...]
    raw = k[...]
    grad_k = head_product(v[...], st[:HD], 0) + st[HD : HD + 1]
    gk_out[...] = jnp.where(raw > 0.0, grad_k, 0.0).astype(bf16)
    gv_out[...] = head_product(jnp.maximum(raw, 0.0), st[:HD], 1).astype(bf16)
    grads = (gq, gk_out, gv_out)
    gl = sum(mm(g[...], u2[i], 1, 1) for i, g in enumerate(grads))
    gl_out[...] = gl
    pair = two(gl)
    w[0].take(0)
    w[0].take(1)
    both = jnp.concatenate([gq[...], gk_out[...]], axis=1)
    total = mm(both, w[0].columns(0, 0, 2 * width), 1, 1) + mm(gv_out[...], w[0].columns(1, 0, width), 1, 1)
    total = total + mm(pair, d2[...], 1, 1)
    put(mine, everything, total[:half])
    put(away, everything, total[half:])


def in_steps(rows, body, step=64):
    def one(i, carry):
        body(pl.ds(pl.multiple_of(i * step, step), step))
        return carry

    lax.fori_loop(0, rows // step, one, 0)


def slope_of_norm(values, grad):
    normed, inverse = row_stats(values)
    return inverse * (
        grad
        - jnp.mean(grad, axis=-1, keepdims=True)
        - normed * jnp.mean(grad * normed, axis=-1, keepdims=True)
    )


def total_of(low, got, at, width):
    return low[at, :width].astype(f32) + got[at, :width].astype(f32)


def end_attn(low, got, x, mods, after_out, own_out):
    def body(at):
        after = x[at, :].astype(f32) + mods[2:3, :] * total_of(low, got, at, x.shape[1])
        after_out[at, :] = after
        put(own_out, at, after)

    in_steps(x.shape[0], body)


def end_cross(low, got, before, mods, after_out, own_out):
    def body(at):
        after = before[at, :] + total_of(low, got, at, before.shape[1])
        after_out[at, :] = after
        normed, unused = row_stats(after)
        put(own_out, at, normed * (1.0 + mods[4:5, :]) + mods[3:4, :])

    in_steps(before.shape[0], body)


def end_output(low, got, before, mods, out):
    def body(at):
        put(out, at, before[at, :] + mods[5:6, :] * total_of(low, got, at, before.shape[1]))

    in_steps(before.shape[0], body)


def end_ffn_back(low, got, after, cot, mods, grad_out, own_out):
    def body(at):
        grad = total_of(low, got, at, after.shape[1]) * (1.0 + mods[4:5, :])
        grad = cot[at, :].astype(f32) + slope_of_norm(after[at, :], grad)
        grad_out[at, :] = grad
        put(own_out, at, grad)

    in_steps(after.shape[0], body)


def end_cross_back(low, got, before, mods, grad_out, own_out):
    def body(at):
        grad = before[at, :] + total_of(low, got, at, before.shape[1])
        grad_out[at, :] = grad
        put(own_out, at, mods[2:3, :] * grad)

    in_steps(before.shape[0], body)


def end_attn_back(low, got, before, x, mods, out):
    def body(at):
        grad = total_of(low, got, at, before.shape[1]) * (1.0 + mods[1:2, :])
        put(out, at, before[at, :] + slope_of_norm(x[at, :].astype(f32), grad))

    in_steps(before.shape[0], body)


def place_rows(where, own, other, out):
    width = out.shape[2]
    out[where[0]] = own[:, :width]
    out[1 - where[0]] = other[:, :width]


def fold(both):
    half = both.shape[0] // 2
    return both[:half] + both[half:]


def turned(v, b):
    half = v.shape[1] // 2
    return jnp.where(b == 0, v, jnp.concatenate([v[:, half:], v[:, :half]], axis=1))


def thin_sum(latent, *rows):
    high = latent.astype(bf16).astype(f32)
    both = jnp.concatenate([high, latent - high], axis=0).astype(bf16)
    total, at = None, 0
    for values in rows:
        size = values.shape[0]
        term = mm(both[:, at : at + size], values[...])
        total = term if total is None else total + term
        at += size
    return fold(total)


def outer_sum(latent, *rows):
    total, at = None, 0
    pair = two(latent)
    for values in rows:
        size = values.shape[0]
        term = mm(pair[at : at + size], values[...], 0, 0)
        total = term if total is None else total + term
        at += size
    return fold(total)


def set_segments(out, segments, width):
    for i, v in enumerate(segments):
        put(out.at[:, i * width : (i + 1) * width], everything, v)


def set_ranks(out, first, pad, values):
    rows = out.shape[1]
    for t in range(out.shape[0]):
        put(out.at[t, :, first : first + pad], everything, values[t * rows : (t + 1) * rows])


def pack_first(where, point, up, l0, l1, l2, l3, sums):
    pieces = [point[0], point[1]] + [up[h, p] for p in range(2) for h in range(2)]
    n = l0.shape[0]
    rank = sums.shape[0] * sums.shape[1]
    first = sums.shape[2] - 4 * n
    pad = first // 6
    for i, v in enumerate(pieces):
        set_ranks(sums, i * pad, pad, fold(v))
    for i, v in enumerate((l0, l1, l2, l3)):
        set_ranks(sums, first + i * n, n, turned(v[...].T[:rank], where[0]))


def to_blocks(home, first, table):
    blocks = home.shape[0]
    size = table.shape[1] // blocks
    rows = table.shape[0]
    for i in range(blocks):
        home[i, first : first + rows, :size] = table[:, i * size : (i + 1) * size]


def set_mark(where, home, first):
    home[:, first:, :] = jnp.zeros((home.shape[0], home.shape[1] - first, home.shape[2]), f32) + where[2].astype(f32)


def second_sums(
    where, sums, gco, gct, fo, ft, gffn, mixo, mixt, cgl, qlat, gq, qgl, gkv, ggot, klat, ku2,
    home_out, projs, out, home,
):
    n, depth = gffn.shape
    b = where[0]
    first = sums.shape[2] - 4 * n
    parts = []
    for i in range(4):
        at = slice(first + i * n, first + (i + 1) * n)
        parts.append(turned(sums[0, :, at] + sums[1, :, at] + sums[2, :, at] + sums[3, :, at], b))
    projs[...] = parts[0]
    rows = parts[0].shape[0]
    home[...] = jnp.zeros(home.shape, f32)
    to_blocks(home, 0, thin_sum(parts[1], gco, gct)[:, :depth])
    to_blocks(home, rows, thin_sum(parts[2], gffn))
    to_blocks(home, 2 * rows, thin_sum(parts[3], fo, ft)[:, :depth])
    pad, hh = first // 6, home.shape[2] * home.shape[0] // 8
    size = home.shape[2]
    for j in range(3):
        for i in range(home.shape[0]):
            t, h, at = i * size // (2 * hh), i * size % (2 * hh) // hh, i * size % hh
            at += (2 * j + h) * pad
            home[i, (3 + j) * rows : (4 + j) * rows, :] = sums[t, :, at : at + size]
    set_mark(where, home, 6 * rows)
    home_out[...] = home[...].astype(home_out.dtype)
    here = ggot.shape[1]
    gk = (gkv[0, :here, :] + ggot[0]).astype(bf16)
    gv = (gkv[1, :here, :] + ggot[1]).astype(bf16)
    segments = [outer_sum(cgl[...], mixo, mixt), outer_sum(qlat[...], gq)]
    segments += [outer_sum(klat[...], gk), outer_sum(klat[...], gv)]
    pad = -(-gq.shape[1] // LANES) * LANES
    set_segments(out, segments, pad)
    rank = out.shape[0]
    out[:, 4 * pad : 4 * pad + n] = turned(qgl[...].T[:rank], b)
    kvgl = mm(gk, ku2[0], 1, 1) + mm(gv, ku2[1], 1, 1)
    put(out.at[:, 4 * pad + n :], everything, kvgl.T[:rank])


def third_sums(where, before, pgl, mixed, qlat, gq, gk, gv, qgl, out):
    rank, first = before.shape
    set_ranks(out, 0, first, before[...])
    segments = [outer_sum(pgl[...], mixed)] + [outer_sum(qlat[...], g) for g in (gq, gk, gv)]
    pad = -(-gq.shape[1] // LANES) * LANES
    for i, v in enumerate(segments):
        set_ranks(out, first + i * pad, pad, v)
    set_ranks(out, first + 4 * pad, qgl.shape[0], turned(qgl[...].T[:rank], where[0]))


def last_sums(ranges, where, sums, projs, gao, gat, xo, xt, cap, a, home_out, home):
    n, depth = a.shape
    b = where[0]
    text = -(-cap.shape[0] // LANES) * LANES
    pad = (sums.shape[2] - 2 * n - text) // 8
    second = 4 * pad + n + text
    rows = projs.shape[0]

    def summed(first, size):
        return sum(sums[t, :, first : first + size] for t in range(sums.shape[0]))

    def heads(first):
        parts = [sums[t, :, first + s * HD : first + (s + m) * HD] for t, (s, m) in enumerate(ranges)]
        return jnp.concatenate(parts, axis=1)

    tables = [
        thin_sum(turned(summed(4 * pad, n), b), xo, xt)[:, :depth],
        thin_sum(summed(4 * pad + n, cap.shape[0]), cap)[:, :depth],
        thin_sum(projs[...], gao, gat)[:, :depth],
    ]
    tables += [heads(j * pad) for j in range(4)] + [heads(second + j * pad) for j in range(4)]
    tables.append(thin_sum(turned(summed(second + 4 * pad, n), b), a))
    for j, table in enumerate(tables):
        to_blocks(home, j * rows, table)
    set_mark(where, home, len(tables) * rows)
    home_out[...] = home[...].astype(home_out.dtype)


def adapter_tables(got, out):
    last = got.shape[1] - 1
    for i in range(out.shape[0]):
        total = None
        for s in range(got.shape[0]):
            values = got[s].astype(f32)
            term = jnp.where(values[last:, :1] == float(i), values, 0.0)
            total = term if total is None else total + term
        out[i] = total


def ring_order(n):
    return list(range(0, n, 2)) + list(range(n - 1 - n % 2, 0, -2))


def ring_pairs(n):
    order = ring_order(n)
    return [(order[i], order[(i + 1) % n]) for i in range(n)]


def ring_source(n, step):
    z = lax.axis_index(W)
    place = jnp.where(z % 2 == 0, z // 2, n - 1 - z // 2)
    from_place = (place - step + n) % n
    return jnp.where(2 * from_place < n, 2 * from_place, 2 * (n - 1 - from_place) + 1)


def swap_pairs(n, distance):
    return [(i, i ^ distance) for i in range(n)]


def across(values, axis, distance=1):
    return lax.ppermute(values, axis, swap_pairs(lax.axis_size(axis), distance))


class Stream:
    def __init__(self, order):
        self.n = lax.axis_size(W)
        self.order = list(order)
        self.own, self.got, self.crossed = {}, {}, {}
        self.flying, self.crossing = [], []

    def launch(self):
        while self.order and (not self.flying or len(self.flying) < 2 and self.order[0][1] == 1):
            name, step = self.order[0]
            if step == 1 and name in self.own:
                moving = self.own[name][0]
            elif (name, step - 1) in self.got:
                moving = self.got[name, step - 1]
            else:
                break
            self.order.pop(0)
            self.flying.append((name, step, lax.ppermute(moving, W, ring_pairs(self.n))))

    def fence(self, values, take=1, cross=None):
        done, self.flying = self.flying[:take], self.flying[take:]
        count = len(self.crossing) if cross is None else cross
        crossed, self.crossing = self.crossing[:count], self.crossing[count:]
        leaves, tree = jax.tree.flatten((values, [d[2] for d in done], [d[2] for d in crossed]))
        values, arrived, over = jax.tree.unflatten(tree, lax.optimization_barrier(leaves))
        for d, v in zip(crossed, over):
            self.crossed[d[0], d[1]] = v
        for d, v in zip(done, arrived):
            self.got[d[0], d[1]] = v
            self.crossing.append((d[0], d[1], across(v, C)))
        self.launch()
        return values

    def fences(self, count, values):
        for i in range(count * (self.n - 1) // 3):
            values = self.fence(values)
        return values

    def ready(self, names, values):
        while not all((name, self.n - 1) in self.crossed for name in names):
            values = self.fence(values)
        return values

    def pieces(self, name):
        steps = range(1, self.n)
        mine = [self.own[name][0]] + [self.got[name, s] for s in steps]
        other = [self.own[name][1]] + [self.crossed[name, s] for s in steps]
        rows = mine[0].shape[0]
        if rows % 16 == 0:
            return mine + other
        c = lax.axis_index(C)
        buf = jnp.zeros((2, self.n * rows, mine[0].shape[1]), bf16)
        for s in range(self.n):
            at = ring_source(self.n, s) * rows
            buf = lax.dynamic_update_slice(buf, mine[s][None], (c, at, 0))
            buf = lax.dynamic_update_slice(buf, other[s][None], (1 - c, at, 0))
        return [buf]


class Weight:
    def __init__(self, meta, pieces, buf, sems, halves):
        self.meta, self.pieces, self.buf, self.sems, self.halves = meta, pieces, buf, sems, halves

    def copies(self, j, pieces):
        rows = pieces[0].shape[0]
        return [
            pltpu.make_async_copy(
                piece,
                self.buf.at[j, pl.ds(pl.multiple_of(self.meta[1 + k] * rows, rows), rows), :],
                self.sems.at[j, k],
            )
            for k, piece in enumerate(pieces)
        ]

    def start(self):
        count = len(self.pieces) // 2
        for j, half in enumerate(self.halves):
            if not count:
                pltpu.make_async_copy(self.pieces[0].at[half], self.buf.at[j], self.sems.at[j, 0]).start()
                continue

            @pl.when(self.meta[0] == half)
            def mine():
                for copy in self.copies(j, self.pieces[:count]):
                    copy.start()

            @pl.when(self.meta[0] != half)
            def other():
                for copy in self.copies(j, self.pieces[count:]):
                    copy.start()

    def take(self, j):
        count = len(self.pieces) // 2
        if not count:
            pltpu.make_async_copy(self.pieces[0].at[0], self.buf.at[j], self.sems.at[j, 0]).wait()
        else:
            for copy in self.copies(j, self.pieces[:count]):
                copy.wait()
        return self.buf[j]

    def columns(self, j, first, size):
        return self.buf[j, :, first : first + size]


def per_step(a):
    zeros = (0,) * (a.ndim - 1)
    return pl.BlockSpec((1,) + tuple(a.shape[1:]), lambda h: (h,) + zeros)


def half_block(i):
    def spec(a):
        zeros = (0,) * (len(a.shape) - 1)
        return pl.BlockSpec((1,) + tuple(a.shape[1:]), lambda *g: (i,) + zeros)

    return spec


def row_block(a):
    return pl.BlockSpec((a.shape[0] // 2, a.shape[1]), lambda i: (i, 0))


def both_blocks(a):
    return pl.BlockSpec((2, a.shape[1] // 2, a.shape[2]), lambda i: (0, i, 0))


def all_of(a):
    zeros = (0,) * len(a.shape)
    return pl.BlockSpec(tuple(a.shape), lambda *g: zeros)


def scalars(a):
    return pl.BlockSpec(memory_space=pltpu.SMEM)


def anywhere(a):
    return pl.BlockSpec(memory_space=pl.ANY)


def run(kernel, ins, outs, scratch=(), steps=1, weights=(), meta=None, same=()):
    args, specs = [], []
    if weights:
        args.append(meta)
        specs.append(scalars(meta))
    counts, extra = [], []
    for pieces, halves in weights:
        counts.append((len(pieces), halves))
        args += pieces
        specs += [anywhere(p) for p in pieces]
        rows = pieces[0].shape[0] * len(pieces) // 2 if len(pieces) > 1 else pieces[0].shape[1]
        extra.append(pltpu.VMEM((len(halves), rows, pieces[0].shape[-1]), bf16))
        extra.append(pltpu.SemaphoreType.DMA((len(halves), max(len(pieces) // 2, 1))))
    first = len(args)
    for item in ins:
        a, spec = item if isinstance(item, tuple) else (item, all_of)
        args.append(a)
        specs.append(spec(a))
    shapes, out_specs = [], []
    for item in outs:
        dims, dtype, spec = item if len(item) == 3 else item + (all_of,)
        shapes.append(shape(dims, dtype))
        out_specs.append(spec(shapes[-1]))

    def body(*refs):
        if not weights:
            return kernel(*refs)
        at, loaders = 1, []
        tail = refs[len(refs) - len(extra) :]
        for i, (count, halves) in enumerate(counts):
            loaders.append(Weight(refs[0], refs[at : at + count], tail[2 * i], tail[2 * i + 1], halves))
            at += count

        @pl.when(pl.program_id(0) == 0)
        def begin():
            for loader in loaders:
                loader.start()

        kernel(loaders, *refs[first : len(refs) - len(extra)])

    return pl.pallas_call(
        body,
        grid=(steps,),
        in_specs=specs,
        out_specs=out_specs,
        out_shape=shapes,
        input_output_aliases={first + i: j for i, j in same},
        scratch_shapes=list(scratch) + extra,
        compiler_params=big,
    )(*args)


def twice(table, axis):
    return jnp.concatenate([table, table], axis=axis)


def slot_layout(groups, rank, heads):
    per, left = heads // groups, heads % groups
    slots = per + (1 if left else 0)
    own_start = rank * per + jnp.minimum(rank, left)
    own_count = per + jnp.where(rank < left, 1, 0)
    first = jnp.minimum(own_start, heads - slots)
    slot = first + jnp.arange(slots, dtype=jnp.int32)
    owned = ((slot >= own_start) & (slot < own_start + own_count)).astype(f32)
    return slots, first, owned


def slot_ranges(groups, heads):
    per, left = heads // groups, heads % groups
    slots = per + (1 if left else 0)
    out = []
    for rank in range(groups):
        own_start = rank * per + min(rank, left)
        count = per + (1 if rank < left else 0)
        out.append((own_start - min(own_start, heads - slots), count))
    return out


def shards(
    tokens, caption, caption_lengths, adapter_index, modulation, cotangent,
    qkv_weight, proj_weight, cross_q_weight, cross_kv_weight, cross_out_weight,
    inverted_weight, depth_weight, point_weight,
    qkv_down, qkv_up, proj_down, proj_up, query_down, query_up, kv_down, kv_up,
    cross_down, cross_up, inverted_down, inverted_up, point_down, point_up,
):
    grid_rows, grid_cols, D = tokens.shape[1:]
    n = grid_rows * grid_cols
    half = n // 2
    heads = D // HD
    groups = lax.axis_size(T)
    rank = lax.axis_index(T)
    c = lax.axis_index(C)
    b = rank % 2
    adapters, R = qkv_up.shape[:2]
    slots, slot_first, owned = slot_layout(groups, rank, heads)
    width = slots * HD
    col = slot_first * HD
    owned = jnp.repeat(owned, HD)[None]
    hid = inverted_weight.shape[2]
    hh = hid // 2
    hid_first = rank * hid
    index = adapter_index[0]
    where = jnp.stack([b, c, index]).astype(jnp.int32)

    def cut(table, start, size, axis):
        return lax.dynamic_slice_in_dim(table, start, size, axis)

    def pick(table):
        return lax.dynamic_index_in_dim(table, index, 0, keepdims=False)

    def own_rows(rows):
        own = cut(rows, b * half, half, 0)
        return own, jnp.concatenate([own, cut(rows, (1 - b) * half, half, 0)])

    def pair_of(first, second):
        return [jnp.where(c == 0, first, second), jnp.where(c == 0, second, first)]

    def taken(table, middle, start, size):
        return lax.dynamic_slice(table, (0, middle, start), (table.shape[0], 1, size))[:, 0]

    def beside(*values):
        return jnp.concatenate(values, axis=1)

    def both(table, start, size=width):
        return beside(taken(table, 0, start, size), taken(table, 1, start, size))

    size = lax.axis_size(W)
    order = [(name, step) for name in ("ab", "cd", "vg", "p") for step in range(1, size)]
    stream = Stream(order)
    fences = stream.fences

    def front_side(c):
        key, out = taken(qkv_weight, 1, col, width), cut(proj_weight, col, width, 0).T
        return beside(taken(qkv_weight, 2 * c, col, width), jnp.where(c == 0, key, out))

    stream.own["ab"] = [front_side(c), None]
    c_late, caption, stream.own["ab"][0] = lax.optimization_barrier((c, caption, stream.own["ab"][0]))
    stream.own["ab"][1] = front_side(1 - c_late)
    stream.launch()
    mods = modulation[0]
    low_tokens = tokens.reshape(n, D)
    x_low, x_rows = own_rows(low_tokens)
    qd2, qu2 = twice(pick(qkv_down), 1), twice(cut(pick(qkv_up), col, width, 2), 0).transpose(1, 0, 2)
    pd2, pu2 = twice(cut(pick(proj_down), col, width, 0), 1), twice(pick(proj_up), 0)
    text_here = caption.shape[1]
    text_rows = -(-text_here // 16) * 16
    padded = -(-D // LANES) * LANES
    cap = jnp.pad(caption[0], ((0, text_rows - text_here), (0, padded - D)))
    cap_other = across(cap, C)
    tables = [query_down, query_up, kv_down, kv_up, cross_down, cross_up]
    tables_f = [inverted_down, inverted_up, point_down, point_up, depth_weight]
    raw = [cross_kv_weight, cross_q_weight, cross_out_weight]
    raw_f = [inverted_weight, point_weight]
    raw, raw_f, tables, tables_f, cap, cap_other, cotangent = fences(
        1, (raw, raw_f, tables, tables_f, cap, cap_other, cotangent)
    )
    pair_cd = pair_of(both(raw[0], col), beside(cut(raw[1], col, width, 1), cut(raw[2], col, width, 0).T))
    query_down, query_up, kv_down, kv_up, cross_down, cross_up = tables
    cd2 = twice(cut(pick(cross_down), col, width, 0), 1)
    cu2 = twice(pick(cross_up), 0)
    xd2, xu2 = twice(pick(query_down), 1), twice(cut(pick(query_up), col, width, 1), 0)
    kd2, ku2 = twice(pick(kv_down), 1), twice(cut(pick(kv_up), col, width, 2), 0).transpose(1, 0, 2)
    front = [x_low, x_rows, qd2, qu2, pd2, pu2, stream.own["ab"][1]]
    pair_cd, raw_f, tables_f, cotangent, front = fences(1, (pair_cd, raw_f, tables_f, cotangent, front))
    stream.own["cd"] = pair_cd
    x_low, x_rows, qd2, qu2, pd2, pu2, stream.own["ab"][1] = front
    pair_vg = [both(raw_f[0], i * hh, hh) for i in (c, 1 - c)]
    pair_p = [cut(raw_f[1], i * hh, hh, 0).T for i in (c, 1 - c)]
    pair_vg, pair_p, tables_f, cotangent = fences(1, (pair_vg, pair_p, tables_f, cotangent))
    stream.own.update(vg=pair_vg, p=pair_p)
    inverted_down, inverted_up, point_down, point_up, depth_weight = tables_f
    fd2, fu2 = twice(pick(inverted_down), 1), twice(cut(pick(inverted_up), hid_first, hid, 2), 0)
    fu2 = fu2.reshape(2 * R, 2, 2, hh).transpose(1, 2, 0, 3)
    od2 = twice(cut(pick(point_down), hid_first, hid, 0), 1).reshape(2, hh, 2 * R)
    ou2 = twice(pick(point_up), 0)
    taps = depth_weight.astype(f32).reshape(9, 2, 2, hh).transpose(2, 1, 0, 3)
    cot_low, cot = own_rows(cotangent.reshape(n, D))
    places = jnp.arange(text_rows)
    live = jnp.concatenate([c * text_here + places, (1 - c) * text_here + places])
    live = (live < caption_lengths[0]) & (jnp.concatenate([places, places]) < text_here)
    live = live.astype(f32)[None]
    tables = [cd2, cu2, xd2, xu2, kd2, ku2, fd2, fu2[0], fu2[1], od2, ou2, taps, cot_low, cot, live]
    x_rows, tables = stream.ready(["ab"], (x_rows, tables))
    cd2, cu2, xd2, xu2, kd2, ku2, fd2, fuv, fug, od2, ou2, taps, cot_low, cot, live = tables

    w_ab = stream.pieces("ab")
    meta = jnp.stack([c] + [ring_source(size, s) for s in range(size)]).astype(jnp.int32)
    rows_bf = ((n, D), bf16)
    thin = ((n, 2 * R), f32)
    wide = ((n, width), f32)
    wide_bf = ((n, width), bf16)
    pair = [((half, padded), bf16)] * 2
    ended = [((half, D), f32, row_block), ((half, padded), bf16, row_block)]

    def finish_rows(kernel, arrays, outs):
        return run(kernel, [(v, row_block) for v in arrays] + [mods], outs, steps=2)

    state_of = ((HD + 8, width), f32)
    attn_in, q_raw, k_raw, qkv_lat = run(
        attn_front, [x_rows, mods, qd2, qu2], [rows_bf, wide, wide, thin], weights=[(w_ab, (0,))], meta=meta,
    )
    v_raw, st_own = run(
        attn_state, [attn_in, k_raw, qkv_lat, qu2], [wide, state_of], weights=[(w_ab, (1,))], meta=meta,
    )
    st_own, st_other = fences(1, (st_own, across(st_own, C)))
    ratio, denom, mixed, proj_lat, mine, away = run(
        attn_back, [q_raw, st_own, st_other, owned, pd2, pu2], [wide, wide, wide_bf, thin] + pair,
        weights=[(w_ab, (1,))], meta=meta,
    )

    def exchanged(mine, away, pace=lambda low: low):
        low, distance = (mine.astype(f32) + across(away, T).astype(f32)).astype(bf16), 2
        while True:
            low = pace(low)
            got = across(low, T, distance)
            distance *= 2
            if distance >= groups:
                return low, got
            low = (low.astype(f32) + got.astype(f32)).astype(bf16)

    def while_streaming(mine, away):
        return exchanged(mine, away)

    mine, away = fences(1, (mine, away))
    low, got = fences(1, while_streaming(mine, away))
    after_attn, cross_own = finish_rows(end_attn, [low, got, x_low], ended)
    cross_other = across(cross_own, T)

    cap, cross_own, cross_other, after_attn = stream.ready(["cd"], (cap, cross_own, cross_other, after_attn))
    w_cd = stream.pieces("cd")
    kv_all, kv_lat = run(
        caption_rows, [cap, cap_other, kd2, ku2], [((2, 2 * text_rows, width), bf16), ((text_rows, 2 * R), f32)],
        weights=[(w_cd, (0,))], meta=meta,
    )
    kv_all, cross_own, cross_other = fences(1, (kv_all, cross_own, cross_other))
    half_bf, half_thin = ((half, width), bf16), ((half, 2 * R), f32)

    def cross_part(rows, kv):
        return run(
            cross_fwd,
            [rows, kv, live, owned, xd2, xu2, cd2, cu2],
            [half_bf, half_bf, half_thin, half_thin, ((LANES, half), f32), ((half, padded), bf16)],
            [pltpu.VMEM((half, LANES), f32)],
            weights=[(w_cd, (1,))], meta=meta,
        )

    *cross_t, away = cross_part(cross_other, kv_all)
    away, cross_tied, kv_tied = lax.optimization_barrier((away, cross_own, kv_all))
    *cross_o, mine = cross_part(cross_tied, kv_tied)
    mine, away = fences(1, (mine, away))
    query, mix, query_lat, cross_lat, lse = zip(cross_o, cross_t)
    low, got = while_streaming(mine, away)
    low, got = stream.fence((stream.fence(low, 1, 0), got), 0, 1)
    after_cross, ffn_own = finish_rows(end_cross, [low, got, after_attn], ended)
    ffn_own, after_cross = stream.fence((ffn_own, after_cross), 1, 1)
    ffn_other = across(ffn_own, T)

    query_lat, cross_lat = jnp.concatenate(query_lat), jnp.concatenate(cross_lat)

    ffn_own, ffn_other, after_cross = stream.ready(["vg"], (ffn_own, ffn_other, after_cross))
    w_vg = stream.pieces("vg")
    hid_bf = ((2, n, hh), bf16, per_step)

    def ffn_part(h, more, same):
        outs = [((2, n, hh), f32)] * 2 + [((2, n, hh), bf16)] * 2 + [((2, grid_cols, hh), bf16)] * 2
        return run(
            functools.partial(ffn_front, h),
            [(where, scalars), ffn_own, ffn_other, fd2, (fuv, half_block(h)), (fug, half_block(h))] + more,
            [out + (half_block(h),) for out in outs] + [thin][h:],
            [pltpu.VMEM((n, D), bf16)],
            weights=[(w_vg, (h,))], meta=meta, same=same,
        )

    *started, inv_lat = ffn_part(0, [], ())
    ffn_own, started, inv_lat = stream.fence((ffn_own, started, inv_lat), 1, 1)
    pre_v, pre_g, hid_v, hid_g, edge_v, edge_g = ffn_part(
        1, [inv_lat] + [(v, anywhere) for v in started], [(7 + i, i) for i in range(6)]
    )
    halo_v, halo_g = across(edge_v, C), across(edge_g, C)
    hid_v, halo_v, halo_g = stream.ready(["p"], (hid_v, halo_v, halo_g))
    w_p = stream.pieces("p")
    grid_buf = pltpu.VMEM((n + 2 * grid_cols, hh), f32)
    row_acc = pltpu.VMEM((n, D), f32)
    gated, gcv, gcg, grad_ffn, point_gl, point_lat, point_down_g, edge, mine, away = run(
        ffn_mid,
        [
            (where, scalars), (hid_v, per_step), (hid_g, per_step), (halo_v, per_step), (halo_g, per_step), (taps, per_step),
            cot, mods[5:6], (od2, per_step), ou2,
        ],
        [hid_bf, hid_bf, hid_bf, rows_bf, thin, thin, ((2, 2 * R, hh), f32, per_step)]
        + [((2, 2, grid_cols, hh), bf16, per_step)] + pair,
        [grid_buf, grid_buf, pltpu.VMEM((n, hh), f32), row_acc],
        2,
        weights=[(w_p, (0, 1))], meta=meta,
    )
    halo = across(edge, C)
    tied = []

    def after_halo(low):
        low, *tied[:] = lax.optimization_barrier((low, halo, gcv, gcg))
        return low

    out_low, out_got = exchanged(mine, away, after_halo)
    halo, gcv, gcg = tied

    gpv, gpg, inv_up_g, inv_gl, mine, away = run(
        ffn_back,
        [
            (where, scalars), (gcv, per_step), (gcg, per_step), (halo, per_step), (taps, per_step),
            (pre_v, per_step), (pre_g, per_step), inv_lat, fd2,
            (fuv, per_step), (fug, per_step),
        ],
        [hid_bf, hid_bf, ((2, 2, 2 * R, hh), f32, per_step), thin] + pair,
        [grid_buf, grid_buf, row_acc],
        2,
        weights=[(w_vg, (0, 1))], meta=meta,
    )
    part_r = R // groups
    blocks = size * lax.axis_size(C)
    ranges = slot_ranges(groups, heads)

    def swapped(sent):
        return lax.all_to_all(sent, T, 0, 0, tiled=True)

    def up_to_tiles(size):
        return -(-size // LANES) * LANES

    def table_rows(table, i, size):
        return table[:, i * part_r : (i + 1) * part_r, : size // blocks]

    def down_rows(table, i, size):
        return table_rows(table, i, size).transpose(0, 2, 1)

    def together(*values):
        return lax.optimization_barrier(values)

    def during(mine, away, inputs, work):
        held = []

        def pace(low):
            low, tied = together(low, inputs)
            held[:] = [tied]
            return low

        low, got = exchanged(mine, away, pace)
        return together(low, got, work(*held[0]))

    def first_work(out_low, out_got, after_cross, inv_up_g, point_down_g, lats):
        (output,) = finish_rows(end_output, [out_low, out_got, after_cross], [((half, padded), f32, row_block)])
        (sums,) = run(
            pack_first, [(where, scalars), point_down_g, inv_up_g, *lats], [((groups, part_r, 6 * up_to_tiles(hh) + 4 * n), f32)],
        )
        return output, sums

    mine, away, out_low, out_got = together(mine, away, out_low, out_got)
    low, got, (output, sums_f) = during(
        mine, away,
        (out_low, out_got, after_cross, inv_up_g, point_down_g, (proj_lat, cross_lat, point_lat, inv_gl)),
        first_work,
    )
    grad_cross, gc_own = finish_rows(end_ffn_back, [low, got, after_cross, cot_low], ended)
    gc_other = across(gc_own, T)

    gc_own, gc_other, output, sums_f = together(gc_own, gc_other, output, sums_f)
    output_other = across(output, T)
    sums_f = swapped(sums_f)
    grad_query, gkv, query_gl, cross_gl, mine, away = run(
        cross_bwd,
        [
            gc_own, gc_other, kv_all, live.T, owned,
            xd2, xu2, cd2, cu2, *query, *lse,
        ],
        [wide_bf, ((2, 2 * text_rows, width), f32), thin, thin] + pair,
        [pltpu.VMEM((half, width), bf16), pltpu.VMEM((n, width), f32)],
        weights=[(w_cd, (1,))], meta=meta,
    )
    mine, away, output_other, sums_f, gkv = together(mine, away, output_other, sums_f, gkv)
    gkv_got = across(gkv[:, text_rows:], C)

    def in_order(own, other):
        (rows,) = run(
            place_rows, [(where, scalars), (own, row_block), (other, row_block)],
            [((2, half, D), f32, both_blocks)], steps=2,
        )
        return rows.reshape(tokens.shape)

    seg = up_to_tiles(width)

    seg = up_to_tiles(width)
    home_dims = (blocks, 8 * part_r, 4 * 2 * hh // blocks)
    last_dims = (blocks, 16 * part_r, D // blocks)

    def second_work(output, output_other, sums, cross_gl, grad_query, query_gl):
        return [in_order(output, output_other)] + list(run(
            second_sums,
            [
                (where, scalars), sums, gc_own, gc_other, ffn_own, ffn_other, grad_ffn, *mix, cross_gl,
                query_lat, grad_query, query_gl, gkv, gkv_got, kv_lat, ku2,
            ],
            [(home_dims, bf16), ((part_r, n), f32), ((R, 4 * seg + n + up_to_tiles(text_rows)), f32)],
            [pltpu.VMEM(home_dims, f32)],
        ))

    low, got, (output, home, proj_s, sums_c) = during(
        mine, away, (output, output_other, sums_f, cross_gl, grad_query, query_gl), second_work
    )
    grad_after, ga_own = finish_rows(end_cross_back, [low, got, grad_cross], ended)
    ga_other = across(ga_own, T)

    grad_q, proj_gl, sg_own = run(
        linear_bwd,
        [ga_own, ga_other, q_raw, st_own, st_other, ratio, denom, owned, pd2, pu2],
        [wide_bf, thin, state_of],
        [pltpu.VMEM((n, width), f32)],
        weights=[(w_ab, (1,))], meta=meta,
    )
    sg_other = across(sg_own, C)
    grad_k, grad_v, qkv_gl, mine, away = run(
        linear_end,
        [grad_q, k_raw, v_raw, sg_own, sg_other, qd2, qu2],
        [wide_bf, wide_bf, thin] + pair,
        weights=[(w_ab, (0, 1))], meta=meta,
    )

    def third_work(home, sums_c, proj_gl, qkv_gl, grad_q, grad_k, grad_v):
        home = lax.all_to_all(home, (W, C), 0, 0, tiled=True)
        (sums,) = run(
            third_sums, [(where, scalars), sums_c, proj_gl, mixed, qkv_lat, grad_q, grad_k, grad_v, qkv_gl],
            [((groups, part_r, sums_c.shape[1] + 4 * seg + n), f32)],
        )
        return swapped(sums), run(adapter_tables, [home], [((adapters,) + home.shape[1:], f32)])[0]

    low, got, (sums, tables) = during(
        mine, away, (home, sums_c, proj_gl, qkv_gl, grad_q, grad_k, grad_v), third_work
    )
    (input_grad,) = finish_rows(end_attn_back, [low, got, grad_after, x_low], [((half, padded), f32, row_block)])
    input_other = across(input_grad, T)
    (last,) = run(
        functools.partial(last_sums, ranges),
        [(where, scalars), sums, proj_s, ga_own, ga_other, cross_own, cross_other, cap, attn_in],
        [(last_dims, bf16)],
        [pltpu.VMEM(last_dims, f32)],
    )
    last = lax.all_to_all(last, (W, C), 0, 0, tiled=True)
    input_grad = in_order(input_grad, input_other)
    last, input_grad = together(last, input_grad)
    (last,) = run(adapter_tables, [last], [((adapters,) + last.shape[1:], f32)])

    def rows_of(i):
        return table_rows(last, i, D)

    return (
        output,
        input_grad,
        down_rows(last, 11, D),
        jnp.stack([rows_of(8), rows_of(9), rows_of(10)], axis=2),
        down_rows(last, 7, D),
        rows_of(2),
        down_rows(last, 0, D),
        rows_of(4),
        down_rows(last, 1, D),
        jnp.stack([rows_of(5), rows_of(6)], axis=2),
        down_rows(last, 3, D),
        table_rows(tables, 0, D),
        down_rows(tables, 2, D),
        jnp.stack([table_rows(tables, i, 8 * hh) for i in (4, 5)], axis=2),
        down_rows(tables, 3, 8 * hh),
        table_rows(tables, 1, D),
    )


def solution(mesh):
    down = P(None, (W, C), T)
    up3 = P(None, T, (W, C))
    up4 = P(None, T, None, (W, C))
    rows = P(W, C)
    return jax.shard_map(
        shards,
        mesh=mesh,
        in_specs=(
            rows, rows, P(W), P(W), P(W), rows,
            P(W), P(None, W), P(W), P(W), P(None, W),
            P(W, None, T), P(None, None, None, T), P(T, W),
        )
        + (P(),) * 14,
        out_specs=(
            rows, rows, down, up4, down, up3, down, up3, down, up4, down, up3, down, up4, down, up3,
        ),
        check_vma=False,
    )
```

```python
import functools
import jax
import jax.numpy as jnp
from jax import lax
from jax.experimental import pallas as pl
from jax.experimental.pallas import tpu as pltpu
from jax.sharding import PartitionSpec as P

W, C, T = "weight", "context", "tensor"
HD = 32
LANES = 128
bf16, f32 = jnp.bfloat16, jnp.float32
full_precision = lax.Precision.HIGHEST
norm_eps = 1e-06
attention_epsilon = 1e-06
masked_score = -1000000000.0
LOG2E = 1.4426950408889634
big = pltpu.CompilerParams(vmem_limit_bytes=58 * 1024 * 1024)


def shape(dims, dtype):
    return jax.ShapeDtypeStruct(dims, dtype)


def mm(a, b, ca=1, cb=0):
    return lax.dot_general(a, b, (((ca,), (cb,)), ((), ())), preferred_element_type=f32)


def two(pair):
    high = pair.astype(bf16)
    rest = (pair - high.astype(f32)).astype(bf16)
    lane = lax.broadcasted_iota(jnp.int32, pair.shape, 1)
    return jnp.where(lane < pair.shape[1] // 2, high.astype(f32), rest.astype(f32)).astype(bf16)


def split(values):
    high = values.astype(bf16)
    return high, (values - high.astype(f32)).astype(bf16)


def mm3(a, b, ca=1, cb=0):
    ah, al = split(a)
    bh, bl = split(b)
    return mm(ah, bh, ca, cb) + mm(ah, bl, ca, cb) + mm(al, bh, ca, cb)


def head_blocks(width):
    return [slice(at, min(at + 2 * LANES, width)) for at in range(0, width, 2 * LANES)]


def head_mask(width):
    row = lax.broadcasted_iota(jnp.int32, (width, width), 0) // HD
    col = lax.broadcasted_iota(jnp.int32, (width, width), 1) // HD
    return (row == col).astype(f32)


def by_blocks(one, *arrays):
    parts = [one(*[v[:, cols] for v in arrays]) for cols in head_blocks(arrays[0].shape[1])]
    return jnp.concatenate(parts, axis=1)


def head_total(values):
    def one(v):
        high, low = split(v)
        mask = head_mask(v.shape[1]).astype(bf16)
        return mm(high, mask) + mm(low, mask)

    return by_blocks(one, values)


def head_outer(a, b):
    def one(x, y):
        kept = mm3(x, y, 0, 0) * head_mask(x.shape[1])
        return sum(kept[h * HD : (h + 1) * HD] for h in range(kept.shape[0] // HD))

    return by_blocks(one, a, b)


def head_product(values, state, over):
    def one(v, s):
        size = v.shape[1]
        wide = jnp.concatenate([s] * (size // HD), axis=0) * head_mask(size)
        return mm3(v, wide, 1, over)

    return by_blocks(one, values, state)


def sigmoid(values):
    return 1.0 / (1.0 + jnp.exp(-values))


def row_stats(values):
    center = values - jnp.mean(values, axis=-1, keepdims=True)
    inverse = lax.rsqrt(jnp.mean(center * center, axis=-1, keepdims=True) + norm_eps)
    return center * inverse, inverse


def put(out, rows, values):
    width = values.shape[1]
    out[rows, :width] = values.astype(out.dtype)
    if width < out.shape[1]:
        out[rows, width:] = jnp.zeros((values.shape[0], out.shape[1] - width), out.dtype)


everything = slice(None)


def attn_front(w, x, mods, d2, u2, a_out, q_out, k_out, lat_out):
    n = x.shape[0]
    step = 64

    def norm(i, carry):
        at = pl.ds(pl.multiple_of(i * step, step), step)
        normed, unused = row_stats(x[at, :].astype(f32))
        a_out[at, :] = (normed * (1.0 + mods[1:2, :]) + mods[0:1, :]).astype(bf16)
        return carry

    lax.fori_loop(0, n // step, norm, 0)
    a = a_out[...]
    lat = mm(a, d2[...])
    lat_out[...] = lat
    pair = two(lat)
    width = q_out.shape[1]
    both = mm(a, w[0].take(0))
    q_out[...] = both[:, :width] + mm(pair, u2[0])
    k_out[...] = both[:, width:] + mm(pair, u2[1])


def attn_state(w, a, k, lat, u2, v_out, st_out):
    w[0].take(0)
    v_out[...] = mm(a[...], w[0].columns(0, 0, v_out.shape[1])) + mm(two(lat[...]), u2[2])
    keys = jnp.maximum(k[...], 0.0)
    width = keys.shape[1]
    st_out[:HD, :] = head_outer(v_out[...], keys)
    st_out[HD:, :] = jnp.broadcast_to(jnp.sum(keys, axis=0, keepdims=True), (8, width))


def put_partial(low, lat_pair, w, u2, mine, away):
    half = mine.shape[0]
    put(mine, everything, mm(low[:half], w, 1, 1) + mm(lat_pair[:half], u2))
    put(away, everything, mm(low[half:], w, 1, 1) + mm(lat_pair[half:], u2))


def attn_back(w, q, st1, st2, owned, d2, u2, ratio_out, den_out, mixed_out, lat_out, mine, away):
    st = st1[...] + st2[...]
    width = q.shape[1]
    queries = jnp.maximum(q[...], 0.0)
    numer = head_product(queries, st[:HD], 1)
    den = head_total(queries * st[HD : HD + 1]) + attention_epsilon
    ratio = numer / den
    ratio_out[...] = ratio
    den_out[...] = den
    mixed = (ratio * owned[...]).astype(bf16)
    mixed_out[...] = mixed
    lat = mm(mixed, d2[...])
    lat_out[...] = lat
    w[0].take(0)
    put_partial(mixed, two(lat), w[0].columns(0, width, width), u2[...], mine, away)


def caption_rows(w, own, other, d2, u2, kv_out, lat_out):
    here = own.shape[0]
    depth = d2.shape[0]
    width = u2.shape[2]
    weight = w[0].take(0)
    for i, rows in enumerate((own, other)):
        lat = mm(rows[:, :depth], d2[...])
        if i == 0:
            lat_out[...] = lat
        both = mm(rows[:, :depth], weight)
        for j in range(2):
            out = both[:, j * width : (j + 1) * width] + mm(two(lat), u2[j])
            kv_out[j, i * here : (i + 1) * here, :] = out.astype(bf16)


def lane_groups(width):
    return [(at, min(LANES, width - at)) for at in range(0, width, LANES)]


def only_head(values, j):
    lane = lax.broadcasted_iota(jnp.int32, (1, values.shape[1]), 1) // HD
    return values * (lane == j).astype(f32).astype(values.dtype)


def cross_fwd(
    w, rows, kv, live, owned, qd2, qu2, cd2, cu2, q_out, mix_out, qlat_out, clat_out, lse_out, part, logs,
):
    width = q_out.shape[1]
    depth = qd2.shape[0]
    w[0].take(0)
    lat = mm(rows[:, :depth], qd2[...])
    qlat_out[...] = lat
    q_out[...] = (mm(rows[:, :depth], w[0].columns(0, 0, width)) + mm(two(lat), qu2[...])).astype(bf16)
    for first, size in lane_groups(width):
        cols = slice(first, first + size)
        query = q_out[:, cols]
        total = None
        for j in range(size // HD):
            scores = mm(query, only_head(kv[0, :, cols], j), 1, 1) * HD ** (-0.5)
            scores = jnp.where(live[...] > 0.0, scores, masked_score)
            top = jnp.max(scores, axis=-1, keepdims=True)
            exps = jnp.exp(scores - top)
            tot = jnp.sum(exps, axis=-1, keepdims=True)
            h = first // HD + j
            logs[:, h : h + 1] = top + jnp.log(tot)
            probs = (exps * (1.0 / tot)).astype(bf16)
            term = mm(probs, only_head(kv[1, :, cols], j))
            total = term if total is None else total + term
        mix_out[:, cols] = (total * owned[:, cols]).astype(bf16)
    lse_out[...] = logs[...].T
    mix = mix_out[...]
    lat = mm(mix, cd2[...])
    clat_out[...] = lat
    put(part, everything, mm(mix, w[0].columns(0, width, width), 1, 1) + mm(two(lat), cu2[...]))


def edge_rows(where, rows, edge):
    r = jnp.where(where[1] == 0, rows // edge - 1, 0)
    return pl.ds(own_first(r, edge, rows // 2, where[0]), edge)


def ffn_front(h, w, where, xo, xt, d2, uv, ug, *refs):
    half = xo.shape[0]
    depth = d2.shape[0]
    pv, pg, hv, hg, ev, eg = refs[:6] if h == 0 else refs[-7:-1]
    u = refs[-1]
    u[:half, :] = xo[:, :depth]
    u[half:, :] = xt[:, :depth]
    if h == 0:
        refs[6][...] = mm(u[...], d2[...])
    pair = two(refs[6][...] if h == 0 else refs[0][...])
    both = mm(u[...], w[0].take(0))
    hh = uv.shape[2]
    at = edge_rows(where, u.shape[0], ev.shape[1])
    for i, (up, pre, hid, edge) in enumerate(((uv, pv, hv, ev), (ug, pg, hg, eg))):
        s = both[:, i * hh : (i + 1) * hh] + mm(pair, up[0])
        pre[0] = s
        hid[0] = (s * sigmoid(s)).astype(bf16)
        edge[0] = hid[0, at, :]


def fill_grid(buf, rows, halo, b, c):
    half = rows.shape[0] // 2
    edge = halo.shape[0]
    buf[pl.ds(pl.multiple_of(edge + b * half, edge), half), :] = rows[:half, :].astype(f32)
    buf[pl.ds(pl.multiple_of(edge + (1 - b) * half, edge), half), :] = rows[half:, :].astype(f32)
    zero = jnp.zeros(halo.shape, f32)
    got = halo.astype(f32)
    buf[:edge, :] = jnp.where(c == 0, zero, got)
    buf[buf.shape[0] - edge :, :] = jnp.where(c == 0, got, zero)


def conv_row(buf, taps, r, edge, flip):
    sums = []
    rows = [buf[pl.ds(pl.multiple_of((r + i) * edge, edge), edge), :] for i in range(3)]
    for j in range(3):
        total = None
        for i in range(3):
            k = (2 - i) * 3 + 2 - j if flip else i * 3 + j
            term = rows[i] * taps[k : k + 1, :]
            total = term if total is None else total + term
        sums.append(total)
    cell = lax.broadcasted_iota(jnp.int32, sums[0].shape, 0)
    left = jnp.where(cell == 0, 0.0, pltpu.roll(sums[0], 1, 0))
    right = jnp.where(cell == edge - 1, 0.0, pltpu.roll(sums[2], edge - 1, 0))
    return left + sums[1] + right


def own_first(r, edge, half, b):
    per = half // edge
    return pl.multiple_of(jnp.where(r // per == b, 0, half) + (r % per) * edge, edge)


def ffn_mid(
    w, where, hv, hg, halo_v, halo_g, taps, cot, gate, d2, u2,
    gated_out, gcv_out, gcg_out, gffn_out, gl_out, lat_out, down_out, edge_out, mine, away, bv, bg, gg, acc,
):
    h = pl.program_id(0)
    b, c = where[0], where[1]
    n = hv.shape[1]
    half = n // 2
    edge = halo_v.shape[1]

    @pl.when(h == 0)
    def first():
        gffn_out[...] = (gate[...] * cot[...].astype(f32)).astype(bf16)
        gl_out[...] = mm(gffn_out[...], u2[...], 1, 1)

    fill_grid(bv, hv[0], halo_v[0], b, c)
    fill_grid(bg, hg[0], halo_g[0], b, c)
    weight = w[0].take(h)
    gg[...] = mm(gffn_out[...], weight) + mm(two(gl_out[...]), d2[0], 1, 1)

    def row(r, carry):
        v = conv_row(bv, taps[0, 0], r, edge, False)
        g = conv_row(bg, taps[0, 1], r, edge, False)
        sig = sigmoid(g)
        act = g * sig
        at = pl.ds(own_first(r, edge, half, b), edge)
        gated_out[0, at, :] = (v * act).astype(bf16)
        grad = gg[at, :]
        gcv_out[0, at, :] = (grad * act).astype(bf16)
        gcg_out[0, at, :] = (grad * v * (sig * (1.0 + g * (1.0 - sig)))).astype(bf16)
        return carry

    lax.fori_loop(0, n // edge, row, 0)
    at = edge_rows(where, n, edge)
    edge_out[0, 0] = gcv_out[0, at, :]
    edge_out[0, 1] = gcg_out[0, at, :]
    gated = gated_out[0]
    down_out[0] = mm(two(gl_out[...]), gated, 0, 0)
    part = mm(gated, weight, 1, 1)
    lat = mm(gated, d2[0])

    @pl.when(h == 0)
    def start():
        acc[...] = part
        lat_out[...] = lat

    @pl.when(h == 1)
    def end():
        total = lat_out[...] + lat
        lat_out[...] = total
        full = acc[...] + part + mm(two(total), u2[...])
        put(mine, everything, full[:half])
        put(away, everything, full[half:])


def ffn_back(
    w, where, gcv, gcg, halo, taps, pv, pg, lat, d2, uv, ug,
    gpv_out, gpg_out, up_out, gl_out, mine, away, bv, bg, acc,
):
    h = pl.program_id(0)
    b, c = where[0], where[1]
    n = gcv.shape[1]
    half = n // 2
    edge = halo.shape[2]
    fill_grid(bv, gcv[0], halo[0, 0], b, c)
    fill_grid(bg, gcg[0], halo[0, 1], b, c)

    def row(r, carry):
        at = pl.ds(own_first(r, edge, half, b), edge)
        for i, (buf, pre, out) in enumerate(((bv, pv, gpv_out), (bg, pg, gpg_out))):
            grad = conv_row(buf, taps[0, i], r, edge, True)
            s = pre[0, at, :]
            sig = sigmoid(s)
            out[0, at, :] = (grad * (sig * (1.0 + s * (1.0 - sig)))).astype(bf16)
        return carry

    lax.fori_loop(0, n // edge, row, 0)
    gpv, gpg = gpv_out[0], gpg_out[0]
    part = mm(jnp.concatenate([gpv, gpg], axis=1), w[0].take(h), 1, 1)
    gl = mm(gpv, uv[0], 1, 1) + mm(gpg, ug[0], 1, 1)
    pair = two(lat[...])
    up_out[0, 0] = mm(pair, gpv, 0, 0)
    up_out[0, 1] = mm(pair, gpg, 0, 0)

    @pl.when(h == 0)
    def start():
        acc[...] = part
        gl_out[...] = gl

    @pl.when(h == 1)
    def end():
        total = gl_out[...] + gl
        gl_out[...] = total
        full = acc[...] + part + mm(two(total), d2[...], 1, 1)
        put(mine, everything, full[:half])
        put(away, everything, full[half:])


def cross_bwd(
    w, go, gt, kv, live, owned, qd2, qu2, cd2, cu2, qo, qt, lo, lt,
    gq_out, gkv_out, qgl_out, cgl_out, mine, away, gm, gqs,
):
    half = go.shape[0]
    width = qo.shape[1]
    w[0].take(0)
    depth = cu2.shape[1]
    weight = w[0].columns(0, width, width)
    scale = HD ** (-0.5)
    hidden_text = jnp.where(live[...] > 0.0, 0.0, masked_score)
    for i, (rows, query, lse) in enumerate(((go, qo, lo), (gt, qt, lt))):
        at = slice(i * half, (i + 1) * half)
        gl = mm(rows[:, :depth], cu2[...], 1, 1)
        cgl_out[at, :] = gl
        grad = mm(rows[:, :depth], weight) + mm(two(gl), cd2[...], 1, 1)
        gm[...] = (grad * owned[...]).astype(bf16)
        for first, size in lane_groups(width):
            cols = slice(first, first + size)
            q_all, g_all = query[:, cols], gm[:, cols]
            grad_q, grad_k, grad_v = 0.0, 0.0, 0.0
            for j in range(size // HD):
                key, val = only_head(kv[0, :, cols], j), only_head(kv[1, :, cols], j)
                h = first // HD + j
                scores = mm(key, q_all, 1, 1) * (scale * LOG2E) + hidden_text
                probs = jnp.exp2(scores - lse[h : h + 1, :] * LOG2E)
                grad_p = mm(val, g_all, 1, 1)
                grad_v = grad_v + mm(probs.astype(bf16), only_head(g_all, j))
                inner = jnp.sum(probs * grad_p, axis=0, keepdims=True)
                grad_s = (probs * (grad_p - inner)).astype(bf16)
                grad_q = grad_q + mm(grad_s, key, 0, 0)
                grad_k = grad_k + mm(grad_s, only_head(q_all, j))
            gqs[at, cols] = grad_q
            for side, new in ((0, grad_k * scale), (1, grad_v)):
                gkv_out[side, :, cols] = new if i == 0 else gkv_out[side, :, cols] + new
    gq = (gqs[...] * scale).astype(bf16)
    gq_out[...] = gq
    gl = mm(gq, qu2[...], 1, 1)
    qgl_out[...] = gl
    pair = two(gl)
    total = mm(gq, w[0].columns(0, 0, width), 1, 1) + mm(pair, qd2[...], 1, 1)
    put(mine, everything, total[:half])
    put(away, everything, total[half:])


def linear_bwd(
    w, go, gt, q, st1, st2, ratio, den, owned, d2, u2, gq_out, gl_out, st_out, gh,
):
    half = go.shape[0]
    width = q.shape[1]
    depth = u2.shape[1]
    w[0].take(0)
    weight = w[0].columns(0, width, width)
    for i, rows in enumerate((go, gt)):
        at = pl.ds(i * half, half)
        gl = mm(rows[:, :depth], u2[...], 1, 1)
        gl_out[at, :] = gl
        gh[at, :] = (mm(rows[:, :depth], weight) + mm(two(gl), d2[...], 1, 1)) * owned[...]
    st = st1[...] + st2[...]
    grad = gh[...]
    inverse = 1.0 / den[...]
    numer = grad * inverse
    grad_den = -head_total(grad * ratio[...]) * inverse
    raw = q[...]
    queries = jnp.maximum(raw, 0.0)
    grad_q = head_product(numer, st[:HD], 0) + grad_den * st[HD : HD + 1]
    gq_out[...] = jnp.where(raw > 0.0, grad_q, 0.0).astype(bf16)
    st_out[:HD, :] = head_outer(numer, queries)
    total = jnp.sum(grad_den * queries, axis=0, keepdims=True)
    st_out[HD:, :] = jnp.broadcast_to(total, (8, width))


def linear_end(
    w, gq, k, v, st1, st2, d2, u2, gk_out, gv_out, gl_out, mine, away,
):
    width = k.shape[1]
    half = mine.shape[0]
    st = st1[...] + st2[...]
    raw = k[...]
    grad_k = head_product(v[...], st[:HD], 0) + st[HD : HD + 1]
    gk_out[...] = jnp.where(raw > 0.0, grad_k, 0.0).astype(bf16)
    gv_out[...] = head_product(jnp.maximum(raw, 0.0), st[:HD], 1).astype(bf16)
    grads = (gq, gk_out, gv_out)
    gl = sum(mm(g[...], u2[i], 1, 1) for i, g in enumerate(grads))
    gl_out[...] = gl
    pair = two(gl)
    w[0].take(0)
    w[0].take(1)
    both = jnp.concatenate([gq[...], gk_out[...]], axis=1)
    total = mm(both, w[0].columns(0, 0, 2 * width), 1, 1) + mm(gv_out[...], w[0].columns(1, 0, width), 1, 1)
    total = total + mm(pair, d2[...], 1, 1)
    put(mine, everything, total[:half])
    put(away, everything, total[half:])


def in_steps(rows, body, step=64):
    def one(i, carry):
        body(pl.ds(pl.multiple_of(i * step, step), step))
        return carry

    lax.fori_loop(0, rows // step, one, 0)


def slope_of_norm(values, grad):
    normed, inverse = row_stats(values)
    return inverse * (
        grad
        - jnp.mean(grad, axis=-1, keepdims=True)
        - normed * jnp.mean(grad * normed, axis=-1, keepdims=True)
    )


def total_of(low, got, at, width):
    return low[at, :width].astype(f32) + got[at, :width].astype(f32)


def end_attn(low, got, x, mods, after_out, own_out):
    def body(at):
        after = x[at, :].astype(f32) + mods[2:3, :] * total_of(low, got, at, x.shape[1])
        after_out[at, :] = after
        put(own_out, at, after)

    in_steps(x.shape[0], body)


def end_cross(low, got, before, mods, after_out, own_out):
    def body(at):
        after = before[at, :] + total_of(low, got, at, before.shape[1])
        after_out[at, :] = after
        normed, unused = row_stats(after)
        put(own_out, at, normed * (1.0 + mods[4:5, :]) + mods[3:4, :])

    in_steps(before.shape[0], body)


def end_output(low, got, before, mods, out):
    def body(at):
        put(out, at, before[at, :] + mods[5:6, :] * total_of(low, got, at, before.shape[1]))

    in_steps(before.shape[0], body)


def end_ffn_back(low, got, after, cot, mods, grad_out, own_out):
    def body(at):
        grad = total_of(low, got, at, after.shape[1]) * (1.0 + mods[4:5, :])
        grad = cot[at, :].astype(f32) + slope_of_norm(after[at, :], grad)
        grad_out[at, :] = grad
        put(own_out, at, grad)

    in_steps(after.shape[0], body)


def end_cross_back(low, got, before, mods, grad_out, own_out):
    def body(at):
        grad = before[at, :] + total_of(low, got, at, before.shape[1])
        grad_out[at, :] = grad
        put(own_out, at, mods[2:3, :] * grad)

    in_steps(before.shape[0], body)


def end_attn_back(low, got, before, x, mods, out):
    def body(at):
        grad = total_of(low, got, at, before.shape[1]) * (1.0 + mods[1:2, :])
        put(out, at, before[at, :] + slope_of_norm(x[at, :].astype(f32), grad))

    in_steps(before.shape[0], body)


def place_rows(where, own, other, out):
    width = out.shape[2]
    out[where[0]] = own[:, :width]
    out[1 - where[0]] = other[:, :width]


def fold(both):
    half = both.shape[0] // 2
    return both[:half] + both[half:]


def turned(v, b):
    half = v.shape[1] // 2
    return jnp.where(b == 0, v, jnp.concatenate([v[:, half:], v[:, :half]], axis=1))


def thin_sum(latent, *rows):
    high = latent.astype(bf16).astype(f32)
    both = jnp.concatenate([high, latent - high], axis=0).astype(bf16)
    total, at = None, 0
    for values in rows:
        size = values.shape[0]
        term = mm(both[:, at : at + size], values[...])
        total = term if total is None else total + term
        at += size
    return fold(total)


def outer_sum(latent, *rows):
    total, at = None, 0
    pair = two(latent)
    for values in rows:
        size = values.shape[0]
        term = mm(pair[at : at + size], values[...], 0, 0)
        total = term if total is None else total + term
        at += size
    return fold(total)


def set_segments(out, segments, width):
    for i, v in enumerate(segments):
        put(out.at[:, i * width : (i + 1) * width], everything, v)


def set_ranks(out, first, pad, values):
    rows = out.shape[1]
    for t in range(out.shape[0]):
        put(out.at[t, :, first : first + pad], everything, values[t * rows : (t + 1) * rows])


def pack_first(where, point, up, l0, l1, l2, l3, sums):
    pieces = [point[0], point[1]] + [up[h, p] for p in range(2) for h in range(2)]
    n = l0.shape[0]
    rank = sums.shape[0] * sums.shape[1]
    first = sums.shape[2] - 4 * n
    pad = first // 6
    for i, v in enumerate(pieces):
        set_ranks(sums, i * pad, pad, fold(v))
    for i, v in enumerate((l0, l1, l2, l3)):
        set_ranks(sums, first + i * n, n, turned(v[...].T[:rank], where[0]))


def to_blocks(home, first, table):
    blocks = home.shape[0]
    size = table.shape[1] // blocks
    rows = table.shape[0]
    for i in range(blocks):
        home[i, first : first + rows, :size] = table[:, i * size : (i + 1) * size]


def set_mark(where, home, last):
    home[:, :, last:] = jnp.zeros((home.shape[0], home.shape[1], 1), f32) + where[2].astype(f32)


def second_sums(
    where, sums, gco, gct, fo, ft, gffn, mixo, mixt, cgl, qlat, gq, qgl, gkv, ggot, klat, ku2,
    home_out, projs, out, home,
):
    n, depth = gffn.shape
    b = where[0]
    first = sums.shape[2] - 4 * n
    parts = []
    for i in range(4):
        at = slice(first + i * n, first + (i + 1) * n)
        parts.append(turned(sums[0, :, at] + sums[1, :, at] + sums[2, :, at] + sums[3, :, at], b))
    projs[...] = parts[0]
    rows = parts[0].shape[0]
    home[...] = jnp.zeros(home.shape, f32)
    to_blocks(home, 0, thin_sum(parts[1], gco, gct)[:, :depth])
    to_blocks(home, rows, thin_sum(parts[2], gffn))
    to_blocks(home, 2 * rows, thin_sum(parts[3], fo, ft)[:, :depth])
    size = home.shape[2] - 1
    pad, hh = first // 6, size * home.shape[0] // 8
    for j in range(3):
        for i in range(home.shape[0]):
            t, h, at = i * size // (2 * hh), i * size % (2 * hh) // hh, i * size % hh
            at += (2 * j + h) * pad
            home[i, (3 + j) * rows : (4 + j) * rows, :size] = sums[t, :, at : at + size]
    set_mark(where, home, size)
    home_out[...] = home[...].astype(home_out.dtype)
    here = ggot.shape[1]
    gk = (gkv[0, :here, :] + ggot[0]).astype(bf16)
    gv = (gkv[1, :here, :] + ggot[1]).astype(bf16)
    segments = [outer_sum(cgl[...], mixo, mixt), outer_sum(qlat[...], gq)]
    segments += [outer_sum(klat[...], gk), outer_sum(klat[...], gv)]
    pad = -(-gq.shape[1] // LANES) * LANES
    set_segments(out, segments, pad)
    rank = out.shape[0]
    out[:, 4 * pad : 4 * pad + n] = turned(qgl[...].T[:rank], b)
    kvgl = mm(gk, ku2[0], 1, 1) + mm(gv, ku2[1], 1, 1)
    put(out.at[:, 4 * pad + n :], everything, kvgl.T[:rank])


def third_sums(where, before, pgl, mixed, qlat, gq, gk, gv, qgl, out):
    rank, first = before.shape
    set_ranks(out, 0, first, before[...])
    segments = [outer_sum(pgl[...], mixed)] + [outer_sum(qlat[...], g) for g in (gq, gk, gv)]
    pad = -(-gq.shape[1] // LANES) * LANES
    for i, v in enumerate(segments):
        set_ranks(out, first + i * pad, pad, v)
    set_ranks(out, first + 4 * pad, qgl.shape[0], turned(qgl[...].T[:rank], where[0]))


def last_sums(ranges, where, sums, projs, gao, gat, xo, xt, cap, a, home_out, home):
    n, depth = a.shape
    b = where[0]
    text = -(-cap.shape[0] // LANES) * LANES
    pad = (sums.shape[2] - 2 * n - text) // 8
    second = 4 * pad + n + text
    rows = projs.shape[0]

    def summed(first, size):
        return sum(sums[t, :, first : first + size].astype(f32) for t in range(sums.shape[0]))

    def heads(first):
        parts = [sums[t, :, first + s * HD : first + (s + m) * HD] for t, (s, m) in enumerate(ranges)]
        return jnp.concatenate([v.astype(f32) for v in parts], axis=1)

    tables = [
        thin_sum(turned(summed(4 * pad, n), b), xo, xt)[:, :depth],
        thin_sum(summed(4 * pad + n, cap.shape[0]), cap)[:, :depth],
        thin_sum(projs[...], gao, gat)[:, :depth],
    ]
    tables += [heads(j * pad) for j in range(4)] + [heads(second + j * pad) for j in range(4)]
    tables.append(thin_sum(turned(summed(second + 4 * pad, n), b), a))
    for j, table in enumerate(tables):
        to_blocks(home, j * rows, table)
    set_mark(where, home, home.shape[2] - 1)
    home_out[...] = home[...].astype(home_out.dtype)


def adapter_tables(got, out):
    last = got.shape[2] - 1
    for i in range(out.shape[0]):
        total = None
        for s in range(got.shape[0]):
            values = got[s].astype(f32)
            term = jnp.where(values[:1, last:] == float(i), values, 0.0)
            total = term if total is None else total + term
        out[i] = total


def ring_order(n):
    return list(range(0, n, 2)) + list(range(n - 1 - n % 2, 0, -2))


def ring_pairs(n):
    order = ring_order(n)
    return [(order[i], order[(i + 1) % n]) for i in range(n)]


def ring_source(n, step):
    z = lax.axis_index(W)
    place = jnp.where(z % 2 == 0, z // 2, n - 1 - z // 2)
    from_place = (place - step + n) % n
    return jnp.where(2 * from_place < n, 2 * from_place, 2 * (n - 1 - from_place) + 1)


def swap_pairs(n, distance):
    return [(i, i ^ distance) for i in range(n)]


def across(values, axis, distance=1):
    return lax.ppermute(values, axis, swap_pairs(lax.axis_size(axis), distance))


class Stream:
    def __init__(self, order):
        self.n = lax.axis_size(W)
        self.order = list(order)
        self.own, self.got, self.crossed = {}, {}, {}
        self.flying, self.crossing = [], []

    def launch(self):
        while self.order and (not self.flying or len(self.flying) < 2 and self.order[0][1] == 1):
            name, step = self.order[0]
            if step == 1 and name in self.own:
                moving = self.own[name][0]
            elif (name, step - 1) in self.got:
                moving = self.got[name, step - 1]
            else:
                break
            self.order.pop(0)
            self.flying.append((name, step, lax.ppermute(moving, W, ring_pairs(self.n))))

    def fence(self, values, take=1, cross=None):
        done, self.flying = self.flying[:take], self.flying[take:]
        count = len(self.crossing) if cross is None else cross
        crossed, self.crossing = self.crossing[:count], self.crossing[count:]
        leaves, tree = jax.tree.flatten((values, [d[2] for d in done], [d[2] for d in crossed]))
        values, arrived, over = jax.tree.unflatten(tree, lax.optimization_barrier(leaves))
        for d, v in zip(crossed, over):
            self.crossed[d[0], d[1]] = v
        for d, v in zip(done, arrived):
            self.got[d[0], d[1]] = v
            self.crossing.append((d[0], d[1], across(v, C)))
        self.launch()
        return values

    def fences(self, count, values):
        for i in range(count * (self.n - 1) // 3):
            values = self.fence(values)
        return values

    def ready(self, names, values):
        while not all((name, self.n - 1) in self.crossed for name in names):
            values = self.fence(values)
        return values

    def pieces(self, name):
        steps = range(1, self.n)
        mine = [self.own[name][0]] + [self.got[name, s] for s in steps]
        other = [self.own[name][1]] + [self.crossed[name, s] for s in steps]
        rows = mine[0].shape[0]
        if rows % 16 == 0:
            return mine + other
        c = lax.axis_index(C)
        buf = jnp.zeros((2, self.n * rows, mine[0].shape[1]), bf16)
        for s in range(self.n):
            at = ring_source(self.n, s) * rows
            buf = lax.dynamic_update_slice(buf, mine[s][None], (c, at, 0))
            buf = lax.dynamic_update_slice(buf, other[s][None], (1 - c, at, 0))
        return [buf]


class Weight:
    def __init__(self, meta, pieces, buf, sems, halves):
        self.meta, self.pieces, self.buf, self.sems, self.halves = meta, pieces, buf, sems, halves

    def copies(self, j, pieces):
        rows = pieces[0].shape[0]
        return [
            pltpu.make_async_copy(
                piece,
                self.buf.at[j, pl.ds(pl.multiple_of(self.meta[1 + k] * rows, rows), rows), :],
                self.sems.at[j, k],
            )
            for k, piece in enumerate(pieces)
        ]

    def start(self):
        count = len(self.pieces) // 2
        for j, half in enumerate(self.halves):
            if not count:
                pltpu.make_async_copy(self.pieces[0].at[half], self.buf.at[j], self.sems.at[j, 0]).start()
                continue

            @pl.when(self.meta[0] == half)
            def mine():
                for copy in self.copies(j, self.pieces[:count]):
                    copy.start()

            @pl.when(self.meta[0] != half)
            def other():
                for copy in self.copies(j, self.pieces[count:]):
                    copy.start()

    def take(self, j):
        count = len(self.pieces) // 2
        if not count:
            pltpu.make_async_copy(self.pieces[0].at[0], self.buf.at[j], self.sems.at[j, 0]).wait()
        else:
            for copy in self.copies(j, self.pieces[:count]):
                copy.wait()
        return self.buf[j]

    def columns(self, j, first, size):
        return self.buf[j, :, first : first + size]


def per_step(a):
    zeros = (0,) * (a.ndim - 1)
    return pl.BlockSpec((1,) + tuple(a.shape[1:]), lambda h: (h,) + zeros)


def half_block(i):
    def spec(a):
        zeros = (0,) * (len(a.shape) - 1)
        return pl.BlockSpec((1,) + tuple(a.shape[1:]), lambda *g: (i,) + zeros)

    return spec


def row_block(a):
    return pl.BlockSpec((a.shape[0] // 2, a.shape[1]), lambda i: (i, 0))


def both_blocks(a):
    return pl.BlockSpec((2, a.shape[1] // 2, a.shape[2]), lambda i: (0, i, 0))


def all_of(a):
    zeros = (0,) * len(a.shape)
    return pl.BlockSpec(tuple(a.shape), lambda *g: zeros)


def scalars(a):
    return pl.BlockSpec(memory_space=pltpu.SMEM)


def anywhere(a):
    return pl.BlockSpec(memory_space=pl.ANY)


def run(kernel, ins, outs, scratch=(), steps=1, weights=(), meta=None, same=()):
    args, specs = [], []
    if weights:
        args.append(meta)
        specs.append(scalars(meta))
    counts, extra = [], []
    for pieces, halves in weights:
        counts.append((len(pieces), halves))
        args += pieces
        specs += [anywhere(p) for p in pieces]
        rows = pieces[0].shape[0] * len(pieces) // 2 if len(pieces) > 1 else pieces[0].shape[1]
        extra.append(pltpu.VMEM((len(halves), rows, pieces[0].shape[-1]), bf16))
        extra.append(pltpu.SemaphoreType.DMA((len(halves), max(len(pieces) // 2, 1))))
    first = len(args)
    for item in ins:
        a, spec = item if isinstance(item, tuple) else (item, all_of)
        args.append(a)
        specs.append(spec(a))
    shapes, out_specs = [], []
    for item in outs:
        dims, dtype, spec = item if len(item) == 3 else item + (all_of,)
        shapes.append(shape(dims, dtype))
        out_specs.append(spec(shapes[-1]))

    def body(*refs):
        if not weights:
            return kernel(*refs)
        at, loaders = 1, []
        tail = refs[len(refs) - len(extra) :]
        for i, (count, halves) in enumerate(counts):
            loaders.append(Weight(refs[0], refs[at : at + count], tail[2 * i], tail[2 * i + 1], halves))
            at += count

        @pl.when(pl.program_id(0) == 0)
        def begin():
            for loader in loaders:
                loader.start()

        kernel(loaders, *refs[first : len(refs) - len(extra)])

    return pl.pallas_call(
        body,
        grid=(steps,),
        in_specs=specs,
        out_specs=out_specs,
        out_shape=shapes,
        input_output_aliases={first + i: j for i, j in same},
        scratch_shapes=list(scratch) + extra,
        compiler_params=big,
    )(*args)


def twice(table, axis):
    return jnp.concatenate([table, table], axis=axis)


def slot_layout(groups, rank, heads):
    per, left = heads // groups, heads % groups
    slots = per + (1 if left else 0)
    own_start = rank * per + jnp.minimum(rank, left)
    own_count = per + jnp.where(rank < left, 1, 0)
    first = jnp.minimum(own_start, heads - slots)
    slot = first + jnp.arange(slots, dtype=jnp.int32)
    owned = ((slot >= own_start) & (slot < own_start + own_count)).astype(f32)
    return slots, first, owned


def slot_ranges(groups, heads):
    per, left = heads // groups, heads % groups
    slots = per + (1 if left else 0)
    out = []
    for rank in range(groups):
        own_start = rank * per + min(rank, left)
        count = per + (1 if rank < left else 0)
        out.append((own_start - min(own_start, heads - slots), count))
    return out


def shards(
    tokens, caption, caption_lengths, adapter_index, modulation, cotangent,
    qkv_weight, proj_weight, cross_q_weight, cross_kv_weight, cross_out_weight,
    inverted_weight, depth_weight, point_weight,
    qkv_down, qkv_up, proj_down, proj_up, query_down, query_up, kv_down, kv_up,
    cross_down, cross_up, inverted_down, inverted_up, point_down, point_up,
):
    grid_rows, grid_cols, D = tokens.shape[1:]
    n = grid_rows * grid_cols
    half = n // 2
    heads = D // HD
    groups = lax.axis_size(T)
    rank = lax.axis_index(T)
    c = lax.axis_index(C)
    b = rank % 2
    adapters, R = qkv_up.shape[:2]
    slots, slot_first, owned = slot_layout(groups, rank, heads)
    width = slots * HD
    col = slot_first * HD
    owned = jnp.repeat(owned, HD)[None]
    hid = inverted_weight.shape[2]
    hh = hid // 2
    hid_first = rank * hid
    index = adapter_index[0]
    where = jnp.stack([b, c, index]).astype(jnp.int32)

    def cut(table, start, size, axis):
        return lax.dynamic_slice_in_dim(table, start, size, axis)

    def pick(table):
        return lax.dynamic_index_in_dim(table, index, 0, keepdims=False)

    def own_rows(rows):
        own = cut(rows, b * half, half, 0)
        return own, jnp.concatenate([own, cut(rows, (1 - b) * half, half, 0)])

    def pair_of(first, second):
        return [jnp.where(c == 0, first, second), jnp.where(c == 0, second, first)]

    def taken(table, middle, start, size):
        return lax.dynamic_slice(table, (0, middle, start), (table.shape[0], 1, size))[:, 0]

    def beside(*values):
        return jnp.concatenate(values, axis=1)

    def both(table, start, size=width):
        return beside(taken(table, 0, start, size), taken(table, 1, start, size))

    size = lax.axis_size(W)
    order = [(name, step) for name in ("ab", "cd", "vg", "p") for step in range(1, size)]
    stream = Stream(order)
    fences = stream.fences

    def front_side(c):
        key, out = taken(qkv_weight, 1, col, width), cut(proj_weight, col, width, 0).T
        return beside(taken(qkv_weight, 2 * c, col, width), jnp.where(c == 0, key, out))

    stream.own["ab"] = [front_side(c), None]
    c_late, caption, stream.own["ab"][0] = lax.optimization_barrier((c, caption, stream.own["ab"][0]))
    stream.own["ab"][1] = front_side(1 - c_late)
    stream.launch()
    mods = modulation[0]
    low_tokens = tokens.reshape(n, D)
    x_low, x_rows = own_rows(low_tokens)
    qd2, qu2 = twice(pick(qkv_down), 1), twice(cut(pick(qkv_up), col, width, 2), 0).transpose(1, 0, 2)
    pd2, pu2 = twice(cut(pick(proj_down), col, width, 0), 1), twice(pick(proj_up), 0)
    text_here = caption.shape[1]
    text_rows = -(-text_here // 16) * 16
    padded = -(-D // LANES) * LANES
    cap = jnp.pad(caption[0], ((0, text_rows - text_here), (0, padded - D)))
    cap_other = across(cap, C)
    tables = [query_down, query_up, kv_down, kv_up, cross_down, cross_up]
    tables_f = [inverted_down, inverted_up, point_down, point_up, depth_weight]
    raw = [cross_kv_weight, cross_q_weight, cross_out_weight]
    raw_f = [inverted_weight, point_weight]
    raw, raw_f, tables, tables_f, cap, cap_other, cotangent = fences(
        1, (raw, raw_f, tables, tables_f, cap, cap_other, cotangent)
    )
    pair_cd = pair_of(both(raw[0], col), beside(cut(raw[1], col, width, 1), cut(raw[2], col, width, 0).T))
    query_down, query_up, kv_down, kv_up, cross_down, cross_up = tables
    cd2 = twice(cut(pick(cross_down), col, width, 0), 1)
    cu2 = twice(pick(cross_up), 0)
    xd2, xu2 = twice(pick(query_down), 1), twice(cut(pick(query_up), col, width, 1), 0)
    kd2, ku2 = twice(pick(kv_down), 1), twice(cut(pick(kv_up), col, width, 2), 0).transpose(1, 0, 2)
    front = [x_low, x_rows, qd2, qu2, pd2, pu2, stream.own["ab"][1]]
    pair_cd, raw_f, tables_f, cotangent, front = fences(1, (pair_cd, raw_f, tables_f, cotangent, front))
    stream.own["cd"] = pair_cd
    x_low, x_rows, qd2, qu2, pd2, pu2, stream.own["ab"][1] = front
    pair_vg = [both(raw_f[0], i * hh, hh) for i in (c, 1 - c)]
    pair_p = [cut(raw_f[1], i * hh, hh, 0).T for i in (c, 1 - c)]
    pair_vg, pair_p, tables_f, cotangent = fences(1, (pair_vg, pair_p, tables_f, cotangent))
    stream.own.update(vg=pair_vg, p=pair_p)
    inverted_down, inverted_up, point_down, point_up, depth_weight = tables_f
    fd2, fu2 = twice(pick(inverted_down), 1), twice(cut(pick(inverted_up), hid_first, hid, 2), 0)
    fu2 = fu2.reshape(2 * R, 2, 2, hh).transpose(1, 2, 0, 3)
    od2 = twice(cut(pick(point_down), hid_first, hid, 0), 1).reshape(2, hh, 2 * R)
    ou2 = twice(pick(point_up), 0)
    taps = depth_weight.astype(f32).reshape(9, 2, 2, hh).transpose(2, 1, 0, 3)
    cot_low, cot = own_rows(cotangent.reshape(n, D))
    places = jnp.arange(text_rows)
    live = jnp.concatenate([c * text_here + places, (1 - c) * text_here + places])
    live = (live < caption_lengths[0]) & (jnp.concatenate([places, places]) < text_here)
    live = live.astype(f32)[None]
    tables = [cd2, cu2, xd2, xu2, kd2, ku2, fd2, fu2[0], fu2[1], od2, ou2, taps, cot_low, cot, live]
    x_rows, tables = stream.ready(["ab"], (x_rows, tables))
    cd2, cu2, xd2, xu2, kd2, ku2, fd2, fuv, fug, od2, ou2, taps, cot_low, cot, live = tables

    w_ab = stream.pieces("ab")
    meta = jnp.stack([c] + [ring_source(size, s) for s in range(size)]).astype(jnp.int32)
    rows_bf = ((n, D), bf16)
    thin = ((n, 2 * R), f32)
    wide = ((n, width), f32)
    wide_bf = ((n, width), bf16)
    pair = [((half, padded), bf16)] * 2
    ended = [((half, D), f32, row_block), ((half, padded), bf16, row_block)]

    def finish_rows(kernel, arrays, outs):
        return run(kernel, [(v, row_block) for v in arrays] + [mods], outs, steps=2)

    state_of = ((HD + 8, width), f32)
    attn_in, q_raw, k_raw, qkv_lat = run(
        attn_front, [x_rows, mods, qd2, qu2], [rows_bf, wide, wide, thin], weights=[(w_ab, (0,))], meta=meta,
    )
    v_raw, st_own = run(
        attn_state, [attn_in, k_raw, qkv_lat, qu2], [wide, state_of], weights=[(w_ab, (1,))], meta=meta,
    )
    st_own, st_other = fences(1, (st_own, across(st_own, C)))
    ratio, denom, mixed, proj_lat, mine, away = run(
        attn_back, [q_raw, st_own, st_other, owned, pd2, pu2], [wide, wide, wide_bf, thin] + pair,
        weights=[(w_ab, (1,))], meta=meta,
    )

    def exchanged(mine, away, pace=lambda low: low):
        low, distance = (mine.astype(f32) + across(away, T).astype(f32)).astype(bf16), 2
        while True:
            low = pace(low)
            got = across(low, T, distance)
            distance *= 2
            if distance >= groups:
                return low, got
            low = (low.astype(f32) + got.astype(f32)).astype(bf16)

    def while_streaming(mine, away):
        return exchanged(mine, away)

    mine, away = fences(1, (mine, away))
    low, got = fences(1, while_streaming(mine, away))
    after_attn, cross_own = finish_rows(end_attn, [low, got, x_low], ended)
    cross_other = across(cross_own, T)

    cap, cross_own, cross_other, after_attn = stream.ready(["cd"], (cap, cross_own, cross_other, after_attn))
    w_cd = stream.pieces("cd")
    kv_all, kv_lat = run(
        caption_rows, [cap, cap_other, kd2, ku2], [((2, 2 * text_rows, width), bf16), ((text_rows, 2 * R), f32)],
        weights=[(w_cd, (0,))], meta=meta,
    )
    kv_all, cross_own, cross_other = fences(1, (kv_all, cross_own, cross_other))
    half_bf, half_thin = ((half, width), bf16), ((half, 2 * R), f32)

    def cross_part(rows, kv):
        return run(
            cross_fwd,
            [rows, kv, live, owned, xd2, xu2, cd2, cu2],
            [half_bf, half_bf, half_thin, half_thin, ((LANES, half), f32), ((half, padded), bf16)],
            [pltpu.VMEM((half, LANES), f32)],
            weights=[(w_cd, (1,))], meta=meta,
        )

    *cross_t, away = cross_part(cross_other, kv_all)
    away, cross_tied, kv_tied = lax.optimization_barrier((away, cross_own, kv_all))
    *cross_o, mine = cross_part(cross_tied, kv_tied)
    mine, away = fences(1, (mine, away))
    query, mix, query_lat, cross_lat, lse = zip(cross_o, cross_t)
    low, got = while_streaming(mine, away)
    low, got = stream.fence((stream.fence(low, 1, 0), got), 0, 1)
    after_cross, ffn_own = finish_rows(end_cross, [low, got, after_attn], ended)
    ffn_own, after_cross = stream.fence((ffn_own, after_cross), 1, 1)
    ffn_other = across(ffn_own, T)

    query_lat, cross_lat = jnp.concatenate(query_lat), jnp.concatenate(cross_lat)

    ffn_own, ffn_other, after_cross = stream.ready(["vg"], (ffn_own, ffn_other, after_cross))
    w_vg = stream.pieces("vg")
    hid_bf = ((2, n, hh), bf16, per_step)

    def ffn_part(h, more, same):
        outs = [((2, n, hh), f32)] * 2 + [((2, n, hh), bf16)] * 2 + [((2, grid_cols, hh), bf16)] * 2
        return run(
            functools.partial(ffn_front, h),
            [(where, scalars), ffn_own, ffn_other, fd2, (fuv, half_block(h)), (fug, half_block(h))] + more,
            [out + (half_block(h),) for out in outs] + [thin][h:],
            [pltpu.VMEM((n, D), bf16)],
            weights=[(w_vg, (h,))], meta=meta, same=same,
        )

    *started, inv_lat = ffn_part(0, [], ())
    ffn_own, started, inv_lat = stream.fence((ffn_own, started, inv_lat), 1, 1)
    pre_v, pre_g, hid_v, hid_g, edge_v, edge_g = ffn_part(
        1, [inv_lat] + [(v, anywhere) for v in started], [(7 + i, i) for i in range(6)]
    )
    halo_v, halo_g = across(edge_v, C), across(edge_g, C)
    hid_v, halo_v, halo_g = stream.ready(["p"], (hid_v, halo_v, halo_g))
    w_p = stream.pieces("p")
    grid_buf = pltpu.VMEM((n + 2 * grid_cols, hh), f32)
    row_acc = pltpu.VMEM((n, D), f32)
    gated, gcv, gcg, grad_ffn, point_gl, point_lat, point_down_g, edge, mine, away = run(
        ffn_mid,
        [
            (where, scalars), (hid_v, per_step), (hid_g, per_step), (halo_v, per_step), (halo_g, per_step), (taps, per_step),
            cot, mods[5:6], (od2, per_step), ou2,
        ],
        [hid_bf, hid_bf, hid_bf, rows_bf, thin, thin, ((2, 2 * R, hh), f32, per_step)]
        + [((2, 2, grid_cols, hh), bf16, per_step)] + pair,
        [grid_buf, grid_buf, pltpu.VMEM((n, hh), f32), row_acc],
        2,
        weights=[(w_p, (0, 1))], meta=meta,
    )
    halo = across(edge, C)
    tied = []

    def after_halo(low):
        low, *tied[:] = lax.optimization_barrier((low, halo, gcv, gcg))
        return low

    out_low, out_got = exchanged(mine, away, after_halo)
    halo, gcv, gcg = tied

    gpv, gpg, inv_up_g, inv_gl, mine, away = run(
        ffn_back,
        [
            (where, scalars), (gcv, per_step), (gcg, per_step), (halo, per_step), (taps, per_step),
            (pre_v, per_step), (pre_g, per_step), inv_lat, fd2,
            (fuv, per_step), (fug, per_step),
        ],
        [hid_bf, hid_bf, ((2, 2, 2 * R, hh), f32, per_step), thin] + pair,
        [grid_buf, grid_buf, row_acc],
        2,
        weights=[(w_vg, (0, 1))], meta=meta,
    )
    part_r = R // groups
    blocks = size * lax.axis_size(C)
    ranges = slot_ranges(groups, heads)

    def swapped(sent):
        return lax.all_to_all(sent, T, 0, 0, tiled=True)

    def up_to_tiles(size):
        return -(-size // LANES) * LANES

    def table_rows(table, i, size):
        return table[:, i * part_r : (i + 1) * part_r, : size // blocks]

    def down_rows(table, i, size):
        return table_rows(table, i, size).transpose(0, 2, 1)

    def together(*values):
        return lax.optimization_barrier(values)

    def during(mine, away, inputs, work):
        held = []

        def pace(low):
            low, tied = together(low, inputs)
            held[:] = [tied]
            return low

        low, got = exchanged(mine, away, pace)
        return together(low, got, work(*held[0]))

    def first_work(out_low, out_got, after_cross, inv_up_g, point_down_g, lats):
        (output,) = finish_rows(end_output, [out_low, out_got, after_cross], [((half, padded), f32, row_block)])
        (sums,) = run(
            pack_first, [(where, scalars), point_down_g, inv_up_g, *lats], [((groups, part_r, 6 * up_to_tiles(hh) + 4 * n), f32)],
        )
        return output, sums

    mine, away, out_low, out_got = together(mine, away, out_low, out_got)
    low, got, (output, sums_f) = during(
        mine, away,
        (out_low, out_got, after_cross, inv_up_g, point_down_g, (proj_lat, cross_lat, point_lat, inv_gl)),
        first_work,
    )
    grad_cross, gc_own = finish_rows(end_ffn_back, [low, got, after_cross, cot_low], ended)
    gc_other = across(gc_own, T)

    gc_own, gc_other, output, sums_f = together(gc_own, gc_other, output, sums_f)
    output_other = across(output, T)
    sums_f = swapped(sums_f)
    grad_query, gkv, query_gl, cross_gl, mine, away = run(
        cross_bwd,
        [
            gc_own, gc_other, kv_all, live.T, owned,
            xd2, xu2, cd2, cu2, *query, *lse,
        ],
        [wide_bf, ((2, 2 * text_rows, width), f32), thin, thin] + pair,
        [pltpu.VMEM((half, width), bf16), pltpu.VMEM((n, width), f32)],
        weights=[(w_cd, (1,))], meta=meta,
    )
    mine, away, output_other, sums_f, gkv = together(mine, away, output_other, sums_f, gkv)
    gkv_got = across(gkv[:, text_rows:], C)

    def in_order(own, other):
        (rows,) = run(
            place_rows, [(where, scalars), (own, row_block), (other, row_block)],
            [((2, half, D), f32, both_blocks)], steps=2,
        )
        return rows.reshape(tokens.shape)

    seg = up_to_tiles(width)

    seg = up_to_tiles(width)
    home_dims = (blocks, 8 * part_r, 4 * 2 * hh // blocks + 1)
    last_dims = (blocks, 12 * part_r, D // blocks + 1)

    def second_work(output, output_other, sums, cross_gl, grad_query, query_gl):
        return [in_order(output, output_other)] + list(run(
            second_sums,
            [
                (where, scalars), sums, gc_own, gc_other, ffn_own, ffn_other, grad_ffn, *mix, cross_gl,
                query_lat, grad_query, query_gl, gkv, gkv_got, kv_lat, ku2,
            ],
            [(home_dims, bf16), ((part_r, n), f32), ((R, 4 * seg + n + up_to_tiles(text_rows)), f32)],
            [pltpu.VMEM(home_dims, f32)],
        ))

    low, got, (output, home, proj_s, sums_c) = during(
        mine, away, (output, output_other, sums_f, cross_gl, grad_query, query_gl), second_work
    )
    grad_after, ga_own = finish_rows(end_cross_back, [low, got, grad_cross], ended)
    ga_other = across(ga_own, T)

    grad_q, proj_gl, sg_own = run(
        linear_bwd,
        [ga_own, ga_other, q_raw, st_own, st_other, ratio, denom, owned, pd2, pu2],
        [wide_bf, thin, state_of],
        [pltpu.VMEM((n, width), f32)],
        weights=[(w_ab, (1,))], meta=meta,
    )
    sg_other = across(sg_own, C)
    grad_k, grad_v, qkv_gl, mine, away = run(
        linear_end,
        [grad_q, k_raw, v_raw, sg_own, sg_other, qd2, qu2],
        [wide_bf, wide_bf, thin] + pair,
        weights=[(w_ab, (0, 1))], meta=meta,
    )

    def third_work(home, sums_c, proj_gl, qkv_gl, grad_q, grad_k, grad_v):
        home = lax.all_to_all(home, (W, C), 0, 0, tiled=True)
        (sums,) = run(
            third_sums, [(where, scalars), sums_c, proj_gl, mixed, qkv_lat, grad_q, grad_k, grad_v, qkv_gl],
            [((groups, part_r, sums_c.shape[1] + 4 * seg + n), f32)],
        )
        return swapped(sums.astype(bf16)), run(adapter_tables, [home], [((adapters,) + home.shape[1:], f32)])[0]

    low, got, (sums, tables) = during(
        mine, away, (home, sums_c, proj_gl, qkv_gl, grad_q, grad_k, grad_v), third_work
    )
    (input_grad,) = finish_rows(end_attn_back, [low, got, grad_after, x_low], [((half, padded), f32, row_block)])
    input_other = across(input_grad, T)
    (last,) = run(
        functools.partial(last_sums, ranges),
        [(where, scalars), sums, proj_s, ga_own, ga_other, cross_own, cross_other, cap, attn_in],
        [(last_dims, bf16)],
        [pltpu.VMEM(last_dims, f32)],
    )
    last = lax.all_to_all(last, (W, C), 0, 0, tiled=True)
    input_grad = in_order(input_grad, input_other)
    last, input_grad = together(last, input_grad)
    (last,) = run(adapter_tables, [last], [((adapters,) + last.shape[1:], f32)])

    def rows_of(i):
        return table_rows(last, i, D)

    return (
        output,
        input_grad,
        down_rows(last, 11, D),
        jnp.stack([rows_of(8), rows_of(9), rows_of(10)], axis=2),
        down_rows(last, 7, D),
        rows_of(2),
        down_rows(last, 0, D),
        rows_of(4),
        down_rows(last, 1, D),
        jnp.stack([rows_of(5), rows_of(6)], axis=2),
        down_rows(last, 3, D),
        table_rows(tables, 0, D),
        down_rows(tables, 2, D),
        jnp.stack([table_rows(tables, i, 8 * hh) for i in (4, 5)], axis=2),
        down_rows(tables, 3, 8 * hh),
        table_rows(tables, 1, D),
    )


def solution(mesh):
    down = P(None, (W, C), T)
    up3 = P(None, T, (W, C))
    up4 = P(None, T, None, (W, C))
    rows = P(W, C)
    return jax.shard_map(
        shards,
        mesh=mesh,
        in_specs=(
            rows, rows, P(W), P(W), P(W), rows,
            P(W), P(None, W), P(W), P(W), P(None, W),
            P(W, None, T), P(None, None, None, T), P(T, W),
        )
        + (P(),) * 14,
        out_specs=(
            rows, rows, down, up4, down, up3, down, up3, down, up4, down, up3, down, up4, down, up3,
        ),
        check_vma=False,
    )
```

```python
import functools
import jax
import jax.numpy as jnp
from jax import lax
from jax.experimental import pallas as pl
from jax.experimental.pallas import tpu as pltpu
from jax.sharding import PartitionSpec as P

W, C, T = "weight", "context", "tensor"
HD = 32
LANES = 128
bf16, f32 = jnp.bfloat16, jnp.float32
full_precision = lax.Precision.HIGHEST
norm_eps = 1e-06
attention_epsilon = 1e-06
masked_score = -1000000000.0
LOG2E = 1.4426950408889634
big = pltpu.CompilerParams(vmem_limit_bytes=58 * 1024 * 1024)


def shape(dims, dtype):
    return jax.ShapeDtypeStruct(dims, dtype)


def mm(a, b, ca=1, cb=0):
    return lax.dot_general(a, b, (((ca,), (cb,)), ((), ())), preferred_element_type=f32)


def two(pair):
    high = pair.astype(bf16)
    rest = (pair - high.astype(f32)).astype(bf16)
    lane = lax.broadcasted_iota(jnp.int32, pair.shape, 1)
    return jnp.where(lane < pair.shape[1] // 2, high.astype(f32), rest.astype(f32)).astype(bf16)


def split(values):
    high = values.astype(bf16)
    return high, (values - high.astype(f32)).astype(bf16)


def mm3(a, b, ca=1, cb=0):
    ah, al = split(a)
    bh, bl = split(b)
    return mm(ah, bh, ca, cb) + mm(ah, bl, ca, cb) + mm(al, bh, ca, cb)


def head_blocks(width):
    return [slice(at, min(at + 2 * LANES, width)) for at in range(0, width, 2 * LANES)]


def head_mask(width):
    row = lax.broadcasted_iota(jnp.int32, (width, width), 0) // HD
    col = lax.broadcasted_iota(jnp.int32, (width, width), 1) // HD
    return (row == col).astype(f32)


def by_blocks(one, *arrays):
    parts = [one(*[v[:, cols] for v in arrays]) for cols in head_blocks(arrays[0].shape[1])]
    return jnp.concatenate(parts, axis=1)


def head_total(values):
    def one(v):
        high, low = split(v)
        mask = head_mask(v.shape[1]).astype(bf16)
        return mm(high, mask) + mm(low, mask)

    return by_blocks(one, values)


def head_outer(a, b):
    def one(x, y):
        kept = mm3(x, y, 0, 0) * head_mask(x.shape[1])
        return sum(kept[h * HD : (h + 1) * HD] for h in range(kept.shape[0] // HD))

    return by_blocks(one, a, b)


def head_product(values, state, over):
    def one(v, s):
        size = v.shape[1]
        wide = jnp.concatenate([s] * (size // HD), axis=0) * head_mask(size)
        return mm3(v, wide, 1, over)

    return by_blocks(one, values, state)


def sigmoid(values):
    return 1.0 / (1.0 + jnp.exp(-values))


def row_stats(values):
    center = values - jnp.mean(values, axis=-1, keepdims=True)
    inverse = lax.rsqrt(jnp.mean(center * center, axis=-1, keepdims=True) + norm_eps)
    return center * inverse, inverse


def put(out, rows, values):
    width = values.shape[1]
    out[rows, :width] = values.astype(out.dtype)
    if width < out.shape[1]:
        out[rows, width:] = jnp.zeros((values.shape[0], out.shape[1] - width), out.dtype)


everything = slice(None)


def attn_front(w, x, mods, d2, u2, a_out, q_out, k_out, lat_out):
    n = x.shape[0]
    step = 64

    def norm(i, carry):
        at = pl.ds(pl.multiple_of(i * step, step), step)
        normed, unused = row_stats(x[at, :].astype(f32))
        a_out[at, :] = (normed * (1.0 + mods[1:2, :]) + mods[0:1, :]).astype(bf16)
        return carry

    lax.fori_loop(0, n // step, norm, 0)
    a = a_out[...]
    lat = mm(a, d2[...])
    lat_out[...] = lat
    pair = two(lat)
    width = q_out.shape[1]
    both = mm(a, w[0].take(0))
    q_out[...] = both[:, :width] + mm(pair, u2[0])
    k_out[...] = both[:, width:] + mm(pair, u2[1])


def attn_state(w, a, k, lat, u2, v_out, st_out):
    w[0].take(0)
    v_out[...] = mm(a[...], w[0].columns(0, 0, v_out.shape[1])) + mm(two(lat[...]), u2[2])
    keys = jnp.maximum(k[...], 0.0)
    width = keys.shape[1]
    st_out[:HD, :] = head_outer(v_out[...], keys)
    st_out[HD:, :] = jnp.broadcast_to(jnp.sum(keys, axis=0, keepdims=True), (8, width))


def put_partial(low, lat_pair, w, u2, mine, away):
    half = mine.shape[0]
    put(mine, everything, mm(low[:half], w, 1, 1) + mm(lat_pair[:half], u2))
    put(away, everything, mm(low[half:], w, 1, 1) + mm(lat_pair[half:], u2))


def attn_back(w, q, st1, st2, owned, d2, u2, ratio_out, den_out, mixed_out, lat_out, mine, away):
    st = st1[...] + st2[...]
    width = q.shape[1]
    queries = jnp.maximum(q[...], 0.0)
    numer = head_product(queries, st[:HD], 1)
    den = head_total(queries * st[HD : HD + 1]) + attention_epsilon
    ratio = numer / den
    ratio_out[...] = ratio
    den_out[...] = den
    mixed = (ratio * owned[...]).astype(bf16)
    mixed_out[...] = mixed
    lat = mm(mixed, d2[...])
    lat_out[...] = lat
    w[0].take(0)
    put_partial(mixed, two(lat), w[0].columns(0, width, width), u2[...], mine, away)


def caption_rows(w, own, other, d2, u2, kv_out, lat_out):
    here = own.shape[0]
    depth = d2.shape[0]
    width = u2.shape[2]
    weight = w[0].take(0)
    for i, rows in enumerate((own, other)):
        lat = mm(rows[:, :depth], d2[...])
        if i == 0:
            lat_out[...] = lat
        both = mm(rows[:, :depth], weight)
        for j in range(2):
            out = both[:, j * width : (j + 1) * width] + mm(two(lat), u2[j])
            kv_out[j, i * here : (i + 1) * here, :] = out.astype(bf16)


def lane_groups(width):
    return [(at, min(LANES, width - at)) for at in range(0, width, LANES)]


def only_head(values, j):
    lane = lax.broadcasted_iota(jnp.int32, (1, values.shape[1]), 1) // HD
    return values * (lane == j).astype(f32).astype(values.dtype)


def cross_fwd(
    w, rows, kv, live, owned, qd2, qu2, cd2, cu2, q_out, mix_out, qlat_out, clat_out, lse_out, part, logs,
):
    width = q_out.shape[1]
    depth = qd2.shape[0]
    w[0].take(0)
    lat = mm(rows[:, :depth], qd2[...])
    qlat_out[...] = lat
    q_out[...] = (mm(rows[:, :depth], w[0].columns(0, 0, width)) + mm(two(lat), qu2[...])).astype(bf16)
    for first, size in lane_groups(width):
        cols = slice(first, first + size)
        query = q_out[:, cols]
        total = None
        for j in range(size // HD):
            scores = mm(query, only_head(kv[0, :, cols], j), 1, 1) * HD ** (-0.5)
            scores = jnp.where(live[...] > 0.0, scores, masked_score)
            top = jnp.max(scores, axis=-1, keepdims=True)
            exps = jnp.exp(scores - top)
            tot = jnp.sum(exps, axis=-1, keepdims=True)
            h = first // HD + j
            logs[:, h : h + 1] = top + jnp.log(tot)
            probs = (exps * (1.0 / tot)).astype(bf16)
            term = mm(probs, only_head(kv[1, :, cols], j))
            total = term if total is None else total + term
        mix_out[:, cols] = (total * owned[:, cols]).astype(bf16)
    lse_out[...] = logs[...].T
    mix = mix_out[...]
    lat = mm(mix, cd2[...])
    clat_out[...] = lat
    put(part, everything, mm(mix, w[0].columns(0, width, width), 1, 1) + mm(two(lat), cu2[...]))


def edge_rows(where, rows, edge):
    r = jnp.where(where[1] == 0, rows // edge - 1, 0)
    return pl.ds(own_first(r, edge, rows // 2, where[0]), edge)


def ffn_front(h, w, where, xo, xt, d2, uv, ug, *refs):
    half = xo.shape[0]
    depth = d2.shape[0]
    pv, pg, hv, hg, ev, eg = refs[:6] if h == 0 else refs[-7:-1]
    u = refs[-1]
    u[:half, :] = xo[:, :depth]
    u[half:, :] = xt[:, :depth]
    if h == 0:
        refs[6][...] = mm(u[...], d2[...])
    pair = two(refs[6][...] if h == 0 else refs[0][...])
    both = mm(u[...], w[0].take(0))
    hh = uv.shape[2]
    at = edge_rows(where, u.shape[0], ev.shape[1])
    for i, (up, pre, hid, edge) in enumerate(((uv, pv, hv, ev), (ug, pg, hg, eg))):
        s = both[:, i * hh : (i + 1) * hh] + mm(pair, up[0])
        pre[0] = s
        hid[0] = (s * sigmoid(s)).astype(bf16)
        edge[0] = hid[0, at, :]


def fill_grid(buf, rows, halo, b, c):
    half = rows.shape[0] // 2
    edge = halo.shape[0]
    buf[pl.ds(pl.multiple_of(edge + b * half, edge), half), :] = rows[:half, :].astype(f32)
    buf[pl.ds(pl.multiple_of(edge + (1 - b) * half, edge), half), :] = rows[half:, :].astype(f32)
    zero = jnp.zeros(halo.shape, f32)
    got = halo.astype(f32)
    buf[:edge, :] = jnp.where(c == 0, zero, got)
    buf[buf.shape[0] - edge :, :] = jnp.where(c == 0, got, zero)


def conv_row(buf, taps, r, edge, flip):
    sums = []
    rows = [buf[pl.ds(pl.multiple_of((r + i) * edge, edge), edge), :] for i in range(3)]
    for j in range(3):
        total = None
        for i in range(3):
            k = (2 - i) * 3 + 2 - j if flip else i * 3 + j
            term = rows[i] * taps[k : k + 1, :]
            total = term if total is None else total + term
        sums.append(total)
    cell = lax.broadcasted_iota(jnp.int32, sums[0].shape, 0)
    left = jnp.where(cell == 0, 0.0, pltpu.roll(sums[0], 1, 0))
    right = jnp.where(cell == edge - 1, 0.0, pltpu.roll(sums[2], edge - 1, 0))
    return left + sums[1] + right


def own_first(r, edge, half, b):
    per = half // edge
    return pl.multiple_of(jnp.where(r // per == b, 0, half) + (r % per) * edge, edge)


def ffn_mid(
    w, where, hv, hg, halo_v, halo_g, taps, cot, gate, d2, u2,
    gated_out, gcv_out, gcg_out, gffn_out, gl_out, lat_out, down_out, edge_out, mine, away, bv, bg, gg, acc,
):
    h = pl.program_id(0)
    b, c = where[0], where[1]
    n = hv.shape[1]
    half = n // 2
    edge = halo_v.shape[1]

    @pl.when(h == 0)
    def first():
        gffn_out[...] = (gate[...] * cot[...].astype(f32)).astype(bf16)
        gl_out[...] = mm(gffn_out[...], u2[...], 1, 1)

    fill_grid(bv, hv[0], halo_v[0], b, c)
    fill_grid(bg, hg[0], halo_g[0], b, c)
    weight = w[0].take(h)
    gg[...] = mm(gffn_out[...], weight) + mm(two(gl_out[...]), d2[0], 1, 1)

    def row(r, carry):
        v = conv_row(bv, taps[0, 0], r, edge, False)
        g = conv_row(bg, taps[0, 1], r, edge, False)
        sig = sigmoid(g)
        act = g * sig
        at = pl.ds(own_first(r, edge, half, b), edge)
        gated_out[0, at, :] = (v * act).astype(bf16)
        grad = gg[at, :]
        gcv_out[0, at, :] = (grad * act).astype(bf16)
        gcg_out[0, at, :] = (grad * v * (sig * (1.0 + g * (1.0 - sig)))).astype(bf16)
        return carry

    lax.fori_loop(0, n // edge, row, 0)
    at = edge_rows(where, n, edge)
    edge_out[0, 0] = gcv_out[0, at, :]
    edge_out[0, 1] = gcg_out[0, at, :]
    gated = gated_out[0]
    down_out[0] = mm(two(gl_out[...]), gated, 0, 0)
    part = mm(gated, weight, 1, 1)
    lat = mm(gated, d2[0])

    @pl.when(h == 0)
    def start():
        acc[...] = part
        lat_out[...] = lat

    @pl.when(h == 1)
    def end():
        total = lat_out[...] + lat
        lat_out[...] = total
        full = acc[...] + part + mm(two(total), u2[...])
        put(mine, everything, full[:half])
        put(away, everything, full[half:])


def ffn_back(
    w, where, gcv, gcg, halo, taps, pv, pg, lat, d2, uv, ug,
    gpv_out, gpg_out, up_out, gl_out, mine, away, bv, bg, acc,
):
    h = pl.program_id(0)
    b, c = where[0], where[1]
    n = gcv.shape[1]
    half = n // 2
    edge = halo.shape[2]
    fill_grid(bv, gcv[0], halo[0, 0], b, c)
    fill_grid(bg, gcg[0], halo[0, 1], b, c)

    def row(r, carry):
        at = pl.ds(own_first(r, edge, half, b), edge)
        for i, (buf, pre, out) in enumerate(((bv, pv, gpv_out), (bg, pg, gpg_out))):
            grad = conv_row(buf, taps[0, i], r, edge, True)
            s = pre[0, at, :]
            sig = sigmoid(s)
            out[0, at, :] = (grad * (sig * (1.0 + s * (1.0 - sig)))).astype(bf16)
        return carry

    lax.fori_loop(0, n // edge, row, 0)
    gpv, gpg = gpv_out[0], gpg_out[0]
    part = mm(jnp.concatenate([gpv, gpg], axis=1), w[0].take(h), 1, 1)
    gl = mm(gpv, uv[0], 1, 1) + mm(gpg, ug[0], 1, 1)
    pair = two(lat[...])
    up_out[0, 0] = mm(pair, gpv, 0, 0)
    up_out[0, 1] = mm(pair, gpg, 0, 0)

    @pl.when(h == 0)
    def start():
        acc[...] = part
        gl_out[...] = gl

    @pl.when(h == 1)
    def end():
        total = gl_out[...] + gl
        gl_out[...] = total
        full = acc[...] + part + mm(two(total), d2[...], 1, 1)
        put(mine, everything, full[:half])
        put(away, everything, full[half:])


def cross_bwd(
    w, go, gt, kv, live, owned, qd2, qu2, cd2, cu2, qo, qt, lo, lt,
    gq_out, gkv_out, qgl_out, cgl_out, mine, away, gm, gqs,
):
    half = go.shape[0]
    width = qo.shape[1]
    w[0].take(0)
    depth = cu2.shape[1]
    weight = w[0].columns(0, width, width)
    scale = HD ** (-0.5)
    hidden_text = jnp.where(live[...] > 0.0, 0.0, masked_score)
    for i, (rows, query, lse) in enumerate(((go, qo, lo), (gt, qt, lt))):
        at = slice(i * half, (i + 1) * half)
        gl = mm(rows[:, :depth], cu2[...], 1, 1)
        cgl_out[at, :] = gl
        grad = mm(rows[:, :depth], weight) + mm(two(gl), cd2[...], 1, 1)
        gm[...] = (grad * owned[...]).astype(bf16)
        for first, size in lane_groups(width):
            cols = slice(first, first + size)
            q_all, g_all = query[:, cols], gm[:, cols]
            grad_q, grad_k, grad_v = 0.0, 0.0, 0.0
            for j in range(size // HD):
                key, val = only_head(kv[0, :, cols], j), only_head(kv[1, :, cols], j)
                h = first // HD + j
                scores = mm(key, q_all, 1, 1) * (scale * LOG2E) + hidden_text
                probs = jnp.exp2(scores - lse[h : h + 1, :] * LOG2E)
                grad_p = mm(val, g_all, 1, 1)
                grad_v = grad_v + mm(probs.astype(bf16), only_head(g_all, j))
                inner = jnp.sum(probs * grad_p, axis=0, keepdims=True)
                grad_s = (probs * (grad_p - inner)).astype(bf16)
                grad_q = grad_q + mm(grad_s, key, 0, 0)
                grad_k = grad_k + mm(grad_s, only_head(q_all, j))
            gqs[at, cols] = grad_q
            for side, new in ((0, grad_k * scale), (1, grad_v)):
                gkv_out[side, :, cols] = new if i == 0 else gkv_out[side, :, cols] + new
    gq = (gqs[...] * scale).astype(bf16)
    gq_out[...] = gq
    gl = mm(gq, qu2[...], 1, 1)
    qgl_out[...] = gl
    pair = two(gl)
    total = mm(gq, w[0].columns(0, 0, width), 1, 1) + mm(pair, qd2[...], 1, 1)
    put(mine, everything, total[:half])
    put(away, everything, total[half:])


def linear_bwd(
    w, go, gt, q, st1, st2, ratio, den, owned, d2, u2, gq_out, gl_out, st_out, gh,
):
    half = go.shape[0]
    width = q.shape[1]
    depth = u2.shape[1]
    w[0].take(0)
    weight = w[0].columns(0, width, width)
    for i, rows in enumerate((go, gt)):
        at = pl.ds(i * half, half)
        gl = mm(rows[:, :depth], u2[...], 1, 1)
        gl_out[at, :] = gl
        gh[at, :] = (mm(rows[:, :depth], weight) + mm(two(gl), d2[...], 1, 1)) * owned[...]
    st = st1[...] + st2[...]
    grad = gh[...]
    inverse = 1.0 / den[...]
    numer = grad * inverse
    grad_den = -head_total(grad * ratio[...]) * inverse
    raw = q[...]
    queries = jnp.maximum(raw, 0.0)
    grad_q = head_product(numer, st[:HD], 0) + grad_den * st[HD : HD + 1]
    gq_out[...] = jnp.where(raw > 0.0, grad_q, 0.0).astype(bf16)
    st_out[:HD, :] = head_outer(numer, queries)
    total = jnp.sum(grad_den * queries, axis=0, keepdims=True)
    st_out[HD:, :] = jnp.broadcast_to(total, (8, width))


def linear_end(
    w, gq, k, v, st1, st2, d2, u2, gk_out, gv_out, gl_out, mine, away,
):
    width = k.shape[1]
    half = mine.shape[0]
    st = st1[...] + st2[...]
    raw = k[...]
    grad_k = head_product(v[...], st[:HD], 0) + st[HD : HD + 1]
    gk_out[...] = jnp.where(raw > 0.0, grad_k, 0.0).astype(bf16)
    gv_out[...] = head_product(jnp.maximum(raw, 0.0), st[:HD], 1).astype(bf16)
    grads = (gq, gk_out, gv_out)
    gl = sum(mm(g[...], u2[i], 1, 1) for i, g in enumerate(grads))
    gl_out[...] = gl
    pair = two(gl)
    w[0].take(0)
    w[0].take(1)
    both = jnp.concatenate([gq[...], gk_out[...]], axis=1)
    total = mm(both, w[0].columns(0, 0, 2 * width), 1, 1) + mm(gv_out[...], w[0].columns(1, 0, width), 1, 1)
    total = total + mm(pair, d2[...], 1, 1)
    put(mine, everything, total[:half])
    put(away, everything, total[half:])


def in_steps(rows, body, step=64):
    def one(i, carry):
        body(pl.ds(pl.multiple_of(i * step, step), step))
        return carry

    lax.fori_loop(0, rows // step, one, 0)


def slope_of_norm(values, grad):
    normed, inverse = row_stats(values)
    return inverse * (
        grad
        - jnp.mean(grad, axis=-1, keepdims=True)
        - normed * jnp.mean(grad * normed, axis=-1, keepdims=True)
    )


def total_of(low, got, at, width):
    return low[at, :width].astype(f32) + got[at, :width].astype(f32)


def end_attn(low, got, x, mods, after_out, own_out):
    def body(at):
        after = x[at, :].astype(f32) + mods[2:3, :] * total_of(low, got, at, x.shape[1])
        after_out[at, :] = after
        put(own_out, at, after)

    in_steps(x.shape[0], body)


def end_cross(low, got, before, mods, after_out, own_out):
    def body(at):
        after = before[at, :] + total_of(low, got, at, before.shape[1])
        after_out[at, :] = after
        normed, unused = row_stats(after)
        put(own_out, at, normed * (1.0 + mods[4:5, :]) + mods[3:4, :])

    in_steps(before.shape[0], body)


def end_output(low, got, before, mods, out):
    def body(at):
        put(out, at, before[at, :] + mods[5:6, :] * total_of(low, got, at, before.shape[1]))

    in_steps(before.shape[0], body)


def end_ffn_back(low, got, after, cot, mods, grad_out, own_out):
    def body(at):
        grad = total_of(low, got, at, after.shape[1]) * (1.0 + mods[4:5, :])
        grad = cot[at, :].astype(f32) + slope_of_norm(after[at, :], grad)
        grad_out[at, :] = grad
        put(own_out, at, grad)

    in_steps(after.shape[0], body)


def end_cross_back(low, got, before, mods, grad_out, own_out):
    def body(at):
        grad = before[at, :] + total_of(low, got, at, before.shape[1])
        grad_out[at, :] = grad
        put(own_out, at, mods[2:3, :] * grad)

    in_steps(before.shape[0], body)


def end_attn_back(low, got, before, x, mods, out):
    def body(at):
        grad = total_of(low, got, at, before.shape[1]) * (1.0 + mods[1:2, :])
        put(out, at, before[at, :] + slope_of_norm(x[at, :].astype(f32), grad))

    in_steps(before.shape[0], body)


def place_rows(where, own, other, out):
    width = out.shape[2]
    out[where[0]] = own[:, :width]
    out[1 - where[0]] = other[:, :width]


def fold(both):
    half = both.shape[0] // 2
    return both[:half] + both[half:]


def turned(v, b):
    half = v.shape[1] // 2
    return jnp.where(b == 0, v, jnp.concatenate([v[:, half:], v[:, :half]], axis=1))


def thin_sum(latent, *rows):
    high = latent.astype(bf16).astype(f32)
    both = jnp.concatenate([high, latent - high], axis=0).astype(bf16)
    total, at = None, 0
    for values in rows:
        size = values.shape[0]
        term = mm(both[:, at : at + size], values[...])
        total = term if total is None else total + term
        at += size
    return fold(total)


def outer_sum(latent, *rows):
    total, at = None, 0
    pair = two(latent)
    for values in rows:
        size = values.shape[0]
        term = mm(pair[at : at + size], values[...], 0, 0)
        total = term if total is None else total + term
        at += size
    return fold(total)


def set_segments(out, segments, width):
    for i, v in enumerate(segments):
        put(out.at[:, i * width : (i + 1) * width], everything, v)


def set_ranks(out, first, pad, values):
    rows = out.shape[1]
    for t in range(out.shape[0]):
        put(out.at[t, :, first : first + pad], everything, values[t * rows : (t + 1) * rows])


def pack_first(where, point, up, l0, l1, l2, l3, sums):
    pieces = [point[0], point[1]] + [up[h, p] for p in range(2) for h in range(2)]
    n = l0.shape[0]
    rank = sums.shape[0] * sums.shape[1]
    first = sums.shape[2] - 4 * n
    pad = first // 6
    for i, v in enumerate(pieces):
        set_ranks(sums, i * pad, pad, fold(v))
    for i, v in enumerate((l0, l1, l2, l3)):
        set_ranks(sums, first + i * n, n, turned(v[...].T[:rank], where[0]))


def to_blocks(home, first, table):
    blocks = home.shape[0]
    size = table.shape[1] // blocks
    rows = table.shape[0]
    for i in range(blocks):
        home[i, first : first + rows, :size] = table[:, i * size : (i + 1) * size]


def set_mark(where, home, last):
    home[:, :, last:] = jnp.zeros((home.shape[0], home.shape[1], 1), f32) + where[2].astype(f32)


def second_sums(
    where, sums, gco, gct, fo, ft, gffn, mixo, mixt, cgl, qlat, gq, qgl, gkv, ggot, klat, ku2,
    home_out, projs, out, home,
):
    n, depth = gffn.shape
    b = where[0]
    first = sums.shape[2] - 4 * n
    parts = []
    for i in range(4):
        at = slice(first + i * n, first + (i + 1) * n)
        parts.append(turned(sums[0, :, at] + sums[1, :, at] + sums[2, :, at] + sums[3, :, at], b))
    projs[...] = parts[0]
    rows = parts[0].shape[0]
    home[...] = jnp.zeros(home.shape, f32)
    to_blocks(home, 0, thin_sum(parts[1], gco, gct)[:, :depth])
    to_blocks(home, rows, thin_sum(parts[2], gffn))
    to_blocks(home, 2 * rows, thin_sum(parts[3], fo, ft)[:, :depth])
    size = home.shape[2] - 1
    pad, hh = first // 6, size * home.shape[0] // 8
    for j in range(3):
        for i in range(home.shape[0]):
            t, h, at = i * size // (2 * hh), i * size % (2 * hh) // hh, i * size % hh
            at += (2 * j + h) * pad
            home[i, (3 + j) * rows : (4 + j) * rows, :size] = sums[t, :, at : at + size]
    set_mark(where, home, size)
    home_out[...] = home[...].astype(home_out.dtype)
    here = ggot.shape[1]
    gk = (gkv[0, :here, :] + ggot[0]).astype(bf16)
    gv = (gkv[1, :here, :] + ggot[1]).astype(bf16)
    segments = [outer_sum(cgl[...], mixo, mixt), outer_sum(qlat[...], gq)]
    segments += [outer_sum(klat[...], gk), outer_sum(klat[...], gv)]
    pad = -(-gq.shape[1] // LANES) * LANES
    set_segments(out, segments, pad)
    rank = out.shape[0]
    out[:, 4 * pad : 4 * pad + n] = turned(qgl[...].T[:rank], b)
    kvgl = mm(gk, ku2[0], 1, 1) + mm(gv, ku2[1], 1, 1)
    put(out.at[:, 4 * pad + n :], everything, kvgl.T[:rank])


def third_sums(where, before, pgl, mixed, qlat, gq, gk, gv, qgl, out):
    rank, first = before.shape
    set_ranks(out, 0, first, before[...])
    segments = [outer_sum(pgl[...], mixed)] + [outer_sum(qlat[...], g) for g in (gq, gk, gv)]
    pad = -(-gq.shape[1] // LANES) * LANES
    for i, v in enumerate(segments):
        set_ranks(out, first + i * pad, pad, v)
    set_ranks(out, first + 4 * pad, qgl.shape[0], turned(qgl[...].T[:rank], where[0]))


def last_sums(ranges, where, sums, projs, gao, gat, xo, xt, cap, a, home_out, home):
    n, depth = a.shape
    b = where[0]
    text = -(-cap.shape[0] // LANES) * LANES
    pad = (sums.shape[2] - 2 * n - text) // 8
    second = 4 * pad + n + text
    rows = projs.shape[0]

    def summed(first, size):
        return sum(sums[t, :, first : first + size].astype(f32) for t in range(sums.shape[0]))

    def heads(first):
        parts = [sums[t, :, first + s * HD : first + (s + m) * HD] for t, (s, m) in enumerate(ranges)]
        return jnp.concatenate([v.astype(f32) for v in parts], axis=1)

    tables = [
        thin_sum(turned(summed(4 * pad, n), b), xo, xt)[:, :depth],
        thin_sum(summed(4 * pad + n, cap.shape[0]), cap)[:, :depth],
        thin_sum(projs[...], gao, gat)[:, :depth],
    ]
    tables += [heads(j * pad) for j in range(4)] + [heads(second + j * pad) for j in range(4)]
    tables.append(thin_sum(turned(summed(second + 4 * pad, n), b), a))
    for j, table in enumerate(tables):
        to_blocks(home, j * rows, table)
    set_mark(where, home, home.shape[2] - 1)
    home_out[...] = home[...].astype(home_out.dtype)


def adapter_tables(got, out):
    last = got.shape[2] - 1
    for i in range(out.shape[0]):
        total = None
        for s in range(got.shape[0]):
            values = got[s].astype(f32)
            term = jnp.where(values[:1, last:] == float(i), values, 0.0)
            total = term if total is None else total + term
        out[i] = total


def ring_order(n):
    return list(range(0, n, 2)) + list(range(n - 1 - n % 2, 0, -2))


def ring_pairs(n):
    order = ring_order(n)
    return [(order[i], order[(i + 1) % n]) for i in range(n)]


def ring_source(n, step):
    z = lax.axis_index(W)
    place = jnp.where(z % 2 == 0, z // 2, n - 1 - z // 2)
    from_place = (place - step + n) % n
    return jnp.where(2 * from_place < n, 2 * from_place, 2 * (n - 1 - from_place) + 1)


def swap_pairs(n, distance):
    return [(i, i ^ distance) for i in range(n)]


def across(values, axis, distance=1):
    return lax.ppermute(values, axis, swap_pairs(lax.axis_size(axis), distance))


class Stream:
    def __init__(self, order):
        self.n = lax.axis_size(W)
        self.order = list(order)
        self.own, self.got, self.crossed = {}, {}, {}
        self.flying, self.crossing = [], []

    def launch(self):
        while self.order and (not self.flying or len(self.flying) < 2 and self.order[0][1] == 1):
            name, step = self.order[0]
            if step == 1 and name in self.own:
                moving = self.own[name][0]
            elif (name, step - 1) in self.got:
                moving = self.got[name, step - 1]
            else:
                break
            self.order.pop(0)
            self.flying.append((name, step, lax.ppermute(moving, W, ring_pairs(self.n))))

    def fence(self, values, take=1, cross=None):
        done, self.flying = self.flying[:take], self.flying[take:]
        count = len(self.crossing) if cross is None else cross
        crossed, self.crossing = self.crossing[:count], self.crossing[count:]
        leaves, tree = jax.tree.flatten((values, [d[2] for d in done], [d[2] for d in crossed]))
        values, arrived, over = jax.tree.unflatten(tree, lax.optimization_barrier(leaves))
        for d, v in zip(crossed, over):
            self.crossed[d[0], d[1]] = v
        for d, v in zip(done, arrived):
            self.got[d[0], d[1]] = v
            self.crossing.append((d[0], d[1], across(v, C)))
        self.launch()
        return values

    def fences(self, count, values):
        for i in range(count * (self.n - 1) // 3):
            values = self.fence(values)
        return values

    def ready(self, names, values):
        while not all((name, self.n - 1) in self.crossed for name in names):
            values = self.fence(values)
        return values

    def pieces(self, name):
        steps = range(1, self.n)
        mine = [self.own[name][0]] + [self.got[name, s] for s in steps]
        other = [self.own[name][1]] + [self.crossed[name, s] for s in steps]
        rows = mine[0].shape[0]
        if rows % 16 == 0:
            return mine + other
        c = lax.axis_index(C)
        buf = jnp.zeros((2, self.n * rows, mine[0].shape[1]), bf16)
        for s in range(self.n):
            at = ring_source(self.n, s) * rows
            buf = lax.dynamic_update_slice(buf, mine[s][None], (c, at, 0))
            buf = lax.dynamic_update_slice(buf, other[s][None], (1 - c, at, 0))
        return [buf]


class Weight:
    def __init__(self, meta, pieces, buf, sems, halves):
        self.meta, self.pieces, self.buf, self.sems, self.halves = meta, pieces, buf, sems, halves

    def copies(self, j, pieces):
        rows = pieces[0].shape[0]
        return [
            pltpu.make_async_copy(
                piece,
                self.buf.at[j, pl.ds(pl.multiple_of(self.meta[1 + k] * rows, rows), rows), :],
                self.sems.at[j, k],
            )
            for k, piece in enumerate(pieces)
        ]

    def start(self):
        count = len(self.pieces) // 2
        for j, half in enumerate(self.halves):
            if not count:
                pltpu.make_async_copy(self.pieces[0].at[half], self.buf.at[j], self.sems.at[j, 0]).start()
                continue

            @pl.when(self.meta[0] == half)
            def mine():
                for copy in self.copies(j, self.pieces[:count]):
                    copy.start()

            @pl.when(self.meta[0] != half)
            def other():
                for copy in self.copies(j, self.pieces[count:]):
                    copy.start()

    def take(self, j):
        count = len(self.pieces) // 2
        if not count:
            pltpu.make_async_copy(self.pieces[0].at[0], self.buf.at[j], self.sems.at[j, 0]).wait()
        else:
            for copy in self.copies(j, self.pieces[:count]):
                copy.wait()
        return self.buf[j]

    def columns(self, j, first, size):
        return self.buf[j, :, first : first + size]


def per_step(a):
    zeros = (0,) * (a.ndim - 1)
    return pl.BlockSpec((1,) + tuple(a.shape[1:]), lambda h: (h,) + zeros)


def half_block(i):
    def spec(a):
        zeros = (0,) * (len(a.shape) - 1)
        return pl.BlockSpec((1,) + tuple(a.shape[1:]), lambda *g: (i,) + zeros)

    return spec


def row_block(a):
    return pl.BlockSpec((a.shape[0] // 2, a.shape[1]), lambda i: (i, 0))


def both_blocks(a):
    return pl.BlockSpec((2, a.shape[1] // 2, a.shape[2]), lambda i: (0, i, 0))


def all_of(a):
    zeros = (0,) * len(a.shape)
    return pl.BlockSpec(tuple(a.shape), lambda *g: zeros)


def scalars(a):
    return pl.BlockSpec(memory_space=pltpu.SMEM)


def anywhere(a):
    return pl.BlockSpec(memory_space=pl.ANY)


def run(kernel, ins, outs, scratch=(), steps=1, weights=(), meta=None, same=()):
    args, specs = [], []
    if weights:
        args.append(meta)
        specs.append(scalars(meta))
    counts, extra = [], []
    for pieces, halves in weights:
        counts.append((len(pieces), halves))
        args += pieces
        specs += [anywhere(p) for p in pieces]
        rows = pieces[0].shape[0] * len(pieces) // 2 if len(pieces) > 1 else pieces[0].shape[1]
        extra.append(pltpu.VMEM((len(halves), rows, pieces[0].shape[-1]), bf16))
        extra.append(pltpu.SemaphoreType.DMA((len(halves), max(len(pieces) // 2, 1))))
    first = len(args)
    for item in ins:
        a, spec = item if isinstance(item, tuple) else (item, all_of)
        args.append(a)
        specs.append(spec(a))
    shapes, out_specs = [], []
    for item in outs:
        dims, dtype, spec = item if len(item) == 3 else item + (all_of,)
        shapes.append(shape(dims, dtype))
        out_specs.append(spec(shapes[-1]))

    def body(*refs):
        if not weights:
            return kernel(*refs)
        at, loaders = 1, []
        tail = refs[len(refs) - len(extra) :]
        for i, (count, halves) in enumerate(counts):
            loaders.append(Weight(refs[0], refs[at : at + count], tail[2 * i], tail[2 * i + 1], halves))
            at += count

        @pl.when(pl.program_id(0) == 0)
        def begin():
            for loader in loaders:
                loader.start()

        kernel(loaders, *refs[first : len(refs) - len(extra)])

    return pl.pallas_call(
        body,
        grid=(steps,),
        in_specs=specs,
        out_specs=out_specs,
        out_shape=shapes,
        input_output_aliases={first + i: j for i, j in same},
        scratch_shapes=list(scratch) + extra,
        compiler_params=big,
    )(*args)


def twice(table, axis):
    return jnp.concatenate([table, table], axis=axis)


def slot_layout(groups, rank, heads):
    per, left = heads // groups, heads % groups
    slots = per + (1 if left else 0)
    own_start = rank * per + jnp.minimum(rank, left)
    own_count = per + jnp.where(rank < left, 1, 0)
    first = jnp.minimum(own_start, heads - slots)
    slot = first + jnp.arange(slots, dtype=jnp.int32)
    owned = ((slot >= own_start) & (slot < own_start + own_count)).astype(f32)
    return slots, first, owned


def slot_ranges(groups, heads):
    per, left = heads // groups, heads % groups
    slots = per + (1 if left else 0)
    out = []
    for rank in range(groups):
        own_start = rank * per + min(rank, left)
        count = per + (1 if rank < left else 0)
        out.append((own_start - min(own_start, heads - slots), count))
    return out


def shards(
    tokens, caption, caption_lengths, adapter_index, modulation, cotangent,
    qkv_weight, proj_weight, cross_q_weight, cross_kv_weight, cross_out_weight,
    inverted_weight, depth_weight, point_weight,
    qkv_down, qkv_up, proj_down, proj_up, query_down, query_up, kv_down, kv_up,
    cross_down, cross_up, inverted_down, inverted_up, point_down, point_up,
):
    grid_rows, grid_cols, D = tokens.shape[1:]
    n = grid_rows * grid_cols
    half = n // 2
    heads = D // HD
    groups = lax.axis_size(T)
    rank = lax.axis_index(T)
    c = lax.axis_index(C)
    b = rank % 2
    adapters, R = qkv_up.shape[:2]
    slots, slot_first, owned = slot_layout(groups, rank, heads)
    width = slots * HD
    col = slot_first * HD
    owned = jnp.repeat(owned, HD)[None]
    hid = inverted_weight.shape[2]
    hh = hid // 2
    hid_first = rank * hid
    index = adapter_index[0]
    where = jnp.stack([b, c, index]).astype(jnp.int32)

    def cut(table, start, size, axis):
        return lax.dynamic_slice_in_dim(table, start, size, axis)

    def pick(table):
        return lax.dynamic_index_in_dim(table, index, 0, keepdims=False)

    def own_rows(rows):
        own = cut(rows, b * half, half, 0)
        return own, jnp.concatenate([own, cut(rows, (1 - b) * half, half, 0)])

    def pair_of(first, second):
        return [jnp.where(c == 0, first, second), jnp.where(c == 0, second, first)]

    def taken(table, middle, start, size):
        return lax.dynamic_slice(table, (0, middle, start), (table.shape[0], 1, size))[:, 0]

    def beside(*values):
        return jnp.concatenate(values, axis=1)

    def both(table, start, size=width):
        return beside(taken(table, 0, start, size), taken(table, 1, start, size))

    size = lax.axis_size(W)
    order = [(name, step) for name in ("ab", "cd", "vg", "p") for step in range(1, size)]
    stream = Stream(order)
    fences = stream.fences

    def front_side(c):
        key, out = taken(qkv_weight, 1, col, width), cut(proj_weight, col, width, 0).T
        return beside(taken(qkv_weight, 2 * c, col, width), jnp.where(c == 0, key, out))

    stream.own["ab"] = [front_side(c), None]
    c_late, caption, stream.own["ab"][0] = lax.optimization_barrier((c, caption, stream.own["ab"][0]))
    stream.own["ab"][1] = front_side(1 - c_late)
    stream.launch()
    mods = modulation[0]
    low_tokens = tokens.reshape(n, D)
    x_low, x_rows = own_rows(low_tokens)
    qd2, qu2 = twice(pick(qkv_down), 1), twice(cut(pick(qkv_up), col, width, 2), 0).transpose(1, 0, 2)
    pd2, pu2 = twice(cut(pick(proj_down), col, width, 0), 1), twice(pick(proj_up), 0)
    text_here = caption.shape[1]
    text_rows = -(-text_here // 16) * 16
    padded = -(-D // LANES) * LANES
    cap = jnp.pad(caption[0], ((0, text_rows - text_here), (0, padded - D)))
    cap_other = across(cap, C)
    tables = [query_down, query_up, kv_down, kv_up, cross_down, cross_up]
    tables_f = [inverted_down, inverted_up, point_down, point_up, depth_weight]
    raw = [cross_kv_weight, cross_q_weight, cross_out_weight]
    raw_f = [inverted_weight, point_weight]
    raw, raw_f, tables, tables_f, cap, cap_other, cotangent = fences(
        1, (raw, raw_f, tables, tables_f, cap, cap_other, cotangent)
    )
    pair_cd = pair_of(both(raw[0], col), beside(cut(raw[1], col, width, 1), cut(raw[2], col, width, 0).T))
    query_down, query_up, kv_down, kv_up, cross_down, cross_up = tables
    cd2 = twice(cut(pick(cross_down), col, width, 0), 1)
    cu2 = twice(pick(cross_up), 0)
    xd2, xu2 = twice(pick(query_down), 1), twice(cut(pick(query_up), col, width, 1), 0)
    kd2, ku2 = twice(pick(kv_down), 1), twice(cut(pick(kv_up), col, width, 2), 0).transpose(1, 0, 2)
    front = [x_low, x_rows, qd2, qu2, pd2, pu2, stream.own["ab"][1]]
    pair_cd, raw_f, tables_f, cotangent, front = fences(1, (pair_cd, raw_f, tables_f, cotangent, front))
    stream.own["cd"] = pair_cd
    x_low, x_rows, qd2, qu2, pd2, pu2, stream.own["ab"][1] = front
    pair_vg = [both(raw_f[0], i * hh, hh) for i in (c, 1 - c)]
    pair_p = [cut(raw_f[1], i * hh, hh, 0).T for i in (c, 1 - c)]
    pair_vg, pair_p, tables_f, cotangent = fences(1, (pair_vg, pair_p, tables_f, cotangent))
    stream.own.update(vg=pair_vg, p=pair_p)
    inverted_down, inverted_up, point_down, point_up, depth_weight = tables_f
    fd2, fu2 = twice(pick(inverted_down), 1), twice(cut(pick(inverted_up), hid_first, hid, 2), 0)
    fu2 = fu2.reshape(2 * R, 2, 2, hh).transpose(1, 2, 0, 3)
    od2 = twice(cut(pick(point_down), hid_first, hid, 0), 1).reshape(2, hh, 2 * R)
    ou2 = twice(pick(point_up), 0)
    taps = depth_weight.astype(f32).reshape(9, 2, 2, hh).transpose(2, 1, 0, 3)
    cot_low, cot = own_rows(cotangent.reshape(n, D))
    places = jnp.arange(text_rows)
    live = jnp.concatenate([c * text_here + places, (1 - c) * text_here + places])
    live = (live < caption_lengths[0]) & (jnp.concatenate([places, places]) < text_here)
    live = live.astype(f32)[None]
    tables = [cd2, cu2, xd2, xu2, kd2, ku2, fd2, fu2[0], fu2[1], od2, ou2, taps, cot_low, cot, live]
    x_rows, tables = stream.ready(["ab"], (x_rows, tables))
    cd2, cu2, xd2, xu2, kd2, ku2, fd2, fuv, fug, od2, ou2, taps, cot_low, cot, live = tables

    w_ab = stream.pieces("ab")
    meta = jnp.stack([c] + [ring_source(size, s) for s in range(size)]).astype(jnp.int32)
    rows_bf = ((n, D), bf16)
    thin = ((n, 2 * R), f32)
    wide = ((n, width), f32)
    wide_bf = ((n, width), bf16)
    pair = [((half, padded), bf16)] * 2
    ended = [((half, D), f32, row_block), ((half, padded), bf16, row_block)]

    def finish_rows(kernel, arrays, outs):
        return run(kernel, [(v, row_block) for v in arrays] + [mods], outs, steps=2)

    state_of = ((HD + 8, width), f32)
    attn_in, q_raw, k_raw, qkv_lat = run(
        attn_front, [x_rows, mods, qd2, qu2], [rows_bf, wide, wide, thin], weights=[(w_ab, (0,))], meta=meta,
    )
    v_raw, st_own = run(
        attn_state, [attn_in, k_raw, qkv_lat, qu2], [wide, state_of], weights=[(w_ab, (1,))], meta=meta,
    )
    st_own, st_other = fences(1, (st_own, across(st_own, C)))
    ratio, denom, mixed, proj_lat, mine, away = run(
        attn_back, [q_raw, st_own, st_other, owned, pd2, pu2], [wide, wide, wide_bf, thin] + pair,
        weights=[(w_ab, (1,))], meta=meta,
    )

    def exchanged(mine, away, pace=lambda low: low):
        low, distance = (mine.astype(f32) + across(away, T).astype(f32)).astype(bf16), 2
        while True:
            low = pace(low)
            got = across(low, T, distance)
            distance *= 2
            if distance >= groups:
                return low, got
            low = (low.astype(f32) + got.astype(f32)).astype(bf16)

    def while_streaming(mine, away):
        return exchanged(mine, away)

    mine, away = fences(1, (mine, away))
    low, got = fences(1, while_streaming(mine, away))
    after_attn, cross_own = finish_rows(end_attn, [low, got, x_low], ended)
    cross_other = across(cross_own, T)

    cap, cross_own, cross_other, after_attn = stream.ready(["cd"], (cap, cross_own, cross_other, after_attn))
    w_cd = stream.pieces("cd")
    kv_all, kv_lat = run(
        caption_rows, [cap, cap_other, kd2, ku2], [((2, 2 * text_rows, width), bf16), ((text_rows, 2 * R), f32)],
        weights=[(w_cd, (0,))], meta=meta,
    )
    kv_all, cross_own, cross_other = fences(1, (kv_all, cross_own, cross_other))
    half_bf, half_thin = ((half, width), bf16), ((half, 2 * R), f32)

    def cross_part(rows, kv):
        return run(
            cross_fwd,
            [rows, kv, live, owned, xd2, xu2, cd2, cu2],
            [half_bf, half_bf, half_thin, half_thin, ((LANES, half), f32), ((half, padded), bf16)],
            [pltpu.VMEM((half, LANES), f32)],
            weights=[(w_cd, (1,))], meta=meta,
        )

    *cross_t, away = cross_part(cross_other, kv_all)
    away, cross_tied, kv_tied = lax.optimization_barrier((away, cross_own, kv_all))
    *cross_o, mine = cross_part(cross_tied, kv_tied)
    mine, away = fences(1, (mine, away))
    query, mix, query_lat, cross_lat, lse = zip(cross_o, cross_t)
    low, got = while_streaming(mine, away)
    low, got = stream.fence((stream.fence(low, 1, 0), got), 0, 1)
    after_cross, ffn_own = finish_rows(end_cross, [low, got, after_attn], ended)
    ffn_own, after_cross = stream.fence((ffn_own, after_cross), 1, 1)
    ffn_other = across(ffn_own, T)

    query_lat, cross_lat = jnp.concatenate(query_lat), jnp.concatenate(cross_lat)

    ffn_own, ffn_other, after_cross = stream.ready(["vg"], (ffn_own, ffn_other, after_cross))
    w_vg = stream.pieces("vg")
    hid_bf = ((2, n, hh), bf16, per_step)

    def ffn_part(h, more, same):
        outs = [((2, n, hh), f32)] * 2 + [((2, n, hh), bf16)] * 2 + [((2, grid_cols, hh), bf16)] * 2
        return run(
            functools.partial(ffn_front, h),
            [(where, scalars), ffn_own, ffn_other, fd2, (fuv, half_block(h)), (fug, half_block(h))] + more,
            [out + (half_block(h),) for out in outs] + [thin][h:],
            [pltpu.VMEM((n, D), bf16)],
            weights=[(w_vg, (h,))], meta=meta, same=same,
        )

    *started, inv_lat = ffn_part(0, [], ())
    ffn_own, started, inv_lat = stream.fence((ffn_own, started, inv_lat), 1, 1)
    pre_v, pre_g, hid_v, hid_g, edge_v, edge_g = ffn_part(
        1, [inv_lat] + [(v, anywhere) for v in started], [(7 + i, i) for i in range(6)]
    )
    halo_v, halo_g = across(edge_v, C), across(edge_g, C)
    hid_v, halo_v, halo_g = stream.ready(["p"], (hid_v, halo_v, halo_g))
    w_p = stream.pieces("p")
    grid_buf = pltpu.VMEM((n + 2 * grid_cols, hh), f32)
    row_acc = pltpu.VMEM((n, D), f32)
    gated, gcv, gcg, grad_ffn, point_gl, point_lat, point_down_g, edge, mine, away = run(
        ffn_mid,
        [
            (where, scalars), (hid_v, per_step), (hid_g, per_step), (halo_v, per_step), (halo_g, per_step), (taps, per_step),
            cot, mods[5:6], (od2, per_step), ou2,
        ],
        [hid_bf, hid_bf, hid_bf, rows_bf, thin, thin, ((2, 2 * R, hh), f32, per_step)]
        + [((2, 2, grid_cols, hh), bf16, per_step)] + pair,
        [grid_buf, grid_buf, pltpu.VMEM((n, hh), f32), row_acc],
        2,
        weights=[(w_p, (0, 1))], meta=meta,
    )
    halo = across(edge, C)
    tied = []

    def after_halo(low):
        low, *tied[:] = lax.optimization_barrier((low, halo, gcv, gcg))
        return low

    out_low, out_got = exchanged(mine, away, after_halo)
    halo, gcv, gcg = tied

    gpv, gpg, inv_up_g, inv_gl, mine, away = run(
        ffn_back,
        [
            (where, scalars), (gcv, per_step), (gcg, per_step), (halo, per_step), (taps, per_step),
            (pre_v, per_step), (pre_g, per_step), inv_lat, fd2,
            (fuv, per_step), (fug, per_step),
        ],
        [hid_bf, hid_bf, ((2, 2, 2 * R, hh), f32, per_step), thin] + pair,
        [grid_buf, grid_buf, row_acc],
        2,
        weights=[(w_vg, (0, 1))], meta=meta,
    )
    part_r = R // groups
    blocks = size * lax.axis_size(C)
    ranges = slot_ranges(groups, heads)

    def swapped(sent):
        return lax.all_to_all(sent, T, 0, 0, tiled=True)

    def up_to_tiles(size):
        return -(-size // LANES) * LANES

    def table_rows(table, i, size):
        return table[:, i * part_r : (i + 1) * part_r, : size // blocks]

    def down_rows(table, i, size):
        return table_rows(table, i, size).transpose(0, 2, 1)

    def together(*values):
        return lax.optimization_barrier(values)

    def during(mine, away, inputs, work):
        held = []

        def pace(low):
            low, tied = together(low, inputs)
            held[:] = [tied]
            return low

        low, got = exchanged(mine, away, pace)
        return together(low, got, work(*held[0]))

    def first_work(out_low, out_got, after_cross, inv_up_g, point_down_g, lats):
        (output,) = finish_rows(end_output, [out_low, out_got, after_cross], [((half, padded), f32, row_block)])
        (sums,) = run(
            pack_first, [(where, scalars), point_down_g, inv_up_g, *lats], [((groups, part_r, 6 * up_to_tiles(hh) + 4 * n), f32)],
        )
        return output, sums

    mine, away, out_low, out_got = together(mine, away, out_low, out_got)
    low, got, (output, sums_f) = during(
        mine, away,
        (out_low, out_got, after_cross, inv_up_g, point_down_g, (proj_lat, cross_lat, point_lat, inv_gl)),
        first_work,
    )
    grad_cross, gc_own = finish_rows(end_ffn_back, [low, got, after_cross, cot_low], ended)
    gc_other = across(gc_own, T)

    gc_own, gc_other, output, sums_f = together(gc_own, gc_other, output, sums_f)
    output_other = across(output, T)
    sums_f = swapped(sums_f)
    grad_query, gkv, query_gl, cross_gl, mine, away = run(
        cross_bwd,
        [
            gc_own, gc_other, kv_all, live.T, owned,
            xd2, xu2, cd2, cu2, *query, *lse,
        ],
        [wide_bf, ((2, 2 * text_rows, width), f32), thin, thin] + pair,
        [pltpu.VMEM((half, width), bf16), pltpu.VMEM((n, width), f32)],
        weights=[(w_cd, (1,))], meta=meta,
    )
    mine, away, output_other, sums_f, gkv = together(mine, away, output_other, sums_f, gkv)
    gkv_got = across(gkv[:, text_rows:].astype(bf16), C)

    def in_order(own, other):
        (rows,) = run(
            place_rows, [(where, scalars), (own, row_block), (other, row_block)],
            [((2, half, D), f32, both_blocks)], steps=2,
        )
        return rows.reshape(tokens.shape)

    seg = up_to_tiles(width)

    seg = up_to_tiles(width)
    home_dims = (blocks, 8 * part_r, 4 * 2 * hh // blocks + 1)
    last_dims = (blocks, 12 * part_r, D // blocks + 1)

    def second_work(output, output_other, sums, cross_gl, grad_query, query_gl):
        return [in_order(output, output_other)] + list(run(
            second_sums,
            [
                (where, scalars), sums, gc_own, gc_other, ffn_own, ffn_other, grad_ffn, *mix, cross_gl,
                query_lat, grad_query, query_gl, gkv, gkv_got, kv_lat, ku2,
            ],
            [(home_dims, bf16), ((part_r, n), f32), ((R, 4 * seg + n + up_to_tiles(text_rows)), f32)],
            [pltpu.VMEM(home_dims, f32)],
        ))

    low, got, (output, home, proj_s, sums_c) = during(
        mine, away, (output, output_other, sums_f, cross_gl, grad_query, query_gl), second_work
    )
    grad_after, ga_own = finish_rows(end_cross_back, [low, got, grad_cross], ended)
    ga_other = across(ga_own, T)

    grad_q, proj_gl, sg_own = run(
        linear_bwd,
        [ga_own, ga_other, q_raw, st_own, st_other, ratio, denom, owned, pd2, pu2],
        [wide_bf, thin, state_of],
        [pltpu.VMEM((n, width), f32)],
        weights=[(w_ab, (1,))], meta=meta,
    )
    sg_other = across(sg_own, C)
    grad_k, grad_v, qkv_gl, mine, away = run(
        linear_end,
        [grad_q, k_raw, v_raw, sg_own, sg_other, qd2, qu2],
        [wide_bf, wide_bf, thin] + pair,
        weights=[(w_ab, (0, 1))], meta=meta,
    )

    def third_work(home, sums_c, proj_gl, qkv_gl, grad_q, grad_k, grad_v):
        home = lax.all_to_all(home, (W, C), 0, 0, tiled=True)
        (sums,) = run(
            third_sums, [(where, scalars), sums_c, proj_gl, mixed, qkv_lat, grad_q, grad_k, grad_v, qkv_gl],
            [((groups, part_r, sums_c.shape[1] + 4 * seg + n), f32)],
        )
        return swapped(sums.astype(bf16)), run(adapter_tables, [home], [((adapters,) + home.shape[1:], f32)])[0]

    low, got, (sums, tables) = during(
        mine, away, (home, sums_c, proj_gl, qkv_gl, grad_q, grad_k, grad_v), third_work
    )
    (input_grad,) = finish_rows(end_attn_back, [low, got, grad_after, x_low], [((half, padded), f32, row_block)])
    input_other = across(input_grad, T)
    (last,) = run(
        functools.partial(last_sums, ranges),
        [(where, scalars), sums, proj_s, ga_own, ga_other, cross_own, cross_other, cap, attn_in],
        [(last_dims, bf16)],
        [pltpu.VMEM(last_dims, f32)],
    )
    last = lax.all_to_all(last, (W, C), 0, 0, tiled=True)
    input_grad = in_order(input_grad, input_other)
    last, input_grad = together(last, input_grad)
    (last,) = run(adapter_tables, [last], [((adapters,) + last.shape[1:], f32)])

    def rows_of(i):
        return table_rows(last, i, D)

    return (
        output,
        input_grad,
        down_rows(last, 11, D),
        jnp.stack([rows_of(8), rows_of(9), rows_of(10)], axis=2),
        down_rows(last, 7, D),
        rows_of(2),
        down_rows(last, 0, D),
        rows_of(4),
        down_rows(last, 1, D),
        jnp.stack([rows_of(5), rows_of(6)], axis=2),
        down_rows(last, 3, D),
        table_rows(tables, 0, D),
        down_rows(tables, 2, D),
        jnp.stack([table_rows(tables, i, 8 * hh) for i in (4, 5)], axis=2),
        down_rows(tables, 3, 8 * hh),
        table_rows(tables, 1, D),
    )


def solution(mesh):
    down = P(None, (W, C), T)
    up3 = P(None, T, (W, C))
    up4 = P(None, T, None, (W, C))
    rows = P(W, C)
    return jax.shard_map(
        shards,
        mesh=mesh,
        in_specs=(
            rows, rows, P(W), P(W), P(W), rows,
            P(W), P(None, W), P(W), P(W), P(None, W),
            P(W, None, T), P(None, None, None, T), P(T, W),
        )
        + (P(),) * 14,
        out_specs=(
            rows, rows, down, up4, down, up3, down, up3, down, up4, down, up3, down, up4, down, up3,
        ),
        check_vma=False,
    )
```
